32 devices in a mesh: dp: 8 (over z, y), ctx: 4 (over x, core).
Axes of the slice: x: 2, y: 2, z: 4, core: 2. Of those that a mesh axis runs over, the one named last changes fastest.
Arguments:
- tokens_in: bfloat16 [2, 8, 512, 576], P(None, 'dp', 'ctx'), may hold values from -6 to 6
- places: int32 [2, 8, 512], P(None, 'dp', 'ctx'), may hold values from 0 to 511, as said below
- out_grad: bfloat16 [2, 8, 512, 576], P(None, 'dp', 'ctx')
- weights: float32 [3538944], P(('dp', 'ctx'))
- first_moment: float32 [3538944], P(('dp', 'ctx'))
- second_moment: float32 [3538944], P(('dp', 'ctx')), as said below
- vectors: float32 [2112], replicated
- vector_first: float32 [2112], replicated
- vector_second: float32 [2112], replicated, as said below
Outputs:
- block_out: bfloat16 [2, 8, 512, 576], P(None, 'dp', 'ctx')
- input_grad: bfloat16 [2, 8, 512, 576], P(None, 'dp', 'ctx')
- new_weights: float32 [3538944], P(('dp', 'ctx'))
- new_first: float32 [3538944], P(('dp', 'ctx'))
- new_second: float32 [3538944], P(('dp', 'ctx'))
- new_vectors: float32 [2112], replicated
- new_vector_first: float32 [2112], replicated
- new_vector_second: float32 [2112], replicated
The draws below stay inside these ranges and needn't reach their ends.
Inputs may be any that keep to these rules, and one draw needn't show every extreme that they name: `places`: each sequence holds every position 0 to 511 once; the tokens of one index of ctx are two blocks of 64 consecutive positions in rising order, block p and block 7 - p, with p differing between the indices of ctx of one sequence. `second_moment`: every entry is positive. `vector_second`: every entry is positive.
All inputs are finite; a program needn't handle non-finite values.
Results may differ from the reference program's by a relative error of at most 0.014.
The reference program's roundings to bfloat16 on the way count: a program that leaves them out, or rounds other values in their place, can miss the bound.
Values may be sent and summed in bfloat16 or wider, within the bound.
No kernel may reach another device: no remote copies, remote signals or barrier semaphores. Data moves between devices by JAX's collectives and lax.ppermute only.
A program may use at most 128 MiB of HBM per device.

```python
import math
import jax
import jax.numpy as jnp
from jax import lax

MODEL_WIDTH = 576
QUERY_HEADS = 9
KEY_VALUE_HEADS = 3
HEAD_SIZE = 64
FF = 1536
L = 512
MB = 2
STEP = 10
VEC = 2112
PARAMS = 3538944
SEQS = 8
CTX_ROWS = 128
TOKENS = 8192


BETA_ONE = 0.9


BETA_TWO = 0.95


WEIGHT_GRADS = (0.8, 0.8, 2.0, 0.3, 0.3, 0.35, 0.6)


VECTOR_GRADS = (2.0, 0.5, 0.8, 0.8, 2.0)


def matrix_fill(factors):
    query_width = QUERY_HEADS * HEAD_SIZE
    paired_width = KEY_VALUE_HEADS * HEAD_SIZE
    count_list = (MODEL_WIDTH * query_width, MODEL_WIDTH * paired_width, MODEL_WIDTH * paired_width, query_width * MODEL_WIDTH, MODEL_WIDTH * FF, MODEL_WIDTH * FF, FF * MODEL_WIDTH)
    return jnp.concatenate([jnp.full((number,), factor, jnp.float32) for number, factor in zip(count_list, factors)])


def vector_fill(factors):
    count_list = (MODEL_WIDTH, MODEL_WIDTH, QUERY_HEADS * HEAD_SIZE, KEY_VALUE_HEADS * HEAD_SIZE, KEY_VALUE_HEADS * HEAD_SIZE)
    return jnp.concatenate([jnp.full((number,), factor, jnp.float32) for number, factor in zip(count_list, factors)])


def signed_sizes(key, count):
    key_sign, key_size = jax.random.split(key)
    signs = jnp.where(jax.random.bernoulli(key_sign, 0.5, (count,)), 1.0, -1.0)
    return signs * jax.random.uniform(key_size, (count,), jnp.float32, 0.5, 1.5)


def draw_places(key, part):
    key = jax.random.fold_in(key, 5)
    blocks = L // CTX_ROWS
    half_rows = CTX_ROWS // 2
    keys_gathered = jax.random.split(key, MB * SEQS)
    orders = jax.vmap(lambda subkey: jax.random.permutation(subkey, blocks))(keys_gathered)
    device = (jnp.arange(L) // CTX_ROWS).astype(jnp.int32)
    within = (jnp.arange(L) % CTX_ROWS).astype(jnp.int32)
    paired = orders[:, device]
    span = jnp.where(within < half_rows, paired, 2 * blocks - 1 - paired)
    return (span * half_rows + within % half_rows).astype(jnp.int32).reshape(MB, SEQS, L)


def draw_out_grad(key, part):
    key = jax.random.fold_in(key, 7)
    seq_rank = jnp.arange(SEQS, dtype=jnp.float32) / max(SEQS - 1, 1)
    row_rank = jnp.arange(L, dtype=jnp.float32) / (L - 1)
    noise = jnp.clip(jax.random.normal(key, (MB, SEQS, L, MODEL_WIDTH), jnp.float32), -6.0, 6.0)
    rise = (0.5 + seq_rank)[:, None] * (0.5 + row_rank)[None, :]
    return (noise * rise[None, :, :, None]).astype(jnp.bfloat16)


def draw_weights(key, part):
    key = jax.random.fold_in(key, 11)
    spread = matrix_fill((1.5 / math.sqrt(MODEL_WIDTH), 1.3 / math.sqrt(MODEL_WIDTH), 1.0 / math.sqrt(MODEL_WIDTH), 2.0 / math.sqrt(QUERY_HEADS * HEAD_SIZE), 1.0 / math.sqrt(MODEL_WIDTH), 1.0 / math.sqrt(MODEL_WIDTH), 1.0 / math.sqrt(FF)))
    noise = jax.random.normal(key, (PARAMS,), jnp.float32)
    return noise * spread


def draw_first_moment(key, part):
    key = jax.random.fold_in(key, 13)
    scale = matrix_fill(WEIGHT_GRADS) * math.sqrt(TOKENS) * (1.0 - BETA_ONE) / BETA_ONE
    return signed_sizes(key, PARAMS) * scale


def draw_second_moment(key, part):
    key = jax.random.fold_in(key, 17)
    grad_size = matrix_fill(WEIGHT_GRADS) * math.sqrt(TOKENS)
    factor = jax.random.uniform(key, (PARAMS,), jnp.float32, 1.0, 4.0)
    return factor * grad_size * grad_size * (1.0 - BETA_TWO) / BETA_TWO


def draw_vectors(key, part):
    key = jax.random.fold_in(key, 19)
    key_gain, key_bias = jax.random.split(key)
    gains = jax.random.uniform(key_gain, (2 * MODEL_WIDTH,), jnp.float32, 0.6, 1.4)
    bias_total = QUERY_HEADS * HEAD_SIZE + 2 * KEY_VALUE_HEADS * HEAD_SIZE
    bias_factor = jnp.concatenate([jnp.full((QUERY_HEADS * HEAD_SIZE,), 0.5, jnp.float32), jnp.full((KEY_VALUE_HEADS * HEAD_SIZE,), 0.5, jnp.float32), jnp.full((KEY_VALUE_HEADS * HEAD_SIZE,), 0.3, jnp.float32)])
    biases = jax.random.normal(key_bias, (bias_total,), jnp.float32)
    return jnp.concatenate([gains, biases * bias_factor])


def draw_vector_first(key, part):
    key = jax.random.fold_in(key, 23)
    scale = vector_fill(VECTOR_GRADS) * math.sqrt(TOKENS) * (1.0 - BETA_ONE) / BETA_ONE
    return signed_sizes(key, VEC) * scale


def draw_vector_second(key, part):
    key = jax.random.fold_in(key, 29)
    grad_size = vector_fill(VECTOR_GRADS) * math.sqrt(TOKENS)
    factor = jax.random.uniform(key, (VEC,), jnp.float32, 1.0, 4.0)
    return factor * grad_size * grad_size * (1.0 - BETA_TWO) / BETA_TWO


def block_scale(rng, dims, cuts, low, top_value):
    level, own = 1.0, jax.random.fold_in(rng, 6)
    for position, shards_of in cuts:
        draws = jnp.exp(jax.random.uniform(jax.random.fold_in(own, position), (shards_of,), jnp.float32, low / len(cuts), top_value / len(cuts)))
        level = level * jnp.repeat(draws, dims[position] // shards_of).reshape([-1 if axis == position else 1 for axis in range(len(dims))])
    return level


def normal_values(key, shape, scale, bound, shards=(), kind=jnp.bfloat16):
    drawn = scale * jax.random.normal(key, shape, jnp.float32)
    if shards:
        drawn = drawn * block_scale(key, shape, shards, -0.22, 0.18)
    return jnp.clip(drawn, -bound, bound).astype(kind)


def setup_inputs(seed: int = 0) -> dict:
    splits = jax.random.split(jax.random.key(seed), 10)
    tokens_in = normal_values(splits[0], (MB, SEQS, L, MODEL_WIDTH), 1.0, 6.0, ((1, 8), (2, 4)))
    places = draw_places(jax.random.fold_in(splits[9], 71), 0)
    out_grad = draw_out_grad(jax.random.fold_in(splits[9], 71), 0)
    weights = draw_weights(jax.random.fold_in(splits[9], 71), 0)
    first_moment = draw_first_moment(jax.random.fold_in(splits[9], 71), 0)
    second_moment = draw_second_moment(jax.random.fold_in(splits[9], 71), 0)
    vectors = draw_vectors(jax.random.fold_in(splits[9], 71), 0)
    vector_first = draw_vector_first(jax.random.fold_in(splits[9], 71), 0)
    vector_second = draw_vector_second(jax.random.fold_in(splits[9], 71), 0)
    return {"tokens_in": tokens_in, "places": places, "out_grad": out_grad, "weights": weights, "first_moment": first_moment, "second_moment": second_moment, "vectors": vectors, "vector_first": vector_first, "vector_second": vector_second}


EPS_NORM = 1e-05
THETA = 100000.0
BETA_ONE = 0.9
BETA_TWO = 0.95
EPS_ADAM = 1e-08
RATE_MATRIX = 0.06
RATE_VECTOR = 0.3
DECAY = 0.1
MASKED = -1e+30
HIGHEST = lax.Precision.HIGHEST

@jax.custom_vjp
def low(v):
    return lax.optimization_barrier(v.astype(jnp.bfloat16)).astype(jnp.float32)

@jax.custom_vjp
def low_back(v):
    return v

def low_keep(v):
    return (low(v), None)

def low_pass(kept, grad):
    return (grad,)

def back_keep(v):
    return (v, None)

def back_low(kept, grad):
    return (low(grad),)
low.defvjp(low_keep, low_pass)
low_back.defvjp(back_keep, back_low)

def matmul(left, right):
    return jnp.dot(left, right, precision=HIGHEST)

def split_matrices(flat):
    query_width = QUERY_HEADS * HEAD_SIZE
    paired_width = KEY_VALUE_HEADS * HEAD_SIZE
    shapes = ((MODEL_WIDTH, query_width), (MODEL_WIDTH, paired_width), (MODEL_WIDTH, paired_width), (query_width, MODEL_WIDTH), (MODEL_WIDTH, FF), (MODEL_WIDTH, FF), (FF, MODEL_WIDTH))
    pieces = []
    offset = 0
    for rows_count, cols_count in shapes:
        pieces.append(flat[offset:offset + rows_count * cols_count].reshape(rows_count, cols_count))
        offset += rows_count * cols_count
    return pieces

def split_vectors(flat):
    width_list = (MODEL_WIDTH, MODEL_WIDTH, QUERY_HEADS * HEAD_SIZE, KEY_VALUE_HEADS * HEAD_SIZE, KEY_VALUE_HEADS * HEAD_SIZE)
    pieces = []
    offset = 0
    for size_one in width_list:
        pieces.append(flat[offset:offset + size_one])
        offset += size_one
    return pieces

def rope_tables(place_rows):
    half_dim = HEAD_SIZE // 2
    frequency = THETA ** (-2.0 * jnp.arange(half_dim, dtype=jnp.float32) / HEAD_SIZE)
    angles = place_rows.astype(jnp.float32)[:, None] * frequency[None, :]
    return (jnp.cos(angles), jnp.sin(angles))

def apply_rotation(entries, cosine_table, sine_table, sign):
    half_dim = HEAD_SIZE // 2
    front_half = entries[..., :half_dim]
    back_half = entries[..., half_dim:]
    cos_rows = cosine_table[:, None, :]
    sin_rows = sine_table[:, None, :] * sign
    return jnp.concatenate([front_half * cos_rows - back_half * sin_rows, back_half * cos_rows + front_half * sin_rows], axis=-1)

def block_forward(tok_block, place_block, flat, vec_values):
    w_query, w_key, w_value, w_out, w_gate, w_up, w_down = split_matrices(low(flat))
    gain_one, gain_two, bias_query, bias_key, bias_value = split_vectors(vec_values)
    sequence_count, sequence_length, width = tok_block.shape
    row_number = sequence_count * sequence_length
    group_count = QUERY_HEADS // KEY_VALUE_HEADS
    resid_in = tok_block.reshape(row_number, width)
    normed_one = resid_in * lax.rsqrt(lax.optimization_barrier(jnp.mean(resid_in * resid_in, axis=-1, keepdims=True)) + EPS_NORM)
    hidden_one = low(normed_one * gain_one)
    queries = low_back(matmul(hidden_one, w_query) + bias_query)
    keys_before_rope = low_back(matmul(hidden_one, w_key) + bias_key)
    values_lowered = low(low_back(matmul(hidden_one, w_value) + bias_value))
    cosine_table, sine_table = rope_tables(place_block.reshape(row_number))
    rotated_queries = low(apply_rotation(queries.reshape(row_number, QUERY_HEADS, HEAD_SIZE), cosine_table, sine_table, 1.0))
    rotated_keys = low(apply_rotation(keys_before_rope.reshape(row_number, KEY_VALUE_HEADS, HEAD_SIZE), cosine_table, sine_table, 1.0))
    grouped_queries = rotated_queries.reshape(sequence_count, sequence_length, KEY_VALUE_HEADS, group_count, HEAD_SIZE)
    grouped_keys = rotated_keys.reshape(sequence_count, sequence_length, KEY_VALUE_HEADS, HEAD_SIZE)
    grouped_values = values_lowered.reshape(sequence_count, sequence_length, KEY_VALUE_HEADS, HEAD_SIZE)
    scores = low_back(jnp.einsum('sqhgd,skhd->shgqk', grouped_queries, grouped_keys, precision=HIGHEST) * HEAD_SIZE ** (-0.5))
    allowed = place_block[:, None, None, :, None] >= place_block[:, None, None, None, :]
    scores = jnp.where(allowed, scores, MASKED)
    row_top = lax.optimization_barrier(jnp.max(scores, axis=-1, keepdims=True))
    exponents = jnp.exp(scores - row_top)
    probs = low(exponents / lax.optimization_barrier(jnp.sum(exponents, axis=-1, keepdims=True)))
    attended = jnp.einsum('shgqk,skhd->sqhgd', probs, grouped_values, precision=HIGHEST)
    attended = low(low_back(attended.reshape(row_number, QUERY_HEADS * HEAD_SIZE)))
    branch = low_back(matmul(attended, w_out))
    resid_mid = resid_in + branch
    normed_two = resid_mid * lax.rsqrt(lax.optimization_barrier(jnp.mean(resid_mid * resid_mid, axis=-1, keepdims=True)) + EPS_NORM)
    hidden_two = low(normed_two * gain_two)
    gate_pre = low_back(matmul(hidden_two, w_gate))
    up_pre = low_back(matmul(hidden_two, w_up))
    act_low = low(gate_pre * jax.nn.sigmoid(gate_pre) * up_pre)
    result = resid_mid + matmul(act_low, w_down)
    return result.reshape(sequence_count, sequence_length, width)

def adamw(param, grad, mom_one, mom_two, rate, decay):
    new_one = BETA_ONE * mom_one + (1.0 - BETA_ONE) * grad
    new_two = BETA_TWO * mom_two + (1.0 - BETA_TWO) * grad * grad
    fixed_one = new_one / (1.0 - BETA_ONE ** STEP)
    fixed_two = new_two / (1.0 - BETA_TWO ** STEP)
    new_param = param - rate * (fixed_one / (jnp.sqrt(fixed_two) + EPS_ADAM) + decay * param)
    return (new_param, new_one, new_two)

def reference(tokens_in, places, out_grad, weights, first_moment, second_moment, vectors, vector_first, vector_second):
    group_size = math.gcd(SEQS, max(1, 4096 // L))
    blocks = MB * (SEQS // group_size)

    def one_block(totals, inputs):
        grad_flat, grad_vectors = totals
        tok_block, place_block, cot_block = inputs

        def closed(tok_values, flat, vec_values):
            return block_forward(tok_values, place_block, flat, vec_values)
        result, pullback = jax.vjp(closed, tok_block.astype(jnp.float32), weights, vectors)
        d_tokens, d_flat, d_vectors = pullback(cot_block.astype(jnp.float32))
        return ((grad_flat + d_flat, grad_vectors + d_vectors), (result.astype(jnp.bfloat16), d_tokens.astype(jnp.bfloat16)))
    inputs = (tokens_in.reshape(blocks, group_size, L, MODEL_WIDTH), places.reshape(blocks, group_size, L), out_grad.reshape(blocks, group_size, L, MODEL_WIDTH))
    initial = (jnp.zeros((PARAMS,), jnp.float32), jnp.zeros((VEC,), jnp.float32))
    (grad_flat, grad_vectors), (block_outs, input_grads) = lax.scan(one_block, initial, inputs)
    new_weights, new_first, new_second = adamw(weights, grad_flat, first_moment, second_moment, RATE_MATRIX, DECAY)
    new_vectors, new_vector_first, new_vector_second = adamw(vectors, grad_vectors, vector_first, vector_second, RATE_VECTOR, 0.0)
    return (block_outs.reshape(MB, SEQS, L, MODEL_WIDTH), input_grads.reshape(MB, SEQS, L, MODEL_WIDTH), new_weights, new_first, new_second, new_vectors, new_vector_first, new_vector_second)
```

```python
import jax
import jax.numpy as jnp
from jax import lax
from jax.sharding import PartitionSpec as P

MODEL_WIDTH = 576
QUERY_HEADS = 9
KEY_VALUE_HEADS = 3
HEAD_SIZE = 64
FF = 1536
STEP = 10


EPS_NORM = 1e-05
THETA = 100000.0
BETA_ONE = 0.9
BETA_TWO = 0.95
EPS_ADAM = 1e-08
RATE_MATRIX = 0.06
RATE_VECTOR = 0.3
DECAY = 0.1
MASKED = -1e30


def split_matrices(flat):
    query_width = QUERY_HEADS * HEAD_SIZE
    paired_width = KEY_VALUE_HEADS * HEAD_SIZE
    shapes = (
        (MODEL_WIDTH, query_width),
        (MODEL_WIDTH, paired_width),
        (MODEL_WIDTH, paired_width),
        (query_width, MODEL_WIDTH),
        (MODEL_WIDTH, FF),
        (MODEL_WIDTH, FF),
        (FF, MODEL_WIDTH),
    )
    pieces = []
    offset = 0
    for rows_count, cols_count in shapes:
        pieces.append(
            flat[offset : offset + rows_count * cols_count].reshape(rows_count, cols_count)
        )
        offset += rows_count * cols_count
    return pieces


def split_vectors(flat):
    width_list = (
        MODEL_WIDTH,
        MODEL_WIDTH,
        QUERY_HEADS * HEAD_SIZE,
        KEY_VALUE_HEADS * HEAD_SIZE,
        KEY_VALUE_HEADS * HEAD_SIZE,
    )
    pieces = []
    offset = 0
    for size_one in width_list:
        pieces.append(flat[offset : offset + size_one])
        offset += size_one
    return pieces


def rope_tables(place_rows):
    half_dim = HEAD_SIZE // 2
    frequency = THETA ** (-2.0 * jnp.arange(half_dim, dtype=jnp.float32) / HEAD_SIZE)
    angles = place_rows.astype(jnp.float32)[:, None] * frequency[None, :]
    return (jnp.cos(angles), jnp.sin(angles))


def apply_rotation(entries, cosine_table, sine_table, sign):
    half_dim = HEAD_SIZE // 2
    front_half = entries[..., :half_dim]
    back_half = entries[..., half_dim:]
    cos_rows = cosine_table[:, None, :]
    sin_rows = sine_table[:, None, :] * sign
    return jnp.concatenate(
        [
            front_half * cos_rows - back_half * sin_rows,
            back_half * cos_rows + front_half * sin_rows,
        ],
        axis=-1,
    )


def times_transposed(left, right):
    return lax.dot_general(
        left, right, (((1,), (1,)), ((), ())), preferred_element_type=jnp.float32
    )


def rows_product(left, right):
    return lax.dot_general(
        left, right, (((0,), (0,)), ((), ())), preferred_element_type=jnp.float32
    )


def scores_of(grouped_queries, gathered_pairs, places_own, places_keys):
    sequence_count, total_length, pair_twice = gathered_pairs.shape
    paired_width = pair_twice // 2
    keys_gathered = gathered_pairs[..., :paired_width].reshape(
        sequence_count, total_length, KEY_VALUE_HEADS, HEAD_SIZE
    )
    scaled = jnp.einsum(
        "sqhgd,skhd->shgqk", grouped_queries, keys_gathered, preferred_element_type=jnp.float32
    ) * HEAD_SIZE ** (-0.5)
    allowed = places_own[:, None, None, :, None] >= places_keys[:, None, None, None, :]
    return jnp.where(allowed, scaled, MASKED)


def forward(whole, vectors, tokens, places_own, places_keys, cosine_table, sine_table):
    w_query, w_key, w_value, w_out, w_gate, w_up, w_down = split_matrices(whole)
    gain_one, gain_two, bias_query, bias_key, bias_value = split_vectors(vectors)
    sequence_count, rows_per_shard, width = tokens.shape
    row_number = sequence_count * rows_per_shard
    paired_width = KEY_VALUE_HEADS * HEAD_SIZE
    resid_in = tokens.astype(jnp.float32).reshape(row_number, width)
    scale_one = lax.rsqrt(jnp.mean(resid_in * resid_in, axis=-1, keepdims=True) + EPS_NORM)
    normed_one = resid_in * scale_one
    hidden_one = (normed_one * gain_one).astype(jnp.bfloat16)
    queries = jnp.dot(hidden_one, w_query, preferred_element_type=jnp.float32) + bias_query
    keys_local = jnp.dot(hidden_one, w_key, preferred_element_type=jnp.float32) + bias_key
    values_own = jnp.dot(hidden_one, w_value, preferred_element_type=jnp.float32) + bias_value
    rotated_queries = apply_rotation(
        queries.reshape(row_number, QUERY_HEADS, HEAD_SIZE), cosine_table, sine_table, 1.0
    ).astype(jnp.bfloat16)
    rotated_keys = apply_rotation(
        keys_local.reshape(row_number, KEY_VALUE_HEADS, HEAD_SIZE), cosine_table, sine_table, 1.0
    ).astype(jnp.bfloat16)
    pairs = jnp.concatenate(
        [
            rotated_keys.reshape(sequence_count, rows_per_shard, paired_width),
            values_own.astype(jnp.bfloat16).reshape(sequence_count, rows_per_shard, paired_width),
        ],
        axis=-1,
    )
    gathered_pairs = lax.all_gather(pairs, "ctx", axis=1, tiled=True)
    grouped_queries = rotated_queries.reshape(
        sequence_count, rows_per_shard, KEY_VALUE_HEADS, QUERY_HEADS // KEY_VALUE_HEADS, HEAD_SIZE
    )
    scores = scores_of(grouped_queries, gathered_pairs, places_own, places_keys)
    row_top = jnp.max(scores, axis=-1, keepdims=True)
    log_total = row_top + jnp.log(jnp.sum(jnp.exp(scores - row_top), axis=-1, keepdims=True))
    probs_low = jnp.exp(scores - log_total).astype(jnp.bfloat16)
    values_gathered = gathered_pairs[..., paired_width:].reshape(
        sequence_count, -1, KEY_VALUE_HEADS, HEAD_SIZE
    )
    attended = jnp.einsum(
        "shgqk,skhd->sqhgd", probs_low, values_gathered, preferred_element_type=jnp.float32
    )
    attended = attended.reshape(row_number, QUERY_HEADS * HEAD_SIZE).astype(jnp.bfloat16)
    resid_mid = resid_in + jnp.dot(attended, w_out, preferred_element_type=jnp.float32)
    scale_two = lax.rsqrt(jnp.mean(resid_mid * resid_mid, axis=-1, keepdims=True) + EPS_NORM)
    normed_two = resid_mid * scale_two
    hidden_two = (normed_two * gain_two).astype(jnp.bfloat16)
    gate_pre = jnp.dot(hidden_two, w_gate, preferred_element_type=jnp.float32)
    up_pre = jnp.dot(hidden_two, w_up, preferred_element_type=jnp.float32)
    act_low = (gate_pre * jax.nn.sigmoid(gate_pre) * up_pre).astype(jnp.bfloat16)
    result = resid_mid + jnp.dot(act_low, w_down, preferred_element_type=jnp.float32)
    block_out = result.astype(jnp.bfloat16).reshape(sequence_count, rows_per_shard, width)
    kept = (
        normed_one,
        scale_one,
        hidden_one,
        grouped_queries,
        pairs,
        gathered_pairs,
        log_total,
        attended,
        normed_two,
        scale_two,
        hidden_two,
        gate_pre,
        up_pre,
        act_low,
    )
    return (block_out, kept)


def backward(whole, vectors, grad_out, kept, places_own, places_keys, cosine_table, sine_table):
    w_query, w_key, w_value, w_out, w_gate, w_up, w_down = split_matrices(whole)
    gain_one, gain_two, bias_query, bias_key, bias_value = split_vectors(vectors)
    (
        normed_one,
        scale_one,
        hidden_one,
        grouped_queries,
        pairs,
        gathered_pairs,
        log_total,
        attended,
        normed_two,
        scale_two,
        hidden_two,
        gate_pre,
        up_pre,
        act_low,
    ) = kept
    sequence_count, rows_per_shard, width = grad_out.shape
    row_number = sequence_count * rows_per_shard
    paired_width = KEY_VALUE_HEADS * HEAD_SIZE
    score_scale = HEAD_SIZE ** (-0.5)
    grad_rows = grad_out.reshape(row_number, width)
    d_act = times_transposed(grad_rows, w_down)
    sigma = jax.nn.sigmoid(gate_pre)
    d_up = (d_act * gate_pre * sigma).astype(jnp.bfloat16)
    d_gate = (d_act * up_pre * sigma * (1.0 + gate_pre * (1.0 - sigma))).astype(jnp.bfloat16)
    d_hidden_two = times_transposed(d_gate, w_gate) + times_transposed(d_up, w_up)
    grad_gain_two = jnp.sum(d_hidden_two * normed_two, axis=0)
    d_norm_two = d_hidden_two * gain_two
    d_mid = grad_rows.astype(jnp.float32) + scale_two * (
        d_norm_two - normed_two * jnp.mean(d_norm_two * normed_two, axis=-1, keepdims=True)
    )
    d_branch = d_mid.astype(jnp.bfloat16)
    grad_attended = times_transposed(d_branch, w_out).astype(jnp.bfloat16)
    total_length = gathered_pairs.shape[1]
    keys_gathered = gathered_pairs[..., :paired_width].reshape(
        sequence_count, total_length, KEY_VALUE_HEADS, HEAD_SIZE
    )
    values_gathered = gathered_pairs[..., paired_width:].reshape(
        sequence_count, total_length, KEY_VALUE_HEADS, HEAD_SIZE
    )
    scores = scores_of(grouped_queries, gathered_pairs, places_own, places_keys)
    probs = jnp.exp(scores - log_total)
    probs_low = probs.astype(jnp.bfloat16)
    grad_attended_group = grad_attended.reshape(
        sequence_count, rows_per_shard, KEY_VALUE_HEADS, QUERY_HEADS // KEY_VALUE_HEADS, HEAD_SIZE
    )
    d_probs = jnp.einsum(
        "sqhgd,skhd->shgqk",
        grad_attended_group,
        values_gathered,
        preferred_element_type=jnp.float32,
    )
    row_delta = jnp.sum(probs * d_probs, axis=-1, keepdims=True)
    d_scores = (probs * (d_probs - row_delta)).astype(jnp.bfloat16)
    d_query_rot = (
        jnp.einsum("shgqk,skhd->sqhgd", d_scores, keys_gathered, preferred_element_type=jnp.float32)
        * score_scale
    )
    d_key_rot = (
        jnp.einsum(
            "shgqk,sqhgd->skhd", d_scores, grouped_queries, preferred_element_type=jnp.float32
        )
        * score_scale
    )
    d_value_all = jnp.einsum(
        "shgqk,sqhgd->skhd", probs_low, grad_attended_group, preferred_element_type=jnp.float32
    )
    joined = jnp.concatenate(
        [
            d_key_rot.reshape(sequence_count, total_length, paired_width),
            d_value_all.reshape(sequence_count, total_length, paired_width),
        ],
        axis=-1,
    )
    local_portion = lax.psum_scatter(joined, "ctx", scatter_dimension=1, tiled=True)
    d_key = (
        apply_rotation(
            local_portion[..., :paired_width].reshape(row_number, KEY_VALUE_HEADS, HEAD_SIZE),
            cosine_table,
            sine_table,
            -1.0,
        )
        .reshape(row_number, paired_width)
        .astype(jnp.bfloat16)
    )
    d_value = (
        local_portion[..., paired_width:].reshape(row_number, paired_width).astype(jnp.bfloat16)
    )
    d_query = (
        apply_rotation(
            d_query_rot.reshape(row_number, QUERY_HEADS, HEAD_SIZE), cosine_table, sine_table, -1.0
        )
        .reshape(row_number, QUERY_HEADS * HEAD_SIZE)
        .astype(jnp.bfloat16)
    )
    d_hidden_one = times_transposed(d_query, w_query)
    d_hidden_one = d_hidden_one + times_transposed(d_key, w_key)
    d_hidden_one = d_hidden_one + times_transposed(d_value, w_value)
    grad_gain_one = jnp.sum(d_hidden_one * normed_one, axis=0)
    d_norm_one = d_hidden_one * gain_one
    d_input = d_mid + scale_one * (
        d_norm_one - normed_one * jnp.mean(d_norm_one * normed_one, axis=-1, keepdims=True)
    )
    vector_part = jnp.concatenate(
        [
            grad_gain_one,
            grad_gain_two,
            jnp.sum(d_query.astype(jnp.float32), axis=0),
            jnp.sum(d_key.astype(jnp.float32), axis=0),
            jnp.sum(d_value.astype(jnp.float32), axis=0),
        ]
    )
    row_terms = (
        hidden_one,
        d_query,
        d_key,
        d_value,
        attended,
        d_branch,
        hidden_two,
        d_gate,
        d_up,
        act_low,
        grad_rows,
    )
    return (
        d_input.astype(jnp.bfloat16).reshape(sequence_count, rows_per_shard, width),
        vector_part,
        row_terms,
    )


def adamw(param, grad, mom_one, mom_two, rate, decay):
    new_one = BETA_ONE * mom_one + (1.0 - BETA_ONE) * grad
    new_two = BETA_TWO * mom_two + (1.0 - BETA_TWO) * grad * grad
    fixed_one = new_one / (1.0 - BETA_ONE**STEP)
    fixed_two = new_two / (1.0 - BETA_TWO**STEP)
    new_param = param - rate * (fixed_one / (jnp.sqrt(fixed_two) + EPS_ADAM) + decay * param)
    return (new_param, new_one, new_two)


SPLIT_ROWS = 544
LANES = 128


def factor_sizes():
    data_count = lax.axis_size("dp")
    ctx_count = lax.axis_size("ctx")
    return {"z": data_count // 2, "y": 2, "x": ctx_count // 2, "c": 2}


def coordinates(number, sizes):
    found = {}
    for name in ("c", "x", "y", "z"):
        found[name] = number % sizes[name]
        number = number // sizes[name]
    return found


def number_of(found, sizes):
    number = 0
    for name in ("z", "y", "x", "c"):
        number = number * sizes[name] + found[name]
    return number


def shifted(buffer, name, shift):
    sizes = factor_sizes()
    total = 1
    for size in sizes.values():
        total *= size
    pairs = []
    for number in range(total):
        found = coordinates(number, sizes)
        found[name] = (found[name] + shift) % sizes[name]
        pairs.append((number, number_of(found, sizes)))
    return lax.ppermute(buffer, ("dp", "ctx"), pairs)


def own_coordinates():
    sizes = factor_sizes()
    number = lax.axis_index("dp") * lax.axis_size("ctx") + lax.axis_index("ctx")
    return coordinates(number, sizes)


def gather_order(piece, order):
    sizes = factor_sizes()
    buffer = piece[None]
    for name in order:
        received = [buffer] + [shifted(buffer, name, s) for s in range(1, sizes[name])]
        buffer = jnp.concatenate(received, axis=0)
    mine = own_coordinates()
    total = buffer.shape[0]
    rows = []
    for number in range(total):
        found = coordinates(number, sizes)
        slot = 0
        for name in reversed(order):
            slot = slot * sizes[name] + (mine[name] - found[name]) % sizes[name]
        rows.append(lax.dynamic_index_in_dim(buffer, slot, 0, keepdims=False))
    return rows


def gather_weights(flat):
    piece = flat.reshape(-1, LANES)
    cut = piece.shape[0] * SPLIT_ROWS // 864
    first = gather_order(piece[:cut], ("z", "y", "x", "c"))
    second = gather_order(piece[cut:], ("x", "z", "y", "c"))
    joined = []
    for one, two in zip(first, second):
        joined.append(one)
        joined.append(two)
    return jnp.concatenate(joined, axis=0).reshape(-1)


def scatter_order(grid, order):
    sizes = factor_sizes()
    mine = own_coordinates()
    total = grid.shape[0]
    rows = []
    for slot in range(total):
        left = slot
        found = {}
        for name in reversed(order):
            found[name] = (mine[name] + left % sizes[name]) % sizes[name]
            left = left // sizes[name]
        rows.append(lax.dynamic_index_in_dim(grid, number_of(found, sizes), 0, keepdims=False))
    buffer = jnp.stack(rows).astype(jnp.bfloat16)
    for name in order:
        size = sizes[name]
        parts = buffer.reshape((size, -1) + buffer.shape[1:])
        total_sum = parts[0].astype(jnp.float32)
        received = [shifted(parts[s], name, s) for s in range(1, size)]
        for part in received:
            total_sum = total_sum + part.astype(jnp.float32)
        buffer = total_sum if name == order[-1] else total_sum.astype(jnp.bfloat16)
    return buffer[0]


def scatter_grads(grid):
    pieces = grid.reshape(grid.shape[0], -1, LANES)
    cut = pieces.shape[1] * SPLIT_ROWS // 864
    first = scatter_order(pieces[:, :cut], ("c", "x", "y", "z"))
    second = scatter_order(pieces[:, cut:], ("c", "y", "z", "x"))
    return jnp.concatenate([first, second], axis=0).reshape(-1)


def local(
    tokens_in,
    places,
    out_grad,
    weights,
    first_moment,
    second_moment,
    vectors,
    vector_first,
    vector_second,
):
    micro_count = tokens_in.shape[0]
    places_keys_all = lax.all_gather(places, "ctx", axis=2, tiled=True)
    low_weights = weights.astype(jnp.bfloat16)
    gathered_weights = gather_weights(low_weights)
    fetch_forward = lambda: gathered_weights
    fetch_backward = lambda: gathered_weights
    outputs = []
    input_grads = []
    row_lists = []
    grad_vectors = jnp.zeros(vectors.shape, jnp.float32)
    for index_mb in range(micro_count):
        places_own = places[index_mb]
        places_keys = places_keys_all[index_mb]
        cosine_table, sine_table = rope_tables(places_own.reshape(-1))
        whole = fetch_forward()
        block_out, kept = forward(
            whole, vectors, tokens_in[index_mb], places_own, places_keys, cosine_table, sine_table
        )
        whole_back = fetch_backward()
        input_grad, vector_part, row_terms = backward(
            whole_back,
            vectors,
            out_grad[index_mb],
            kept,
            places_own,
            places_keys,
            cosine_table,
            sine_table,
        )
        outputs.append(block_out)
        input_grads.append(input_grad)
        row_lists.append(row_terms)
        grad_vectors = grad_vectors + vector_part
    stacked = [
        jnp.concatenate([terms[position] for terms in row_lists], axis=0)
        for position in range(len(row_lists[0]))
    ]
    (
        hidden_one,
        d_query,
        d_key,
        d_value,
        attended,
        d_branch,
        hidden_two,
        d_gate,
        d_up,
        act_low,
        grad_rows,
    ) = stacked
    grad_list = (
        rows_product(hidden_one, d_query),
        rows_product(hidden_one, d_key),
        rows_product(hidden_one, d_value),
        rows_product(attended, d_branch),
        rows_product(hidden_two, d_gate),
        rows_product(hidden_two, d_up),
        rows_product(act_low, grad_rows),
    )
    grad_flat = jnp.concatenate([matrix.reshape(-1) for matrix in grad_list])
    data_count = lax.axis_size("dp")
    ctx_count = lax.axis_size("ctx")
    grad_grid = grad_flat.reshape(data_count * ctx_count, -1)
    grad_own = scatter_grads(grad_grid)
    grad_vector_all = lax.psum(grad_vectors, ("dp", "ctx"))
    new_weights, new_first, new_second = adamw(
        weights, grad_own, first_moment, second_moment, RATE_MATRIX, DECAY
    )
    new_vectors, new_vector_first, new_vector_second = adamw(
        vectors, grad_vector_all, vector_first, vector_second, RATE_VECTOR, 0.0
    )
    return (
        jnp.stack(outputs),
        jnp.stack(input_grads),
        new_weights,
        new_first,
        new_second,
        new_vectors,
        new_vector_first,
        new_vector_second,
    )


def solution(mesh):
    in_specs = (
        P(None, "dp", "ctx", None),
        P(None, "dp", "ctx"),
        P(None, "dp", "ctx", None),
        P(("dp", "ctx")),
        P(("dp", "ctx")),
        P(("dp", "ctx")),
        P(),
        P(),
        P(),
    )
    out_specs = (
        P(None, "dp", "ctx", None),
        P(None, "dp", "ctx", None),
        P(("dp", "ctx")),
        P(("dp", "ctx")),
        P(("dp", "ctx")),
        P(),
        P(),
        P(),
    )
    return jax.shard_map(local, mesh=mesh, in_specs=in_specs, out_specs=out_specs, check_vma=False)
```

```python
import jax
import jax.numpy as jnp
from jax import lax
from jax.experimental import pallas as pl
from jax.experimental.pallas import tpu as pltpu
from jax.sharding import PartitionSpec as P

MODEL_WIDTH = 576
QUERY_HEADS = 9
KEY_VALUE_HEADS = 3
HEAD_SIZE = 64
FF = 1536
STEP = 10

EPS_NORM = 1e-05
THETA = 100000.0
BETA_ONE = 0.9
BETA_TWO = 0.95
EPS_ADAM = 1e-08
RATE_MATRIX = 0.06
RATE_VECTOR = 0.3
DECAY = 0.1
MASKED = -1e30

LANES = 128
WIDE = 640
BLOCKS = 32
BLOCK_ROWS = 864
HEAD_ROWS = 576
TAIL_ROWS = BLOCK_ROWS - HEAD_ROWS
SIZES = {"z": 4, "y": 2, "x": 2, "c": 2}
ROWS = 128
F32 = jnp.float32
BF16 = jnp.bfloat16


def coordinates(number):
    found = {}
    for name in ("c", "x", "y", "z"):
        found[name] = number % SIZES[name]
        number = number // SIZES[name]
    return found


def number_of(found):
    number = 0
    for name in ("z", "y", "x", "c"):
        number = number * SIZES[name] + found[name]
    return number


def device_number():
    return lax.axis_index("dp") * lax.axis_size("ctx") + lax.axis_index("ctx")


def inner_count():
    return lax.axis_size("dp") * lax.axis_size("ctx") // BLOCKS


def moved(buffer, name, shift):
    inner = inner_count()
    pairs = []
    for number in range(BLOCKS):
        found = coordinates(number)
        found[name] = (found[name] + shift) % SIZES[name]
        target = number_of(found)
        pairs += [(number * inner + k, target * inner + k) for k in range(inner)]
    return lax.ppermute(buffer, ("dp", "ctx"), pairs)


def across(buffer, distance):
    count = lax.axis_size("ctx")
    return lax.ppermute(buffer, "ctx", [(i, i ^ distance) for i in range(count)])


def together(*arrays):
    return lax.optimization_barrier(arrays)


def gather_blocks(head, tail):
    hz = [moved(head, "z", s) for s in (1, 2, 3)]
    tx = moved(tail, "x", 1)
    head, tail, tx, *hz = together(head, tail, tx, *hz)
    own = jnp.stack([head] + hz)
    pair = jnp.stack([tail, tx])
    ay = moved(own, "y", 1)
    ax = moved(own, "x", 1)
    ac = moved(own, "c", 1)
    tz = [moved(pair, "z", s) for s in (1, 2, 3)]
    own, pair, ay, ax, *tz = together(own, pair, ay, ax, *tz)
    eight = jnp.concatenate([pair] + tz)
    axy = moved(ay, "x", 1)
    ty = moved(eight, "y", 1)
    acy = moved(ay, "c", 1)
    acx = moved(ax, "c", 1)
    tc = moved(eight, "c", 1)
    axy, ty = together(axy, ty)
    acxy = moved(axy, "c", 1)
    tcy = moved(ty, "c", 1)
    return [own, ay, ax, axy, ac, acy, acx, acxy], [eight, ty, tc, tcy]


def fold(order, relative):
    slot = 0
    for name in order:
        slot = slot * SIZES[name] + relative[name]
    return slot


def slot_table():
    mine = coordinates(device_number() // inner_count())
    entries = []
    for order in (("c", "x", "y", "z"), ("c", "y", "z", "x")):
        for number in range(BLOCKS):
            found = coordinates(number)
            entries.append(fold(order, {n: (mine[n] - found[n]) % SIZES[n] for n in SIZES}))
    for order in (("x", "y", "z"), ("y", "z", "x")):
        for number in range(0, BLOCKS, 2):
            found = coordinates(number)
            entries.append(fold(order, {n: (found[n] - mine[n]) % SIZES[n] for n in SIZES}))
    entries.append(mine["c"])
    return jnp.stack([jnp.asarray(entry, jnp.int32) for entry in entries])


AT_HEAD, AT_TAIL, TO_HEAD, TO_TAIL, MY_CORE = 0, BLOCKS, 2 * BLOCKS, 2 * BLOCKS + 16, 2 * BLOCKS + 32


def summed(kept, received):
    return kept.astype(F32) + received.astype(F32)


def scatter_blocks(head_send, head_keep, tail_send, tail_keep, vector):
    hr = moved(head_send, "c", 1)
    tr = moved(tail_send, "c", 1)
    vr = moved(vector, "c", 1)
    hr, tr, vr = together(hr, tr, vr)
    hx = summed(head_keep[8:], hr[8:]).astype(BF16)
    ty = summed(tail_keep[8:], tr[8:]).astype(BF16)
    head = summed(head_keep[:8], hr[:8])
    tail = summed(tail_keep[:8], tr[:8])
    vector = vector + vr
    hr = moved(hx, "x", 1)
    tr = moved(ty, "y", 1)
    vr = moved(vector, "x", 1)
    hr, tr, vr = together(hr, tr, vr)
    hy = summed(head[4:], hr[4:]).astype(BF16)
    tz = [summed(tail[2 * s : 2 * s + 2], tr[2 * s : 2 * s + 2]).astype(BF16) for s in (1, 2, 3)]
    head = summed(head[:4], hr[:4])
    tail = summed(tail[:2], tr[:2])
    vector = vector + vr
    hr = moved(hy, "y", 1)
    tr = [moved(tz[s - 1], "z", s) for s in (1, 2, 3)]
    vr = moved(vector, "y", 1)
    hr, vr, *tr = together(hr, vr, *tr)
    hz = [summed(head[s], hr[s]).astype(BF16) for s in (1, 2, 3)]
    head = summed(head[0], hr[0])
    tx = summed(summed(tail[1], tr[0][1]), summed(tr[1][1], tr[2][1])).astype(BF16)
    tail = summed(summed(tail[0], tr[0][0]), summed(tr[1][0], tr[2][0]))
    vector = vector + vr
    hr = [moved(hz[s - 1], "z", s) for s in (1, 2, 3)]
    tr = moved(tx, "x", 1)
    vr = [moved(vector, "z", s) for s in (1, 2, 3)]
    head = summed(summed(head, hr[0]), summed(hr[1], hr[2]))
    place = coordinates(device_number() // inner_count())["z"]
    parts = jnp.stack([vector] + vr)
    vector = sum(
        lax.dynamic_index_in_dim(parts, (place - z) % 4, 0, keepdims=False) for z in range(4)
    )
    return head, summed(tail, tr), vector


def lower_lanes(shape):
    return lax.broadcasted_iota(jnp.int32, shape, 1) < HEAD_SIZE


def half_turn(value):
    return pltpu.roll(value, HEAD_SIZE, 1)


def side_by_side(left, right):
    return jnp.where(lower_lanes(left.shape), left, half_turn(right))


def kind_of(block):
    return jnp.where(block >= 24, 1, jnp.where(block >= 8, 0, jnp.where((block == 3) | (block == 4), 2, 1)))


def tile_kernel(kind_ref, flat_ref, head_ref, tail_ref, tiles, narrow):
    kind = kind_ref[0]

    @pl.when(kind == 0)
    def _():
        for j in range(12):
            tiles[72 * j : 72 * j + 72, :] = flat_ref[pl.ds(j, 72, stride=12), :]

    @pl.when(kind == 1)
    def _():
        lines = [flat_ref[pl.ds(t, 96, stride=9), :] for t in range(9)]
        turned = [half_turn(line) for line in lines[4:]]
        low = lower_lanes((96, LANES))
        for j in range(4):
            tiles[pl.ds(192 * j, 96, stride=2), :] = lines[j]
            tiles[pl.ds(192 * j + 1, 96, stride=2), :] = jnp.where(low, turned[j], turned[j + 1])
        narrow[pl.ds(0, 96, stride=2), :] = lines[4]
        narrow[pl.ds(1, 96, stride=2), :] = turned[4]
        tiles[768:864, :] = side_by_side(narrow[0:96, :], narrow[96:192, :])

    @pl.when(kind == 2)
    def _():
        lines = [flat_ref[pl.ds(t, 288, stride=3), :] for t in range(3)]
        first, second = half_turn(lines[1]), half_turn(lines[2])
        tiles[pl.ds(0, 288, stride=2), :] = lines[0]
        tiles[pl.ds(1, 288, stride=2), :] = jnp.where(lower_lanes((288, LANES)), first, second)
        narrow[pl.ds(0, 288, stride=2), :] = lines[1]
        narrow[pl.ds(1, 288, stride=2), :] = second
        tiles[576:864, :] = side_by_side(narrow[0:288, :], narrow[288:576, :])

    head_ref[...] = tiles[0:HEAD_ROWS, :].astype(BF16)
    tail_ref[...] = tiles[HEAD_ROWS:BLOCK_ROWS, :].astype(BF16)


def to_tiles(kind, flat):
    return pl.pallas_call(
        tile_kernel,
        out_shape=(
            jax.ShapeDtypeStruct((HEAD_ROWS, LANES), BF16),
            jax.ShapeDtypeStruct((TAIL_ROWS, LANES), BF16),
        ),
        in_specs=[
            pl.BlockSpec(memory_space=pltpu.SMEM),
            pl.BlockSpec(memory_space=pltpu.VMEM),
        ],
        out_specs=(pl.BlockSpec(memory_space=pltpu.VMEM),) * 2,
        scratch_shapes=[
            pltpu.VMEM((BLOCK_ROWS, LANES), F32),
            pltpu.VMEM((HEAD_ROWS, LANES), F32),
        ],
        name="to_tiles",
    )(kind, flat)


def flat_kernel(kind_ref, head_ref, tail_ref, flat_ref, tiles, narrow):
    kind = kind_ref[0]
    tiles[0:HEAD_ROWS, :] = head_ref[...]
    tiles[HEAD_ROWS:BLOCK_ROWS, :] = tail_ref[...]

    @pl.when(kind == 0)
    def _():
        for j in range(12):
            flat_ref[pl.ds(j, 72, stride=12), :] = tiles[72 * j : 72 * j + 72, :]

    @pl.when(kind == 1)
    def _():
        low = lower_lanes((96, LANES))
        narrow[0:96, :] = tiles[768:864, :]
        narrow[96:192, :] = half_turn(tiles[768:864, :])
        odd = [half_turn(tiles[pl.ds(192 * j + 1, 96, stride=2), :]) for j in range(4)]
        for j in range(4):
            flat_ref[pl.ds(j, 96, stride=9), :] = tiles[pl.ds(192 * j, 96, stride=2), :]
        flat_ref[pl.ds(4, 96, stride=9), :] = jnp.where(low, narrow[pl.ds(0, 96, stride=2), :], odd[0])
        for j in range(3):
            flat_ref[pl.ds(5 + j, 96, stride=9), :] = jnp.where(low, odd[j], odd[j + 1])
        last = half_turn(narrow[pl.ds(1, 96, stride=2), :])
        flat_ref[pl.ds(8, 96, stride=9), :] = jnp.where(low, odd[3], last)

    @pl.when(kind == 2)
    def _():
        low = lower_lanes((288, LANES))
        narrow[0:288, :] = tiles[576:864, :]
        narrow[288:576, :] = half_turn(tiles[576:864, :])
        odd = half_turn(tiles[pl.ds(1, 288, stride=2), :])
        flat_ref[pl.ds(0, 288, stride=3), :] = tiles[pl.ds(0, 288, stride=2), :]
        flat_ref[pl.ds(1, 288, stride=3), :] = jnp.where(low, narrow[pl.ds(0, 288, stride=2), :], odd)
        last = half_turn(narrow[pl.ds(1, 288, stride=2), :])
        flat_ref[pl.ds(2, 288, stride=3), :] = jnp.where(low, odd, last)


def to_flat(kind, head, tail):
    return pl.pallas_call(
        flat_kernel,
        out_shape=jax.ShapeDtypeStruct((BLOCK_ROWS, LANES), F32),
        in_specs=[
            pl.BlockSpec(memory_space=pltpu.SMEM),
            pl.BlockSpec(memory_space=pltpu.VMEM),
            pl.BlockSpec(memory_space=pltpu.VMEM),
        ],
        out_specs=pl.BlockSpec(memory_space=pltpu.VMEM),
        scratch_shapes=[
            pltpu.VMEM((BLOCK_ROWS, LANES), F32),
            pltpu.VMEM((HEAD_ROWS, LANES), F32),
        ],
        name="to_flat",
    )(kind, head, tail)


def product(left, right):
    return jnp.dot(left, right, preferred_element_type=F32)


def times_transposed(left, right):
    return lax.dot_general(left, right, (((1,), (1,)), ((), ())), preferred_element_type=F32)


def rows_product(left, right):
    return lax.dot_general(left, right, (((0,), (0,)), ((), ())), preferred_element_type=F32)


def swapped(value):
    lane = lax.broadcasted_iota(jnp.int32, value.shape, 1)
    return jnp.where(lane % HEAD_SIZE < HEAD_SIZE // 2, pltpu.roll(value, 96, 1), pltpu.roll(value, 32, 1))


def rope(value, cosines, sines):
    return value * cosines + swapped(value) * sines


def rope_back(value, cosines, sines):
    return value * cosines - swapped(value) * sines


def row_mean(value):
    return jnp.sum(value, axis=-1, keepdims=True) * (1.0 / MODEL_WIDTH)


def normed_rows(value):
    scale = lax.rsqrt(row_mean(value * value) + EPS_NORM)
    return value * scale, scale


def place_rows(ref, head_tile, tail_tile, first):
    for j in range(3):
        ref[first : first + 192, LANES * j : LANES * j + LANES] = head_tile[192 * j : 192 * j + 192, :]
    ref[first : first + 192, 384:512] = tail_tile[0:192, :]
    rest = tail_tile[192:288, :].astype(F32)
    low = lower_lanes(rest.shape)
    ref[first : first + 96, 512:640] = jnp.where(low, rest, 0.0).astype(BF16)
    ref[first + 96 : first + 192, 512:640] = jnp.where(low, half_turn(rest), 0.0).astype(BF16)


def tiles_of_rows(value):
    head = jnp.concatenate([value[:, LANES * j : LANES * j + LANES] for j in range(3)], axis=0)
    rest = side_by_side(value[0:96, 512:640], value[96:192, 512:640])
    return head, jnp.concatenate([value[:, 384:512], rest], axis=0)


def layer_kernel(*refs):
    slots = refs[0]
    head_parts = refs[1:9]
    tail_parts = refs[9:13]
    (tokens_ref, cos_ref, sin_ref, place_q_ref, place_k_ref, gains_ref, bias_q_ref, bias_kv_ref, grad_ref) = refs[13:22]
    (block_out_ref, head_send, head_keep, tail_send, tail_keep, vector_ref, dkv_ref, dq_wq_ref, d_mid_ref, w_kv) = refs[22:32]
    (raw_head, raw_tail, w_q, w_out, w_gate, w_up, w_down, normed_all, hidden_all, keys, values, queries, probs, attended, act_all, block_acc, d_hidden, d_attended, dkv_all, d_query, sems) = refs[32:]

    copies = []
    for k, part in enumerate(head_parts):
        copies.append(pltpu.make_async_copy(part, raw_head.at[pl.ds(4 * k, 4)], sems.at[k]))
    for k, part in enumerate(tail_parts):
        copies.append(pltpu.make_async_copy(part, raw_tail.at[pl.ds(8 * k, 8)], sems.at[8 + k]))
    for copy in copies:
        copy.start()
    for copy in copies:
        copy.wait()

    core = slots[MY_CORE]

    def head_tile(block):
        return raw_head.at[slots[AT_HEAD + block]]

    def tail_tile(block):
        return raw_tail.at[slots[AT_TAIL + block]]

    for ref in (w_q, w_out, w_gate, w_up, w_kv):
        ref[576:640, :] = jnp.zeros((64, ref.shape[1]), BF16)
    for k in range(3):
        place_rows(w_q, head_tile(k), tail_tile(k), 192 * k)
        place_rows(w_out, head_tile(5 + k), tail_tile(5 + k), 192 * k)
    for k in range(8):
        place_rows(w_down, head_tile(24 + k), tail_tile(24 + k), 192 * k)
    w_kv[0:576, 0:128] = head_tile(3)[...]
    w_kv[0:576, 128:256] = head_tile(4)[...]
    rest_key = tail_tile(3)[...].astype(F32)
    rest_value = tail_tile(4)[...].astype(F32)
    low = lower_lanes(rest_key.shape)
    w_kv[0:288, 256:384] = jnp.where(low, rest_key, half_turn(rest_value)).astype(BF16)
    w_kv[288:576, 256:384] = jnp.where(low, half_turn(rest_key), rest_value).astype(BF16)
    for ref, base in ((w_gate, 8), (w_up, 16)):
        for k in range(4):
            for i in range(6):
                if i < 4:
                    even = head_tile(base + 2 * k)[144 * i : 144 * i + 144, :].astype(F32)
                    odd = head_tile(base + 2 * k + 1)[144 * i : 144 * i + 144, :].astype(F32)
                else:
                    even = tail_tile(base + 2 * k)[144 * (i - 4) : 144 * (i - 4) + 144, :].astype(F32)
                    odd = tail_tile(base + 2 * k + 1)[144 * (i - 4) : 144 * (i - 4) + 144, :].astype(F32)
                ref[144 * k : 144 * k + 144, 256 * i : 256 * i + 128] = jnp.concatenate(
                    [even[0:72], odd[0:72]], axis=0
                ).astype(BF16)
                ref[144 * k : 144 * k + 144, 256 * i + 128 : 256 * i + 256] = jnp.concatenate(
                    [even[72:144], odd[72:144]], axis=0
                ).astype(BF16)

    gain_one = gains_ref[0:1, :]
    gain_two = gains_ref[1:2, :]
    low_rows = lower_lanes((ROWS, LANES))

    @pl.loop(0, 8)
    def _(step):
        slot, mb = step // 2, step % 2
        first = pl.multiple_of(mb * 512 + slot * ROWS, ROWS)
        lane = lax.broadcasted_iota(jnp.int32, (ROWS, WIDE), 1)
        x = jnp.where(lane < MODEL_WIDTH, tokens_ref[slot, mb].astype(F32), 0.0)
        normed, _ = normed_rows(x)
        hidden = (normed * gain_one).astype(BF16)
        normed_all[pl.ds(first, ROWS), :] = normed
        hidden_all[pl.ds(first, ROWS), :] = hidden
        pair = product(hidden, w_kv[...]) + bias_kv_ref[...]
        cosines, sines = cos_ref[slot, mb], sin_ref[slot, mb]
        key_a = rope(pair[:, 0:128], cosines, sines)
        key_b = rope(pair[:, 256:384], cosines, sines)
        value_a, value_b = pair[:, 128:256], pair[:, 256:384]
        turned = half_turn(key_a)
        rows = pl.ds(first, ROWS)
        keys[rows, 0:128] = jnp.where(low_rows, key_a, turned).astype(BF16)
        keys[rows, 128:256] = jnp.where(low_rows, turned, key_a).astype(BF16)
        keys[rows, 256:384] = jnp.where(low_rows, key_b, half_turn(key_b)).astype(BF16)
        turned = half_turn(value_a)
        values[rows, 0:128] = jnp.where(low_rows, value_a, turned).astype(BF16)
        values[rows, 128:256] = jnp.where(low_rows, turned, value_a).astype(BF16)
        values[rows, 256:384] = jnp.where(low_rows, half_turn(value_b), value_b).astype(BF16)

    def heads_of(ref, rows, group):
        stacked = []
        for k in range(3):
            number = 3 * group + k
            tile = ref[rows, LANES * (number // 2) : LANES * (number // 2) + LANES]
            keep = low_rows if number % 2 == 0 else jnp.logical_not(low_rows)
            stacked.append(jnp.where(keep, tile.astype(F32), 0.0).astype(BF16))
        return jnp.concatenate(stacked, axis=0)

    def tiles_of_heads(parts):
        found = [jnp.where(low_rows, parts[2 * k], parts[2 * k + 1]) for k in range(4)]
        return found + [jnp.where(low_rows, parts[8], 0.0)]

    @pl.loop(0, 2)
    def _(mb):
        rows = pl.ds(pl.multiple_of(mb * ROWS, ROWS), ROWS)
        key_rows = pl.ds(pl.multiple_of(mb * 512, 512), 512)
        cosines, sines = cos_ref[0, mb], sin_ref[0, mb]
        made = product(hidden_all[pl.ds(pl.multiple_of(mb * 512, 512), ROWS), :], w_q[...]) + bias_q_ref[...]
        for k in range(5):
            queries[rows, LANES * k : LANES * k + LANES] = rope(
                made[:, LANES * k : LANES * k + LANES], cosines, sines
            ).astype(BF16)
        allowed = place_q_ref[mb] >= place_k_ref[mb]
        allowed = jnp.concatenate([allowed.astype(F32)] * 3, axis=0) > 0.5
        parts = []
        for group in range(KEY_VALUE_HEADS):
            lanes = slice(LANES * group, LANES * group + LANES)
            scores = times_transposed(heads_of(queries, rows, group), keys[key_rows, lanes])
            scores = jnp.where(allowed, scores * HEAD_SIZE ** (-0.5), MASKED)
            top = jnp.max(scores, axis=-1, keepdims=True)
            powers = jnp.exp(scores - top)
            found = powers * (1.0 / jnp.sum(powers, axis=-1, keepdims=True))
            probs[mb, group] = found
            out = product(found.astype(BF16), values[key_rows, lanes])
            parts += [out[ROWS * k : ROWS * k + ROWS] for k in range(3)]
        for k, tile in enumerate(tiles_of_heads(parts)):
            attended[rows, LANES * k : LANES * k + LANES] = tile.astype(BF16)

    lane = lax.broadcasted_iota(jnp.int32, (2 * ROWS, WIDE), 1)
    x_own = tokens_ref[0].astype(F32).reshape(2 * ROWS, WIDE)
    x_own = jnp.where(lane < MODEL_WIDTH, x_own, 0.0)
    resid_mid = x_own + product(attended[...], w_out[...])
    normed_two, scale_two = normed_rows(resid_mid)
    hidden_two = (normed_two * gain_two).astype(BF16)
    grad_low = grad_ref[...]
    block_acc[...] = resid_mid
    d_hidden[...] = jnp.zeros_like(d_hidden)

    def store_pair(at, even, odd, send, keep, table, rows):
        slot = slots[table + at]
        send[slot, rows, :] = jnp.where(core == 0, odd, even).astype(BF16)
        keep[slot, rows, :] = jnp.where(core == 0, even, odd).astype(BF16)

    def feed_forward(chunk, first, send, keep, table):
        cols = pl.ds(pl.multiple_of(chunk * 256, 256), 256)
        gate = product(hidden_two, w_gate[:, cols])
        up = product(hidden_two, w_up[:, cols])
        sigma = 1.0 / (1.0 + jnp.exp(-gate))
        act = (gate * sigma * up).astype(BF16)
        act_all[:, cols] = act
        down = w_down[cols, :]
        d_act = times_transposed(grad_low, down)
        block_acc[...] += product(act, down)
        d_up = (d_act * gate * sigma).astype(BF16)
        d_gate = (d_act * up * sigma * (1.0 + gate * (1.0 - sigma))).astype(BF16)
        d_hidden[...] += times_transposed(d_gate, w_gate[:, cols]) + times_transposed(d_up, w_up[:, cols])
        rows = pl.ds(pl.multiple_of((chunk - first) * 144, 144), 144)
        for base, cotangent in ((4, d_gate), (8, d_up)):
            made = rows_product(hidden_two, cotangent)
            for k in range(4):
                part = made[144 * k : 144 * k + 144, :]
                even = jnp.concatenate([part[0:72, 0:128], part[0:72, 128:256]], axis=0)
                odd = jnp.concatenate([part[72:144, 0:128], part[72:144, 128:256]], axis=0)
                store_pair(base + k, even, odd, send, keep, table, rows)

    @pl.loop(0, 4)
    def _(chunk):
        feed_forward(chunk, 0, head_send, head_keep, TO_HEAD)

    @pl.loop(4, 6)
    def _(chunk):
        feed_forward(chunk, 4, tail_send, tail_keep, TO_TAIL)

    def store_rows(at, even, odd):
        even_head, even_tail = even
        odd_head, odd_tail = odd
        store_pair(at, even_head, odd_head, head_send, head_keep, TO_HEAD, slice(0, HEAD_ROWS))
        store_pair(at, even_tail, odd_tail, tail_send, tail_keep, TO_TAIL, slice(0, TAIL_ROWS))

    @pl.loop(0, 4)
    def _(k):
        made = rows_product(act_all[:, pl.ds(pl.multiple_of(k * 384, 128), 384)], grad_low)
        store_rows(12 + k, tiles_of_rows(made[0:192]), tiles_of_rows(made[192:384]))

    block_out_ref[...] = block_acc[...][:, 0:MODEL_WIDTH].astype(BF16).reshape(2, ROWS, MODEL_WIDTH)

    d_two = d_hidden[...]
    vector_ref[...] = jnp.zeros_like(vector_ref)
    vector_ref[1:2, :] = jnp.sum(d_two * normed_two, axis=0, keepdims=True)
    d_norm = d_two * gain_two
    d_mid = grad_low.astype(F32) + scale_two * (d_norm - normed_two * row_mean(d_norm * normed_two))
    d_mid_ref[...] = d_mid
    d_branch = d_mid.astype(BF16)
    d_attended[...] = times_transposed(d_branch, w_out[...]).astype(BF16)
    grad_out = rows_product(attended[...], d_branch)

    @pl.loop(0, 2)
    def _(mb):
        rows = pl.ds(pl.multiple_of(mb * ROWS, ROWS), ROWS)
        key_rows = pl.ds(pl.multiple_of(mb * 512, 512), 512)
        parts = []
        d_keys = []
        d_values = []
        for group in range(KEY_VALUE_HEADS):
            lanes = slice(LANES * group, LANES * group + LANES)
            query_rows = heads_of(queries, rows, group)
            cotangent = heads_of(d_attended, rows, group)
            found = probs[mb, group]
            d_probs = times_transposed(cotangent, values[key_rows, lanes])
            delta = jnp.sum(found * d_probs, axis=-1, keepdims=True)
            d_scores = (found * (d_probs - delta)).astype(BF16)
            out = product(d_scores, keys[key_rows, lanes]) * HEAD_SIZE ** (-0.5)
            parts += [out[ROWS * k : ROWS * k + ROWS] for k in range(3)]
            d_key = rows_product(d_scores, query_rows) * HEAD_SIZE ** (-0.5)
            d_value = rows_product(found.astype(BF16), cotangent)
            d_keys.append(d_key + half_turn(d_key))
            d_values.append(d_value + half_turn(d_value))
        cosines, sines = cos_ref[0, mb], sin_ref[0, mb]
        for k, tile in enumerate(tiles_of_heads(parts)):
            d_query[rows, LANES * k : LANES * k + LANES] = rope_back(tile, cosines, sines).astype(BF16)
        low_keys = lower_lanes((512, LANES))
        cosines = cos_ref[:, mb].reshape(512, LANES)
        sines = sin_ref[:, mb].reshape(512, LANES)
        key_a = rope_back(jnp.where(low_keys, d_keys[0], d_keys[1]), cosines, sines)
        key_b = rope_back(d_keys[2], cosines, sines)
        dkv_all[key_rows, 0:128] = key_a.astype(BF16)
        dkv_all[key_rows, 128:256] = jnp.where(low_keys, d_values[0], d_values[1]).astype(BF16)
        dkv_all[key_rows, 256:384] = jnp.where(low_keys, key_b, d_values[2]).astype(BF16)
        for slot in range(4):
            dkv_ref[slot, mb] = dkv_all[pl.ds(pl.multiple_of(mb * 512 + slot * ROWS, ROWS), ROWS), :]

    dkv = dkv_all[...]
    d_q = d_query[...]
    dq_wq = times_transposed(d_q, w_q[...])
    dq_wq_ref[...] = dq_wq
    vector_ref[2:3, :] = jnp.sum(d_q.astype(F32), axis=0, keepdims=True)
    vector_ref[3:4, 0:384] = jnp.sum(dkv.astype(F32), axis=0, keepdims=True)
    gain_sum = jnp.zeros((1, WIDE), F32)
    for mb in range(2):
        gain_sum += jnp.sum(dq_wq[ROWS * mb : ROWS * mb + ROWS] * normed_all[512 * mb : 512 * mb + ROWS, :], axis=0, keepdims=True)
    for k in range(4):
        part = slice(256 * k, 256 * k + 256)
        gain_sum += jnp.sum(times_transposed(dkv_all[part, :], w_kv[...]) * normed_all[part, :], axis=0, keepdims=True)
    vector_ref[0:1, :] = gain_sum

    hidden_own = jnp.concatenate([hidden_all[0:ROWS, :], hidden_all[512 : 512 + ROWS, :]], axis=0)
    grad_q = rows_product(hidden_own, d_q)
    grad_kv = rows_product(hidden_all[...], dkv)
    rest = grad_kv[0:576, 256:384]
    low = lower_lanes((288, LANES))
    key_tiles = (grad_kv[0:576, 0:128], jnp.where(low, rest[0:288], half_turn(rest[288:576])))
    value_tiles = (grad_kv[0:576, 128:256], jnp.where(low, half_turn(rest[0:288]), rest[288:576]))
    query_tiles = [tiles_of_rows(grad_q[192 * k : 192 * k + 192]) for k in range(3)]
    out_tiles = [tiles_of_rows(grad_out[192 * k : 192 * k + 192]) for k in range(3)]
    store_rows(0, query_tiles[0], query_tiles[1])
    store_rows(1, query_tiles[2], key_tiles)
    store_rows(2, value_tiles, out_tiles[0])
    store_rows(3, out_tiles[1], out_tiles[2])


def run_layer(slots, heads, tails, tokens, cosines, sines, place_q, place_k, gains, bias_q, bias_kv, grad):
    shape = jax.ShapeDtypeStruct
    vmem = pl.BlockSpec(memory_space=pltpu.VMEM)
    anywhere = pl.BlockSpec(memory_space=pl.ANY)
    scratch = [
        ((BLOCKS, HEAD_ROWS, LANES), BF16),
        ((BLOCKS, TAIL_ROWS, LANES), BF16),
        ((WIDE, WIDE), BF16),
        ((WIDE, WIDE), BF16),
        ((WIDE, FF), BF16),
        ((WIDE, FF), BF16),
        ((FF, WIDE), BF16),
        ((1024, WIDE), F32),
        ((1024, WIDE), BF16),
        ((1024, 384), BF16),
        ((1024, 384), BF16),
        ((256, WIDE), BF16),
        ((2, 3, 384, 512), F32),
        ((256, WIDE), BF16),
        ((256, FF), BF16),
        ((256, WIDE), F32),
        ((256, WIDE), F32),
        ((256, WIDE), BF16),
        ((1024, 384), BF16),
        ((256, WIDE), BF16),
    ]
    return pl.pallas_call(
        layer_kernel,
        out_shape=(
            shape((2, ROWS, MODEL_WIDTH), BF16),
            shape((16, HEAD_ROWS, LANES), BF16),
            shape((16, HEAD_ROWS, LANES), BF16),
            shape((16, TAIL_ROWS, LANES), BF16),
            shape((16, TAIL_ROWS, LANES), BF16),
            shape((8, WIDE), F32),
            shape((4, 2, ROWS, 384), BF16),
            shape((256, WIDE), F32),
            shape((256, WIDE), F32),
            shape((WIDE, 384), BF16),
        ),
        in_specs=[pl.BlockSpec(memory_space=pltpu.SMEM)] + [anywhere] * 12 + [vmem] * 9,
        out_specs=(vmem,) * 10,
        scratch_shapes=[pltpu.VMEM(dims, kind) for dims, kind in scratch]
        + [pltpu.SemaphoreType.DMA((12,))],
        compiler_params=pltpu.CompilerParams(vmem_limit_bytes=56 * 1024 * 1024),
        name="layer",
    )(slots, *heads, *tails, tokens, cosines, sines, place_q, place_k, gains, bias_q, bias_kv, grad)


def input_kernel(tokens_ref, gains_ref, w_kv_ref, dq_wq_ref, d_mid_ref, own_ref, one_ref, two_ref, three_ref, out_ref):
    lane = lax.broadcasted_iota(jnp.int32, (2 * ROWS, WIDE), 1)
    x = jnp.where(lane < MODEL_WIDTH, tokens_ref[0].astype(F32).reshape(2 * ROWS, WIDE), 0.0)
    normed, scale = normed_rows(x)
    total = (own_ref[...].astype(F32) + one_ref[...].astype(F32)) + (two_ref[...].astype(F32) + three_ref[...].astype(F32))
    total = total.reshape(2 * ROWS, 384).astype(BF16)
    d_norm = (dq_wq_ref[...] + times_transposed(total, w_kv_ref[...])) * gains_ref[0:1, :]
    d_input = d_mid_ref[...] + scale * (d_norm - normed * row_mean(d_norm * normed))
    out_ref[...] = d_input[:, 0:MODEL_WIDTH].astype(BF16).reshape(2, ROWS, MODEL_WIDTH)


def run_input(tokens, gains, w_kv, dq_wq, d_mid, parts):
    return pl.pallas_call(
        input_kernel,
        out_shape=jax.ShapeDtypeStruct((2, ROWS, MODEL_WIDTH), BF16),
        in_specs=[pl.BlockSpec(memory_space=pltpu.VMEM)] * 9,
        out_specs=pl.BlockSpec(memory_space=pltpu.VMEM),
        name="input_grad",
    )(tokens, gains, w_kv, dq_wq, d_mid, *parts)


def adamw(param, grad, mom_one, mom_two, rate, decay):
    new_one = BETA_ONE * mom_one + (1.0 - BETA_ONE) * grad
    new_two = BETA_TWO * mom_two + (1.0 - BETA_TWO) * grad * grad
    fixed_one = new_one / (1.0 - BETA_ONE**STEP)
    fixed_two = new_two / (1.0 - BETA_TWO**STEP)
    new_param = param - rate * (fixed_one / (jnp.sqrt(fixed_two) + EPS_ADAM) + decay * param)
    return (new_param, new_one, new_two)


def inner_groups():
    inner = inner_count()
    data_inner = inner // lax.axis_size("ctx")
    data_count = lax.axis_size("dp")
    return [list(range(k, k + data_inner)) for k in range(0, data_count, data_inner)]


def whole_block(flat):
    if inner_count() == 1:
        return flat
    flat = lax.all_gather(flat, "ctx", axis=0, tiled=True)
    return lax.all_gather(flat, "dp", axis=0, tiled=True, axis_index_groups=inner_groups())


def own_slice(block):
    if inner_count() == 1:
        return block
    block = lax.psum_scatter(
        block, "dp", scatter_dimension=0, tiled=True, axis_index_groups=inner_groups()
    )
    return lax.psum_scatter(block, "ctx", scatter_dimension=0, tiled=True)


def bias_tiles(bias_key, bias_value):
    return jnp.concatenate([bias_key[:128], bias_value[:128], bias_key[128:], bias_value[128:]])


def local(tokens_in, places, out_grad, weights, first_moment, second_moment, vectors, vector_first, vector_second):
    kind = kind_of(device_number() // inner_count()).astype(jnp.int32).reshape(1)
    slots = slot_table()
    block = whole_block(weights).reshape(BLOCK_ROWS, LANES)
    head, tail = to_tiles(kind, block)

    own_tokens = tokens_in.reshape(2, ROWS, MODEL_WIDTH)
    own_places = places.reshape(2, ROWS)
    marks = jnp.stack([own_places // 16, own_places % 16], axis=-1).astype(BF16)
    packed = jnp.concatenate(
        [own_tokens, marks, jnp.zeros((2, ROWS, WIDE - MODEL_WIDTH - 2), BF16)], axis=-1
    )
    tokens = jnp.stack([packed] + [across(packed, d) for d in (1, 2, 3)])
    heads, tails = gather_blocks(head, tail)

    found = tokens[..., MODEL_WIDTH : MODEL_WIDTH + 2].astype(F32)
    place_all = found[..., 0] * 16.0 + found[..., 1]
    half_dim = HEAD_SIZE // 2
    frequency = THETA ** (-2.0 * jnp.arange(half_dim, dtype=F32) / HEAD_SIZE)
    angles = place_all[..., None] * jnp.tile(frequency, 4)
    sign = jnp.where(jnp.arange(LANES) % HEAD_SIZE < half_dim, -1.0, 1.0).astype(F32)
    cosines = jnp.cos(angles)
    sines = jnp.sin(angles) * sign
    place_q = place_all[0][..., None]
    place_k = jnp.transpose(place_all, (1, 0, 2)).reshape(2, 1, 4 * ROWS)
    padding = ((0, 0), (0, WIDE - MODEL_WIDTH))
    gains = jnp.pad(vectors[: 2 * MODEL_WIDTH].reshape(2, MODEL_WIDTH), padding)
    bias_q = jnp.pad(vectors[2 * MODEL_WIDTH : 3 * MODEL_WIDTH].reshape(1, MODEL_WIDTH), padding)
    bias_kv = bias_tiles(vectors[1728:1920], vectors[1920:2112]).reshape(1, 384)
    grad = jnp.pad(out_grad.reshape(2 * ROWS, MODEL_WIDTH), padding)

    (block_out, head_send, head_keep, tail_send, tail_keep, vector, dkv, dq_wq, d_mid, w_kv) = run_layer(
        slots, heads, tails, tokens, cosines, sines, place_q, place_k, gains, bias_q, bias_kv, grad
    )
    parts = [dkv[0]] + [across(dkv[d], d) for d in (1, 2, 3)]
    input_grad = run_input(tokens, gains, w_kv, dq_wq, d_mid, parts)
    head, tail, vector = scatter_blocks(head_send, head_keep, tail_send, tail_keep, vector)
    if inner_count() > 1:
        vector = lax.psum(vector, "ctx")
        vector = lax.psum(vector, "dp", axis_index_groups=inner_groups())
    grad_own = own_slice(to_flat(kind, head, tail).reshape(-1))
    new_weights, new_first, new_second = adamw(
        weights, grad_own, first_moment, second_moment, RATE_MATRIX, DECAY
    )
    pair = vector[3]
    vector_grad = jnp.concatenate(
        [
            vector[0, :MODEL_WIDTH],
            vector[1, :MODEL_WIDTH],
            vector[2, :MODEL_WIDTH],
            pair[0:128],
            pair[256:320],
            pair[128:256],
            pair[320:384],
        ]
    )
    new_vectors, new_vector_first, new_vector_second = adamw(
        vectors, vector_grad, vector_first, vector_second, RATE_VECTOR, 0.0
    )
    shape = tokens_in.shape
    return (
        block_out.reshape(shape),
        input_grad.reshape(shape),
        new_weights,
        new_first,
        new_second,
        new_vectors,
        new_vector_first,
        new_vector_second,
    )


def solution(mesh):
    in_specs = (
        P(None, "dp", "ctx", None),
        P(None, "dp", "ctx"),
        P(None, "dp", "ctx", None),
        P(("dp", "ctx")),
        P(("dp", "ctx")),
        P(("dp", "ctx")),
        P(),
        P(),
        P(),
    )
    out_specs = (
        P(None, "dp", "ctx", None),
        P(None, "dp", "ctx", None),
        P(("dp", "ctx")),
        P(("dp", "ctx")),
        P(("dp", "ctx")),
        P(),
        P(),
        P(),
    )
    return jax.shard_map(local, mesh=mesh, in_specs=in_specs, out_specs=out_specs, check_vma=False)
```

```python
import jax
import jax.numpy as jnp
from jax import lax
from jax.experimental import pallas as pl
from jax.experimental.pallas import tpu as pltpu
from jax.sharding import PartitionSpec as P

MODEL_WIDTH = 576
QUERY_HEADS = 9
KEY_VALUE_HEADS = 3
HEAD_SIZE = 64
FF = 1536
STEP = 10

EPS_NORM = 1e-05
THETA = 100000.0
BETA_ONE = 0.9
BETA_TWO = 0.95
EPS_ADAM = 1e-08
RATE_MATRIX = 0.06
RATE_VECTOR = 0.3
DECAY = 0.1
MASKED = -1e30

LANES = 128
WIDE = 640
BLOCKS = 32
BLOCK_ROWS = 864
HEAD_ROWS = 576
TAIL_ROWS = BLOCK_ROWS - HEAD_ROWS
SIZES = {"z": 4, "y": 2, "x": 2, "c": 2}
ROWS = 128
F32 = jnp.float32
BF16 = jnp.bfloat16


def coordinates(number):
    found = {}
    for name in ("c", "x", "y", "z"):
        found[name] = number % SIZES[name]
        number = number // SIZES[name]
    return found


def number_of(found):
    number = 0
    for name in ("z", "y", "x", "c"):
        number = number * SIZES[name] + found[name]
    return number


def device_number():
    return lax.axis_index("dp") * lax.axis_size("ctx") + lax.axis_index("ctx")


def inner_count():
    return lax.axis_size("dp") * lax.axis_size("ctx") // BLOCKS


def moved(buffer, name, shift):
    inner = inner_count()
    pairs = []
    for number in range(BLOCKS):
        found = coordinates(number)
        found[name] = (found[name] + shift) % SIZES[name]
        target = number_of(found)
        pairs += [(number * inner + k, target * inner + k) for k in range(inner)]
    return lax.ppermute(buffer, ("dp", "ctx"), pairs)


def across(buffer, distance):
    count = lax.axis_size("ctx")
    return lax.ppermute(buffer, "ctx", [(i, i ^ distance) for i in range(count)])


def together(*arrays):
    return lax.optimization_barrier(arrays)


def gather_all(head, tail, packed):
    hz = [moved(head, "z", s) for s in (1, 2, 3)]
    tx = moved(tail, "x", 1)
    two = across(packed, 2)
    one = across(packed, 1)
    head, tail, tx, one, two, *hz = together(head, tail, tx, one, two, *hz)
    own = jnp.stack([head] + hz)
    pair = jnp.stack([tail, tx])
    ay = moved(own, "y", 1)
    ax = moved(own, "x", 1)
    ac = moved(own, "c", 1)
    tz = [moved(pair, "z", s) for s in (1, 2, 3)]
    three = across(two, 1)
    own, pair, ay, ax, three, *tz = together(own, pair, ay, ax, three, *tz)
    tokens = jnp.stack([packed, one, two, three])
    tables = place_tables(tokens)
    eight = jnp.concatenate([pair] + tz)
    axy = moved(ay, "x", 1)
    ty = moved(eight, "y", 1)
    acy = moved(ay, "c", 1)
    acx = moved(ax, "c", 1)
    tc = moved(eight, "c", 1)
    axy, ty, tokens, *tables = together(axy, ty, tokens, *tables)
    acxy = moved(axy, "c", 1)
    tcy = moved(ty, "c", 1)
    return [own, ay, ax, axy, ac, acy, acx, acxy], [eight, ty, tc, tcy], tokens, tables


def place_tables(tokens):
    found = tokens[..., MODEL_WIDTH : MODEL_WIDTH + 2].astype(F32)
    place_all = found[..., 0] * 16.0 + found[..., 1]
    half_dim = HEAD_SIZE // 2
    frequency = THETA ** (-2.0 * jnp.arange(half_dim, dtype=F32) / HEAD_SIZE)
    angles = place_all[..., None] * jnp.tile(frequency, 4)
    sign = jnp.where(jnp.arange(LANES) % HEAD_SIZE < half_dim, -1.0, 1.0).astype(F32)
    place_q = place_all[0][..., None]
    place_k = jnp.transpose(place_all, (1, 0, 2)).reshape(2, 1, 4 * ROWS)
    return jnp.cos(angles), jnp.sin(angles) * sign, place_q, place_k


def fold(order, relative):
    slot = 0
    for name in order:
        slot = slot * SIZES[name] + relative[name]
    return slot


def slot_table():
    mine = coordinates(device_number() // inner_count())
    entries = []
    for order in (("c", "x", "y", "z"), ("c", "y", "z", "x")):
        for number in range(BLOCKS):
            found = coordinates(number)
            entries.append(fold(order, {n: (mine[n] - found[n]) % SIZES[n] for n in SIZES}))
    for order in (("x", "y", "z"), ("y", "z", "x")):
        for number in range(0, BLOCKS, 2):
            found = coordinates(number)
            entries.append(fold(order, {n: (found[n] - mine[n]) % SIZES[n] for n in SIZES}))
    entries.append(mine["c"])
    return jnp.stack([jnp.asarray(entry, jnp.int32) for entry in entries])


AT_HEAD, AT_TAIL, TO_HEAD, TO_TAIL, MY_CORE = 0, BLOCKS, 2 * BLOCKS, 2 * BLOCKS + 16, 2 * BLOCKS + 32


def summed(kept, received):
    return kept.astype(F32) + received.astype(F32)


def scatter_blocks(head_sends, head_keep, tail_sends, tail_keep, vector, pairs):
    head_first, head_rest = head_sends
    tail_first, tail_rest = tail_sends
    h1 = moved(head_first, "c", 1)
    t1 = moved(tail_first, "c", 1)
    hr = moved(head_rest, "c", 1)
    tr = moved(tail_rest, "c", 1)
    vr = moved(vector, "c", 1)
    h1, t1 = together(h1, t1)
    hx = summed(head_keep[12:], h1).astype(BF16)
    ty = summed(tail_keep[8:], t1).astype(BF16)
    hx1 = moved(hx, "x", 1)
    tr1 = moved(ty, "y", 1)
    hx = summed(head_keep[8:12], hr[8:]).astype(BF16)
    hy = summed(head_keep[4:8], hr[4:8])
    hz = summed(head_keep[:4], hr[:4])
    tail = summed(tail_keep[:8], tr)
    vector = vector + vr
    vr = moved(vector, "x", 1)
    hx1, tr1, vr, hx, hy, hz, tail = together(hx1, tr1, vr, hx, hy, hz, tail)
    hy = summed(hy, hx1).astype(BF16)
    tz = [summed(tail[2 * s : 2 * s + 2], tr1[2 * s : 2 * s + 2]).astype(BF16) for s in (1, 2, 3)]
    vector = vector + vr
    hy1 = moved(hy, "y", 1)
    hx1 = moved(hx, "x", 1)
    tzr = [moved(tz[s - 1], "z", s) for s in (1, 2, 3)]
    vr = moved(vector, "y", 1)
    tail = summed(tail[:2], tr1[:2])
    hy1, hx1, vr, tail, pairs, *tzr = together(hy1, hx1, vr, tail, pairs, *tzr)
    head = [summed(summed(hz[s], hx1[s]), hy1[s]) for s in range(4)]
    tx = summed(summed(tail[1], tzr[0][1]), summed(tzr[1][1], tzr[2][1])).astype(BF16)
    tail = summed(summed(tail[0], tzr[0][0]), summed(tzr[1][0], tzr[2][0]))
    vector = vector + vr
    hzr = [moved(head[s].astype(BF16), "z", s) for s in (1, 2, 3)]
    txr = moved(tx, "x", 1)
    pairs = [pairs[0]] + [across(pairs[d], d) for d in (1, 2, 3)]
    vr = [moved(vector, "z", s) for s in (1, 2, 3)]
    place = coordinates(device_number() // inner_count())["z"]
    parts = jnp.stack([vector] + vr)
    vector = sum(
        lax.dynamic_index_in_dim(parts, (place - z) % 4, 0, keepdims=False) for z in range(4)
    )
    return head[0], hzr, tail, txr, vector, pairs


def lower_lanes(shape):
    return lax.broadcasted_iota(jnp.int32, shape, 1) < HEAD_SIZE


def half_turn(value):
    return pltpu.roll(value, HEAD_SIZE, 1)


def side_by_side(left, right):
    return jnp.where(lower_lanes(left.shape), left, half_turn(right))


def kind_of(block):
    return jnp.where(block >= 24, 1, jnp.where(block >= 8, 0, jnp.where((block == 3) | (block == 4), 2, 1)))


def tile_kernel(kind_ref, flat_ref, head_ref, tail_ref, tiles, narrow):
    kind = kind_ref[0]

    @pl.when(kind == 0)
    def _():
        for j in range(12):
            tiles[72 * j : 72 * j + 72, :] = flat_ref[pl.ds(j, 72, stride=12), :]

    @pl.when(kind == 1)
    def _():
        lines = [flat_ref[pl.ds(t, 96, stride=9), :] for t in range(9)]
        turned = [half_turn(line) for line in lines[4:]]
        low = lower_lanes((96, LANES))
        for j in range(4):
            tiles[pl.ds(192 * j, 96, stride=2), :] = lines[j]
            tiles[pl.ds(192 * j + 1, 96, stride=2), :] = jnp.where(low, turned[j], turned[j + 1])
        narrow[pl.ds(0, 96, stride=2), :] = lines[4]
        narrow[pl.ds(1, 96, stride=2), :] = turned[4]
        tiles[768:864, :] = side_by_side(narrow[0:96, :], narrow[96:192, :])

    @pl.when(kind == 2)
    def _():
        lines = [flat_ref[pl.ds(t, 288, stride=3), :] for t in range(3)]
        first, second = half_turn(lines[1]), half_turn(lines[2])
        tiles[pl.ds(0, 288, stride=2), :] = lines[0]
        tiles[pl.ds(1, 288, stride=2), :] = jnp.where(lower_lanes((288, LANES)), first, second)
        narrow[pl.ds(0, 288, stride=2), :] = lines[1]
        narrow[pl.ds(1, 288, stride=2), :] = second
        tiles[576:864, :] = side_by_side(narrow[0:288, :], narrow[288:576, :])

    head_ref[...] = tiles[0:HEAD_ROWS, :].astype(BF16)
    tail_ref[...] = tiles[HEAD_ROWS:BLOCK_ROWS, :].astype(BF16)


def to_tiles(kind, flat):
    return pl.pallas_call(
        tile_kernel,
        out_shape=(
            jax.ShapeDtypeStruct((HEAD_ROWS, LANES), BF16),
            jax.ShapeDtypeStruct((TAIL_ROWS, LANES), BF16),
        ),
        in_specs=[
            pl.BlockSpec(memory_space=pltpu.SMEM),
            pl.BlockSpec(memory_space=pltpu.VMEM),
        ],
        out_specs=(pl.BlockSpec(memory_space=pltpu.VMEM),) * 2,
        scratch_shapes=[
            pltpu.VMEM((BLOCK_ROWS, LANES), F32),
            pltpu.VMEM((HEAD_ROWS, LANES), F32),
        ],
        name="to_tiles",
    )(kind, flat)


def flat_kernel(kind_ref, head_ref, one_ref, two_ref, three_ref, tail_ref, other_ref, *refs):
    kind = kind_ref[0]
    tiles, narrow, flat_ref = refs[-3:]
    tiles[0:HEAD_ROWS, :] = (head_ref[...] + one_ref[...].astype(F32)) + (
        two_ref[...].astype(F32) + three_ref[...].astype(F32)
    )
    tiles[HEAD_ROWS:BLOCK_ROWS, :] = tail_ref[...] + other_ref[...].astype(F32)

    @pl.when(kind == 0)
    def _():
        for j in range(12):
            flat_ref[pl.ds(j, 72, stride=12), :] = tiles[72 * j : 72 * j + 72, :]

    @pl.when(kind == 1)
    def _():
        low = lower_lanes((96, LANES))
        narrow[0:96, :] = tiles[768:864, :]
        narrow[96:192, :] = half_turn(tiles[768:864, :])
        odd = [half_turn(tiles[pl.ds(192 * j + 1, 96, stride=2), :]) for j in range(4)]
        for j in range(4):
            flat_ref[pl.ds(j, 96, stride=9), :] = tiles[pl.ds(192 * j, 96, stride=2), :]
        flat_ref[pl.ds(4, 96, stride=9), :] = jnp.where(low, narrow[pl.ds(0, 96, stride=2), :], odd[0])
        for j in range(3):
            flat_ref[pl.ds(5 + j, 96, stride=9), :] = jnp.where(low, odd[j], odd[j + 1])
        last = half_turn(narrow[pl.ds(1, 96, stride=2), :])
        flat_ref[pl.ds(8, 96, stride=9), :] = jnp.where(low, odd[3], last)

    @pl.when(kind == 2)
    def _():
        low = lower_lanes((288, LANES))
        narrow[0:288, :] = tiles[576:864, :]
        narrow[288:576, :] = half_turn(tiles[576:864, :])
        odd = half_turn(tiles[pl.ds(1, 288, stride=2), :])
        flat_ref[pl.ds(0, 288, stride=3), :] = tiles[pl.ds(0, 288, stride=2), :]
        flat_ref[pl.ds(1, 288, stride=3), :] = jnp.where(low, narrow[pl.ds(0, 288, stride=2), :], odd)
        last = half_turn(narrow[pl.ds(1, 288, stride=2), :])
        flat_ref[pl.ds(2, 288, stride=3), :] = jnp.where(low, odd, last)


    if len(refs) == 4:
        refs[0][...] = flat_ref[...]
        return
    weight_ref, first_ref, second_ref, new_weight, new_first, new_second = refs[:6]

    @pl.loop(0, 6)
    def _(k):
        rows = pl.ds(pl.multiple_of(k * 144, 8), 144)
        new_weight[rows, :], new_first[rows, :], new_second[rows, :] = adamw(
            weight_ref[rows, :], flat_ref[rows, :], first_ref[rows, :], second_ref[rows, :], RATE_MATRIX, DECAY
        )


def finish(kind, parts, state):
    vmem = pl.BlockSpec(memory_space=pltpu.VMEM)
    flat = jax.ShapeDtypeStruct((BLOCK_ROWS, LANES), F32)
    count = max(1, len(state))
    return pl.pallas_call(
        flat_kernel,
        out_shape=(flat,) * count,
        in_specs=[pl.BlockSpec(memory_space=pltpu.SMEM)] + [vmem] * (6 + len(state)),
        out_specs=(vmem,) * count,
        scratch_shapes=[
            pltpu.VMEM((BLOCK_ROWS, LANES), F32),
            pltpu.VMEM((HEAD_ROWS, LANES), F32),
            pltpu.VMEM((BLOCK_ROWS, LANES), F32),
        ],
        name="finish",
    )(kind, *parts, *state)


def product(left, right):
    return jnp.dot(left, right, preferred_element_type=F32)


def times_transposed(left, right):
    return lax.dot_general(left, right, (((1,), (1,)), ((), ())), preferred_element_type=F32)


def rows_product(left, right):
    return lax.dot_general(left, right, (((0,), (0,)), ((), ())), preferred_element_type=F32)


def swapped(value):
    lane = lax.broadcasted_iota(jnp.int32, value.shape, 1)
    return jnp.where(lane % HEAD_SIZE < HEAD_SIZE // 2, pltpu.roll(value, 96, 1), pltpu.roll(value, 32, 1))


def rope(value, cosines, sines):
    return value * cosines + swapped(value) * sines


def rope_back(value, cosines, sines):
    return value * cosines - swapped(value) * sines


def row_mean(value):
    return jnp.sum(value, axis=-1, keepdims=True) * (1.0 / MODEL_WIDTH)


def normed_rows(value):
    scale = lax.rsqrt(row_mean(value * value) + EPS_NORM)
    return value * scale, scale


def place_rows(ref, head_tile, tail_tile, first):
    for j in range(3):
        ref[first : first + 192, LANES * j : LANES * j + LANES] = head_tile[192 * j : 192 * j + 192, :]
    ref[first : first + 192, 384:512] = tail_tile[0:192, :]
    rest = tail_tile[192:288, :].astype(F32)
    low = lower_lanes(rest.shape)
    ref[first : first + 96, 512:640] = jnp.where(low, rest, 0.0).astype(BF16)
    ref[first + 96 : first + 192, 512:640] = jnp.where(low, half_turn(rest), 0.0).astype(BF16)


def tiles_of_rows(value):
    head = jnp.concatenate([value[:, LANES * j : LANES * j + LANES] for j in range(3)], axis=0)
    rest = side_by_side(value[0:96, 512:640], value[96:192, 512:640])
    return head, jnp.concatenate([value[:, 384:512], rest], axis=0)


def layer_kernel(*refs):
    slots = refs[0]
    head_parts = refs[1:9]
    tail_parts = refs[9:13]
    (tokens_ref, cos_ref, sin_ref, place_q_ref, place_k_ref, gains_ref, bias_q_ref, bias_kv_ref, grad_ref) = refs[13:22]
    (block_out_ref, head_first, head_rest, head_keep_out, tail_first, tail_rest, tail_keep_out, vector_ref, dkv_ref, dq_wq_ref, d_mid_ref, w_kv) = refs[22:34]
    (raw_head, raw_tail, w_q, w_out, w_gate, w_up, w_down, normed_all, hidden_all, keys, values, queries, probs, attended, act_all, block_acc, d_hidden, d_attended, dkv_all, d_query, head_send, head_keep, tail_send, tail_keep, sems) = refs[34:]

    copies = []
    for k, part in enumerate(head_parts):
        copies.append(pltpu.make_async_copy(part, raw_head.at[pl.ds(4 * k, 4)], sems.at[k]))
    for k, part in enumerate(tail_parts):
        copies.append(pltpu.make_async_copy(part, raw_tail.at[pl.ds(8 * k, 8)], sems.at[8 + k]))
    for copy in copies:
        copy.start()
    for copy in copies:
        copy.wait()

    core = slots[MY_CORE]

    def head_tile(block):
        return raw_head.at[slots[AT_HEAD + block]]

    def tail_tile(block):
        return raw_tail.at[slots[AT_TAIL + block]]

    for ref in (w_q, w_out, w_gate, w_up, w_kv):
        ref[576:640, :] = jnp.zeros((64, ref.shape[1]), BF16)
    for k in range(3):
        place_rows(w_q, head_tile(k), tail_tile(k), 192 * k)
        place_rows(w_out, head_tile(5 + k), tail_tile(5 + k), 192 * k)
    for k in range(8):
        place_rows(w_down, head_tile(24 + k), tail_tile(24 + k), 192 * k)
    w_kv[0:576, 0:128] = head_tile(3)[...]
    w_kv[0:576, 128:256] = head_tile(4)[...]
    rest_key = tail_tile(3)[...].astype(F32)
    rest_value = tail_tile(4)[...].astype(F32)
    low = lower_lanes(rest_key.shape)
    w_kv[0:288, 256:384] = jnp.where(low, rest_key, half_turn(rest_value)).astype(BF16)
    w_kv[288:576, 256:384] = jnp.where(low, half_turn(rest_key), rest_value).astype(BF16)
    for ref, base in ((w_gate, 8), (w_up, 16)):
        for k in range(4):
            for i in range(6):
                if i < 4:
                    even = head_tile(base + 2 * k)[144 * i : 144 * i + 144, :].astype(F32)
                    odd = head_tile(base + 2 * k + 1)[144 * i : 144 * i + 144, :].astype(F32)
                else:
                    even = tail_tile(base + 2 * k)[144 * (i - 4) : 144 * (i - 4) + 144, :].astype(F32)
                    odd = tail_tile(base + 2 * k + 1)[144 * (i - 4) : 144 * (i - 4) + 144, :].astype(F32)
                ref[144 * k : 144 * k + 144, 256 * i : 256 * i + 128] = jnp.concatenate(
                    [even[0:72], odd[0:72]], axis=0
                ).astype(BF16)
                ref[144 * k : 144 * k + 144, 256 * i + 128 : 256 * i + 256] = jnp.concatenate(
                    [even[72:144], odd[72:144]], axis=0
                ).astype(BF16)

    gain_one = gains_ref[0:1, :]
    gain_two = gains_ref[1:2, :]
    low_rows = lower_lanes((ROWS, LANES))

    @pl.loop(0, 8)
    def _(step):
        slot, mb = step // 2, step % 2
        first = pl.multiple_of(mb * 512 + slot * ROWS, ROWS)
        lane = lax.broadcasted_iota(jnp.int32, (ROWS, WIDE), 1)
        x = jnp.where(lane < MODEL_WIDTH, tokens_ref[slot, mb].astype(F32), 0.0)
        normed, _ = normed_rows(x)
        hidden = (normed * gain_one).astype(BF16)
        normed_all[pl.ds(first, ROWS), :] = normed
        hidden_all[pl.ds(first, ROWS), :] = hidden
        pair = product(hidden, w_kv[...]) + bias_kv_ref[...]
        cosines, sines = cos_ref[slot, mb], sin_ref[slot, mb]
        key_a = rope(pair[:, 0:128], cosines, sines)
        key_b = rope(pair[:, 256:384], cosines, sines)
        value_a, value_b = pair[:, 128:256], pair[:, 256:384]
        turned = half_turn(key_a)
        rows = pl.ds(first, ROWS)
        keys[rows, 0:128] = jnp.where(low_rows, key_a, turned).astype(BF16)
        keys[rows, 128:256] = jnp.where(low_rows, turned, key_a).astype(BF16)
        keys[rows, 256:384] = jnp.where(low_rows, key_b, half_turn(key_b)).astype(BF16)
        turned = half_turn(value_a)
        values[rows, 0:128] = jnp.where(low_rows, value_a, turned).astype(BF16)
        values[rows, 128:256] = jnp.where(low_rows, turned, value_a).astype(BF16)
        values[rows, 256:384] = jnp.where(low_rows, half_turn(value_b), value_b).astype(BF16)

    def heads_of(ref, rows, group):
        stacked = []
        for k in range(3):
            number = 3 * group + k
            tile = ref[rows, LANES * (number // 2) : LANES * (number // 2) + LANES]
            keep = low_rows if number % 2 == 0 else jnp.logical_not(low_rows)
            stacked.append(jnp.where(keep, tile.astype(F32), 0.0).astype(BF16))
        return jnp.concatenate(stacked, axis=0)

    def tiles_of_heads(parts):
        found = [jnp.where(low_rows, parts[2 * k], parts[2 * k + 1]) for k in range(4)]
        return found + [jnp.where(low_rows, parts[8], 0.0)]

    @pl.loop(0, 2)
    def _(mb):
        rows = pl.ds(pl.multiple_of(mb * ROWS, ROWS), ROWS)
        key_rows = pl.ds(pl.multiple_of(mb * 512, 512), 512)
        cosines, sines = cos_ref[0, mb], sin_ref[0, mb]
        made = product(hidden_all[pl.ds(pl.multiple_of(mb * 512, 512), ROWS), :], w_q[...]) + bias_q_ref[...]
        for k in range(5):
            queries[rows, LANES * k : LANES * k + LANES] = rope(
                made[:, LANES * k : LANES * k + LANES], cosines, sines
            ).astype(BF16)
        allowed = place_q_ref[mb] >= place_k_ref[mb]
        allowed = jnp.concatenate([allowed.astype(F32)] * 3, axis=0) > 0.5
        parts = []
        for group in range(KEY_VALUE_HEADS):
            lanes = slice(LANES * group, LANES * group + LANES)
            scores = times_transposed(heads_of(queries, rows, group), keys[key_rows, lanes])
            scores = jnp.where(allowed, scores * HEAD_SIZE ** (-0.5), MASKED)
            top = jnp.max(scores, axis=-1, keepdims=True)
            powers = jnp.exp(scores - top)
            found = powers * (1.0 / jnp.sum(powers, axis=-1, keepdims=True))
            probs[mb, group] = found
            out = product(found.astype(BF16), values[key_rows, lanes])
            parts += [out[ROWS * k : ROWS * k + ROWS] for k in range(3)]
        for k, tile in enumerate(tiles_of_heads(parts)):
            attended[rows, LANES * k : LANES * k + LANES] = tile.astype(BF16)

    lane = lax.broadcasted_iota(jnp.int32, (2 * ROWS, WIDE), 1)
    x_own = tokens_ref[0].astype(F32).reshape(2 * ROWS, WIDE)
    x_own = jnp.where(lane < MODEL_WIDTH, x_own, 0.0)
    resid_mid = x_own + product(attended[...], w_out[...])
    normed_two, scale_two = normed_rows(resid_mid)
    hidden_two = (normed_two * gain_two).astype(BF16)
    grad_low = grad_ref[...]
    block_acc[...] = resid_mid
    d_hidden[...] = jnp.zeros_like(d_hidden)

    def store_pair(at, even, odd, send, keep, table, rows):
        slot = slots[table + at]
        send[slot, rows, :] = jnp.where(core == 0, odd, even).astype(BF16)
        keep[slot, rows, :] = jnp.where(core == 0, even, odd).astype(BF16)

    def feed_forward(chunk, first, send, keep, table):
        cols = pl.ds(pl.multiple_of(chunk * 256, 256), 256)
        gate = product(hidden_two, w_gate[:, cols])
        up = product(hidden_two, w_up[:, cols])
        sigma = 1.0 / (1.0 + jnp.exp(-gate))
        act = (gate * sigma * up).astype(BF16)
        act_all[:, cols] = act
        down = w_down[cols, :]
        d_act = times_transposed(grad_low, down)
        block_acc[...] += product(act, down)
        d_up = (d_act * gate * sigma).astype(BF16)
        d_gate = (d_act * up * sigma * (1.0 + gate * (1.0 - sigma))).astype(BF16)
        d_hidden[...] += times_transposed(d_gate, w_gate[:, cols]) + times_transposed(d_up, w_up[:, cols])
        rows = pl.ds(pl.multiple_of((chunk - first) * 144, 144), 144)
        for base, cotangent in ((4, d_gate), (8, d_up)):
            made = rows_product(hidden_two, cotangent)
            for k in range(4):
                part = made[144 * k : 144 * k + 144, :]
                even = jnp.concatenate([part[0:72, 0:128], part[0:72, 128:256]], axis=0)
                odd = jnp.concatenate([part[72:144, 0:128], part[72:144, 128:256]], axis=0)
                store_pair(base + k, even, odd, send, keep, table, rows)

    @pl.loop(0, 4)
    def _(chunk):
        feed_forward(chunk, 0, head_send, head_keep, TO_HEAD)

    @pl.loop(4, 6)
    def _(chunk):
        feed_forward(chunk, 4, tail_send, tail_keep, TO_TAIL)

    def store_rows(at, even, odd):
        even_head, even_tail = even
        odd_head, odd_tail = odd
        store_pair(at, even_head, odd_head, head_send, head_keep, TO_HEAD, slice(0, HEAD_ROWS))
        store_pair(at, even_tail, odd_tail, tail_send, tail_keep, TO_TAIL, slice(0, TAIL_ROWS))

    @pl.loop(0, 4)
    def _(k):
        made = rows_product(act_all[:, pl.ds(pl.multiple_of(k * 384, 128), 384)], grad_low)
        store_rows(12 + k, tiles_of_rows(made[0:192]), tiles_of_rows(made[192:384]))

    for mb in range(2):
        block_out_ref[mb] = block_acc[ROWS * mb : ROWS * mb + ROWS, :].T[0:MODEL_WIDTH].astype(BF16)

    d_two = d_hidden[...]
    vector_ref[...] = jnp.zeros_like(vector_ref)
    vector_ref[1:2, :] = jnp.sum(d_two * normed_two, axis=0, keepdims=True)
    d_norm = d_two * gain_two
    d_mid = grad_low.astype(F32) + scale_two * (d_norm - normed_two * row_mean(d_norm * normed_two))
    d_mid_ref[...] = d_mid
    d_branch = d_mid.astype(BF16)
    d_attended[...] = times_transposed(d_branch, w_out[...]).astype(BF16)
    grad_out = rows_product(attended[...], d_branch)

    @pl.loop(0, 2)
    def _(mb):
        rows = pl.ds(pl.multiple_of(mb * ROWS, ROWS), ROWS)
        key_rows = pl.ds(pl.multiple_of(mb * 512, 512), 512)
        parts = []
        d_keys = []
        d_values = []
        for group in range(KEY_VALUE_HEADS):
            lanes = slice(LANES * group, LANES * group + LANES)
            query_rows = heads_of(queries, rows, group)
            cotangent = heads_of(d_attended, rows, group)
            found = probs[mb, group]
            d_probs = times_transposed(cotangent, values[key_rows, lanes])
            delta = jnp.sum(found * d_probs, axis=-1, keepdims=True)
            d_scores = (found * (d_probs - delta)).astype(BF16)
            out = product(d_scores, keys[key_rows, lanes]) * HEAD_SIZE ** (-0.5)
            parts += [out[ROWS * k : ROWS * k + ROWS] for k in range(3)]
            d_key = rows_product(d_scores, query_rows) * HEAD_SIZE ** (-0.5)
            d_value = rows_product(found.astype(BF16), cotangent)
            d_keys.append(d_key + half_turn(d_key))
            d_values.append(d_value + half_turn(d_value))
        cosines, sines = cos_ref[0, mb], sin_ref[0, mb]
        for k, tile in enumerate(tiles_of_heads(parts)):
            d_query[rows, LANES * k : LANES * k + LANES] = rope_back(tile, cosines, sines).astype(BF16)
        low_keys = lower_lanes((512, LANES))
        cosines = cos_ref[:, mb].reshape(512, LANES)
        sines = sin_ref[:, mb].reshape(512, LANES)
        key_a = rope_back(jnp.where(low_keys, d_keys[0], d_keys[1]), cosines, sines)
        key_b = rope_back(d_keys[2], cosines, sines)
        dkv_all[key_rows, 0:128] = key_a.astype(BF16)
        dkv_all[key_rows, 128:256] = jnp.where(low_keys, d_values[0], d_values[1]).astype(BF16)
        dkv_all[key_rows, 256:384] = jnp.where(low_keys, key_b, d_values[2]).astype(BF16)
        for slot in range(4):
            dkv_ref[slot, mb] = dkv_all[pl.ds(pl.multiple_of(mb * 512 + slot * ROWS, ROWS), ROWS), :]

    dkv = dkv_all[...]
    d_q = d_query[...]
    dq_wq = times_transposed(d_q, w_q[...])
    dq_wq_ref[...] = dq_wq
    vector_ref[2:3, :] = jnp.sum(d_q.astype(F32), axis=0, keepdims=True)
    vector_ref[3:4, 0:384] = jnp.sum(dkv.astype(F32), axis=0, keepdims=True)
    gain_sum = jnp.zeros((1, WIDE), F32)
    for mb in range(2):
        gain_sum += jnp.sum(dq_wq[ROWS * mb : ROWS * mb + ROWS] * normed_all[512 * mb : 512 * mb + ROWS, :], axis=0, keepdims=True)
    for k in range(4):
        part = slice(256 * k, 256 * k + 256)
        gain_sum += jnp.sum(times_transposed(dkv_all[part, :], w_kv[...]) * normed_all[part, :], axis=0, keepdims=True)
    vector_ref[0:1, :] = gain_sum

    hidden_own = jnp.concatenate([hidden_all[0:ROWS, :], hidden_all[512 : 512 + ROWS, :]], axis=0)
    grad_q = rows_product(hidden_own, d_q)
    grad_kv = rows_product(hidden_all[...], dkv)
    rest = grad_kv[0:576, 256:384]
    low = lower_lanes((288, LANES))
    key_tiles = (grad_kv[0:576, 0:128], jnp.where(low, rest[0:288], half_turn(rest[288:576])))
    value_tiles = (grad_kv[0:576, 128:256], jnp.where(low, half_turn(rest[0:288]), rest[288:576]))
    query_tiles = [tiles_of_rows(grad_q[192 * k : 192 * k + 192]) for k in range(3)]
    out_tiles = [tiles_of_rows(grad_out[192 * k : 192 * k + 192]) for k in range(3)]
    store_rows(0, query_tiles[0], query_tiles[1])
    store_rows(1, query_tiles[2], key_tiles)
    store_rows(2, value_tiles, out_tiles[0])
    store_rows(3, out_tiles[1], out_tiles[2])
    copies = [
        pltpu.make_async_copy(head_send.at[pl.ds(12, 4)], head_first, sems.at[0]),
        pltpu.make_async_copy(tail_send.at[pl.ds(8, 8)], tail_first, sems.at[1]),
        pltpu.make_async_copy(head_send.at[pl.ds(0, 12)], head_rest, sems.at[2]),
        pltpu.make_async_copy(tail_send.at[pl.ds(0, 8)], tail_rest, sems.at[3]),
        pltpu.make_async_copy(head_keep, head_keep_out, sems.at[4]),
        pltpu.make_async_copy(tail_keep, tail_keep_out, sems.at[5]),
    ]
    for copy in copies:
        copy.start()
    for copy in copies:
        copy.wait()


def run_layer(slots, heads, tails, tokens, cosines, sines, place_q, place_k, gains, bias_q, bias_kv, grad):
    shape = jax.ShapeDtypeStruct
    vmem = pl.BlockSpec(memory_space=pltpu.VMEM)
    anywhere = pl.BlockSpec(memory_space=pl.ANY)
    scratch = [
        ((BLOCKS, HEAD_ROWS, LANES), BF16),
        ((BLOCKS, TAIL_ROWS, LANES), BF16),
        ((WIDE, WIDE), BF16),
        ((WIDE, WIDE), BF16),
        ((WIDE, FF), BF16),
        ((WIDE, FF), BF16),
        ((FF, WIDE), BF16),
        ((1024, WIDE), F32),
        ((1024, WIDE), BF16),
        ((1024, 384), BF16),
        ((1024, 384), BF16),
        ((256, WIDE), BF16),
        ((2, 3, 384, 512), F32),
        ((256, WIDE), BF16),
        ((256, FF), BF16),
        ((256, WIDE), F32),
        ((256, WIDE), F32),
        ((256, WIDE), BF16),
        ((1024, 384), BF16),
        ((256, WIDE), BF16),
        ((16, HEAD_ROWS, LANES), BF16),
        ((16, HEAD_ROWS, LANES), BF16),
        ((16, TAIL_ROWS, LANES), BF16),
        ((16, TAIL_ROWS, LANES), BF16),
    ]
    return pl.pallas_call(
        layer_kernel,
        out_shape=(
            shape((2, MODEL_WIDTH, ROWS), BF16),
            shape((4, HEAD_ROWS, LANES), BF16),
            shape((12, HEAD_ROWS, LANES), BF16),
            shape((16, HEAD_ROWS, LANES), BF16),
            shape((8, TAIL_ROWS, LANES), BF16),
            shape((8, TAIL_ROWS, LANES), BF16),
            shape((16, TAIL_ROWS, LANES), BF16),
            shape((8, WIDE), F32),
            shape((4, 2, ROWS, 384), BF16),
            shape((256, WIDE), F32),
            shape((256, WIDE), F32),
            shape((WIDE, 384), BF16),
        ),
        in_specs=[pl.BlockSpec(memory_space=pltpu.SMEM)] + [anywhere] * 12 + [vmem] * 9,
        out_specs=(vmem,) + (anywhere,) * 6 + (vmem,) * 5,
        scratch_shapes=[pltpu.VMEM(dims, kind) for dims, kind in scratch]
        + [pltpu.SemaphoreType.DMA((12,))],
        compiler_params=pltpu.CompilerParams(vmem_limit_bytes=56 * 1024 * 1024),
        name="layer",
    )(slots, *heads, *tails, tokens, cosines, sines, place_q, place_k, gains, bias_q, bias_kv, grad)


def input_kernel(tokens_ref, gains_ref, w_kv_ref, dq_wq_ref, d_mid_ref, own_ref, one_ref, two_ref, three_ref, out_ref):
    lane = lax.broadcasted_iota(jnp.int32, (2 * ROWS, WIDE), 1)
    x = jnp.where(lane < MODEL_WIDTH, tokens_ref[0].astype(F32).reshape(2 * ROWS, WIDE), 0.0)
    normed, scale = normed_rows(x)
    total = (own_ref[...].astype(F32) + one_ref[...].astype(F32)) + (two_ref[...].astype(F32) + three_ref[...].astype(F32))
    total = total.reshape(2 * ROWS, 384).astype(BF16)
    d_norm = (dq_wq_ref[...] + times_transposed(total, w_kv_ref[...])) * gains_ref[0:1, :]
    d_input = d_mid_ref[...] + scale * (d_norm - normed * row_mean(d_norm * normed))
    for mb in range(2):
        out_ref[mb] = d_input[ROWS * mb : ROWS * mb + ROWS].T[0:MODEL_WIDTH].astype(BF16)


def run_input(tokens, gains, w_kv, dq_wq, d_mid, parts):
    return pl.pallas_call(
        input_kernel,
        out_shape=jax.ShapeDtypeStruct((2, MODEL_WIDTH, ROWS), BF16),
        in_specs=[pl.BlockSpec(memory_space=pltpu.VMEM)] * 9,
        out_specs=pl.BlockSpec(memory_space=pltpu.VMEM),
        name="input_grad",
    )(tokens, gains, w_kv, dq_wq, d_mid, *parts)


def adamw(param, grad, mom_one, mom_two, rate, decay):
    new_one = BETA_ONE * mom_one + (1.0 - BETA_ONE) * grad
    new_two = BETA_TWO * mom_two + (1.0 - BETA_TWO) * grad * grad
    fixed_one = new_one / (1.0 - BETA_ONE**STEP)
    fixed_two = new_two / (1.0 - BETA_TWO**STEP)
    new_param = param - rate * (fixed_one / (jnp.sqrt(fixed_two) + EPS_ADAM) + decay * param)
    return (new_param, new_one, new_two)


def inner_groups():
    inner = inner_count()
    data_inner = inner // lax.axis_size("ctx")
    data_count = lax.axis_size("dp")
    return [list(range(k, k + data_inner)) for k in range(0, data_count, data_inner)]


def whole_block(flat):
    if inner_count() == 1:
        return flat
    flat = lax.all_gather(flat, "ctx", axis=0, tiled=True)
    return lax.all_gather(flat, "dp", axis=0, tiled=True, axis_index_groups=inner_groups())


def own_slice(block):
    if inner_count() == 1:
        return block
    block = lax.psum_scatter(
        block, "dp", scatter_dimension=0, tiled=True, axis_index_groups=inner_groups()
    )
    return lax.psum_scatter(block, "ctx", scatter_dimension=0, tiled=True)


def bias_tiles(bias_key, bias_value):
    return jnp.concatenate([bias_key[:128], bias_value[:128], bias_key[128:], bias_value[128:]])


def local(tokens_in, places, out_grad, weights, first_moment, second_moment, vectors, vector_first, vector_second):
    kind = kind_of(device_number() // inner_count()).astype(jnp.int32).reshape(1)
    slots = slot_table()
    block = whole_block(weights).reshape(BLOCK_ROWS, LANES)
    head, tail = to_tiles(kind, block)

    own_tokens = tokens_in.reshape(2, ROWS, MODEL_WIDTH)
    own_places = places.reshape(2, ROWS)
    marks = jnp.stack([own_places // 16, own_places % 16], axis=-1).astype(BF16)
    packed = jnp.concatenate(
        [own_tokens, marks, jnp.zeros((2, ROWS, WIDE - MODEL_WIDTH - 2), BF16)], axis=-1
    )
    heads, tails, tokens, tables = gather_all(head, tail, packed)
    padding = ((0, 0), (0, WIDE - MODEL_WIDTH))
    gains = jnp.pad(vectors[: 2 * MODEL_WIDTH].reshape(2, MODEL_WIDTH), padding)
    bias_q = jnp.pad(vectors[2 * MODEL_WIDTH : 3 * MODEL_WIDTH].reshape(1, MODEL_WIDTH), padding)
    bias_kv = bias_tiles(vectors[1728:1920], vectors[1920:2112]).reshape(1, 384)
    grad = jnp.pad(out_grad.reshape(2 * ROWS, MODEL_WIDTH), padding)

    (block_out, head_first, head_rest, head_keep, tail_first, tail_rest, tail_keep, vector, dkv, dq_wq, d_mid, w_kv) = run_layer(
        slots, heads, tails, tokens, *tables, gains, bias_q, bias_kv, grad
    )
    head, hzr, tail, txr, vector, pairs = scatter_blocks(
        (head_first, head_rest), head_keep, (tail_first, tail_rest), tail_keep, vector, dkv
    )
    input_grad = run_input(tokens, gains, w_kv, dq_wq, d_mid, pairs)
    state = (weights, first_moment, second_moment)
    parts = (head, *hzr, tail, txr)
    if inner_count() == 1:
        updated = finish(kind, parts, [array.reshape(BLOCK_ROWS, LANES) for array in state])
        new_weights, new_first, new_second = [array.reshape(-1) for array in updated]
    else:
        vector = lax.psum(vector, "ctx")
        vector = lax.psum(vector, "dp", axis_index_groups=inner_groups())
        (block_grad,) = finish(kind, parts, [])
        grad_own = own_slice(block_grad.reshape(-1))
        new_weights, new_first, new_second = adamw(
            weights, grad_own, first_moment, second_moment, RATE_MATRIX, DECAY
        )
    pair = vector[3]
    vector_grad = jnp.concatenate(
        [
            vector[0, :MODEL_WIDTH],
            vector[1, :MODEL_WIDTH],
            vector[2, :MODEL_WIDTH],
            pair[0:128],
            pair[256:320],
            pair[128:256],
            pair[320:384],
        ]
    )
    new_vectors, new_vector_first, new_vector_second = adamw(
        vectors, vector_grad, vector_first, vector_second, RATE_VECTOR, 0.0
    )
    shape = tokens_in.shape
    return (
        jnp.transpose(block_out, (0, 2, 1)).reshape(shape),
        jnp.transpose(input_grad, (0, 2, 1)).reshape(shape),
        new_weights,
        new_first,
        new_second,
        new_vectors,
        new_vector_first,
        new_vector_second,
    )


def solution(mesh):
    in_specs = (
        P(None, "dp", "ctx", None),
        P(None, "dp", "ctx"),
        P(None, "dp", "ctx", None),
        P(("dp", "ctx")),
        P(("dp", "ctx")),
        P(("dp", "ctx")),
        P(),
        P(),
        P(),
    )
    out_specs = (
        P(None, "dp", "ctx", None),
        P(None, "dp", "ctx", None),
        P(("dp", "ctx")),
        P(("dp", "ctx")),
        P(("dp", "ctx")),
        P(),
        P(),
        P(),
    )
    return jax.shard_map(local, mesh=mesh, in_specs=in_specs, out_specs=out_specs, check_vma=False)
```

```python
import jax
import jax.numpy as jnp
from jax import lax
from jax.experimental import pallas as pl
from jax.experimental.pallas import tpu as pltpu
from jax.sharding import PartitionSpec as P

MODEL_WIDTH = 576
QUERY_HEADS = 9
KEY_VALUE_HEADS = 3
HEAD_SIZE = 64
FF = 1536
STEP = 10

EPS_NORM = 1e-05
THETA = 100000.0
BETA_ONE = 0.9
BETA_TWO = 0.95
EPS_ADAM = 1e-08
RATE_MATRIX = 0.06
RATE_VECTOR = 0.3
DECAY = 0.1
MASKED = -1e30

LANES = 128
WIDE = 640
BLOCKS = 32
BLOCK_ROWS = 864
VECTOR_ROWS = 48
HEAD_ROWS = 576
TAIL_ROWS = BLOCK_ROWS - HEAD_ROWS
SIZES = {"z": 4, "y": 2, "x": 2, "c": 2}
ROWS = 128
F32 = jnp.float32
BF16 = jnp.bfloat16


def coordinates(number):
    found = {}
    for name in ("c", "x", "y", "z"):
        found[name] = number % SIZES[name]
        number = number // SIZES[name]
    return found


def number_of(found):
    number = 0
    for name in ("z", "y", "x", "c"):
        number = number * SIZES[name] + found[name]
    return number


def device_number():
    return lax.axis_index("dp") * lax.axis_size("ctx") + lax.axis_index("ctx")


def inner_count():
    return lax.axis_size("dp") * lax.axis_size("ctx") // BLOCKS


def moved(buffer, name, shift):
    inner = inner_count()
    pairs = []
    for number in range(BLOCKS):
        found = coordinates(number)
        found[name] = (found[name] + shift) % SIZES[name]
        target = number_of(found)
        pairs += [(number * inner + k, target * inner + k) for k in range(inner)]
    return lax.ppermute(buffer, ("dp", "ctx"), pairs)


def across(buffer, distance):
    count = lax.axis_size("ctx")
    return lax.ppermute(buffer, "ctx", [(i, i ^ distance) for i in range(count)])


def together(*arrays):
    return lax.optimization_barrier(arrays)


def gather_all(head, tail, packed, others):
    hz = [moved(head, "z", s) for s in (1, 2, 3)]
    tx = moved(tail, "x", 1)
    two = across(packed, 2)
    head, tail, tx, two, *hz = together(head, tail, tx, two, *hz)
    near = jnp.stack([packed, two])
    own = jnp.stack([head] + hz)
    pair = jnp.stack([tail, tx])
    far = across(near, 1)
    ay = moved(own, "y", 1)
    ax = moved(own, "x", 1)
    tz = [moved(pair, "z", s) for s in (1, 2, 3)]
    own, pair, ay, ax, near, far, others, *tz = together(own, pair, ay, ax, near, far, others, *tz)
    tokens = jnp.stack([near[0], far[0], near[1], far[1]])
    tables = place_tables(tokens)
    eight = jnp.concatenate([pair] + tz)
    axy = moved(ay, "x", 1)
    ty = moved(eight, "y", 1)
    ac = moved(own, "c", 1)
    acy = moved(ay, "c", 1)
    acx = moved(ax, "c", 1)
    tc = moved(eight, "c", 1)
    axy, ty, ac, acy, acx, tc, tokens, *tables = together(axy, ty, ac, acy, acx, tc, tokens, *tables)
    acxy = moved(axy, "c", 1)
    tcy = moved(ty, "c", 1)
    heads = [own, ay, ax, axy, ac, acy, acx, acxy]
    return heads, [eight, ty, tc, tcy], tokens, tables, others


def place_tables(tokens):
    found = tokens[..., MODEL_WIDTH : MODEL_WIDTH + 2].astype(F32)
    place_all = found[..., 0] * 16.0 + found[..., 1]
    half_dim = HEAD_SIZE // 2
    frequency = THETA ** (-2.0 * jnp.arange(half_dim, dtype=F32) / HEAD_SIZE)
    angles = place_all[..., None] * jnp.tile(frequency, 4)
    sign = jnp.where(jnp.arange(LANES) % HEAD_SIZE < half_dim, -1.0, 1.0).astype(F32)
    place_q = place_all[0][..., None]
    place_k = jnp.transpose(place_all, (1, 0, 2)).reshape(2, 1, 4 * ROWS)
    return jnp.cos(angles), jnp.sin(angles) * sign, place_q, place_k


def fold(order, relative):
    slot = 0
    for name in order:
        slot = slot * SIZES[name] + relative[name]
    return slot


def slot_table():
    mine = coordinates(device_number() // inner_count())
    entries = []
    for order in (("c", "x", "y", "z"), ("c", "y", "z", "x")):
        for number in range(BLOCKS):
            found = coordinates(number)
            entries.append(fold(order, {n: (mine[n] - found[n]) % SIZES[n] for n in SIZES}))
    for order in (("x", "y", "z"), ("y", "z", "x")):
        for number in range(0, BLOCKS, 2):
            found = coordinates(number)
            entries.append(fold(order, {n: (found[n] - mine[n]) % SIZES[n] for n in SIZES}))
    entries.append(mine["c"])
    return jnp.stack([jnp.asarray(entry, jnp.int32) for entry in entries])


AT_HEAD, AT_TAIL, TO_HEAD, TO_TAIL, MY_CORE = 0, BLOCKS, 2 * BLOCKS, 2 * BLOCKS + 16, 2 * BLOCKS + 32


def summed(kept, received):
    return kept.astype(F32) + received.astype(F32)


def packed_vector(vector):
    high = lax.reduce_precision(vector, 8, 7)
    return jnp.concatenate([high.astype(BF16), (vector - high).astype(BF16)])


def unpacked_vector(rows):
    return rows[:VECTOR_ROWS].astype(F32) + rows[VECTOR_ROWS:].astype(F32)


def scatter_blocks(head_sends, head_keep, tail_sends, tail_keep, vector, dkv_send, dkv_keep):
    head_first, head_rest = head_sends
    tail_first, tail_rest = tail_sends
    h1 = moved(head_first, "c", 1)
    t1 = moved(tail_first, "c", 1)
    hr = moved(head_rest, "c", 1)
    tr = moved(tail_rest, "c", 1)
    dr = across(dkv_send, 1)
    h1, t1 = together(h1, t1)
    cut = 4 * HEAD_ROWS
    hx = summed(head_keep[12:].reshape(cut, LANES), h1[:cut]).astype(BF16)
    vector = unpacked_vector(vector) + unpacked_vector(h1[cut:])
    vector = packed_vector(vector)
    ty = summed(tail_keep[8:], t1).astype(BF16)
    hx1 = moved(jnp.concatenate([hx, vector]), "x", 1)
    tr1 = moved(ty, "y", 1)
    hx = summed(head_keep[8:12], hr[8:]).astype(BF16)
    hy = summed(head_keep[4:8], hr[4:8]).reshape(cut, LANES)
    hz = summed(head_keep[:4], hr[:4])
    tail = summed(tail_keep[:8], tr)
    dkv = summed(dkv_keep, dr).astype(BF16)
    hx1, tr1, hx, hy, hz, tail, dkv, vector = together(hx1, tr1, hx, hy, hz, tail, dkv, vector)
    hy = summed(hy, hx1[:cut]).astype(BF16)
    vector = packed_vector(unpacked_vector(vector) + unpacked_vector(hx1[cut:]))
    tz = [summed(tail[2 * s : 2 * s + 2], tr1[2 * s : 2 * s + 2]).astype(BF16) for s in (1, 2, 3)]
    hy1 = moved(jnp.concatenate([hy, vector]), "y", 1)
    hx1 = moved(hx, "x", 1)
    tzr = [moved(tz[s - 1], "z", s) for s in (1, 2, 3)]
    tail = summed(tail[:2], tr1[:2])
    hy1, hx1, tail, dkv, vector, *tzr = together(hy1, hx1, tail, dkv, vector, *tzr)
    vector = packed_vector(unpacked_vector(vector) + unpacked_vector(hy1[cut:]))
    hy1 = hy1[:cut].reshape(4, HEAD_ROWS, LANES)
    head = [summed(summed(hz[s], hx1[s]), hy1[s]) for s in range(4)]
    tx = summed(summed(tail[1], tzr[0][1]), summed(tzr[1][1], tzr[2][1])).astype(BF16)
    tail = summed(summed(tail[0], tzr[0][0]), summed(tzr[1][0], tzr[2][0]))
    hzr = [moved(jnp.concatenate([head[s].astype(BF16), vector]), "z", s) for s in (1, 2, 3)]
    dr = across(dkv[1], 2)
    txr = moved(tx, "x", 1)
    place = coordinates(device_number() // inner_count())["z"]
    parts = jnp.stack([vector] + [part[HEAD_ROWS:] for part in hzr])
    vector = sum(
        unpacked_vector(lax.dynamic_index_in_dim(parts, (place - z) % 4, 0, keepdims=False))
        for z in range(4)
    )
    return head[0], hzr, tail, txr, vector, (dkv[0], dr)


def lower_lanes(shape):
    return lax.broadcasted_iota(jnp.int32, shape, 1) < HEAD_SIZE


def half_turn(value):
    return pltpu.roll(value, HEAD_SIZE, 1)


def side_by_side(left, right):
    return jnp.where(lower_lanes(left.shape), left, half_turn(right))


def kind_of(block):
    return jnp.where(block >= 24, 1, jnp.where(block >= 8, 0, jnp.where((block == 3) | (block == 4), 2, 1)))


def tile_kernel(kind_ref, flat_ref, head_ref, tail_ref, tiles, narrow):
    kind = kind_ref[0]

    @pl.when(kind == 0)
    def _():
        for j in range(12):
            tiles[72 * j : 72 * j + 72, :] = flat_ref[pl.ds(j, 72, stride=12), :]

    @pl.when(kind == 1)
    def _():
        lines = [flat_ref[pl.ds(t, 96, stride=9), :] for t in range(9)]
        turned = [half_turn(line) for line in lines[4:]]
        low = lower_lanes((96, LANES))
        for j in range(4):
            tiles[pl.ds(192 * j, 96, stride=2), :] = lines[j]
            tiles[pl.ds(192 * j + 1, 96, stride=2), :] = jnp.where(low, turned[j], turned[j + 1])
        narrow[pl.ds(0, 96, stride=2), :] = lines[4]
        narrow[pl.ds(1, 96, stride=2), :] = turned[4]
        tiles[768:864, :] = side_by_side(narrow[0:96, :], narrow[96:192, :])

    @pl.when(kind == 2)
    def _():
        lines = [flat_ref[pl.ds(t, 288, stride=3), :] for t in range(3)]
        first, second = half_turn(lines[1]), half_turn(lines[2])
        tiles[pl.ds(0, 288, stride=2), :] = lines[0]
        tiles[pl.ds(1, 288, stride=2), :] = jnp.where(lower_lanes((288, LANES)), first, second)
        narrow[pl.ds(0, 288, stride=2), :] = lines[1]
        narrow[pl.ds(1, 288, stride=2), :] = second
        tiles[576:864, :] = side_by_side(narrow[0:288, :], narrow[288:576, :])

    head_ref[...] = tiles[0:HEAD_ROWS, :].astype(BF16)
    tail_ref[...] = tiles[HEAD_ROWS:BLOCK_ROWS, :].astype(BF16)


def to_tiles(kind, flat):
    return pl.pallas_call(
        tile_kernel,
        out_shape=(
            jax.ShapeDtypeStruct((HEAD_ROWS, LANES), BF16),
            jax.ShapeDtypeStruct((TAIL_ROWS, LANES), BF16),
        ),
        in_specs=[
            pl.BlockSpec(memory_space=pltpu.SMEM),
            pl.BlockSpec(memory_space=pltpu.VMEM),
        ],
        out_specs=(pl.BlockSpec(memory_space=pltpu.VMEM),) * 2,
        scratch_shapes=[
            pltpu.VMEM((BLOCK_ROWS, LANES), F32),
            pltpu.VMEM((HEAD_ROWS, LANES), F32),
        ],
        name="to_tiles",
    )(kind, flat)


def flat_kernel(kind_ref, head_ref, one_ref, two_ref, three_ref, tail_ref, other_ref, *refs):
    kind = kind_ref[0]
    tiles, narrow, flat_ref = refs[-3:]
    tiles[0:HEAD_ROWS, :] = (head_ref[...] + one_ref[0:HEAD_ROWS, :].astype(F32)) + (
        two_ref[0:HEAD_ROWS, :].astype(F32) + three_ref[0:HEAD_ROWS, :].astype(F32)
    )
    tiles[HEAD_ROWS:BLOCK_ROWS, :] = tail_ref[...] + other_ref[...].astype(F32)

    @pl.when(kind == 0)
    def _():
        for j in range(12):
            flat_ref[pl.ds(j, 72, stride=12), :] = tiles[72 * j : 72 * j + 72, :]

    @pl.when(kind == 1)
    def _():
        low = lower_lanes((96, LANES))
        narrow[0:96, :] = tiles[768:864, :]
        narrow[96:192, :] = half_turn(tiles[768:864, :])
        odd = [half_turn(tiles[pl.ds(192 * j + 1, 96, stride=2), :]) for j in range(4)]
        for j in range(4):
            flat_ref[pl.ds(j, 96, stride=9), :] = tiles[pl.ds(192 * j, 96, stride=2), :]
        flat_ref[pl.ds(4, 96, stride=9), :] = jnp.where(low, narrow[pl.ds(0, 96, stride=2), :], odd[0])
        for j in range(3):
            flat_ref[pl.ds(5 + j, 96, stride=9), :] = jnp.where(low, odd[j], odd[j + 1])
        last = half_turn(narrow[pl.ds(1, 96, stride=2), :])
        flat_ref[pl.ds(8, 96, stride=9), :] = jnp.where(low, odd[3], last)

    @pl.when(kind == 2)
    def _():
        low = lower_lanes((288, LANES))
        narrow[0:288, :] = tiles[576:864, :]
        narrow[288:576, :] = half_turn(tiles[576:864, :])
        odd = half_turn(tiles[pl.ds(1, 288, stride=2), :])
        flat_ref[pl.ds(0, 288, stride=3), :] = tiles[pl.ds(0, 288, stride=2), :]
        flat_ref[pl.ds(1, 288, stride=3), :] = jnp.where(low, narrow[pl.ds(0, 288, stride=2), :], odd)
        last = half_turn(narrow[pl.ds(1, 288, stride=2), :])
        flat_ref[pl.ds(2, 288, stride=3), :] = jnp.where(low, odd, last)


    if len(refs) == 4:
        refs[0][...] = flat_ref[...]
        return
    weight_ref, first_ref, second_ref, new_weight, new_first, new_second = refs[:6]

    @pl.loop(0, 6)
    def _(k):
        rows = pl.ds(pl.multiple_of(k * 144, 8), 144)
        new_weight[rows, :], new_first[rows, :], new_second[rows, :] = adamw(
            weight_ref[rows, :], flat_ref[rows, :], first_ref[rows, :], second_ref[rows, :], RATE_MATRIX, DECAY
        )


def finish(kind, parts, state):
    vmem = pl.BlockSpec(memory_space=pltpu.VMEM)
    flat = jax.ShapeDtypeStruct((BLOCK_ROWS, LANES), F32)
    count = max(1, len(state))
    return pl.pallas_call(
        flat_kernel,
        out_shape=(flat,) * count,
        in_specs=[pl.BlockSpec(memory_space=pltpu.SMEM)] + [vmem] * (6 + len(state)),
        out_specs=(vmem,) * count,
        scratch_shapes=[
            pltpu.VMEM((BLOCK_ROWS, LANES), F32),
            pltpu.VMEM((HEAD_ROWS, LANES), F32),
            pltpu.VMEM((BLOCK_ROWS, LANES), F32),
        ],
        name="finish",
    )(kind, *parts, *state)


def product(left, right):
    return jnp.dot(left, right, preferred_element_type=F32)


def times_transposed(left, right):
    return lax.dot_general(left, right, (((1,), (1,)), ((), ())), preferred_element_type=F32)


def rows_product(left, right):
    return lax.dot_general(left, right, (((0,), (0,)), ((), ())), preferred_element_type=F32)


def swapped(value):
    lane = lax.broadcasted_iota(jnp.int32, value.shape, 1)
    return jnp.where(lane % HEAD_SIZE < HEAD_SIZE // 2, pltpu.roll(value, 96, 1), pltpu.roll(value, 32, 1))


def rope(value, cosines, sines):
    return value * cosines + swapped(value) * sines


def rope_back(value, cosines, sines):
    return value * cosines - swapped(value) * sines


def row_mean(value):
    return jnp.sum(value, axis=-1, keepdims=True) * (1.0 / MODEL_WIDTH)


def normed_rows(value):
    scale = lax.rsqrt(row_mean(value * value) + EPS_NORM)
    return value * scale, scale


def place_rows(ref, head_tile, tail_tile, first):
    for j in range(3):
        ref[first : first + 192, LANES * j : LANES * j + LANES] = head_tile[192 * j : 192 * j + 192, :]
    ref[first : first + 192, 384:512] = tail_tile[0:192, :]
    rest = tail_tile[192:288, :].astype(F32)
    low = lower_lanes(rest.shape)
    ref[first : first + 96, 512:640] = jnp.where(low, rest, 0.0).astype(BF16)
    ref[first + 96 : first + 192, 512:640] = jnp.where(low, half_turn(rest), 0.0).astype(BF16)


def tiles_of_rows(value):
    head = jnp.concatenate([value[:, LANES * j : LANES * j + LANES] for j in range(3)], axis=0)
    rest = side_by_side(value[0:96, 512:640], value[96:192, 512:640])
    return head, jnp.concatenate([value[:, 384:512], rest], axis=0)


def layer_kernel(*refs):
    slots = refs[0]
    head_parts = refs[1:9]
    tail_parts = refs[9:13]
    (tokens_ref, cos_ref, sin_ref, place_q_ref, place_k_ref, gains_ref, bias_q_ref, bias_kv_ref, grad_ref) = refs[13:22]
    (block_out_ref, head_first, head_rest, head_keep_out, tail_first, tail_rest, tail_keep_out, vector_out, dkv_send, dkv_keep, dq_wq_ref, d_mid_ref, w_kv) = refs[22:35]
    (raw_head, raw_tail, w_q, w_out, w_gate, w_up, w_down, normed_all, hidden_all, keys, values, queries, probs, attended, act_all, block_acc, d_hidden, d_attended, dkv_all, d_query, head_send, head_keep, tail_send, tail_keep, vector_ref, sems) = refs[35:]

    copies = []
    for k, part in enumerate(head_parts):
        copies.append(pltpu.make_async_copy(part, raw_head.at[pl.ds(4 * k, 4)], sems.at[k]))
    for k, part in enumerate(tail_parts):
        copies.append(pltpu.make_async_copy(part, raw_tail.at[pl.ds(8 * k, 8)], sems.at[8 + k]))
    for copy in copies:
        copy.start()
    for copy in copies:
        copy.wait()

    core = slots[MY_CORE]

    def head_tile(block):
        return raw_head.at[slots[AT_HEAD + block]]

    def tail_tile(block):
        return raw_tail.at[slots[AT_TAIL + block]]

    for ref in (w_q, w_out, w_gate, w_up, w_kv):
        ref[576:640, :] = jnp.zeros((64, ref.shape[1]), BF16)
    for k in range(3):
        place_rows(w_q, head_tile(k), tail_tile(k), 192 * k)
        place_rows(w_out, head_tile(5 + k), tail_tile(5 + k), 192 * k)
    for k in range(8):
        place_rows(w_down, head_tile(24 + k), tail_tile(24 + k), 192 * k)
    w_kv[0:576, 0:128] = head_tile(3)[...]
    w_kv[0:576, 128:256] = head_tile(4)[...]
    rest_key = tail_tile(3)[...].astype(F32)
    rest_value = tail_tile(4)[...].astype(F32)
    low = lower_lanes(rest_key.shape)
    w_kv[0:288, 256:384] = jnp.where(low, rest_key, half_turn(rest_value)).astype(BF16)
    w_kv[288:576, 256:384] = jnp.where(low, half_turn(rest_key), rest_value).astype(BF16)
    for ref, base in ((w_gate, 8), (w_up, 16)):
        for k in range(4):
            for i in range(6):
                if i < 4:
                    even = head_tile(base + 2 * k)[144 * i : 144 * i + 144, :].astype(F32)
                    odd = head_tile(base + 2 * k + 1)[144 * i : 144 * i + 144, :].astype(F32)
                else:
                    even = tail_tile(base + 2 * k)[144 * (i - 4) : 144 * (i - 4) + 144, :].astype(F32)
                    odd = tail_tile(base + 2 * k + 1)[144 * (i - 4) : 144 * (i - 4) + 144, :].astype(F32)
                ref[144 * k : 144 * k + 144, 256 * i : 256 * i + 128] = jnp.concatenate(
                    [even[0:72], odd[0:72]], axis=0
                ).astype(BF16)
                ref[144 * k : 144 * k + 144, 256 * i + 128 : 256 * i + 256] = jnp.concatenate(
                    [even[72:144], odd[72:144]], axis=0
                ).astype(BF16)

    gain_one = gains_ref[0:1, :]
    gain_two = gains_ref[1:2, :]
    low_rows = lower_lanes((ROWS, LANES))

    @pl.loop(0, 8)
    def _(step):
        slot, mb = step // 2, step % 2
        first = pl.multiple_of(mb * 512 + slot * ROWS, ROWS)
        lane = lax.broadcasted_iota(jnp.int32, (ROWS, WIDE), 1)
        x = jnp.where(lane < MODEL_WIDTH, tokens_ref[slot, mb].astype(F32), 0.0)
        normed, _ = normed_rows(x)
        hidden = (normed * gain_one).astype(BF16)
        normed_all[pl.ds(first, ROWS), :] = normed
        hidden_all[pl.ds(first, ROWS), :] = hidden
        pair = product(hidden, w_kv[...]) + bias_kv_ref[...]
        cosines, sines = cos_ref[slot, mb], sin_ref[slot, mb]
        key_a = rope(pair[:, 0:128], cosines, sines)
        key_b = rope(pair[:, 256:384], cosines, sines)
        value_a, value_b = pair[:, 128:256], pair[:, 256:384]
        turned = half_turn(key_a)
        rows = pl.ds(first, ROWS)
        keys[rows, 0:128] = jnp.where(low_rows, key_a, turned).astype(BF16)
        keys[rows, 128:256] = jnp.where(low_rows, turned, key_a).astype(BF16)
        keys[rows, 256:384] = jnp.where(low_rows, key_b, half_turn(key_b)).astype(BF16)
        turned = half_turn(value_a)
        values[rows, 0:128] = jnp.where(low_rows, value_a, turned).astype(BF16)
        values[rows, 128:256] = jnp.where(low_rows, turned, value_a).astype(BF16)
        values[rows, 256:384] = jnp.where(low_rows, half_turn(value_b), value_b).astype(BF16)

    def heads_of(ref, rows, group):
        stacked = []
        for k in range(3):
            number = 3 * group + k
            tile = ref[rows, LANES * (number // 2) : LANES * (number // 2) + LANES]
            keep = low_rows if number % 2 == 0 else jnp.logical_not(low_rows)
            stacked.append(jnp.where(keep, tile.astype(F32), 0.0).astype(BF16))
        return jnp.concatenate(stacked, axis=0)

    def tiles_of_heads(parts):
        found = [jnp.where(low_rows, parts[2 * k], parts[2 * k + 1]) for k in range(4)]
        return found + [jnp.where(low_rows, parts[8], 0.0)]

    @pl.loop(0, 2)
    def _(mb):
        rows = pl.ds(pl.multiple_of(mb * ROWS, ROWS), ROWS)
        key_rows = pl.ds(pl.multiple_of(mb * 512, 512), 512)
        cosines, sines = cos_ref[0, mb], sin_ref[0, mb]
        made = product(hidden_all[pl.ds(pl.multiple_of(mb * 512, 512), ROWS), :], w_q[...]) + bias_q_ref[...]
        for k in range(5):
            queries[rows, LANES * k : LANES * k + LANES] = rope(
                made[:, LANES * k : LANES * k + LANES], cosines, sines
            ).astype(BF16)
        allowed = place_q_ref[mb] >= place_k_ref[mb]
        allowed = jnp.concatenate([allowed.astype(F32)] * 3, axis=0) > 0.5
        parts = []
        for group in range(KEY_VALUE_HEADS):
            lanes = slice(LANES * group, LANES * group + LANES)
            scores = times_transposed(heads_of(queries, rows, group), keys[key_rows, lanes])
            scores = jnp.where(allowed, scores * HEAD_SIZE ** (-0.5), MASKED)
            top = jnp.max(scores, axis=-1, keepdims=True)
            powers = jnp.exp(scores - top)
            found = powers * (1.0 / jnp.sum(powers, axis=-1, keepdims=True))
            probs[mb, group] = found
            out = product(found.astype(BF16), values[key_rows, lanes])
            parts += [out[ROWS * k : ROWS * k + ROWS] for k in range(3)]
        for k, tile in enumerate(tiles_of_heads(parts)):
            attended[rows, LANES * k : LANES * k + LANES] = tile.astype(BF16)

    lane = lax.broadcasted_iota(jnp.int32, (2 * ROWS, WIDE), 1)
    x_own = tokens_ref[0].astype(F32).reshape(2 * ROWS, WIDE)
    x_own = jnp.where(lane < MODEL_WIDTH, x_own, 0.0)
    resid_mid = x_own + product(attended[...], w_out[...])
    normed_two, scale_two = normed_rows(resid_mid)
    hidden_two = (normed_two * gain_two).astype(BF16)
    grad_low = grad_ref[...]
    block_acc[...] = resid_mid
    d_hidden[...] = jnp.zeros_like(d_hidden)

    def store_pair(at, even, odd, send, keep, table, rows):
        slot = slots[table + at]
        send[slot, rows, :] = jnp.where(core == 0, odd, even).astype(BF16)
        keep[slot, rows, :] = jnp.where(core == 0, even, odd).astype(BF16)

    def feed_forward(chunk, first, send, keep, table):
        cols = pl.ds(pl.multiple_of(chunk * 512, 512), 512)
        gate = product(hidden_two, w_gate[:, cols])
        up = product(hidden_two, w_up[:, cols])
        sigma = 1.0 / (1.0 + jnp.exp(-gate))
        act = (gate * sigma * up).astype(BF16)
        act_all[:, cols] = act
        down = w_down[cols, :]
        d_act = times_transposed(grad_low, down)
        block_acc[...] += product(act, down)
        d_up = (d_act * gate * sigma).astype(BF16)
        d_gate = (d_act * up * sigma * (1.0 + gate * (1.0 - sigma))).astype(BF16)
        d_hidden[...] += times_transposed(d_gate, w_gate[:, cols]) + times_transposed(d_up, w_up[:, cols])
        rows = pl.ds(pl.multiple_of((chunk - first) * 288, 288), 288)
        for base, cotangent in ((4, d_gate), (8, d_up)):
            made = rows_product(hidden_two, cotangent)
            for k in range(4):
                part = made[144 * k : 144 * k + 144, :]
                even = jnp.concatenate([part[0:72, LANES * j : LANES * j + LANES] for j in range(4)], axis=0)
                odd = jnp.concatenate([part[72:144, LANES * j : LANES * j + LANES] for j in range(4)], axis=0)
                store_pair(base + k, even, odd, send, keep, table, rows)

    @pl.loop(0, 2)
    def _(chunk):
        feed_forward(chunk, 0, head_send, head_keep, TO_HEAD)

    feed_forward(2, 2, tail_send, tail_keep, TO_TAIL)

    def store_rows(at, even, odd):
        even_head, even_tail = even
        odd_head, odd_tail = odd
        store_pair(at, even_head, odd_head, head_send, head_keep, TO_HEAD, slice(0, HEAD_ROWS))
        store_pair(at, even_tail, odd_tail, tail_send, tail_keep, TO_TAIL, slice(0, TAIL_ROWS))

    @pl.loop(0, 4)
    def _(k):
        made = rows_product(act_all[:, pl.ds(pl.multiple_of(k * 384, 128), 384)], grad_low)
        store_rows(12 + k, tiles_of_rows(made[0:192]), tiles_of_rows(made[192:384]))

    for mb in range(2):
        block_out_ref[mb] = block_acc[ROWS * mb : ROWS * mb + ROWS, :].T[0:MODEL_WIDTH].astype(BF16)

    d_two = d_hidden[...]
    vector_ref[...] = jnp.zeros_like(vector_ref)
    vector_ref[1:2, :] = jnp.sum(d_two * normed_two, axis=0, keepdims=True)
    d_norm = d_two * gain_two
    d_mid = grad_low.astype(F32) + scale_two * (d_norm - normed_two * row_mean(d_norm * normed_two))
    d_mid_ref[...] = d_mid
    d_branch = d_mid.astype(BF16)
    d_attended[...] = times_transposed(d_branch, w_out[...]).astype(BF16)
    grad_out = rows_product(attended[...], d_branch)

    @pl.loop(0, 2)
    def _(mb):
        rows = pl.ds(pl.multiple_of(mb * ROWS, ROWS), ROWS)
        key_rows = pl.ds(pl.multiple_of(mb * 512, 512), 512)
        parts = []
        d_keys = []
        d_values = []
        for group in range(KEY_VALUE_HEADS):
            lanes = slice(LANES * group, LANES * group + LANES)
            query_rows = heads_of(queries, rows, group)
            cotangent = heads_of(d_attended, rows, group)
            found = probs[mb, group]
            d_probs = times_transposed(cotangent, values[key_rows, lanes])
            delta = jnp.sum(found * d_probs, axis=-1, keepdims=True)
            d_scores = (found * (d_probs - delta)).astype(BF16)
            out = product(d_scores, keys[key_rows, lanes]) * HEAD_SIZE ** (-0.5)
            parts += [out[ROWS * k : ROWS * k + ROWS] for k in range(3)]
            d_key = rows_product(d_scores, query_rows) * HEAD_SIZE ** (-0.5)
            d_value = rows_product(found.astype(BF16), cotangent)
            d_keys.append(d_key + half_turn(d_key))
            d_values.append(d_value + half_turn(d_value))
        cosines, sines = cos_ref[0, mb], sin_ref[0, mb]
        for k, tile in enumerate(tiles_of_heads(parts)):
            d_query[rows, LANES * k : LANES * k + LANES] = rope_back(tile, cosines, sines).astype(BF16)
        low_keys = lower_lanes((512, LANES))
        cosines = cos_ref[:, mb].reshape(512, LANES)
        sines = sin_ref[:, mb].reshape(512, LANES)
        key_a = rope_back(jnp.where(low_keys, d_keys[0], d_keys[1]), cosines, sines)
        key_b = rope_back(d_keys[2], cosines, sines)
        dkv_all[key_rows, 0:128] = key_a.astype(BF16)
        dkv_all[key_rows, 128:256] = jnp.where(low_keys, d_values[0], d_values[1]).astype(BF16)
        dkv_all[key_rows, 256:384] = jnp.where(low_keys, key_b, d_values[2]).astype(BF16)
        for slot in range(4):
            target = dkv_send if slot % 2 else dkv_keep
            target[slot // 2, mb] = dkv_all[pl.ds(pl.multiple_of(mb * 512 + slot * ROWS, ROWS), ROWS), :]

    dkv = dkv_all[...]
    d_q = d_query[...]
    dq_wq = times_transposed(d_q, w_q[...])
    dq_wq_ref[...] = dq_wq
    vector_ref[2:3, :] = jnp.sum(d_q.astype(F32), axis=0, keepdims=True)
    vector_ref[3:4, 0:384] = jnp.sum(dkv.astype(F32), axis=0, keepdims=True)
    gain_sum = jnp.zeros((1, WIDE), F32)
    for mb in range(2):
        gain_sum += jnp.sum(dq_wq[ROWS * mb : ROWS * mb + ROWS] * normed_all[512 * mb : 512 * mb + ROWS, :], axis=0, keepdims=True)
    for k in range(4):
        part = slice(256 * k, 256 * k + 256)
        gain_sum += jnp.sum(times_transposed(dkv_all[part, :], w_kv[...]) * normed_all[part, :], axis=0, keepdims=True)
    vector_ref[0:1, :] = gain_sum

    hidden_own = jnp.concatenate([hidden_all[0:ROWS, :], hidden_all[512 : 512 + ROWS, :]], axis=0)
    grad_q = rows_product(hidden_own, d_q)
    grad_kv = rows_product(hidden_all[...], dkv)
    rest = grad_kv[0:576, 256:384]
    low = lower_lanes((288, LANES))
    key_tiles = (grad_kv[0:576, 0:128], jnp.where(low, rest[0:288], half_turn(rest[288:576])))
    value_tiles = (grad_kv[0:576, 128:256], jnp.where(low, half_turn(rest[0:288]), rest[288:576]))
    query_tiles = [tiles_of_rows(grad_q[192 * k : 192 * k + 192]) for k in range(3)]
    out_tiles = [tiles_of_rows(grad_out[192 * k : 192 * k + 192]) for k in range(3)]
    store_rows(0, query_tiles[0], query_tiles[1])
    store_rows(1, query_tiles[2], key_tiles)
    store_rows(2, value_tiles, out_tiles[0])
    store_rows(3, out_tiles[1], out_tiles[2])
    vector = jnp.concatenate(
        [vector_ref[:, LANES * k : LANES * k + LANES] for k in range(5)] + [jnp.zeros((8, LANES), F32)], axis=0
    )
    high = vector.astype(BF16)
    vector_out[0:VECTOR_ROWS, :] = high
    vector_out[VECTOR_ROWS:, :] = (vector - high.astype(F32)).astype(BF16)
    copies = [
        pltpu.make_async_copy(head_send.at[12 + k], head_first.at[pl.ds(HEAD_ROWS * k, HEAD_ROWS)], sems.at[6 + k])
        for k in range(4)
    ]
    copies += [
        pltpu.make_async_copy(vector_out, head_first.at[pl.ds(4 * HEAD_ROWS, 2 * VECTOR_ROWS)], sems.at[0]),
        pltpu.make_async_copy(tail_send.at[pl.ds(8, 8)], tail_first, sems.at[1]),
        pltpu.make_async_copy(head_send.at[pl.ds(0, 12)], head_rest, sems.at[2]),
        pltpu.make_async_copy(tail_send.at[pl.ds(0, 8)], tail_rest, sems.at[3]),
        pltpu.make_async_copy(head_keep, head_keep_out, sems.at[4]),
        pltpu.make_async_copy(tail_keep, tail_keep_out, sems.at[5]),
    ]
    for copy in copies:
        copy.start()
    for copy in copies:
        copy.wait()


def run_layer(slots, heads, tails, tokens, cosines, sines, place_q, place_k, gains, bias_q, bias_kv, grad):
    shape = jax.ShapeDtypeStruct
    vmem = pl.BlockSpec(memory_space=pltpu.VMEM)
    anywhere = pl.BlockSpec(memory_space=pl.ANY)
    scratch = [
        ((BLOCKS, HEAD_ROWS, LANES), BF16),
        ((BLOCKS, TAIL_ROWS, LANES), BF16),
        ((WIDE, WIDE), BF16),
        ((WIDE, WIDE), BF16),
        ((WIDE, FF), BF16),
        ((WIDE, FF), BF16),
        ((FF, WIDE), BF16),
        ((1024, WIDE), F32),
        ((1024, WIDE), BF16),
        ((1024, 384), BF16),
        ((1024, 384), BF16),
        ((256, WIDE), BF16),
        ((2, 3, 384, 512), F32),
        ((256, WIDE), BF16),
        ((256, FF), BF16),
        ((256, WIDE), F32),
        ((256, WIDE), F32),
        ((256, WIDE), BF16),
        ((1024, 384), BF16),
        ((256, WIDE), BF16),
        ((16, HEAD_ROWS, LANES), BF16),
        ((16, HEAD_ROWS, LANES), BF16),
        ((16, TAIL_ROWS, LANES), BF16),
        ((16, TAIL_ROWS, LANES), BF16),
        ((8, WIDE), F32),
    ]
    return pl.pallas_call(
        layer_kernel,
        out_shape=(
            shape((2, MODEL_WIDTH, ROWS), BF16),
            shape((4 * HEAD_ROWS + 2 * VECTOR_ROWS, LANES), BF16),
            shape((12, HEAD_ROWS, LANES), BF16),
            shape((16, HEAD_ROWS, LANES), BF16),
            shape((8, TAIL_ROWS, LANES), BF16),
            shape((8, TAIL_ROWS, LANES), BF16),
            shape((16, TAIL_ROWS, LANES), BF16),
            shape((2 * VECTOR_ROWS, LANES), BF16),
            shape((2, 2, ROWS, 384), BF16),
            shape((2, 2, ROWS, 384), BF16),
            shape((256, WIDE), F32),
            shape((256, WIDE), F32),
            shape((WIDE, 384), BF16),
        ),
        in_specs=[pl.BlockSpec(memory_space=pltpu.SMEM)] + [anywhere] * 12 + [vmem] * 9,
        out_specs=(vmem,) + (anywhere,) * 6 + (vmem,) * 6,
        scratch_shapes=[pltpu.VMEM(dims, kind) for dims, kind in scratch]
        + [pltpu.SemaphoreType.DMA((12,))],
        compiler_params=pltpu.CompilerParams(vmem_limit_bytes=50 * 1024 * 1024),
        name="layer",
    )(slots, *heads, *tails, tokens, cosines, sines, place_q, place_k, gains, bias_q, bias_kv, grad)


def input_kernel(tokens_ref, gains_ref, w_kv_ref, dq_wq_ref, d_mid_ref, own_ref, other_ref, out_ref):
    lane = lax.broadcasted_iota(jnp.int32, (2 * ROWS, WIDE), 1)
    x = jnp.where(lane < MODEL_WIDTH, tokens_ref[0].astype(F32).reshape(2 * ROWS, WIDE), 0.0)
    normed, scale = normed_rows(x)
    total = own_ref[...].astype(F32) + other_ref[...].astype(F32)
    total = total.reshape(2 * ROWS, 384).astype(BF16)
    d_norm = (dq_wq_ref[...] + times_transposed(total, w_kv_ref[...])) * gains_ref[0:1, :]
    d_input = d_mid_ref[...] + scale * (d_norm - normed * row_mean(d_norm * normed))
    for mb in range(2):
        out_ref[mb] = d_input[ROWS * mb : ROWS * mb + ROWS].T[0:MODEL_WIDTH].astype(BF16)


def run_input(tokens, gains, w_kv, dq_wq, d_mid, parts):
    return pl.pallas_call(
        input_kernel,
        out_shape=jax.ShapeDtypeStruct((2, MODEL_WIDTH, ROWS), BF16),
        in_specs=[pl.BlockSpec(memory_space=pltpu.VMEM)] * 7,
        out_specs=pl.BlockSpec(memory_space=pltpu.VMEM),
        name="input_grad",
    )(tokens, gains, w_kv, dq_wq, d_mid, *parts)


def adamw(param, grad, mom_one, mom_two, rate, decay):
    new_one = BETA_ONE * mom_one + (1.0 - BETA_ONE) * grad
    new_two = BETA_TWO * mom_two + (1.0 - BETA_TWO) * grad * grad
    fixed_one = new_one / (1.0 - BETA_ONE**STEP)
    fixed_two = new_two / (1.0 - BETA_TWO**STEP)
    new_param = param - rate * (fixed_one / (jnp.sqrt(fixed_two) + EPS_ADAM) + decay * param)
    return (new_param, new_one, new_two)


def inner_groups():
    inner = inner_count()
    data_inner = inner // lax.axis_size("ctx")
    data_count = lax.axis_size("dp")
    return [list(range(k, k + data_inner)) for k in range(0, data_count, data_inner)]


def whole_block(flat):
    if inner_count() == 1:
        return flat
    flat = lax.all_gather(flat, "ctx", axis=0, tiled=True)
    return lax.all_gather(flat, "dp", axis=0, tiled=True, axis_index_groups=inner_groups())


def own_slice(block):
    if inner_count() == 1:
        return block
    block = lax.psum_scatter(
        block, "dp", scatter_dimension=0, tiled=True, axis_index_groups=inner_groups()
    )
    return lax.psum_scatter(block, "ctx", scatter_dimension=0, tiled=True)


def bias_tiles(bias_key, bias_value):
    return jnp.concatenate([bias_key[:128], bias_value[:128], bias_key[128:], bias_value[128:]])


def local(tokens_in, places, out_grad, weights, first_moment, second_moment, vectors, vector_first, vector_second):
    kind = kind_of(device_number() // inner_count()).astype(jnp.int32).reshape(1)
    block = whole_block(weights).reshape(BLOCK_ROWS, LANES)
    head, tail = to_tiles(kind, block)

    head, tail, tokens_in, places = together(head, tail, tokens_in, places)
    own_tokens = tokens_in.reshape(2, ROWS, MODEL_WIDTH)
    own_places = places.reshape(2, ROWS)
    marks = jnp.stack([own_places // 16, own_places % 16], axis=-1).astype(BF16)
    packed = jnp.concatenate(
        [own_tokens, marks, jnp.zeros((2, ROWS, WIDE - MODEL_WIDTH - 2), BF16)], axis=-1
    )
    padding = ((0, 0), (0, WIDE - MODEL_WIDTH))
    gains = jnp.pad(vectors[: 2 * MODEL_WIDTH].reshape(2, MODEL_WIDTH), padding)
    bias_q = jnp.pad(vectors[2 * MODEL_WIDTH : 3 * MODEL_WIDTH].reshape(1, MODEL_WIDTH), padding)
    bias_kv = bias_tiles(vectors[1728:1920], vectors[1920:2112]).reshape(1, 384)
    grad = jnp.pad(out_grad.reshape(2 * ROWS, MODEL_WIDTH), padding)
    others = (slot_table(), gains, bias_q, bias_kv, grad)
    heads, tails, tokens, tables, others = gather_all(head, tail, packed, others)
    slots, gains, bias_q, bias_kv, grad = others

    (block_out, head_first, head_rest, head_keep, tail_first, tail_rest, tail_keep, vector, dkv_send, dkv_keep, dq_wq, d_mid, w_kv) = run_layer(
        slots, heads, tails, tokens, *tables, gains, bias_q, bias_kv, grad
    )
    head, hzr, tail, txr, vector, pairs = scatter_blocks(
        (head_first, head_rest), head_keep, (tail_first, tail_rest), tail_keep, vector, dkv_send, dkv_keep
    )
    input_grad = run_input(tokens, gains, w_kv, dq_wq, d_mid, pairs)
    head, input_grad = together(head, input_grad)
    state = (weights, first_moment, second_moment)
    parts = (head, *hzr, tail, txr)
    if inner_count() == 1:
        updated = finish(kind, parts, [array.reshape(BLOCK_ROWS, LANES) for array in state])
        new_weights, new_first, new_second = [array.reshape(-1) for array in updated]
    else:
        vector = lax.psum(vector, "ctx")
        vector = lax.psum(vector, "dp", axis_index_groups=inner_groups())
        (block_grad,) = finish(kind, parts, [])
        grad_own = own_slice(block_grad.reshape(-1))
        new_weights, new_first, new_second = adamw(
            weights, grad_own, first_moment, second_moment, RATE_MATRIX, DECAY
        )
    vector = jnp.transpose(vector.reshape(6, 8, LANES), (1, 0, 2)).reshape(8, 6 * LANES)
    pair = vector[3]
    vector_grad = jnp.concatenate(
        [
            vector[0, :MODEL_WIDTH],
            vector[1, :MODEL_WIDTH],
            vector[2, :MODEL_WIDTH],
            pair[0:128],
            pair[256:320],
            pair[128:256],
            pair[320:384],
        ]
    )
    new_vectors, new_vector_first, new_vector_second = adamw(
        vectors, vector_grad, vector_first, vector_second, RATE_VECTOR, 0.0
    )
    shape = tokens_in.shape
    return (
        jnp.transpose(block_out, (0, 2, 1)).reshape(shape),
        jnp.transpose(input_grad, (0, 2, 1)).reshape(shape),
        new_weights,
        new_first,
        new_second,
        new_vectors,
        new_vector_first,
        new_vector_second,
    )


def solution(mesh):
    in_specs = (
        P(None, "dp", "ctx", None),
        P(None, "dp", "ctx"),
        P(None, "dp", "ctx", None),
        P(("dp", "ctx")),
        P(("dp", "ctx")),
        P(("dp", "ctx")),
        P(),
        P(),
        P(),
    )
    out_specs = (
        P(None, "dp", "ctx", None),
        P(None, "dp", "ctx", None),
        P(("dp", "ctx")),
        P(("dp", "ctx")),
        P(("dp", "ctx")),
        P(),
        P(),
        P(),
    )
    return jax.shard_map(local, mesh=mesh, in_specs=in_specs, out_specs=out_specs, check_vma=False)
```

```python
import jax
import jax.numpy as jnp
from jax import lax
from jax.experimental import pallas as pl
from jax.experimental.pallas import tpu as pltpu
from jax.sharding import PartitionSpec as P

MODEL_WIDTH = 576
QUERY_HEADS = 9
KEY_VALUE_HEADS = 3
HEAD_SIZE = 64
FF = 1536
STEP = 10

EPS_NORM = 1e-05
THETA = 100000.0
BETA_ONE = 0.9
BETA_TWO = 0.95
EPS_ADAM = 1e-08
RATE_MATRIX = 0.06
RATE_VECTOR = 0.3
DECAY = 0.1
MASKED = -1e30

LANES = 128
WIDE = 640
BLOCKS = 32
BLOCK_ROWS = 864
HEAD_ROWS = 576
TAIL_ROWS = BLOCK_ROWS - HEAD_ROWS
VECTOR_ROWS = 48
PART = 4 * HEAD_ROWS
FIRST_AT = 4 * PART
FIRST_ROWS = 2 * PART + 2 * VECTOR_ROWS
SIZES = {"z": 4, "y": 2, "x": 2, "c": 2}
ROWS = 128
F32 = jnp.float32
BF16 = jnp.bfloat16


def coordinates(number):
    found = {}
    for name in ("c", "x", "y", "z"):
        found[name] = number % SIZES[name]
        number = number // SIZES[name]
    return found


def number_of(found):
    number = 0
    for name in ("z", "y", "x", "c"):
        number = number * SIZES[name] + found[name]
    return number


def device_number():
    return lax.axis_index("dp") * lax.axis_size("ctx") + lax.axis_index("ctx")


def inner_count():
    return lax.axis_size("dp") * lax.axis_size("ctx") // BLOCKS


def moved(buffer, name, shift):
    inner = inner_count()
    pairs = []
    for number in range(BLOCKS):
        found = coordinates(number)
        found[name] = (found[name] + shift) % SIZES[name]
        target = number_of(found)
        pairs += [(number * inner + k, target * inner + k) for k in range(inner)]
    return lax.ppermute(buffer, ("dp", "ctx"), pairs)


def across(buffer, distance):
    count = lax.axis_size("ctx")
    return lax.ppermute(buffer, "ctx", [(i, i ^ distance) for i in range(count)])


def together(*arrays):
    return lax.optimization_barrier(arrays)


def gather_all(head, tail, packed, others):
    hz = [moved(head, "z", s) for s in (1, 2, 3)]
    tx = moved(tail, "x", 1)
    two = across(packed, 2)
    head, tail, tx, two, *hz = together(head, tail, tx, two, *hz)
    own = jnp.stack([head] + hz)
    pair = jnp.stack([tail, tx])
    ay = moved(own, "y", 1)
    ax = moved(own, "x", 1)
    tz = [moved(pair, "z", s) for s in (1, 2, 3)]
    near = jnp.stack([packed, two])
    tables = place_tables(near)
    own, pair, ay, ax, near, tables, others, *tz = together(own, pair, ay, ax, near, tables, others, *tz)
    eight = jnp.concatenate([pair] + tz)
    far = across(near, 1)
    axy = moved(ay, "x", 1)
    ty = moved(eight, "y", 1)
    ac = moved(own, "c", 1)
    acy = moved(ay, "c", 1)
    acx = moved(ax, "c", 1)
    tc = moved(eight, "c", 1)
    axy, ty, ac, acy, acx, tc, far = together(axy, ty, ac, acy, acx, tc, far)
    acxy = moved(axy, "c", 1)
    tcy = moved(ty, "c", 1)
    heads = [own, ay, ax, axy, ac, acy, acx, acxy]
    return heads, [eight, ty, tc, tcy], (near, far), tables, others


def places_of(tokens):
    found = tokens[..., MODEL_WIDTH : MODEL_WIDTH + 2].astype(F32)
    return found[..., 0] * 16.0 + found[..., 1]


def place_tables(tokens):
    half_dim = HEAD_SIZE // 2
    frequency = THETA ** (-2.0 * jnp.arange(half_dim, dtype=F32) / HEAD_SIZE)
    angles = places_of(tokens)[..., None] * jnp.tile(frequency, 4)
    sign = jnp.where(jnp.arange(LANES) % HEAD_SIZE < half_dim, -1.0, 1.0).astype(F32)
    return jnp.cos(angles), jnp.sin(angles) * sign


def fold(order, relative):
    slot = 0
    for name in order:
        slot = slot * SIZES[name] + relative[name]
    return slot


def slot_table():
    mine = coordinates(device_number() // inner_count())
    entries = []
    for order in (("c", "x", "y", "z"), ("c", "y", "z", "x")):
        for number in range(BLOCKS):
            found = coordinates(number)
            entries.append(fold(order, {n: (mine[n] - found[n]) % SIZES[n] for n in SIZES}))
    for number in range(0, BLOCKS, 2):
        found = coordinates(number)
        slot = fold(("x", "y", "z"), {n: (found[n] - mine[n]) % SIZES[n] for n in SIZES})
        entries.append(slot * HEAD_ROWS + jnp.where(slot < 12, 0, FIRST_AT - 12 * HEAD_ROWS))
    for number in range(0, BLOCKS, 2):
        found = coordinates(number)
        slot = fold(("y", "z", "x"), {n: (found[n] - mine[n]) % SIZES[n] for n in SIZES})
        entries.append(slot * TAIL_ROWS + jnp.where(slot < 8, 12 * HEAD_ROWS, FIRST_AT + 4 * HEAD_ROWS - 8 * TAIL_ROWS))
    entries.append(mine["c"])
    return jnp.stack([jnp.asarray(entry, jnp.int32) for entry in entries])


AT_HEAD, AT_TAIL, TO_HEAD, TO_TAIL, MY_CORE = 0, BLOCKS, 2 * BLOCKS, 2 * BLOCKS + 16, 2 * BLOCKS + 32


def rows_of(*counts):
    return [jax.ShapeDtypeStruct((count, LANES), BF16) for count in counts]


def on_chip(kernel, name, shapes, *arrays):
    vmem = pl.BlockSpec(memory_space=pltpu.VMEM)
    return pl.pallas_call(
        kernel,
        out_shape=tuple(shapes),
        in_specs=[vmem] * len(arrays),
        out_specs=(vmem,) * len(shapes),
        name=name,
    )(*arrays)


def summed(*parts):
    total = parts[0].astype(F32)
    for part in parts[1:]:
        total = total + part.astype(F32)
    return total


def summed_vector(mine, other):
    total = summed(mine[0:VECTOR_ROWS], other[0:VECTOR_ROWS]) + summed(mine[VECTOR_ROWS:], other[VECTOR_ROWS:])
    high = total.astype(BF16)
    return jnp.concatenate([high, (total - high.astype(F32)).astype(BF16)], axis=0)


def first_kernel(keep, got, hx, ty, vector):
    hx[0:PART, :] = summed(keep[0:PART, :], got[0:PART, :]).astype(BF16)
    ty[...] = summed(keep[PART : 2 * PART, :], got[PART : 2 * PART, :]).astype(BF16)
    total = summed_vector(keep[2 * PART :, :], got[2 * PART :, :])
    hx[PART:, :] = total
    vector[...] = total


def rest_kernel(keep, got, hx, mid, low, tail):
    for at, ref in enumerate((low, mid, hx, tail)):
        rows = slice(PART * at, PART * at + PART)
        ref[...] = summed(keep[rows, :], got[rows, :]).astype(BF16)


def middle_kernel(mid, hx, mine, tail, ty, hy, one, two, three, own, vector):
    hy[0:PART, :] = summed(mid[...], hx[0:PART, :]).astype(BF16)
    total = summed_vector(mine[...], hx[PART:, :])
    hy[PART:, :] = total
    vector[...] = total
    for at, ref in enumerate((own, one, two, three)):
        rows = slice(HEAD_ROWS * at, HEAD_ROWS * at + HEAD_ROWS)
        ref[...] = summed(tail[rows, :], ty[rows, :]).astype(BF16)


def last_kernel(low, hx, hy, mine, tail, got_one, got_two, got_three, one, two, three, tx, vector, own, own_tail):
    total = summed_vector(mine[...], hy[PART:, :])
    vector[...] = total
    for at, ref in enumerate((own, one, two, three)):
        rows = slice(HEAD_ROWS * at, HEAD_ROWS * at + HEAD_ROWS)
        found = summed(low[rows, :], hx[rows, :], hy[rows, :])
        if at == 0:
            own[...] = found
        else:
            ref[0:HEAD_ROWS, :] = found.astype(BF16)
            ref[HEAD_ROWS:, :] = total
    found = summed(tail[...], got_one[...], got_two[...], got_three[...])
    own_tail[...] = found[0:TAIL_ROWS]
    tx[...] = found[TAIL_ROWS:].astype(BF16)


def scatter_blocks(send_first, send_rest, keep_first, keep_rest, pairs, make_input):
    float_rows = lambda count: jax.ShapeDtypeStruct((count, LANES), F32)
    got_first = moved(send_first, "c", 1)
    got_rest = moved(send_rest, "c", 1)
    parts = [pairs[0]] + [across(pairs[d], d) for d in (1, 2, 3)]
    hx, ty, vector = on_chip(first_kernel, "sum_first", rows_of(PART + 2 * VECTOR_ROWS, PART, 2 * VECTOR_ROWS), keep_first, got_first)
    got_hx = moved(hx, "x", 1)
    got_ty = moved(ty, "y", 1)
    hx, mid, low, tail = on_chip(rest_kernel, "sum_rest", rows_of(PART, PART, PART, PART), keep_rest, got_rest)
    input_grad = make_input(parts)
    got_hx, got_ty, hx, mid, low, tail, vector, input_grad = together(got_hx, got_ty, hx, mid, low, tail, vector, input_grad)
    hy, one, two, three, tail, vector = on_chip(
        middle_kernel,
        "sum_middle",
        rows_of(PART + 2 * VECTOR_ROWS, HEAD_ROWS, HEAD_ROWS, HEAD_ROWS, HEAD_ROWS, 2 * VECTOR_ROWS),
        mid, got_hx, vector, tail, got_ty,
    )
    got_hy = moved(hy, "y", 1)
    got_hx = moved(hx, "x", 1)
    got_tz = [moved(part, "z", s + 1) for s, part in enumerate((one, two, three))]
    got_hy, got_hx, low, tail, vector, *got_tz = together(got_hy, got_hx, low, tail, vector, *got_tz)
    one, two, three, tx, vector, own, own_tail = on_chip(
        last_kernel,
        "sum_last",
        rows_of(*(HEAD_ROWS + 2 * VECTOR_ROWS,) * 3, TAIL_ROWS, 2 * VECTOR_ROWS) + [float_rows(HEAD_ROWS), float_rows(TAIL_ROWS)],
        low, got_hx, got_hy, vector, tail, *got_tz,
    )
    got_hz = [moved(part, "z", s + 1) for s, part in enumerate((one, two, three))]
    got_tx = moved(tx, "x", 1)
    place = coordinates(device_number() // inner_count())["z"]
    stacked = jnp.stack([vector] + [part[HEAD_ROWS:] for part in got_hz])
    total = sum(
        summed(found[:VECTOR_ROWS], found[VECTOR_ROWS:])
        for found in (lax.dynamic_index_in_dim(stacked, (place - z) % 4, 0, keepdims=False) for z in range(4))
    )
    return (own, *got_hz, own_tail, got_tx), total, input_grad


def lower_lanes(shape):
    return lax.broadcasted_iota(jnp.int32, shape, 1) < HEAD_SIZE


def half_turn(value):
    return pltpu.roll(value, HEAD_SIZE, 1)


def side_by_side(left, right):
    return jnp.where(lower_lanes(left.shape), left, half_turn(right))


def kind_of(block):
    return jnp.where(block >= 24, 1, jnp.where(block >= 8, 0, jnp.where((block == 3) | (block == 4), 2, 1)))


def tile_kernel(kind_ref, flat_ref, head_ref, tail_ref, tiles, narrow):
    kind = kind_ref[0]

    @pl.when(kind == 0)
    def _():
        for j in range(12):
            tiles[72 * j : 72 * j + 72, :] = flat_ref[pl.ds(j, 72, stride=12), :]

    @pl.when(kind == 1)
    def _():
        lines = [flat_ref[pl.ds(t, 96, stride=9), :] for t in range(9)]
        turned = [half_turn(line) for line in lines[4:]]
        low = lower_lanes((96, LANES))
        for j in range(4):
            tiles[pl.ds(192 * j, 96, stride=2), :] = lines[j]
            tiles[pl.ds(192 * j + 1, 96, stride=2), :] = jnp.where(low, turned[j], turned[j + 1])
        narrow[pl.ds(0, 96, stride=2), :] = lines[4]
        narrow[pl.ds(1, 96, stride=2), :] = turned[4]
        tiles[768:864, :] = side_by_side(narrow[0:96, :], narrow[96:192, :])

    @pl.when(kind == 2)
    def _():
        lines = [flat_ref[pl.ds(t, 288, stride=3), :] for t in range(3)]
        first, second = half_turn(lines[1]), half_turn(lines[2])
        tiles[pl.ds(0, 288, stride=2), :] = lines[0]
        tiles[pl.ds(1, 288, stride=2), :] = jnp.where(lower_lanes((288, LANES)), first, second)
        narrow[pl.ds(0, 288, stride=2), :] = lines[1]
        narrow[pl.ds(1, 288, stride=2), :] = second
        tiles[576:864, :] = side_by_side(narrow[0:288, :], narrow[288:576, :])

    head_ref[...] = tiles[0:HEAD_ROWS, :].astype(BF16)
    tail_ref[...] = tiles[HEAD_ROWS:BLOCK_ROWS, :].astype(BF16)


def to_tiles(kind, flat):
    return pl.pallas_call(
        tile_kernel,
        out_shape=(
            jax.ShapeDtypeStruct((HEAD_ROWS, LANES), BF16),
            jax.ShapeDtypeStruct((TAIL_ROWS, LANES), BF16),
        ),
        in_specs=[
            pl.BlockSpec(memory_space=pltpu.SMEM),
            pl.BlockSpec(memory_space=pltpu.VMEM),
        ],
        out_specs=(pl.BlockSpec(memory_space=pltpu.VMEM),) * 2,
        scratch_shapes=[
            pltpu.VMEM((BLOCK_ROWS, LANES), F32),
            pltpu.VMEM((HEAD_ROWS, LANES), F32),
        ],
        name="to_tiles",
    )(kind, flat)


def flat_kernel(kind_ref, head_ref, one_ref, two_ref, three_ref, tail_ref, other_ref, *refs):
    kind = kind_ref[0]
    tiles, narrow, flat_ref = refs[-3:]
    tiles[0:HEAD_ROWS, :] = (head_ref[...] + one_ref[0:HEAD_ROWS, :].astype(F32)) + (
        two_ref[0:HEAD_ROWS, :].astype(F32) + three_ref[0:HEAD_ROWS, :].astype(F32)
    )
    tiles[HEAD_ROWS:BLOCK_ROWS, :] = tail_ref[...] + other_ref[...].astype(F32)

    @pl.when(kind == 0)
    def _():
        for j in range(12):
            flat_ref[pl.ds(j, 72, stride=12), :] = tiles[72 * j : 72 * j + 72, :]

    @pl.when(kind == 1)
    def _():
        low = lower_lanes((96, LANES))
        narrow[0:96, :] = tiles[768:864, :]
        narrow[96:192, :] = half_turn(tiles[768:864, :])
        odd = [half_turn(tiles[pl.ds(192 * j + 1, 96, stride=2), :]) for j in range(4)]
        for j in range(4):
            flat_ref[pl.ds(j, 96, stride=9), :] = tiles[pl.ds(192 * j, 96, stride=2), :]
        flat_ref[pl.ds(4, 96, stride=9), :] = jnp.where(low, narrow[pl.ds(0, 96, stride=2), :], odd[0])
        for j in range(3):
            flat_ref[pl.ds(5 + j, 96, stride=9), :] = jnp.where(low, odd[j], odd[j + 1])
        last = half_turn(narrow[pl.ds(1, 96, stride=2), :])
        flat_ref[pl.ds(8, 96, stride=9), :] = jnp.where(low, odd[3], last)

    @pl.when(kind == 2)
    def _():
        low = lower_lanes((288, LANES))
        narrow[0:288, :] = tiles[576:864, :]
        narrow[288:576, :] = half_turn(tiles[576:864, :])
        odd = half_turn(tiles[pl.ds(1, 288, stride=2), :])
        flat_ref[pl.ds(0, 288, stride=3), :] = tiles[pl.ds(0, 288, stride=2), :]
        flat_ref[pl.ds(1, 288, stride=3), :] = jnp.where(low, narrow[pl.ds(0, 288, stride=2), :], odd)
        last = half_turn(narrow[pl.ds(1, 288, stride=2), :])
        flat_ref[pl.ds(2, 288, stride=3), :] = jnp.where(low, odd, last)


    if len(refs) == 4:
        refs[0][...] = flat_ref[...]
        return
    weight_ref, first_ref, second_ref, new_weight, new_first, new_second = refs[:6]

    @pl.loop(0, 6)
    def _(k):
        rows = pl.ds(pl.multiple_of(k * 144, 8), 144)
        new_weight[rows, :], new_first[rows, :], new_second[rows, :] = adamw(
            weight_ref[rows, :], flat_ref[rows, :], first_ref[rows, :], second_ref[rows, :], RATE_MATRIX, DECAY
        )


def finish(kind, parts, state):
    vmem = pl.BlockSpec(memory_space=pltpu.VMEM)
    flat = jax.ShapeDtypeStruct((BLOCK_ROWS, LANES), F32)
    count = max(1, len(state))
    return pl.pallas_call(
        flat_kernel,
        out_shape=(flat,) * count,
        in_specs=[pl.BlockSpec(memory_space=pltpu.SMEM)] + [vmem] * (6 + len(state)),
        out_specs=(vmem,) * count,
        scratch_shapes=[
            pltpu.VMEM((BLOCK_ROWS, LANES), F32),
            pltpu.VMEM((HEAD_ROWS, LANES), F32),
            pltpu.VMEM((BLOCK_ROWS, LANES), F32),
        ],
        name="finish",
    )(kind, *parts, *state)


def product(left, right):
    return jnp.dot(left, right, preferred_element_type=F32)


def times_transposed(left, right):
    return lax.dot_general(left, right, (((1,), (1,)), ((), ())), preferred_element_type=F32)


def rows_product(left, right):
    return lax.dot_general(left, right, (((0,), (0,)), ((), ())), preferred_element_type=F32)


def swapped(value):
    lane = lax.broadcasted_iota(jnp.int32, value.shape, 1)
    return jnp.where(lane % HEAD_SIZE < HEAD_SIZE // 2, pltpu.roll(value, 96, 1), pltpu.roll(value, 32, 1))


def rope(value, cosines, sines):
    return value * cosines + swapped(value) * sines


def rope_back(value, cosines, sines):
    return value * cosines - swapped(value) * sines


def row_mean(value):
    return jnp.sum(value, axis=-1, keepdims=True) * (1.0 / MODEL_WIDTH)


def normed_rows(value):
    scale = lax.rsqrt(row_mean(value * value) + EPS_NORM)
    return value * scale, scale


def place_rows(ref, head_tile, tail_tile, first):
    for j in range(3):
        ref[first : first + 192, LANES * j : LANES * j + LANES] = head_tile[192 * j : 192 * j + 192, :]
    ref[first : first + 192, 384:512] = tail_tile[0:192, :]
    rest = tail_tile[192:288, :].astype(F32)
    low = lower_lanes(rest.shape)
    ref[first : first + 96, 512:640] = jnp.where(low, rest, 0.0).astype(BF16)
    ref[first + 96 : first + 192, 512:640] = jnp.where(low, half_turn(rest), 0.0).astype(BF16)


def tiles_of_rows(value):
    head = jnp.concatenate([value[:, LANES * j : LANES * j + LANES] for j in range(3)], axis=0)
    rest = side_by_side(value[0:96, 512:640], value[96:192, 512:640])
    return head, jnp.concatenate([value[:, 384:512], rest], axis=0)


def layer_kernel(*refs):
    slots = refs[0]
    head_parts = refs[1:9]
    tail_parts = refs[9:13]
    tokens_pair, cos_pair, sin_pair = refs[13:15], refs[15:17], refs[17:19]
    (place_q_ref, place_k_ref, gains_ref, bias_q_ref, bias_kv_ref, grad_ref) = refs[19:25]
    (block_out_ref, send_first, send_rest, keep_first, keep_rest) = refs[25:30]
    dkv_refs = refs[30:34]
    (dq_wq_ref, d_mid_ref, w_kv) = refs[34:37]
    (raw_head, raw_tail, w_q, w_out, w_gate, w_up, w_down, normed_all, hidden_all, keys, values, queries, probs, attended, act_all, block_acc, d_hidden, d_attended, dkv_all, d_query, send_all, keep_all, vector_ref, sems) = refs[37:]

    copies = []
    for k, part in enumerate(head_parts):
        copies.append(pltpu.make_async_copy(part, raw_head.at[pl.ds(4 * k, 4)], sems.at[k]))
    for k, part in enumerate(tail_parts):
        copies.append(pltpu.make_async_copy(part, raw_tail.at[pl.ds(8 * k, 8)], sems.at[8 + k]))
    for copy in copies:
        copy.start()
    for copy in copies:
        copy.wait()

    core = slots[MY_CORE]

    def at_slot(pair, slot):
        return pair[slot % 2].at[slot // 2]

    def head_tile(block):
        return raw_head.at[slots[AT_HEAD + block]]

    def tail_tile(block):
        return raw_tail.at[slots[AT_TAIL + block]]

    for ref in (w_q, w_out, w_gate, w_up, w_kv):
        ref[576:640, :] = jnp.zeros((64, ref.shape[1]), BF16)
    for k in range(3):
        place_rows(w_q, head_tile(k), tail_tile(k), 192 * k)
        place_rows(w_out, head_tile(5 + k), tail_tile(5 + k), 192 * k)
    for k in range(8):
        place_rows(w_down, head_tile(24 + k), tail_tile(24 + k), 192 * k)
    w_kv[0:576, 0:128] = head_tile(3)[...]
    w_kv[0:576, 128:256] = head_tile(4)[...]
    rest_key = tail_tile(3)[...].astype(F32)
    rest_value = tail_tile(4)[...].astype(F32)
    low = lower_lanes(rest_key.shape)
    w_kv[0:288, 256:384] = jnp.where(low, rest_key, half_turn(rest_value)).astype(BF16)
    w_kv[288:576, 256:384] = jnp.where(low, half_turn(rest_key), rest_value).astype(BF16)
    for ref, base in ((w_gate, 8), (w_up, 16)):
        for k in range(4):
            for i in range(6):
                if i < 4:
                    even = head_tile(base + 2 * k)[144 * i : 144 * i + 144, :].astype(F32)
                    odd = head_tile(base + 2 * k + 1)[144 * i : 144 * i + 144, :].astype(F32)
                else:
                    even = tail_tile(base + 2 * k)[144 * (i - 4) : 144 * (i - 4) + 144, :].astype(F32)
                    odd = tail_tile(base + 2 * k + 1)[144 * (i - 4) : 144 * (i - 4) + 144, :].astype(F32)
                ref[144 * k : 144 * k + 144, 256 * i : 256 * i + 128] = jnp.concatenate(
                    [even[0:72], odd[0:72]], axis=0
                ).astype(BF16)
                ref[144 * k : 144 * k + 144, 256 * i + 128 : 256 * i + 256] = jnp.concatenate(
                    [even[72:144], odd[72:144]], axis=0
                ).astype(BF16)

    gain_one = gains_ref[0:1, :]
    gain_two = gains_ref[1:2, :]
    low_rows = lower_lanes((ROWS, LANES))

    @pl.loop(0, 2)
    def _(mb):
        lane = lax.broadcasted_iota(jnp.int32, (ROWS, WIDE), 1)
        for slot in range(4):
            rows = pl.ds(pl.multiple_of(mb * 512 + slot * ROWS, ROWS), ROWS)
            x = jnp.where(lane < MODEL_WIDTH, at_slot(tokens_pair, slot)[mb].astype(F32), 0.0)
            normed, _ = normed_rows(x)
            normed_all[rows, :] = normed
            hidden_all[rows, :] = (normed * gain_one).astype(BF16)
        rows = pl.ds(pl.multiple_of(mb * 512, 512), 512)
        pair = product(hidden_all[rows, :], w_kv[...]) + bias_kv_ref[...]
        cosines = jnp.concatenate([at_slot(cos_pair, slot)[mb] for slot in range(4)], axis=0)
        sines = jnp.concatenate([at_slot(sin_pair, slot)[mb] for slot in range(4)], axis=0)
        key_a = rope(pair[:, 0:128], cosines, sines)
        key_b = rope(pair[:, 256:384], cosines, sines)
        value_a, value_b = pair[:, 128:256], pair[:, 256:384]
        low_keys = lower_lanes((512, LANES))
        turned = half_turn(key_a)
        keys[rows, 0:128] = jnp.where(low_keys, key_a, turned).astype(BF16)
        keys[rows, 128:256] = jnp.where(low_keys, turned, key_a).astype(BF16)
        keys[rows, 256:384] = jnp.where(low_keys, key_b, half_turn(key_b)).astype(BF16)
        turned = half_turn(value_a)
        values[rows, 0:128] = jnp.where(low_keys, value_a, turned).astype(BF16)
        values[rows, 128:256] = jnp.where(low_keys, turned, value_a).astype(BF16)
        values[rows, 256:384] = jnp.where(low_keys, half_turn(value_b), value_b).astype(BF16)

    def heads_of(ref, rows, group):
        stacked = []
        for k in range(3):
            number = 3 * group + k
            tile = ref[rows, LANES * (number // 2) : LANES * (number // 2) + LANES]
            keep = low_rows if number % 2 == 0 else jnp.logical_not(low_rows)
            stacked.append(jnp.where(keep, tile.astype(F32), 0.0).astype(BF16))
        return jnp.concatenate(stacked, axis=0)

    def tiles_of_heads(parts):
        found = [jnp.where(low_rows, parts[2 * k], parts[2 * k + 1]) for k in range(4)]
        return found + [jnp.where(low_rows, parts[8], 0.0)]

    @pl.loop(0, 2)
    def _(mb):
        rows = pl.ds(pl.multiple_of(mb * ROWS, ROWS), ROWS)
        key_rows = pl.ds(pl.multiple_of(mb * 512, 512), 512)
        cosines, sines = cos_pair[0][0, mb], sin_pair[0][0, mb]
        made = product(hidden_all[pl.ds(pl.multiple_of(mb * 512, 512), ROWS), :], w_q[...]) + bias_q_ref[...]
        for k in range(5):
            queries[rows, LANES * k : LANES * k + LANES] = rope(
                made[:, LANES * k : LANES * k + LANES], cosines, sines
            ).astype(BF16)
        allowed = place_q_ref[mb] >= place_k_ref[mb]
        allowed = jnp.concatenate([allowed.astype(F32)] * 3, axis=0) > 0.5
        parts = []
        for group in range(KEY_VALUE_HEADS):
            lanes = slice(LANES * group, LANES * group + LANES)
            scores = times_transposed(heads_of(queries, rows, group), keys[key_rows, lanes])
            scores = jnp.where(allowed, scores * HEAD_SIZE ** (-0.5), MASKED)
            top = jnp.max(scores, axis=-1, keepdims=True)
            powers = jnp.exp(scores - top)
            found = powers * (1.0 / jnp.sum(powers, axis=-1, keepdims=True))
            probs[mb, group] = found
            out = product(found.astype(BF16), values[key_rows, lanes])
            parts += [out[ROWS * k : ROWS * k + ROWS] for k in range(3)]
        for k, tile in enumerate(tiles_of_heads(parts)):
            attended[rows, LANES * k : LANES * k + LANES] = tile.astype(BF16)

    lane = lax.broadcasted_iota(jnp.int32, (2 * ROWS, WIDE), 1)
    x_own = tokens_pair[0][0].astype(F32).reshape(2 * ROWS, WIDE)
    x_own = jnp.where(lane < MODEL_WIDTH, x_own, 0.0)
    resid_mid = x_own + product(attended[...], w_out[...])
    normed_two, scale_two = normed_rows(resid_mid)
    hidden_two = (normed_two * gain_two).astype(BF16)
    hidden_turned = hidden_two.T
    grad_low = grad_ref[...]
    block_acc[...] = resid_mid
    d_hidden[...] = jnp.zeros_like(d_hidden)

    def store_pair(at, even, odd, table, first):
        rows = pl.ds(pl.multiple_of(slots[table + at] + first, 16), even.shape[0])
        send_all[rows, :] = jnp.where(core == 0, odd, even).astype(BF16)
        keep_all[rows, :] = jnp.where(core == 0, even, odd).astype(BF16)

    def feed_forward(chunk, first, table):
        cols = pl.ds(pl.multiple_of(chunk * 512, 512), 512)
        gate = product(hidden_two, w_gate[:, cols])
        up = product(hidden_two, w_up[:, cols])
        sigma = 1.0 / (1.0 + jnp.exp(-gate))
        act = (gate * sigma * up).astype(BF16)
        act_all[:, cols] = act
        down = w_down[cols, :]
        d_act = times_transposed(grad_low, down)
        block_acc[...] += product(act, down)
        d_up = (d_act * gate * sigma).astype(BF16)
        d_gate = (d_act * up * sigma * (1.0 + gate * (1.0 - sigma))).astype(BF16)
        d_hidden[...] += times_transposed(d_gate, w_gate[:, cols]) + times_transposed(d_up, w_up[:, cols])
        for base, cotangent in ((4, d_gate), (8, d_up)):
            made = product(hidden_turned, cotangent)
            for k in range(4):
                part = made[144 * k : 144 * k + 144, :]
                even = jnp.concatenate([part[0:72, LANES * j : LANES * j + LANES] for j in range(4)], axis=0)
                odd = jnp.concatenate([part[72:144, LANES * j : LANES * j + LANES] for j in range(4)], axis=0)
                store_pair(base + k, even, odd, table, (chunk - first) * 288)

    @pl.loop(0, 2)
    def _(chunk):
        feed_forward(chunk, 0, TO_HEAD)

    feed_forward(2, 2, TO_TAIL)

    def store_rows(at, even, odd):
        even_head, even_tail = even
        odd_head, odd_tail = odd
        store_pair(at, even_head, odd_head, TO_HEAD, 0)
        store_pair(at, even_tail, odd_tail, TO_TAIL, 0)

    @pl.loop(0, 4)
    def _(k):
        made = rows_product(act_all[:, pl.ds(pl.multiple_of(k * 384, 128), 384)], grad_low)
        store_rows(12 + k, tiles_of_rows(made[0:192]), tiles_of_rows(made[192:384]))

    for mb in range(2):
        block_out_ref[mb] = block_acc[ROWS * mb : ROWS * mb + ROWS, :].T[0:MODEL_WIDTH].astype(BF16)

    d_two = d_hidden[...]
    vector_ref[...] = jnp.zeros_like(vector_ref)
    vector_ref[1:2, :] = jnp.sum(d_two * normed_two, axis=0, keepdims=True)
    d_norm = d_two * gain_two
    d_mid = grad_low.astype(F32) + scale_two * (d_norm - normed_two * row_mean(d_norm * normed_two))
    d_mid_ref[...] = d_mid
    d_branch = d_mid.astype(BF16)
    d_attended[...] = times_transposed(d_branch, w_out[...]).astype(BF16)
    grad_out = rows_product(attended[...], d_branch)

    @pl.loop(0, 2)
    def _(mb):
        rows = pl.ds(pl.multiple_of(mb * ROWS, ROWS), ROWS)
        key_rows = pl.ds(pl.multiple_of(mb * 512, 512), 512)
        parts = []
        d_keys = []
        d_values = []
        for group in range(KEY_VALUE_HEADS):
            lanes = slice(LANES * group, LANES * group + LANES)
            query_rows = heads_of(queries, rows, group)
            cotangent = heads_of(d_attended, rows, group)
            found = probs[mb, group]
            d_probs = times_transposed(cotangent, values[key_rows, lanes])
            delta = jnp.sum(found * d_probs, axis=-1, keepdims=True)
            d_scores = (found * (d_probs - delta)).astype(BF16)
            out = product(d_scores, keys[key_rows, lanes]) * HEAD_SIZE ** (-0.5)
            parts += [out[ROWS * k : ROWS * k + ROWS] for k in range(3)]
            d_key = rows_product(d_scores, query_rows) * HEAD_SIZE ** (-0.5)
            d_value = rows_product(found.astype(BF16), cotangent)
            d_keys.append(d_key + half_turn(d_key))
            d_values.append(d_value + half_turn(d_value))
        cosines, sines = cos_pair[0][0, mb], sin_pair[0][0, mb]
        for k, tile in enumerate(tiles_of_heads(parts)):
            d_query[rows, LANES * k : LANES * k + LANES] = rope_back(tile, cosines, sines).astype(BF16)
        low_keys = lower_lanes((512, LANES))
        cosines = jnp.concatenate([at_slot(cos_pair, slot)[mb] for slot in range(4)], axis=0)
        sines = jnp.concatenate([at_slot(sin_pair, slot)[mb] for slot in range(4)], axis=0)
        key_a = rope_back(jnp.where(low_keys, d_keys[0], d_keys[1]), cosines, sines)
        key_b = rope_back(d_keys[2], cosines, sines)
        dkv_all[key_rows, 0:128] = key_a.astype(BF16)
        dkv_all[key_rows, 128:256] = jnp.where(low_keys, d_values[0], d_values[1]).astype(BF16)
        dkv_all[key_rows, 256:384] = jnp.where(low_keys, key_b, d_values[2]).astype(BF16)
        for slot in range(4):
            dkv_refs[slot][mb] = dkv_all[pl.ds(pl.multiple_of(mb * 512 + slot * ROWS, ROWS), ROWS), :]

    dkv = dkv_all[...]
    d_q = d_query[...]
    dq_wq = times_transposed(d_q, w_q[...])
    dq_wq_ref[...] = dq_wq
    vector_ref[2:3, :] = jnp.sum(d_q.astype(F32), axis=0, keepdims=True)
    vector_ref[3:4, 0:384] = jnp.sum(dkv.astype(F32), axis=0, keepdims=True)
    gain_sum = jnp.zeros((1, WIDE), F32)
    for mb in range(2):
        gain_sum += jnp.sum(dq_wq[ROWS * mb : ROWS * mb + ROWS] * normed_all[512 * mb : 512 * mb + ROWS, :], axis=0, keepdims=True)
    for k in range(4):
        part = slice(256 * k, 256 * k + 256)
        gain_sum += jnp.sum(times_transposed(dkv_all[part, :], w_kv[...]) * normed_all[part, :], axis=0, keepdims=True)
    vector_ref[0:1, :] = gain_sum

    hidden_own = jnp.concatenate([hidden_all[0:ROWS, :], hidden_all[512 : 512 + ROWS, :]], axis=0)
    grad_q = rows_product(hidden_own, d_q)
    grad_kv = rows_product(hidden_all[...], dkv)
    rest = grad_kv[0:576, 256:384]
    low = lower_lanes((288, LANES))
    key_tiles = (grad_kv[0:576, 0:128], jnp.where(low, rest[0:288], half_turn(rest[288:576])))
    value_tiles = (grad_kv[0:576, 128:256], jnp.where(low, half_turn(rest[0:288]), rest[288:576]))
    query_tiles = [tiles_of_rows(grad_q[192 * k : 192 * k + 192]) for k in range(3)]
    out_tiles = [tiles_of_rows(grad_out[192 * k : 192 * k + 192]) for k in range(3)]
    store_rows(0, query_tiles[0], query_tiles[1])
    store_rows(1, query_tiles[2], key_tiles)
    store_rows(2, value_tiles, out_tiles[0])
    store_rows(3, out_tiles[1], out_tiles[2])
    vector = jnp.concatenate(
        [vector_ref[:, LANES * k : LANES * k + LANES] for k in range(5)] + [jnp.zeros((8, LANES), F32)], axis=0
    )
    high = vector.astype(BF16)
    rest = (vector - high.astype(F32)).astype(BF16)
    at = FIRST_AT + 2 * PART
    for ref in (send_all, keep_all):
        ref[at : at + VECTOR_ROWS, :] = high
        ref[at + VECTOR_ROWS : at + 2 * VECTOR_ROWS, :] = rest
    copies = [
        pltpu.make_async_copy(send_all.at[pl.ds(FIRST_AT, FIRST_ROWS)], send_first, sems.at[0]),
        pltpu.make_async_copy(send_all.at[pl.ds(0, FIRST_AT)], send_rest, sems.at[1]),
        pltpu.make_async_copy(keep_all.at[pl.ds(FIRST_AT, FIRST_ROWS)], keep_first, sems.at[2]),
        pltpu.make_async_copy(keep_all.at[pl.ds(0, FIRST_AT)], keep_rest, sems.at[3]),
    ]
    for copy in copies:
        copy.start()
    for copy in copies:
        copy.wait()


def run_layer(slots, heads, tails, *others):
    shape = jax.ShapeDtypeStruct
    vmem = pl.BlockSpec(memory_space=pltpu.VMEM)
    anywhere = pl.BlockSpec(memory_space=pl.ANY)
    scratch = [
        ((BLOCKS, HEAD_ROWS, LANES), BF16),
        ((BLOCKS, TAIL_ROWS, LANES), BF16),
        ((WIDE, WIDE), BF16),
        ((WIDE, WIDE), BF16),
        ((WIDE, FF), BF16),
        ((WIDE, FF), BF16),
        ((FF, WIDE), BF16),
        ((1024, WIDE), F32),
        ((1024, WIDE), BF16),
        ((1024, 384), BF16),
        ((1024, 384), BF16),
        ((256, WIDE), BF16),
        ((2, 3, 384, 512), F32),
        ((256, WIDE), BF16),
        ((256, FF), BF16),
        ((256, WIDE), F32),
        ((256, WIDE), F32),
        ((256, WIDE), BF16),
        ((1024, 384), BF16),
        ((256, WIDE), BF16),
        ((FIRST_AT + FIRST_ROWS, LANES), BF16),
        ((FIRST_AT + FIRST_ROWS, LANES), BF16),
        ((8, WIDE), F32),
    ]
    return pl.pallas_call(
        layer_kernel,
        out_shape=(
            shape((2, MODEL_WIDTH, ROWS), BF16),
            shape((FIRST_ROWS, LANES), BF16),
            shape((FIRST_AT, LANES), BF16),
            shape((FIRST_ROWS, LANES), BF16),
            shape((FIRST_AT, LANES), BF16),
            shape((2, ROWS, 384), BF16),
            shape((2, ROWS, 384), BF16),
            shape((2, ROWS, 384), BF16),
            shape((2, ROWS, 384), BF16),
            shape((256, WIDE), F32),
            shape((256, WIDE), F32),
            shape((WIDE, 384), BF16),
        ),
        in_specs=[pl.BlockSpec(memory_space=pltpu.SMEM)] + [anywhere] * 12 + [vmem] * 12,
        out_specs=(vmem,) + (anywhere,) * 4 + (vmem,) * 7,
        scratch_shapes=[pltpu.VMEM(dims, kind) for dims, kind in scratch]
        + [pltpu.SemaphoreType.DMA((12,))],
        compiler_params=pltpu.CompilerParams(vmem_limit_bytes=50 * 1024 * 1024),
        name="layer",
    )(slots, *heads, *tails, *others)


def input_kernel(tokens_ref, gains_ref, w_kv_ref, dq_wq_ref, d_mid_ref, own_ref, one_ref, two_ref, three_ref, out_ref):
    lane = lax.broadcasted_iota(jnp.int32, (2 * ROWS, WIDE), 1)
    x = jnp.where(lane < MODEL_WIDTH, tokens_ref[0].astype(F32).reshape(2 * ROWS, WIDE), 0.0)
    normed, scale = normed_rows(x)
    total = summed(own_ref[...], one_ref[...], two_ref[...], three_ref[...])
    total = total.reshape(2 * ROWS, 384).astype(BF16)
    d_norm = (dq_wq_ref[...] + times_transposed(total, w_kv_ref[...])) * gains_ref[0:1, :]
    d_input = d_mid_ref[...] + scale * (d_norm - normed * row_mean(d_norm * normed))
    for mb in range(2):
        out_ref[mb] = d_input[ROWS * mb : ROWS * mb + ROWS].T[0:MODEL_WIDTH].astype(BF16)


def run_input(tokens, gains, w_kv, dq_wq, d_mid, parts):
    return pl.pallas_call(
        input_kernel,
        out_shape=jax.ShapeDtypeStruct((2, MODEL_WIDTH, ROWS), BF16),
        in_specs=[pl.BlockSpec(memory_space=pltpu.VMEM)] * 9,
        out_specs=pl.BlockSpec(memory_space=pltpu.VMEM),
        name="input_grad",
    )(tokens, gains, w_kv, dq_wq, d_mid, *parts)


def adamw(param, grad, mom_one, mom_two, rate, decay):
    new_one = BETA_ONE * mom_one + (1.0 - BETA_ONE) * grad
    new_two = BETA_TWO * mom_two + (1.0 - BETA_TWO) * grad * grad
    fixed_one = new_one / (1.0 - BETA_ONE**STEP)
    fixed_two = new_two / (1.0 - BETA_TWO**STEP)
    new_param = param - rate * (fixed_one / (jnp.sqrt(fixed_two) + EPS_ADAM) + decay * param)
    return (new_param, new_one, new_two)


def inner_groups():
    inner = inner_count()
    data_inner = inner // lax.axis_size("ctx")
    data_count = lax.axis_size("dp")
    return [list(range(k, k + data_inner)) for k in range(0, data_count, data_inner)]


def whole_block(flat):
    if inner_count() == 1:
        return flat
    flat = lax.all_gather(flat, "ctx", axis=0, tiled=True)
    return lax.all_gather(flat, "dp", axis=0, tiled=True, axis_index_groups=inner_groups())


def own_slice(block):
    if inner_count() == 1:
        return block
    block = lax.psum_scatter(
        block, "dp", scatter_dimension=0, tiled=True, axis_index_groups=inner_groups()
    )
    return lax.psum_scatter(block, "ctx", scatter_dimension=0, tiled=True)


def bias_tiles(bias_key, bias_value):
    return jnp.concatenate([bias_key[:128], bias_value[:128], bias_key[128:], bias_value[128:]])


def local(tokens_in, places, out_grad, weights, first_moment, second_moment, vectors, vector_first, vector_second):
    kind = kind_of(device_number() // inner_count()).astype(jnp.int32).reshape(1)
    block = whole_block(weights).reshape(BLOCK_ROWS, LANES)
    head, tail = to_tiles(kind, block)

    head, tail, tokens_in, places = together(head, tail, tokens_in, places)
    own_tokens = tokens_in.reshape(2, ROWS, MODEL_WIDTH)
    own_places = places.reshape(2, ROWS)
    marks = jnp.stack([own_places // 16, own_places % 16], axis=-1).astype(BF16)
    packed = jnp.concatenate(
        [own_tokens, marks, jnp.zeros((2, ROWS, WIDE - MODEL_WIDTH - 2), BF16)], axis=-1
    )
    padding = ((0, 0), (0, WIDE - MODEL_WIDTH))
    gains = jnp.pad(vectors[: 2 * MODEL_WIDTH].reshape(2, MODEL_WIDTH), padding)
    bias_q = jnp.pad(vectors[2 * MODEL_WIDTH : 3 * MODEL_WIDTH].reshape(1, MODEL_WIDTH), padding)
    bias_kv = bias_tiles(vectors[1728:1920], vectors[1920:2112]).reshape(1, 384)
    grad = jnp.pad(out_grad.reshape(2 * ROWS, MODEL_WIDTH), padding)
    others = (slot_table(), gains, bias_q, bias_kv, grad)
    heads, tails, (near, far), (cosines, sines), others = gather_all(head, tail, packed, others)
    slots, gains, bias_q, bias_kv, grad = others
    cosines_far, sines_far = place_tables(far)
    place_all = jnp.stack([places_of(near), places_of(far)], axis=1)
    place_q = place_all[0, 0][..., None]
    place_k = jnp.transpose(place_all.reshape(4, 2, ROWS), (1, 0, 2)).reshape(2, 1, 4 * ROWS)

    (block_out, send_first, send_rest, keep_first, keep_rest, *pairs, dq_wq, d_mid, w_kv) = run_layer(
        slots, heads, tails, near, far, cosines, cosines_far, sines, sines_far, place_q, place_k, gains, bias_q, bias_kv, grad
    )
    make_input = lambda parts: run_input(near, gains, w_kv, dq_wq, d_mid, parts)
    parts, vector, input_grad = scatter_blocks(send_first, send_rest, keep_first, keep_rest, pairs, make_input)
    state = (weights, first_moment, second_moment)
    if inner_count() == 1:
        updated = finish(kind, parts, [array.reshape(BLOCK_ROWS, LANES) for array in state])
        new_weights, new_first, new_second = [array.reshape(-1) for array in updated]
    else:
        vector = lax.psum(vector, "ctx")
        vector = lax.psum(vector, "dp", axis_index_groups=inner_groups())
        (block_grad,) = finish(kind, parts, [])
        grad_own = own_slice(block_grad.reshape(-1))
        new_weights, new_first, new_second = adamw(
            weights, grad_own, first_moment, second_moment, RATE_MATRIX, DECAY
        )
    vector = jnp.transpose(vector.reshape(6, 8, LANES), (1, 0, 2)).reshape(8, 6 * LANES)
    pair = vector[3]
    vector_grad = jnp.concatenate(
        [
            vector[0, :MODEL_WIDTH],
            vector[1, :MODEL_WIDTH],
            vector[2, :MODEL_WIDTH],
            pair[0:128],
            pair[256:320],
            pair[128:256],
            pair[320:384],
        ]
    )
    new_vectors, new_vector_first, new_vector_second = adamw(
        vectors, vector_grad, vector_first, vector_second, RATE_VECTOR, 0.0
    )
    shape = tokens_in.shape
    return (
        jnp.transpose(block_out, (0, 2, 1)).reshape(shape),
        jnp.transpose(input_grad, (0, 2, 1)).reshape(shape),
        new_weights,
        new_first,
        new_second,
        new_vectors,
        new_vector_first,
        new_vector_second,
    )


def solution(mesh):
    in_specs = (
        P(None, "dp", "ctx", None),
        P(None, "dp", "ctx"),
        P(None, "dp", "ctx", None),
        P(("dp", "ctx")),
        P(("dp", "ctx")),
        P(("dp", "ctx")),
        P(),
        P(),
        P(),
    )
    out_specs = (
        P(None, "dp", "ctx", None),
        P(None, "dp", "ctx", None),
        P(("dp", "ctx")),
        P(("dp", "ctx")),
        P(("dp", "ctx")),
        P(),
        P(),
        P(),
    )
    return jax.shard_map(local, mesh=mesh, in_specs=in_specs, out_specs=out_specs, check_vma=False)
```

```python
import jax
import jax.numpy as jnp
from jax import lax
from jax.experimental import pallas as pl
from jax.experimental.pallas import tpu as pltpu
from jax.sharding import PartitionSpec as P

MODEL_WIDTH = 576
QUERY_HEADS = 9
KEY_VALUE_HEADS = 3
HEAD_SIZE = 64
FF = 1536
STEP = 10

EPS_NORM = 1e-05
THETA = 100000.0
BETA_ONE = 0.9
BETA_TWO = 0.95
EPS_ADAM = 1e-08
RATE_MATRIX = 0.06
RATE_VECTOR = 0.3
DECAY = 0.1
MASKED = -1e30

LANES = 128
WIDE = 640
BLOCKS = 32
BLOCK_ROWS = 864
HEAD_ROWS = 576
TAIL_ROWS = BLOCK_ROWS - HEAD_ROWS
VECTOR_ROWS = 48
PART = 4 * HEAD_ROWS
FIRST_AT = 4 * PART
TAIL_AT = FIRST_AT + PART + 2 * VECTOR_ROWS
ALL_ROWS = TAIL_AT + PART
SEND_PARTS = [(FIRST_AT, PART + 2 * VECTOR_ROWS), (TAIL_AT, PART), (0, 3 * PART), (3 * PART, PART)]
KEEP_PARTS = SEND_PARTS[:2] + [(PART * k, PART) for k in range(4)]
SIZES = {"z": 4, "y": 2, "x": 2, "c": 2}
ROWS = 128
F32 = jnp.float32
BF16 = jnp.bfloat16


def coordinates(number):
    found = {}
    for name in ("c", "x", "y", "z"):
        found[name] = number % SIZES[name]
        number = number // SIZES[name]
    return found


def number_of(found):
    number = 0
    for name in ("z", "y", "x", "c"):
        number = number * SIZES[name] + found[name]
    return number


def device_number():
    return lax.axis_index("dp") * lax.axis_size("ctx") + lax.axis_index("ctx")


def inner_count():
    return lax.axis_size("dp") * lax.axis_size("ctx") // BLOCKS


def moved(buffer, name, shift):
    inner = inner_count()
    pairs = []
    for number in range(BLOCKS):
        found = coordinates(number)
        found[name] = (found[name] + shift) % SIZES[name]
        target = number_of(found)
        pairs += [(number * inner + k, target * inner + k) for k in range(inner)]
    return lax.ppermute(buffer, ("dp", "ctx"), pairs)


def across(buffer, distance):
    count = lax.axis_size("ctx")
    return lax.ppermute(buffer, "ctx", [(i, i ^ distance) for i in range(count)])


def together(*arrays):
    return lax.optimization_barrier(arrays)


def gather_all(head, tail, packed, others):
    hz = [moved(head, "z", s) for s in (1, 2, 3)]
    tx = moved(tail, "x", 1)
    two = across(packed, 2)
    head, tail, tx, two, *hz = together(head, tail, tx, two, *hz)
    own = jnp.stack([head] + hz)
    pair = jnp.stack([tail, tx])
    ay = moved(own, "y", 1)
    ax = moved(own, "x", 1)
    tz = [moved(pair, "z", s) for s in (1, 2, 3)]
    near = jnp.stack([packed, two])
    tables = place_tables(near)
    own, pair, ay, ax, near, tables, others, *tz = together(own, pair, ay, ax, near, tables, others, *tz)
    eight = jnp.concatenate([pair] + tz)
    far = across(near, 1)
    axy = moved(ay, "x", 1)
    ty = moved(eight, "y", 1)
    ac = moved(own, "c", 1)
    acy = moved(ay, "c", 1)
    acx = moved(ax, "c", 1)
    tc = moved(eight, "c", 1)
    axy, ty, ac, acy, acx, tc, far = together(axy, ty, ac, acy, acx, tc, far)
    acxy = moved(axy, "c", 1)
    tcy = moved(ty, "c", 1)
    heads = [own, ay, ax, axy, ac, acy, acx, acxy]
    return heads, [eight, ty, tc, tcy], (near, far), tables, others


def places_of(tokens):
    found = tokens[..., MODEL_WIDTH : MODEL_WIDTH + 2].astype(F32)
    return found[..., 0] * 16.0 + found[..., 1]


def place_tables(tokens):
    half_dim = HEAD_SIZE // 2
    frequency = THETA ** (-2.0 * jnp.arange(half_dim, dtype=F32) / HEAD_SIZE)
    angles = places_of(tokens)[..., None] * jnp.tile(frequency, 4)
    sign = jnp.where(jnp.arange(LANES) % HEAD_SIZE < half_dim, -1.0, 1.0).astype(F32)
    return jnp.cos(angles), jnp.sin(angles) * sign


def fold(order, relative):
    slot = 0
    for name in order:
        slot = slot * SIZES[name] + relative[name]
    return slot


def slot_table():
    mine = coordinates(device_number() // inner_count())
    entries = []
    for order in (("c", "x", "y", "z"), ("c", "y", "z", "x")):
        for number in range(BLOCKS):
            found = coordinates(number)
            entries.append(fold(order, {n: (mine[n] - found[n]) % SIZES[n] for n in SIZES}))
    for number in range(0, BLOCKS, 2):
        found = coordinates(number)
        slot = fold(("x", "y", "z"), {n: (found[n] - mine[n]) % SIZES[n] for n in SIZES})
        entries.append(slot * HEAD_ROWS + jnp.where(slot < 12, 0, FIRST_AT - 12 * HEAD_ROWS))
    for number in range(0, BLOCKS, 2):
        found = coordinates(number)
        slot = fold(("y", "z", "x"), {n: (found[n] - mine[n]) % SIZES[n] for n in SIZES})
        entries.append(slot * TAIL_ROWS + jnp.where(slot < 8, 3 * PART, TAIL_AT - 8 * TAIL_ROWS))
    entries.append(mine["c"])
    return jnp.stack([jnp.asarray(entry, jnp.int32) for entry in entries])


AT_HEAD, AT_TAIL, TO_HEAD, TO_TAIL, MY_CORE = 0, BLOCKS, 2 * BLOCKS, 2 * BLOCKS + 16, 2 * BLOCKS + 32


def summed(*parts):
    total = parts[0].astype(F32)
    for part in parts[1:]:
        total = total + part.astype(F32)
    return total


def summed_vector(mine, other):
    total = summed(mine[:VECTOR_ROWS], other[:VECTOR_ROWS]) + summed(mine[VECTOR_ROWS:], other[VECTOR_ROWS:])
    high = lax.reduce_precision(total, 8, 7)
    return jnp.concatenate([high.astype(BF16), (total - high).astype(BF16)])


def scatter_blocks(sends, keeps, dkv_send, dkv_keep, make_input):
    keep_head, keep_tail, keep_low, keep_mid, keep_far, keep_rest = keeps
    got_head, got_tail = moved(sends[0], "c", 1), moved(sends[1], "c", 1)
    got_head, got_tail, rest_head, rest_tail, dkv_send = together(got_head, got_tail, *sends[2:], dkv_send)
    got_rest_head, got_rest_tail = moved(rest_head, "c", 1), moved(rest_tail, "c", 1)
    got_dkv = across(dkv_send, 1)
    vector = summed_vector(keep_head[PART:], got_head[PART:])
    hx = jnp.concatenate([summed(keep_head[:PART], got_head[:PART]).astype(BF16), vector])
    ty = summed(keep_tail, got_tail).astype(BF16)
    got_hx = moved(hx, "x", 1)
    got_ty = moved(ty, "y", 1)
    low, mid, far = [
        summed(keep, got_rest_head[PART * k : PART * k + PART]).astype(BF16)
        for k, keep in enumerate((keep_low, keep_mid, keep_far))
    ]
    tail = summed(keep_rest, got_rest_tail).astype(BF16)
    dkv = summed(dkv_keep, got_dkv).astype(BF16)
    got_hx, got_ty, low, mid, far, tail, dkv, vector = together(got_hx, got_ty, low, mid, far, tail, dkv, vector)
    vector = summed_vector(vector, got_hx[PART:])
    hy = jnp.concatenate([summed(mid, got_hx[:PART]).astype(BF16), vector])
    cuts = [slice(HEAD_ROWS * k, HEAD_ROWS * k + HEAD_ROWS) for k in range(4)]
    tz = [summed(tail[cut], got_ty[cut]).astype(BF16) for cut in cuts]
    got_hy = moved(hy, "y", 1)
    got_far = moved(far, "x", 1)
    got_tz = [moved(tz[s], "z", s) for s in (1, 2, 3)]
    got_hy, got_far, low, own_tail, vector, dkv, *got_tz = together(got_hy, got_far, low, tz[0], vector, dkv, *got_tz)
    vector = summed_vector(vector, got_hy[PART:])
    head = [summed(low[cut], got_far[cut], got_hy[cut]) for cut in cuts]
    got_hz = [moved(jnp.concatenate([head[s].astype(BF16), vector]), "z", s) for s in (1, 2, 3)]
    got_dkv = across(dkv[1], 2)
    tx = summed(own_tail[TAIL_ROWS:], *[part[TAIL_ROWS:] for part in got_tz]).astype(BF16)
    own_tail = summed(own_tail[:TAIL_ROWS], *[part[:TAIL_ROWS] for part in got_tz])
    input_grad = make_input((dkv[0], got_dkv))
    tx, input_grad = together(tx, input_grad)
    got_tx, vector = together(moved(tx, "x", 1), vector)
    place = coordinates(device_number() // inner_count())["z"]
    stacked = jnp.stack([vector] + [part[HEAD_ROWS:] for part in got_hz])
    total = sum(
        summed(found[:VECTOR_ROWS], found[VECTOR_ROWS:])
        for found in (lax.dynamic_index_in_dim(stacked, (place - z) % 4, 0, keepdims=False) for z in range(4))
    )
    return (head[0], *got_hz, own_tail, got_tx), total, input_grad


def lower_lanes(shape):
    return lax.broadcasted_iota(jnp.int32, shape, 1) < HEAD_SIZE


def half_turn(value):
    return pltpu.roll(value, HEAD_SIZE, 1)


def side_by_side(left, right):
    return jnp.where(lower_lanes(left.shape), left, half_turn(right))


def kind_of(block):
    return jnp.where(block >= 24, 1, jnp.where(block >= 8, 0, jnp.where((block == 3) | (block == 4), 2, 1)))


def tile_kernel(kind_ref, flat_ref, head_ref, tail_ref, tiles, narrow):
    kind = kind_ref[0]

    @pl.when(kind == 0)
    def _():
        for j in range(12):
            tiles[72 * j : 72 * j + 72, :] = flat_ref[pl.ds(j, 72, stride=12), :]

    @pl.when(kind == 1)
    def _():
        lines = [flat_ref[pl.ds(t, 96, stride=9), :] for t in range(9)]
        turned = [half_turn(line) for line in lines[4:]]
        low = lower_lanes((96, LANES))
        for j in range(4):
            tiles[pl.ds(192 * j, 96, stride=2), :] = lines[j]
            tiles[pl.ds(192 * j + 1, 96, stride=2), :] = jnp.where(low, turned[j], turned[j + 1])
        narrow[pl.ds(0, 96, stride=2), :] = lines[4]
        narrow[pl.ds(1, 96, stride=2), :] = turned[4]
        tiles[768:864, :] = side_by_side(narrow[0:96, :], narrow[96:192, :])

    @pl.when(kind == 2)
    def _():
        lines = [flat_ref[pl.ds(t, 288, stride=3), :] for t in range(3)]
        first, second = half_turn(lines[1]), half_turn(lines[2])
        tiles[pl.ds(0, 288, stride=2), :] = lines[0]
        tiles[pl.ds(1, 288, stride=2), :] = jnp.where(lower_lanes((288, LANES)), first, second)
        narrow[pl.ds(0, 288, stride=2), :] = lines[1]
        narrow[pl.ds(1, 288, stride=2), :] = second
        tiles[576:864, :] = side_by_side(narrow[0:288, :], narrow[288:576, :])

    head_ref[...] = tiles[0:HEAD_ROWS, :].astype(BF16)
    tail_ref[...] = tiles[HEAD_ROWS:BLOCK_ROWS, :].astype(BF16)


def to_tiles(kind, flat):
    return pl.pallas_call(
        tile_kernel,
        out_shape=(
            jax.ShapeDtypeStruct((HEAD_ROWS, LANES), BF16),
            jax.ShapeDtypeStruct((TAIL_ROWS, LANES), BF16),
        ),
        in_specs=[
            pl.BlockSpec(memory_space=pltpu.SMEM),
            pl.BlockSpec(memory_space=pltpu.VMEM),
        ],
        out_specs=(pl.BlockSpec(memory_space=pltpu.VMEM),) * 2,
        scratch_shapes=[
            pltpu.VMEM((BLOCK_ROWS, LANES), F32),
            pltpu.VMEM((HEAD_ROWS, LANES), F32),
        ],
        name="to_tiles",
    )(kind, flat)


def flat_kernel(kind_ref, head_ref, one_ref, two_ref, three_ref, tail_ref, other_ref, *refs):
    kind = kind_ref[0]
    tiles, narrow, flat_ref = refs[-3:]
    tiles[0:HEAD_ROWS, :] = (head_ref[...] + one_ref[0:HEAD_ROWS, :].astype(F32)) + (
        two_ref[0:HEAD_ROWS, :].astype(F32) + three_ref[0:HEAD_ROWS, :].astype(F32)
    )
    tiles[HEAD_ROWS:BLOCK_ROWS, :] = tail_ref[...] + other_ref[...].astype(F32)

    @pl.when(kind == 0)
    def _():
        for j in range(12):
            flat_ref[pl.ds(j, 72, stride=12), :] = tiles[72 * j : 72 * j + 72, :]

    @pl.when(kind == 1)
    def _():
        low = lower_lanes((96, LANES))
        narrow[0:96, :] = tiles[768:864, :]
        narrow[96:192, :] = half_turn(tiles[768:864, :])
        odd = [half_turn(tiles[pl.ds(192 * j + 1, 96, stride=2), :]) for j in range(4)]
        for j in range(4):
            flat_ref[pl.ds(j, 96, stride=9), :] = tiles[pl.ds(192 * j, 96, stride=2), :]
        flat_ref[pl.ds(4, 96, stride=9), :] = jnp.where(low, narrow[pl.ds(0, 96, stride=2), :], odd[0])
        for j in range(3):
            flat_ref[pl.ds(5 + j, 96, stride=9), :] = jnp.where(low, odd[j], odd[j + 1])
        last = half_turn(narrow[pl.ds(1, 96, stride=2), :])
        flat_ref[pl.ds(8, 96, stride=9), :] = jnp.where(low, odd[3], last)

    @pl.when(kind == 2)
    def _():
        low = lower_lanes((288, LANES))
        narrow[0:288, :] = tiles[576:864, :]
        narrow[288:576, :] = half_turn(tiles[576:864, :])
        odd = half_turn(tiles[pl.ds(1, 288, stride=2), :])
        flat_ref[pl.ds(0, 288, stride=3), :] = tiles[pl.ds(0, 288, stride=2), :]
        flat_ref[pl.ds(1, 288, stride=3), :] = jnp.where(low, narrow[pl.ds(0, 288, stride=2), :], odd)
        last = half_turn(narrow[pl.ds(1, 288, stride=2), :])
        flat_ref[pl.ds(2, 288, stride=3), :] = jnp.where(low, odd, last)


    if len(refs) == 4:
        refs[0][...] = flat_ref[...]
        return
    weight_ref, first_ref, second_ref, new_weight, new_first, new_second = refs[:6]

    @pl.loop(0, 6)
    def _(k):
        rows = pl.ds(pl.multiple_of(k * 144, 8), 144)
        new_weight[rows, :], new_first[rows, :], new_second[rows, :] = adamw(
            weight_ref[rows, :], flat_ref[rows, :], first_ref[rows, :], second_ref[rows, :], RATE_MATRIX, DECAY
        )


def finish(kind, parts, state):
    vmem = pl.BlockSpec(memory_space=pltpu.VMEM)
    flat = jax.ShapeDtypeStruct((BLOCK_ROWS, LANES), F32)
    count = max(1, len(state))
    return pl.pallas_call(
        flat_kernel,
        out_shape=(flat,) * count,
        in_specs=[pl.BlockSpec(memory_space=pltpu.SMEM)] + [vmem] * (6 + len(state)),
        out_specs=(vmem,) * count,
        scratch_shapes=[
            pltpu.VMEM((BLOCK_ROWS, LANES), F32),
            pltpu.VMEM((HEAD_ROWS, LANES), F32),
            pltpu.VMEM((BLOCK_ROWS, LANES), F32),
        ],
        name="finish",
    )(kind, *parts, *state)


def product(left, right):
    return jnp.dot(left, right, preferred_element_type=F32)


def times_transposed(left, right):
    return lax.dot_general(left, right, (((1,), (1,)), ((), ())), preferred_element_type=F32)


def rows_product(left, right):
    return lax.dot_general(left, right, (((0,), (0,)), ((), ())), preferred_element_type=F32)


def swapped(value):
    lane = lax.broadcasted_iota(jnp.int32, value.shape, 1)
    return jnp.where(lane % HEAD_SIZE < HEAD_SIZE // 2, pltpu.roll(value, 96, 1), pltpu.roll(value, 32, 1))


def rope(value, cosines, sines):
    return value * cosines + swapped(value) * sines


def rope_back(value, cosines, sines):
    return value * cosines - swapped(value) * sines


def row_mean(value):
    return jnp.sum(value, axis=-1, keepdims=True) * (1.0 / MODEL_WIDTH)


def normed_rows(value):
    scale = lax.rsqrt(row_mean(value * value) + EPS_NORM)
    return value * scale, scale


def place_rows(ref, head_tile, tail_tile, first):
    for j in range(3):
        ref[first : first + 192, LANES * j : LANES * j + LANES] = head_tile[192 * j : 192 * j + 192, :]
    ref[first : first + 192, 384:512] = tail_tile[0:192, :]
    rest = tail_tile[192:288, :].astype(F32)
    low = lower_lanes(rest.shape)
    ref[first : first + 96, 512:640] = jnp.where(low, rest, 0.0).astype(BF16)
    ref[first + 96 : first + 192, 512:640] = jnp.where(low, half_turn(rest), 0.0).astype(BF16)


def tiles_of_rows(value):
    head = jnp.concatenate([value[:, LANES * j : LANES * j + LANES] for j in range(3)], axis=0)
    rest = side_by_side(value[0:96, 512:640], value[96:192, 512:640])
    return head, jnp.concatenate([value[:, 384:512], rest], axis=0)


def layer_kernel(*refs):
    slots = refs[0]
    head_parts = refs[1:9]
    tail_parts = refs[9:13]
    tokens_pair, cos_pair, sin_pair = refs[13:15], refs[15:17], refs[17:19]
    (place_q_ref, place_k_ref, gains_ref, bias_q_ref, bias_kv_ref, grad_ref) = refs[19:25]
    block_out_ref, parts_out = refs[25], refs[26:36]
    (dkv_send, dkv_keep, dq_wq_ref, d_mid_ref, w_kv) = refs[36:41]
    (raw_head, raw_tail, w_q, w_out, w_gate, w_up, w_down, normed_all, hidden_all, keys, values, queries, probs, attended, act_all, block_acc, d_hidden, d_attended, dkv_all, d_query, send_all, keep_all, vector_ref, sems) = refs[41:]

    copies = []
    for k, part in enumerate(head_parts):
        copies.append(pltpu.make_async_copy(part, raw_head.at[pl.ds(4 * k, 4)], sems.at[k]))
    for k, part in enumerate(tail_parts):
        copies.append(pltpu.make_async_copy(part, raw_tail.at[pl.ds(8 * k, 8)], sems.at[8 + k]))
    for copy in copies:
        copy.start()
    for copy in copies:
        copy.wait()

    core = slots[MY_CORE]

    def at_slot(pair, slot):
        return pair[slot % 2].at[slot // 2]

    def head_tile(block):
        return raw_head.at[slots[AT_HEAD + block]]

    def tail_tile(block):
        return raw_tail.at[slots[AT_TAIL + block]]

    for ref in (w_q, w_out, w_gate, w_up, w_kv):
        ref[576:640, :] = jnp.zeros((64, ref.shape[1]), BF16)
    for k in range(3):
        place_rows(w_q, head_tile(k), tail_tile(k), 192 * k)
        place_rows(w_out, head_tile(5 + k), tail_tile(5 + k), 192 * k)
    for k in range(8):
        place_rows(w_down, head_tile(24 + k), tail_tile(24 + k), 192 * k)
    w_kv[0:576, 0:128] = head_tile(3)[...]
    w_kv[0:576, 128:256] = head_tile(4)[...]
    rest_key = tail_tile(3)[...].astype(F32)
    rest_value = tail_tile(4)[...].astype(F32)
    low = lower_lanes(rest_key.shape)
    w_kv[0:288, 256:384] = jnp.where(low, rest_key, half_turn(rest_value)).astype(BF16)
    w_kv[288:576, 256:384] = jnp.where(low, half_turn(rest_key), rest_value).astype(BF16)
    for ref, base in ((w_gate, 8), (w_up, 16)):
        for k in range(4):
            for i in range(6):
                if i < 4:
                    even = head_tile(base + 2 * k)[144 * i : 144 * i + 144, :].astype(F32)
                    odd = head_tile(base + 2 * k + 1)[144 * i : 144 * i + 144, :].astype(F32)
                else:
                    even = tail_tile(base + 2 * k)[144 * (i - 4) : 144 * (i - 4) + 144, :].astype(F32)
                    odd = tail_tile(base + 2 * k + 1)[144 * (i - 4) : 144 * (i - 4) + 144, :].astype(F32)
                ref[144 * k : 144 * k + 144, 256 * i : 256 * i + 128] = jnp.concatenate(
                    [even[0:72], odd[0:72]], axis=0
                ).astype(BF16)
                ref[144 * k : 144 * k + 144, 256 * i + 128 : 256 * i + 256] = jnp.concatenate(
                    [even[72:144], odd[72:144]], axis=0
                ).astype(BF16)

    gain_one = gains_ref[0:1, :]
    gain_two = gains_ref[1:2, :]
    low_rows = lower_lanes((ROWS, LANES))

    @pl.loop(0, 2)
    def _(mb):
        lane = lax.broadcasted_iota(jnp.int32, (ROWS, WIDE), 1)
        for slot in range(4):
            rows = pl.ds(pl.multiple_of(mb * 512 + slot * ROWS, ROWS), ROWS)
            x = jnp.where(lane < MODEL_WIDTH, at_slot(tokens_pair, slot)[mb].astype(F32), 0.0)
            normed, _ = normed_rows(x)
            normed_all[rows, :] = normed
            hidden_all[rows, :] = (normed * gain_one).astype(BF16)
        rows = pl.ds(pl.multiple_of(mb * 512, 512), 512)
        pair = product(hidden_all[rows, :], w_kv[...]) + bias_kv_ref[...]
        cosines = jnp.concatenate([at_slot(cos_pair, slot)[mb] for slot in range(4)], axis=0)
        sines = jnp.concatenate([at_slot(sin_pair, slot)[mb] for slot in range(4)], axis=0)
        key_a = rope(pair[:, 0:128], cosines, sines)
        key_b = rope(pair[:, 256:384], cosines, sines)
        value_a, value_b = pair[:, 128:256], pair[:, 256:384]
        low_keys = lower_lanes((512, LANES))
        turned = half_turn(key_a)
        keys[rows, 0:128] = jnp.where(low_keys, key_a, turned).astype(BF16)
        keys[rows, 128:256] = jnp.where(low_keys, turned, key_a).astype(BF16)
        keys[rows, 256:384] = jnp.where(low_keys, key_b, half_turn(key_b)).astype(BF16)
        turned = half_turn(value_a)
        values[rows, 0:128] = jnp.where(low_keys, value_a, turned).astype(BF16)
        values[rows, 128:256] = jnp.where(low_keys, turned, value_a).astype(BF16)
        values[rows, 256:384] = jnp.where(low_keys, half_turn(value_b), value_b).astype(BF16)

    def heads_of(ref, rows, group):
        stacked = []
        for k in range(3):
            number = 3 * group + k
            tile = ref[rows, LANES * (number // 2) : LANES * (number // 2) + LANES]
            keep = low_rows if number % 2 == 0 else jnp.logical_not(low_rows)
            stacked.append(jnp.where(keep, tile.astype(F32), 0.0).astype(BF16))
        return jnp.concatenate(stacked, axis=0)

    def tiles_of_heads(parts):
        found = [jnp.where(low_rows, parts[2 * k], parts[2 * k + 1]) for k in range(4)]
        return found + [jnp.where(low_rows, parts[8], 0.0)]

    @pl.loop(0, 2)
    def _(mb):
        rows = pl.ds(pl.multiple_of(mb * ROWS, ROWS), ROWS)
        key_rows = pl.ds(pl.multiple_of(mb * 512, 512), 512)
        cosines, sines = cos_pair[0][0, mb], sin_pair[0][0, mb]
        made = product(hidden_all[pl.ds(pl.multiple_of(mb * 512, 512), ROWS), :], w_q[...]) + bias_q_ref[...]
        for k in range(5):
            queries[rows, LANES * k : LANES * k + LANES] = rope(
                made[:, LANES * k : LANES * k + LANES], cosines, sines
            ).astype(BF16)
        allowed = place_q_ref[mb] >= place_k_ref[mb]
        allowed = jnp.concatenate([allowed.astype(F32)] * 3, axis=0) > 0.5
        parts = []
        for group in range(KEY_VALUE_HEADS):
            lanes = slice(LANES * group, LANES * group + LANES)
            scores = times_transposed(heads_of(queries, rows, group), keys[key_rows, lanes])
            scores = jnp.where(allowed, scores * HEAD_SIZE ** (-0.5), MASKED)
            top = jnp.max(scores, axis=-1, keepdims=True)
            powers = jnp.exp(scores - top)
            found = powers * (1.0 / jnp.sum(powers, axis=-1, keepdims=True))
            probs[mb, group] = found
            out = product(found.astype(BF16), values[key_rows, lanes])
            parts += [out[ROWS * k : ROWS * k + ROWS] for k in range(3)]
        for k, tile in enumerate(tiles_of_heads(parts)):
            attended[rows, LANES * k : LANES * k + LANES] = tile.astype(BF16)

    lane = lax.broadcasted_iota(jnp.int32, (2 * ROWS, WIDE), 1)
    x_own = tokens_pair[0][0].astype(F32).reshape(2 * ROWS, WIDE)
    x_own = jnp.where(lane < MODEL_WIDTH, x_own, 0.0)
    resid_mid = x_own + product(attended[...], w_out[...])
    normed_two, scale_two = normed_rows(resid_mid)
    hidden_two = (normed_two * gain_two).astype(BF16)
    hidden_turned = hidden_two.T
    grad_low = grad_ref[...]
    block_acc[...] = resid_mid
    d_hidden[...] = jnp.zeros_like(d_hidden)

    def store_pair(at, even, odd, table, first):
        rows = pl.ds(pl.multiple_of(slots[table + at] + first, 16), even.shape[0])
        send_all[rows, :] = jnp.where(core == 0, odd, even).astype(BF16)
        keep_all[rows, :] = jnp.where(core == 0, even, odd).astype(BF16)

    def feed_forward(chunk, first, table):
        cols = pl.ds(pl.multiple_of(chunk * 512, 512), 512)
        gate = product(hidden_two, w_gate[:, cols])
        up = product(hidden_two, w_up[:, cols])
        sigma = 1.0 / (1.0 + jnp.exp(-gate))
        act = (gate * sigma * up).astype(BF16)
        act_all[:, cols] = act
        down = w_down[cols, :]
        d_act = times_transposed(grad_low, down)
        block_acc[...] += product(act, down)
        d_up = (d_act * gate * sigma).astype(BF16)
        d_gate = (d_act * up * sigma * (1.0 + gate * (1.0 - sigma))).astype(BF16)
        d_hidden[...] += times_transposed(d_gate, w_gate[:, cols]) + times_transposed(d_up, w_up[:, cols])
        for base, cotangent in ((4, d_gate), (8, d_up)):
            made = product(hidden_turned, cotangent)
            for k in range(4):
                part = made[144 * k : 144 * k + 144, :]
                even = jnp.concatenate([part[0:72, LANES * j : LANES * j + LANES] for j in range(4)], axis=0)
                odd = jnp.concatenate([part[72:144, LANES * j : LANES * j + LANES] for j in range(4)], axis=0)
                store_pair(base + k, even, odd, table, (chunk - first) * 288)

    @pl.loop(0, 2)
    def _(chunk):
        feed_forward(chunk, 0, TO_HEAD)

    feed_forward(2, 2, TO_TAIL)

    def store_rows(at, even, odd):
        even_head, even_tail = even
        odd_head, odd_tail = odd
        store_pair(at, even_head, odd_head, TO_HEAD, 0)
        store_pair(at, even_tail, odd_tail, TO_TAIL, 0)

    @pl.loop(0, 4)
    def _(k):
        made = rows_product(act_all[:, pl.ds(pl.multiple_of(k * 384, 128), 384)], grad_low)
        store_rows(12 + k, tiles_of_rows(made[0:192]), tiles_of_rows(made[192:384]))

    for mb in range(2):
        block_out_ref[mb] = block_acc[ROWS * mb : ROWS * mb + ROWS, :].T[0:MODEL_WIDTH].astype(BF16)

    d_two = d_hidden[...]
    vector_ref[...] = jnp.zeros_like(vector_ref)
    vector_ref[1:2, :] = jnp.sum(d_two * normed_two, axis=0, keepdims=True)
    d_norm = d_two * gain_two
    d_mid = grad_low.astype(F32) + scale_two * (d_norm - normed_two * row_mean(d_norm * normed_two))
    d_mid_ref[...] = d_mid
    d_branch = d_mid.astype(BF16)
    d_attended[...] = times_transposed(d_branch, w_out[...]).astype(BF16)
    grad_out = rows_product(attended[...], d_branch)

    @pl.loop(0, 2)
    def _(mb):
        rows = pl.ds(pl.multiple_of(mb * ROWS, ROWS), ROWS)
        key_rows = pl.ds(pl.multiple_of(mb * 512, 512), 512)
        parts = []
        d_keys = []
        d_values = []
        for group in range(KEY_VALUE_HEADS):
            lanes = slice(LANES * group, LANES * group + LANES)
            query_rows = heads_of(queries, rows, group)
            cotangent = heads_of(d_attended, rows, group)
            found = probs[mb, group]
            d_probs = times_transposed(cotangent, values[key_rows, lanes])
            delta = jnp.sum(found * d_probs, axis=-1, keepdims=True)
            d_scores = (found * (d_probs - delta)).astype(BF16)
            out = product(d_scores, keys[key_rows, lanes]) * HEAD_SIZE ** (-0.5)
            parts += [out[ROWS * k : ROWS * k + ROWS] for k in range(3)]
            d_key = rows_product(d_scores, query_rows) * HEAD_SIZE ** (-0.5)
            d_value = rows_product(found.astype(BF16), cotangent)
            d_keys.append(d_key + half_turn(d_key))
            d_values.append(d_value + half_turn(d_value))
        cosines, sines = cos_pair[0][0, mb], sin_pair[0][0, mb]
        for k, tile in enumerate(tiles_of_heads(parts)):
            d_query[rows, LANES * k : LANES * k + LANES] = rope_back(tile, cosines, sines).astype(BF16)
        low_keys = lower_lanes((512, LANES))
        cosines = jnp.concatenate([at_slot(cos_pair, slot)[mb] for slot in range(4)], axis=0)
        sines = jnp.concatenate([at_slot(sin_pair, slot)[mb] for slot in range(4)], axis=0)
        key_a = rope_back(jnp.where(low_keys, d_keys[0], d_keys[1]), cosines, sines)
        key_b = rope_back(d_keys[2], cosines, sines)
        dkv_all[key_rows, 0:128] = key_a.astype(BF16)
        dkv_all[key_rows, 128:256] = jnp.where(low_keys, d_values[0], d_values[1]).astype(BF16)
        dkv_all[key_rows, 256:384] = jnp.where(low_keys, key_b, d_values[2]).astype(BF16)
        for slot in range(4):
            target = dkv_send if slot % 2 else dkv_keep
            target[slot // 2, mb] = dkv_all[pl.ds(pl.multiple_of(mb * 512 + slot * ROWS, ROWS), ROWS), :]

    dkv = dkv_all[...]
    d_q = d_query[...]
    dq_wq = times_transposed(d_q, w_q[...])
    dq_wq_ref[...] = dq_wq
    vector_ref[2:3, :] = jnp.sum(d_q.astype(F32), axis=0, keepdims=True)
    vector_ref[3:4, 0:384] = jnp.sum(dkv.astype(F32), axis=0, keepdims=True)
    gain_sum = jnp.zeros((1, WIDE), F32)
    for mb in range(2):
        gain_sum += jnp.sum(dq_wq[ROWS * mb : ROWS * mb + ROWS] * normed_all[512 * mb : 512 * mb + ROWS, :], axis=0, keepdims=True)
    for k in range(4):
        part = slice(256 * k, 256 * k + 256)
        gain_sum += jnp.sum(times_transposed(dkv_all[part, :], w_kv[...]) * normed_all[part, :], axis=0, keepdims=True)
    vector_ref[0:1, :] = gain_sum

    hidden_own = jnp.concatenate([hidden_all[0:ROWS, :], hidden_all[512 : 512 + ROWS, :]], axis=0)
    grad_q = rows_product(hidden_own, d_q)
    grad_kv = rows_product(hidden_all[...], dkv)
    rest = grad_kv[0:576, 256:384]
    low = lower_lanes((288, LANES))
    key_tiles = (grad_kv[0:576, 0:128], jnp.where(low, rest[0:288], half_turn(rest[288:576])))
    value_tiles = (grad_kv[0:576, 128:256], jnp.where(low, half_turn(rest[0:288]), rest[288:576]))
    query_tiles = [tiles_of_rows(grad_q[192 * k : 192 * k + 192]) for k in range(3)]
    out_tiles = [tiles_of_rows(grad_out[192 * k : 192 * k + 192]) for k in range(3)]
    store_rows(0, query_tiles[0], query_tiles[1])
    store_rows(1, query_tiles[2], key_tiles)
    store_rows(2, value_tiles, out_tiles[0])
    store_rows(3, out_tiles[1], out_tiles[2])
    vector = jnp.concatenate(
        [vector_ref[:, LANES * k : LANES * k + LANES] for k in range(5)] + [jnp.zeros((8, LANES), F32)], axis=0
    )
    high = vector.astype(BF16)
    rest = (vector - high.astype(F32)).astype(BF16)
    at = FIRST_AT + PART
    for ref in (send_all, keep_all):
        ref[at : at + VECTOR_ROWS, :] = high
        ref[at + VECTOR_ROWS : at + 2 * VECTOR_ROWS, :] = rest
    copies = [
        pltpu.make_async_copy(ref.at[pl.ds(first, count)], out, sems.at[k])
        for k, (ref, out, (first, count)) in enumerate(
            zip([send_all] * 4 + [keep_all] * 6, parts_out, SEND_PARTS + KEEP_PARTS)
        )
    ]
    for copy in copies:
        copy.start()
    for copy in copies:
        copy.wait()


def run_layer(slots, heads, tails, *others):
    shape = jax.ShapeDtypeStruct
    vmem = pl.BlockSpec(memory_space=pltpu.VMEM)
    anywhere = pl.BlockSpec(memory_space=pl.ANY)
    scratch = [
        ((BLOCKS, HEAD_ROWS, LANES), BF16),
        ((BLOCKS, TAIL_ROWS, LANES), BF16),
        ((WIDE, WIDE), BF16),
        ((WIDE, WIDE), BF16),
        ((WIDE, FF), BF16),
        ((WIDE, FF), BF16),
        ((FF, WIDE), BF16),
        ((1024, WIDE), F32),
        ((1024, WIDE), BF16),
        ((1024, 384), BF16),
        ((1024, 384), BF16),
        ((256, WIDE), BF16),
        ((2, 3, 384, 512), F32),
        ((256, WIDE), BF16),
        ((256, FF), BF16),
        ((256, WIDE), F32),
        ((256, WIDE), F32),
        ((256, WIDE), BF16),
        ((1024, 384), BF16),
        ((256, WIDE), BF16),
        ((ALL_ROWS, LANES), BF16),
        ((ALL_ROWS, LANES), BF16),
        ((8, WIDE), F32),
    ]
    return pl.pallas_call(
        layer_kernel,
        out_shape=(
            shape((2, MODEL_WIDTH, ROWS), BF16),
            *[shape((count, LANES), BF16) for _, count in SEND_PARTS + KEEP_PARTS],
            shape((2, 2, ROWS, 384), BF16),
            shape((2, 2, ROWS, 384), BF16),
            shape((256, WIDE), F32),
            shape((256, WIDE), F32),
            shape((WIDE, 384), BF16),
        ),
        in_specs=[pl.BlockSpec(memory_space=pltpu.SMEM)] + [anywhere] * 12 + [vmem] * 12,
        out_specs=(vmem,) + (anywhere,) * 10 + (vmem,) * 5,
        scratch_shapes=[pltpu.VMEM(dims, kind) for dims, kind in scratch]
        + [pltpu.SemaphoreType.DMA((12,))],
        compiler_params=pltpu.CompilerParams(vmem_limit_bytes=50 * 1024 * 1024),
        name="layer",
    )(slots, *heads, *tails, *others)


def input_kernel(tokens_ref, gains_ref, w_kv_ref, dq_wq_ref, d_mid_ref, own_ref, other_ref, out_ref):
    lane = lax.broadcasted_iota(jnp.int32, (2 * ROWS, WIDE), 1)
    x = jnp.where(lane < MODEL_WIDTH, tokens_ref[0].astype(F32).reshape(2 * ROWS, WIDE), 0.0)
    normed, scale = normed_rows(x)
    total = summed(own_ref[...], other_ref[...])
    total = total.reshape(2 * ROWS, 384).astype(BF16)
    d_norm = (dq_wq_ref[...] + times_transposed(total, w_kv_ref[...])) * gains_ref[0:1, :]
    d_input = d_mid_ref[...] + scale * (d_norm - normed * row_mean(d_norm * normed))
    for mb in range(2):
        out_ref[mb] = d_input[ROWS * mb : ROWS * mb + ROWS].T[0:MODEL_WIDTH].astype(BF16)


def run_input(tokens, gains, w_kv, dq_wq, d_mid, parts):
    return pl.pallas_call(
        input_kernel,
        out_shape=jax.ShapeDtypeStruct((2, MODEL_WIDTH, ROWS), BF16),
        in_specs=[pl.BlockSpec(memory_space=pltpu.VMEM)] * 7,
        out_specs=pl.BlockSpec(memory_space=pltpu.VMEM),
        cost_estimate=pl.CostEstimate(flops=3_500_000_000, bytes_accessed=6_000_000, transcendentals=0),
        name="input_grad",
    )(tokens, gains, w_kv, dq_wq, d_mid, *parts)


def adamw(param, grad, mom_one, mom_two, rate, decay):
    new_one = BETA_ONE * mom_one + (1.0 - BETA_ONE) * grad
    new_two = BETA_TWO * mom_two + (1.0 - BETA_TWO) * grad * grad
    fixed_one = new_one / (1.0 - BETA_ONE**STEP)
    fixed_two = new_two / (1.0 - BETA_TWO**STEP)
    new_param = param - rate * (fixed_one / (jnp.sqrt(fixed_two) + EPS_ADAM) + decay * param)
    return (new_param, new_one, new_two)


def inner_groups():
    inner = inner_count()
    data_inner = inner // lax.axis_size("ctx")
    data_count = lax.axis_size("dp")
    return [list(range(k, k + data_inner)) for k in range(0, data_count, data_inner)]


def whole_block(flat):
    if inner_count() == 1:
        return flat
    flat = lax.all_gather(flat, "ctx", axis=0, tiled=True)
    return lax.all_gather(flat, "dp", axis=0, tiled=True, axis_index_groups=inner_groups())


def own_slice(block):
    if inner_count() == 1:
        return block
    block = lax.psum_scatter(
        block, "dp", scatter_dimension=0, tiled=True, axis_index_groups=inner_groups()
    )
    return lax.psum_scatter(block, "ctx", scatter_dimension=0, tiled=True)


def bias_tiles(bias_key, bias_value):
    return jnp.concatenate([bias_key[:128], bias_value[:128], bias_key[128:], bias_value[128:]])


def local(tokens_in, places, out_grad, weights, first_moment, second_moment, vectors, vector_first, vector_second):
    kind = kind_of(device_number() // inner_count()).astype(jnp.int32).reshape(1)
    block = whole_block(weights).reshape(BLOCK_ROWS, LANES)
    head, tail = to_tiles(kind, block)

    head, tail, tokens_in, places = together(head, tail, tokens_in, places)
    own_tokens = tokens_in.reshape(2, ROWS, MODEL_WIDTH)
    own_places = places.reshape(2, ROWS)
    marks = jnp.stack([own_places // 16, own_places % 16], axis=-1).astype(BF16)
    packed = jnp.concatenate(
        [own_tokens, marks, jnp.zeros((2, ROWS, WIDE - MODEL_WIDTH - 2), BF16)], axis=-1
    )
    padding = ((0, 0), (0, WIDE - MODEL_WIDTH))
    gains = jnp.pad(vectors[: 2 * MODEL_WIDTH].reshape(2, MODEL_WIDTH), padding)
    bias_q = jnp.pad(vectors[2 * MODEL_WIDTH : 3 * MODEL_WIDTH].reshape(1, MODEL_WIDTH), padding)
    bias_kv = bias_tiles(vectors[1728:1920], vectors[1920:2112]).reshape(1, 384)
    grad = jnp.pad(out_grad.reshape(2 * ROWS, MODEL_WIDTH), padding)
    others = (slot_table(), gains, bias_q, bias_kv, grad)
    heads, tails, (near, far), (cosines, sines), others = gather_all(head, tail, packed, others)
    slots, gains, bias_q, bias_kv, grad = others
    cosines_far, sines_far = place_tables(far)
    place_all = jnp.stack([places_of(near), places_of(far)], axis=1)
    place_q = place_all[0, 0][..., None]
    place_k = jnp.transpose(place_all.reshape(4, 2, ROWS), (1, 0, 2)).reshape(2, 1, 4 * ROWS)

    block_out, *found = run_layer(
        slots, heads, tails, near, far, cosines, cosines_far, sines, sines_far, place_q, place_k, gains, bias_q, bias_kv, grad
    )
    sends, keeps = found[:4], found[4:10]
    dkv_send, dkv_keep, dq_wq, d_mid, w_kv = found[10:]
    make_input = lambda parts: run_input(near, gains, w_kv, dq_wq, d_mid, parts)
    parts, vector, input_grad = scatter_blocks(sends, keeps, dkv_send, dkv_keep, make_input)
    state = (weights, first_moment, second_moment)
    if inner_count() == 1:
        updated = finish(kind, parts, [array.reshape(BLOCK_ROWS, LANES) for array in state])
        new_weights, new_first, new_second = [array.reshape(-1) for array in updated]
    else:
        vector = lax.psum(vector, "ctx")
        vector = lax.psum(vector, "dp", axis_index_groups=inner_groups())
        (block_grad,) = finish(kind, parts, [])
        grad_own = own_slice(block_grad.reshape(-1))
        new_weights, new_first, new_second = adamw(
            weights, grad_own, first_moment, second_moment, RATE_MATRIX, DECAY
        )
    vector = jnp.transpose(vector.reshape(6, 8, LANES), (1, 0, 2)).reshape(8, 6 * LANES)
    pair = vector[3]
    vector_grad = jnp.concatenate(
        [
            vector[0, :MODEL_WIDTH],
            vector[1, :MODEL_WIDTH],
            vector[2, :MODEL_WIDTH],
            pair[0:128],
            pair[256:320],
            pair[128:256],
            pair[320:384],
        ]
    )
    new_vectors, new_vector_first, new_vector_second = adamw(
        vectors, vector_grad, vector_first, vector_second, RATE_VECTOR, 0.0
    )
    shape = tokens_in.shape
    return (
        jnp.transpose(block_out, (0, 2, 1)).reshape(shape),
        jnp.transpose(input_grad, (0, 2, 1)).reshape(shape),
        new_weights,
        new_first,
        new_second,
        new_vectors,
        new_vector_first,
        new_vector_second,
    )


def solution(mesh):
    in_specs = (
        P(None, "dp", "ctx", None),
        P(None, "dp", "ctx"),
        P(None, "dp", "ctx", None),
        P(("dp", "ctx")),
        P(("dp", "ctx")),
        P(("dp", "ctx")),
        P(),
        P(),
        P(),
    )
    out_specs = (
        P(None, "dp", "ctx", None),
        P(None, "dp", "ctx", None),
        P(("dp", "ctx")),
        P(("dp", "ctx")),
        P(("dp", "ctx")),
        P(),
        P(),
        P(),
    )
    return jax.shard_map(local, mesh=mesh, in_specs=in_specs, out_specs=out_specs, check_vma=False)
```

```python
import jax
import jax.numpy as jnp
from jax import lax
from jax.experimental import pallas as pl
from jax.experimental.pallas import tpu as pltpu
from jax.sharding import PartitionSpec as P

MODEL_WIDTH = 576
QUERY_HEADS = 9
KEY_VALUE_HEADS = 3
HEAD_SIZE = 64
FF = 1536
STEP = 10

EPS_NORM = 1e-05
THETA = 100000.0
BETA_ONE = 0.9
BETA_TWO = 0.95
EPS_ADAM = 1e-08
RATE_MATRIX = 0.06
RATE_VECTOR = 0.3
DECAY = 0.1
MASKED = -1e30

LANES = 128
WIDE = 640
BLOCKS = 32
BLOCK_ROWS = 864
HEAD_ROWS = 576
TAIL_ROWS = BLOCK_ROWS - HEAD_ROWS
VECTOR_ROWS = 24
PART = 4 * HEAD_ROWS
FIRST_AT = 4 * PART
TAIL_AT = FIRST_AT + PART + 2 * VECTOR_ROWS
ALL_ROWS = TAIL_AT + PART
SEND_PARTS = [(FIRST_AT, PART + 2 * VECTOR_ROWS), (TAIL_AT, PART), (0, 3 * PART), (3 * PART, PART)]
KEEP_PARTS = SEND_PARTS[:2] + [(PART * k, PART) for k in range(4)]
SIZES = {"z": 4, "y": 2, "x": 2, "c": 2}
ROWS = 128
F32 = jnp.float32
BF16 = jnp.bfloat16


def coordinates(number):
    found = {}
    for name in ("c", "x", "y", "z"):
        found[name] = number % SIZES[name]
        number = number // SIZES[name]
    return found


def number_of(found):
    number = 0
    for name in ("z", "y", "x", "c"):
        number = number * SIZES[name] + found[name]
    return number


def device_number():
    return lax.axis_index("dp") * lax.axis_size("ctx") + lax.axis_index("ctx")


def inner_count():
    return lax.axis_size("dp") * lax.axis_size("ctx") // BLOCKS


def moved(buffer, name, shift):
    inner = inner_count()
    pairs = []
    for number in range(BLOCKS):
        found = coordinates(number)
        found[name] = (found[name] + shift) % SIZES[name]
        target = number_of(found)
        pairs += [(number * inner + k, target * inner + k) for k in range(inner)]
    return lax.ppermute(buffer, ("dp", "ctx"), pairs)


def across(buffer, distance):
    count = lax.axis_size("ctx")
    return lax.ppermute(buffer, "ctx", [(i, i ^ distance) for i in range(count)])


def together(*arrays):
    return lax.optimization_barrier(arrays)


def gather_all(head, tail, packed, others):
    hz = [moved(head, "z", s) for s in (1, 2, 3)]
    tx = moved(tail, "x", 1)
    two = across(packed, 2)
    head, tail, tx, two, *hz = together(head, tail, tx, two, *hz)
    own = jnp.stack([head] + hz)
    pair = jnp.stack([tail, tx])
    ay = moved(own, "y", 1)
    ax = moved(own, "x", 1)
    tz = [moved(pair, "z", s) for s in (1, 2, 3)]
    near = jnp.stack([packed, two])
    tables = place_tables(near)
    own, pair, ay, ax, near, tables, others, *tz = together(own, pair, ay, ax, near, tables, others, *tz)
    eight = jnp.concatenate([pair] + tz)
    far = across(near, 1)
    axy = moved(ay, "x", 1)
    ty = moved(eight, "y", 1)
    ac = moved(own, "c", 1)
    acy = moved(ay, "c", 1)
    acx = moved(ax, "c", 1)
    tc = moved(eight, "c", 1)
    axy, ty, ac, acy, acx, tc, far = together(axy, ty, ac, acy, acx, tc, far)
    acxy = moved(axy, "c", 1)
    tcy = moved(ty, "c", 1)
    heads = [own, ay, ax, axy, ac, acy, acx, acxy]
    return heads, [eight, ty, tc, tcy], (near, far), tables, others


def places_of(tokens):
    found = tokens[..., MODEL_WIDTH : MODEL_WIDTH + 2].astype(F32)
    return found[..., 0] * 16.0 + found[..., 1]


def place_tables(tokens):
    half_dim = HEAD_SIZE // 2
    frequency = THETA ** (-2.0 * jnp.arange(half_dim, dtype=F32) / HEAD_SIZE)
    angles = places_of(tokens)[..., None] * jnp.tile(frequency, 4)
    sign = jnp.where(jnp.arange(LANES) % HEAD_SIZE < half_dim, -1.0, 1.0).astype(F32)
    return jnp.cos(angles), jnp.sin(angles) * sign


def fold(order, relative):
    slot = 0
    for name in order:
        slot = slot * SIZES[name] + relative[name]
    return slot


def head_row(slot, z, _):
    return slot * PART + jnp.where(slot < 3, 0, FIRST_AT - 3 * PART) + z * HEAD_ROWS


def tail_row(slot, z, inside):
    return jnp.where(slot < 1, 3 * PART, TAIL_AT) + (2 * z + inside) * TAIL_ROWS


def slot_table():
    mine = coordinates(device_number() // inner_count())
    entries = []
    for order in (("c", "x", "y", "z"), ("c", "y", "z", "x")):
        for number in range(BLOCKS):
            found = coordinates(number)
            entries.append(fold(order, {n: (mine[n] - found[n]) % SIZES[n] for n in SIZES}))
    for order, start in ((("x", "y"), head_row), (("y",), tail_row)):
        for number in range(0, BLOCKS, 2):
            found = coordinates(number)
            slot = fold(order, {n: (found[n] - mine[n]) % SIZES[n] for n in SIZES})
            inside = (found["x"] - mine["x"]) % SIZES["x"]
            entries.append(start(slot, found["z"], inside))
    entries.append(mine["c"])
    entries.append(mine["z"])
    return jnp.stack([jnp.asarray(entry, jnp.int32) for entry in entries])


AT_HEAD, AT_TAIL, TO_HEAD, TO_TAIL = 0, BLOCKS, 2 * BLOCKS, 2 * BLOCKS + 16
MY_CORE, MY_Z = 2 * BLOCKS + 32, 2 * BLOCKS + 33


def summed(*parts):
    total = parts[0].astype(F32)
    for part in parts[1:]:
        total = total + part.astype(F32)
    return total


def summed_vector(mine, other):
    total = summed(mine[:VECTOR_ROWS], other[:VECTOR_ROWS]) + summed(mine[VECTOR_ROWS:], other[VECTOR_ROWS:])
    high = lax.reduce_precision(total, 8, 7)
    return jnp.concatenate([high.astype(BF16), (total - high).astype(BF16)])


def scatter_blocks(sends, keeps, dkv_send, dkv_keep):
    keep_head, keep_tail, keep_low, keep_mid, keep_far, keep_rest = keeps
    got_head, got_tail = moved(sends[0], "c", 1), moved(sends[1], "c", 1)
    got_head, got_tail, rest_head, rest_tail, dkv_send = together(got_head, got_tail, *sends[2:], dkv_send)
    got_rest_head, got_rest_tail = moved(rest_head, "c", 1), moved(rest_tail, "c", 1)
    got_dkv = across(dkv_send, 1)
    vector = summed_vector(keep_head[PART:], got_head[PART:])
    hx = jnp.concatenate([summed(keep_head[:PART], got_head[:PART]).astype(BF16), vector])
    ty = summed(keep_tail, got_tail).astype(BF16)
    got_hx = moved(hx, "x", 1)
    got_ty = moved(ty, "y", 1)
    low, mid, far = [
        summed(keep, got_rest_head[PART * k : PART * k + PART]).astype(BF16)
        for k, keep in enumerate((keep_low, keep_mid, keep_far))
    ]
    tail = summed(keep_rest, got_rest_tail).astype(BF16)
    dkv = summed(dkv_keep, got_dkv).astype(BF16)
    got_hx, got_ty, low, mid, far, tail, dkv, vector = together(got_hx, got_ty, low, mid, far, tail, dkv, vector)
    place = coordinates(device_number() // inner_count())["z"]

    def part_for(array, shift):
        return lax.dynamic_slice_in_dim(array, HEAD_ROWS * ((place + shift) % SIZES["z"]), HEAD_ROWS, 0)

    vector = summed_vector(vector, got_hx[PART:])
    hy = jnp.concatenate([summed(mid, got_hx[:PART]).astype(BF16), vector])
    tz = [summed(part_for(tail, s), part_for(got_ty, s)).astype(BF16) for s in range(4)]
    got_hy = moved(hy, "y", 1)
    got_far = moved(far, "x", 1)
    got_tz = [moved(tz[s], "z", s) for s in (1, 2, 3)]
    got_hy, got_far, low, own_tail, vector, dkv, *got_tz = together(got_hy, got_far, low, tz[0], vector, dkv, *got_tz)
    vector = summed_vector(vector, got_hy[PART:])
    head = [summed(part_for(low, s), part_for(got_far, s), part_for(got_hy, s)) for s in range(4)]
    got_hz = [moved(jnp.concatenate([head[s].astype(BF16), vector]), "z", s) for s in (1, 2, 3)]
    tx = summed(own_tail[TAIL_ROWS:], *[part[TAIL_ROWS:] for part in got_tz]).astype(BF16)
    own_tail = summed(own_tail[:TAIL_ROWS], *[part[:TAIL_ROWS] for part in got_tz])
    got_tx = moved(tx, "x", 1)
    got_dkv = across(dkv[1], 2)
    return (head[0], *got_hz, own_tail, got_tx, vector), (dkv[0], got_dkv)


def lower_lanes(shape):
    return lax.broadcasted_iota(jnp.int32, shape, 1) < HEAD_SIZE


def half_turn(value):
    return pltpu.roll(value, HEAD_SIZE, 1)


def side_by_side(left, right):
    return jnp.where(lower_lanes(left.shape), left, half_turn(right))


def kind_of(block):
    return jnp.where(block >= 24, 1, jnp.where(block >= 8, 0, jnp.where((block == 3) | (block == 4), 2, 1)))


def tile_kernel(kind_ref, flat_ref, head_ref, tail_ref, tiles, narrow):
    kind = kind_ref[0]

    @pl.when(kind == 0)
    def _():
        for j in range(12):
            tiles[72 * j : 72 * j + 72, :] = flat_ref[pl.ds(j, 72, stride=12), :]

    @pl.when(kind == 1)
    def _():
        lines = [flat_ref[pl.ds(t, 96, stride=9), :] for t in range(9)]
        turned = [half_turn(line) for line in lines[4:]]
        low = lower_lanes((96, LANES))
        for j in range(4):
            tiles[pl.ds(192 * j, 96, stride=2), :] = lines[j]
            tiles[pl.ds(192 * j + 1, 96, stride=2), :] = jnp.where(low, turned[j], turned[j + 1])
        narrow[pl.ds(0, 96, stride=2), :] = lines[4]
        narrow[pl.ds(1, 96, stride=2), :] = turned[4]
        tiles[768:864, :] = side_by_side(narrow[0:96, :], narrow[96:192, :])

    @pl.when(kind == 2)
    def _():
        lines = [flat_ref[pl.ds(t, 288, stride=3), :] for t in range(3)]
        first, second = half_turn(lines[1]), half_turn(lines[2])
        tiles[pl.ds(0, 288, stride=2), :] = lines[0]
        tiles[pl.ds(1, 288, stride=2), :] = jnp.where(lower_lanes((288, LANES)), first, second)
        narrow[pl.ds(0, 288, stride=2), :] = lines[1]
        narrow[pl.ds(1, 288, stride=2), :] = second
        tiles[576:864, :] = side_by_side(narrow[0:288, :], narrow[288:576, :])

    head_ref[...] = tiles[0:HEAD_ROWS, :].astype(BF16)
    tail_ref[...] = tiles[HEAD_ROWS:BLOCK_ROWS, :].astype(BF16)


def to_tiles(kind, flat):
    return pl.pallas_call(
        tile_kernel,
        out_shape=(
            jax.ShapeDtypeStruct((HEAD_ROWS, LANES), BF16),
            jax.ShapeDtypeStruct((TAIL_ROWS, LANES), BF16),
        ),
        in_specs=[
            pl.BlockSpec(memory_space=pltpu.SMEM),
            pl.BlockSpec(memory_space=pltpu.VMEM),
        ],
        out_specs=(pl.BlockSpec(memory_space=pltpu.VMEM),) * 2,
        scratch_shapes=[
            pltpu.VMEM((BLOCK_ROWS, LANES), F32),
            pltpu.VMEM((HEAD_ROWS, LANES), F32),
        ],
        name="to_tiles",
    )(kind, flat)


def finish_kernel(table_ref, head_ref, one_ref, two_ref, three_ref, tail_ref, other_ref, mine_ref, *refs):
    kind, place = table_ref[0], table_ref[1]
    tiles, narrow, flat_ref, vector_parts = refs[-4:]
    tokens_ref, gains_ref, w_kv_ref, dq_wq_ref, d_mid_ref, own_dkv, other_dkv = refs[:7]
    states = refs[7:-4]
    tiles[0:HEAD_ROWS, :] = (head_ref[...] + one_ref[0:HEAD_ROWS, :].astype(F32)) + (
        two_ref[0:HEAD_ROWS, :].astype(F32) + three_ref[0:HEAD_ROWS, :].astype(F32)
    )
    tiles[HEAD_ROWS:BLOCK_ROWS, :] = tail_ref[...] + other_ref[...].astype(F32)

    for at, ref in enumerate((mine_ref, one_ref, two_ref, three_ref)):
        rows = ref.shape[0]
        part = ref[rows - 2 * VECTOR_ROWS : rows, :].astype(F32)
        vector_parts[at] = part[:VECTOR_ROWS] + part[VECTOR_ROWS:]
    vector = vector_parts[lax.rem(place, 4)]
    for z in (1, 2, 3):
        vector = vector + vector_parts[lax.rem(place + 4 - z, 4)]

    lane = lax.broadcasted_iota(jnp.int32, (2 * ROWS, WIDE), 1)
    x = jnp.where(lane < MODEL_WIDTH, tokens_ref[0].astype(F32).reshape(2 * ROWS, WIDE), 0.0)
    normed, scale = normed_rows(x)
    total = summed(own_dkv[...], other_dkv[...]).reshape(2 * ROWS, 384).astype(BF16)
    d_norm = (dq_wq_ref[...] + times_transposed(total, w_kv_ref[...])) * gains_ref[0:1, :]
    d_input = d_mid_ref[...] + scale * (d_norm - normed * row_mean(d_norm * normed))
    out_ref = states[-1]
    for mb in range(2):
        out_ref[mb] = d_input[ROWS * mb : ROWS * mb + ROWS].T[0:MODEL_WIDTH].astype(BF16)

    @pl.when(kind == 0)
    def _():
        for j in range(12):
            flat_ref[pl.ds(j, 72, stride=12), :] = tiles[72 * j : 72 * j + 72, :]

    @pl.when(kind == 1)
    def _():
        low = lower_lanes((96, LANES))
        narrow[0:96, :] = tiles[768:864, :]
        narrow[96:192, :] = half_turn(tiles[768:864, :])
        odd = [half_turn(tiles[pl.ds(192 * j + 1, 96, stride=2), :]) for j in range(4)]
        for j in range(4):
            flat_ref[pl.ds(j, 96, stride=9), :] = tiles[pl.ds(192 * j, 96, stride=2), :]
        flat_ref[pl.ds(4, 96, stride=9), :] = jnp.where(low, narrow[pl.ds(0, 96, stride=2), :], odd[0])
        for j in range(3):
            flat_ref[pl.ds(5 + j, 96, stride=9), :] = jnp.where(low, odd[j], odd[j + 1])
        last = half_turn(narrow[pl.ds(1, 96, stride=2), :])
        flat_ref[pl.ds(8, 96, stride=9), :] = jnp.where(low, odd[3], last)

    @pl.when(kind == 2)
    def _():
        low = lower_lanes((288, LANES))
        narrow[0:288, :] = tiles[576:864, :]
        narrow[288:576, :] = half_turn(tiles[576:864, :])
        odd = half_turn(tiles[pl.ds(1, 288, stride=2), :])
        flat_ref[pl.ds(0, 288, stride=3), :] = tiles[pl.ds(0, 288, stride=2), :]
        flat_ref[pl.ds(1, 288, stride=3), :] = jnp.where(low, narrow[pl.ds(0, 288, stride=2), :], odd)
        last = half_turn(narrow[pl.ds(1, 288, stride=2), :])
        flat_ref[pl.ds(2, 288, stride=3), :] = jnp.where(low, odd, last)


    if len(states) == 3:
        states[0][...], states[1][...] = flat_ref[...], vector
        return
    old_vectors, old_block, new_vectors, new_block = states[0:3], states[3:6], states[6:9], states[9:12]
    found = adamw(old_vectors[0][...], vector, old_vectors[1][...], old_vectors[2][...], RATE_VECTOR, 0.0)
    for ref, value in zip(new_vectors, found):
        ref[...] = value

    @pl.loop(0, 6)
    def _(k):
        rows = pl.ds(pl.multiple_of(k * 144, 8), 144)
        found = adamw(
            old_block[0][rows, :], flat_ref[rows, :], old_block[1][rows, :], old_block[2][rows, :], RATE_MATRIX, DECAY
        )
        for ref, value in zip(new_block, found):
            ref[rows, :] = value


def finish(table, parts, inputs, state):
    vmem = pl.BlockSpec(memory_space=pltpu.VMEM)
    flat = jax.ShapeDtypeStruct((BLOCK_ROWS, LANES), F32)
    vector = jax.ShapeDtypeStruct((VECTOR_ROWS, LANES), F32)
    shapes = (vector,) * 3 + (flat,) * 3 if state else (flat, vector)
    shapes += (jax.ShapeDtypeStruct((2, MODEL_WIDTH, ROWS), BF16),)
    return pl.pallas_call(
        finish_kernel,
        out_shape=shapes,
        in_specs=[pl.BlockSpec(memory_space=pltpu.SMEM)] + [vmem] * (len(parts) + len(inputs) + len(state)),
        out_specs=(vmem,) * len(shapes),
        scratch_shapes=[
            pltpu.VMEM((BLOCK_ROWS, LANES), F32),
            pltpu.VMEM((HEAD_ROWS, LANES), F32),
            pltpu.VMEM((BLOCK_ROWS, LANES), F32),
            pltpu.VMEM((4, VECTOR_ROWS, LANES), F32),
        ],
        name="finish",
    )(table, *parts, *inputs, *state)


def product(left, right):
    return jnp.dot(left, right, preferred_element_type=F32)


def times_transposed(left, right):
    return lax.dot_general(left, right, (((1,), (1,)), ((), ())), preferred_element_type=F32)


def rows_product(left, right):
    return lax.dot_general(left, right, (((0,), (0,)), ((), ())), preferred_element_type=F32)


def swapped(value):
    lane = lax.broadcasted_iota(jnp.int32, value.shape, 1)
    return jnp.where(lane % HEAD_SIZE < HEAD_SIZE // 2, pltpu.roll(value, 96, 1), pltpu.roll(value, 32, 1))


def rope(value, cosines, sines):
    return value * cosines + swapped(value) * sines


def rope_back(value, cosines, sines):
    return value * cosines - swapped(value) * sines


def row_mean(value):
    return jnp.sum(value, axis=-1, keepdims=True) * (1.0 / MODEL_WIDTH)


def normed_rows(value):
    scale = lax.rsqrt(row_mean(value * value) + EPS_NORM)
    return value * scale, scale


def place_rows(ref, head_tile, tail_tile, first):
    for j in range(3):
        ref[first : first + 192, LANES * j : LANES * j + LANES] = head_tile[192 * j : 192 * j + 192, :]
    ref[first : first + 192, 384:512] = tail_tile[0:192, :]
    rest = tail_tile[192:288, :].astype(F32)
    low = lower_lanes(rest.shape)
    ref[first : first + 96, 512:640] = jnp.where(low, rest, 0.0).astype(BF16)
    ref[first + 96 : first + 192, 512:640] = jnp.where(low, half_turn(rest), 0.0).astype(BF16)


def tiles_of_rows(value):
    head = jnp.concatenate([value[:, LANES * j : LANES * j + LANES] for j in range(3)], axis=0)
    rest = side_by_side(value[0:96, 512:640], value[96:192, 512:640])
    return head, jnp.concatenate([value[:, 384:512], rest], axis=0)


def layer_kernel(*refs):
    slots = refs[0]
    head_parts = refs[1:9]
    tail_parts = refs[9:13]
    tokens_pair, cos_pair, sin_pair = refs[13:15], refs[15:17], refs[17:19]
    (place_q_ref, place_k_ref, gains_ref, bias_q_ref, bias_kv_ref, grad_ref) = refs[19:25]
    block_out_ref, parts_out = refs[25], refs[26:36]
    (dkv_send, dkv_keep, dq_wq_ref, d_mid_ref, w_kv) = refs[36:41]
    (raw_head, raw_tail, w_q, w_out, w_gate, w_up, w_down, normed_all, hidden_all, keys, values, queries, probs, attended, act_all, block_acc, d_hidden, d_attended, dkv_all, d_query, send_all, keep_all, vector_ref, outs, sems, out_sems) = refs[41:]

    place = slots[MY_Z]

    def fetches(shift, sem):
        at = lax.rem(place + shift, 4)
        copies = []
        for k, part in enumerate(head_parts):
            copies.append(pltpu.make_async_copy(part.at[at], raw_head.at[4 * k + at], sems.at[sem + k]))
        for k, part in enumerate(tail_parts):
            rows = pl.ds(2 * at, 2)
            copies.append(pltpu.make_async_copy(part.at[rows], raw_tail.at[pl.ds(8 * k + 2 * at, 2)], sems.at[sem + 8 + k]))
        return copies

    attention_blocks = fetches(0, 0)
    other_blocks = fetches(1, 12) + fetches(2, 24) + fetches(3, 36)
    for copy in attention_blocks + other_blocks:
        copy.start()

    core = slots[MY_CORE]

    def at_slot(pair, slot):
        return pair[slot % 2].at[slot // 2]

    def head_tile(block):
        return raw_head.at[slots[AT_HEAD + block]]

    def tail_tile(block):
        return raw_tail.at[slots[AT_TAIL + block]]

    gain_one = gains_ref[0:1, :]
    gain_two = gains_ref[1:2, :]
    low_rows = lower_lanes((ROWS, LANES))

    @pl.loop(0, 2)
    def _(mb):
        lane = lax.broadcasted_iota(jnp.int32, (ROWS, WIDE), 1)
        for slot in range(4):
            rows = pl.ds(pl.multiple_of(mb * 512 + slot * ROWS, ROWS), ROWS)
            x = jnp.where(lane < MODEL_WIDTH, at_slot(tokens_pair, slot)[mb].astype(F32), 0.0)
            normed, _ = normed_rows(x)
            normed_all[rows, :] = normed
            hidden_all[rows, :] = (normed * gain_one).astype(BF16)

    for copy in attention_blocks:
        copy.wait()
    for ref in (w_q, w_out, w_gate, w_up, w_kv):
        ref[576:640, :] = jnp.zeros((64, ref.shape[1]), BF16)
    for k in range(3):
        place_rows(w_q, head_tile(k), tail_tile(k), 192 * k)
        place_rows(w_out, head_tile(5 + k), tail_tile(5 + k), 192 * k)
    w_kv[0:576, 0:128] = head_tile(3)[...]
    w_kv[0:576, 128:256] = head_tile(4)[...]
    rest_key = tail_tile(3)[...].astype(F32)
    rest_value = tail_tile(4)[...].astype(F32)
    low = lower_lanes(rest_key.shape)
    w_kv[0:288, 256:384] = jnp.where(low, rest_key, half_turn(rest_value)).astype(BF16)
    w_kv[288:576, 256:384] = jnp.where(low, half_turn(rest_key), rest_value).astype(BF16)

    @pl.loop(0, 2)
    def _(mb):
        rows = pl.ds(pl.multiple_of(mb * 512, 512), 512)
        pair = product(hidden_all[rows, :], w_kv[...]) + bias_kv_ref[...]
        cosines = jnp.concatenate([at_slot(cos_pair, slot)[mb] for slot in range(4)], axis=0)
        sines = jnp.concatenate([at_slot(sin_pair, slot)[mb] for slot in range(4)], axis=0)
        key_a = rope(pair[:, 0:128], cosines, sines)
        key_b = rope(pair[:, 256:384], cosines, sines)
        value_a, value_b = pair[:, 128:256], pair[:, 256:384]
        low_keys = lower_lanes((512, LANES))
        turned = half_turn(key_a)
        keys[rows, 0:128] = jnp.where(low_keys, key_a, turned).astype(BF16)
        keys[rows, 128:256] = jnp.where(low_keys, turned, key_a).astype(BF16)
        keys[rows, 256:384] = jnp.where(low_keys, key_b, half_turn(key_b)).astype(BF16)
        turned = half_turn(value_a)
        values[rows, 0:128] = jnp.where(low_keys, value_a, turned).astype(BF16)
        values[rows, 128:256] = jnp.where(low_keys, turned, value_a).astype(BF16)
        values[rows, 256:384] = jnp.where(low_keys, half_turn(value_b), value_b).astype(BF16)

    def heads_of(ref, rows, group):
        stacked = []
        for k in range(3):
            number = 3 * group + k
            tile = ref[rows, LANES * (number // 2) : LANES * (number // 2) + LANES]
            keep = low_rows if number % 2 == 0 else jnp.logical_not(low_rows)
            stacked.append(jnp.where(keep, tile.astype(F32), 0.0).astype(BF16))
        return jnp.concatenate(stacked, axis=0)

    def tiles_of_heads(parts):
        found = [jnp.where(low_rows, parts[2 * k], parts[2 * k + 1]) for k in range(4)]
        return found + [jnp.where(low_rows, parts[8], 0.0)]

    @pl.loop(0, 2)
    def _(mb):
        rows = pl.ds(pl.multiple_of(mb * ROWS, ROWS), ROWS)
        key_rows = pl.ds(pl.multiple_of(mb * 512, 512), 512)
        cosines, sines = cos_pair[0][0, mb], sin_pair[0][0, mb]
        made = product(hidden_all[pl.ds(pl.multiple_of(mb * 512, 512), ROWS), :], w_q[...]) + bias_q_ref[...]
        for k in range(5):
            turned = rope(made[:, LANES * k : LANES * k + LANES], cosines, sines)
            queries[rows, LANES * k : LANES * k + LANES] = (turned * HEAD_SIZE ** (-0.5)).astype(BF16)
        masked = jnp.where(place_q_ref[mb] >= place_k_ref[mb], 0.0, MASKED)
        masked = jnp.concatenate([masked] * 3, axis=0)
        parts = []
        for group in range(KEY_VALUE_HEADS):
            lanes = slice(LANES * group, LANES * group + LANES)
            scores = times_transposed(heads_of(queries, rows, group), keys[key_rows, lanes])
            scores = scores + masked
            top = jnp.max(scores, axis=-1, keepdims=True)
            powers = jnp.exp(scores - top)
            found = powers * (1.0 / jnp.sum(powers, axis=-1, keepdims=True))
            probs[mb, group] = found
            out = product(found.astype(BF16), values[key_rows, lanes])
            outs[mb, group] = out
            parts += [out[ROWS * k : ROWS * k + ROWS] for k in range(3)]
        for k, tile in enumerate(tiles_of_heads(parts)):
            attended[rows, LANES * k : LANES * k + LANES] = tile.astype(BF16)

    for copy in other_blocks:
        copy.wait()
    for k in range(8):
        place_rows(w_down, head_tile(24 + k), tail_tile(24 + k), 192 * k)
    for ref, base in ((w_gate, 8), (w_up, 16)):
        for k in range(4):
            for i in range(6):
                if i < 4:
                    even = head_tile(base + 2 * k)[144 * i : 144 * i + 144, :].astype(F32)
                    odd = head_tile(base + 2 * k + 1)[144 * i : 144 * i + 144, :].astype(F32)
                else:
                    even = tail_tile(base + 2 * k)[144 * (i - 4) : 144 * (i - 4) + 144, :].astype(F32)
                    odd = tail_tile(base + 2 * k + 1)[144 * (i - 4) : 144 * (i - 4) + 144, :].astype(F32)
                ref[144 * k : 144 * k + 144, 256 * i : 256 * i + 128] = jnp.concatenate(
                    [even[0:72], odd[0:72]], axis=0
                ).astype(BF16)
                ref[144 * k : 144 * k + 144, 256 * i + 128 : 256 * i + 256] = jnp.concatenate(
                    [even[72:144], odd[72:144]], axis=0
                ).astype(BF16)

    lane = lax.broadcasted_iota(jnp.int32, (2 * ROWS, WIDE), 1)
    x_own = tokens_pair[0][0].astype(F32).reshape(2 * ROWS, WIDE)
    x_own = jnp.where(lane < MODEL_WIDTH, x_own, 0.0)
    resid_mid = x_own + product(attended[...], w_out[...])
    normed_two, scale_two = normed_rows(resid_mid)
    hidden_two = (normed_two * gain_two).astype(BF16)
    hidden_turned = hidden_two.T
    grad_low = grad_ref[...]
    block_acc[...] = resid_mid
    d_hidden[...] = jnp.zeros_like(d_hidden)

    def store_pair(at, even, odd, table, first):
        rows = pl.ds(pl.multiple_of(slots[table + at] + first, 16), even.shape[0])
        send_all[rows, :] = jnp.where(core == 0, odd, even).astype(BF16)
        keep_all[rows, :] = jnp.where(core == 0, even, odd).astype(BF16)

    def feed_forward(chunk, first, table):
        cols = pl.ds(pl.multiple_of(chunk * 512, 512), 512)
        gate = product(hidden_two, w_gate[:, cols])
        up = product(hidden_two, w_up[:, cols])
        sigma = 1.0 / (1.0 + jnp.exp(-gate))
        act = (gate * sigma * up).astype(BF16)
        act_all[:, cols] = act
        down = w_down[cols, :]
        d_act = times_transposed(grad_low, down)
        block_acc[...] += product(act, down)
        d_up = (d_act * gate * sigma).astype(BF16)
        d_gate = (d_act * up * sigma * (1.0 + gate * (1.0 - sigma))).astype(BF16)
        d_hidden[...] += times_transposed(d_gate, w_gate[:, cols]) + times_transposed(d_up, w_up[:, cols])
        for base, cotangent in ((4, d_gate), (8, d_up)):
            made = product(hidden_turned, cotangent)
            for k in range(4):
                part = made[144 * k : 144 * k + 144, :]
                even = jnp.concatenate([part[0:72, LANES * j : LANES * j + LANES] for j in range(4)], axis=0)
                odd = jnp.concatenate([part[72:144, LANES * j : LANES * j + LANES] for j in range(4)], axis=0)
                store_pair(base + k, even, odd, table, (chunk - first) * 288)

    @pl.loop(0, 2)
    def _(chunk):
        feed_forward(chunk, 0, TO_HEAD)

    feed_forward(2, 2, TO_TAIL)

    def store_rows(at, even, odd):
        even_head, even_tail = even
        odd_head, odd_tail = odd
        store_pair(at, even_head, odd_head, TO_HEAD, 0)
        store_pair(at, even_tail, odd_tail, TO_TAIL, 0)

    @pl.loop(0, 4)
    def _(k):
        made = rows_product(act_all[:, pl.ds(pl.multiple_of(k * 384, 128), 384)], grad_low)
        store_rows(12 + k, tiles_of_rows(made[0:192]), tiles_of_rows(made[192:384]))

    def deliveries(first, count, sem):
        copies = []
        for base, outs_of in ((send_all, parts_out[0:4]), (keep_all, parts_out[4:10])):
            rest = [(outs_of[2], PART * k) for k in range(3)] if len(outs_of) == 4 else [(out, 0) for out in outs_of[2:5]]
            targets = [(outs_of[0], 0, FIRST_AT), (outs_of[1], 0, TAIL_AT)]
            targets += [(out, into, PART * k) for k, (out, into) in enumerate(rest)]
            targets.append((outs_of[-1], 0, 3 * PART))
            for out, into, start in targets:
                rows = HEAD_ROWS * count
                copies.append(
                    pltpu.make_async_copy(
                        base.at[pl.ds(start + HEAD_ROWS * first, rows)],
                        out.at[pl.ds(into + HEAD_ROWS * first, rows)],
                        out_sems.at[sem + len(copies)],
                    )
                )
        return copies

    early = deliveries(1, 3, 12)
    for copy in early:
        copy.start()

    for mb in range(2):
        block_out_ref[mb] = block_acc[ROWS * mb : ROWS * mb + ROWS, :].T[0:MODEL_WIDTH].astype(BF16)

    d_two = d_hidden[...]
    gain_two_sum = jnp.sum(d_two * normed_two, axis=0, keepdims=True)
    d_norm = d_two * gain_two
    d_mid = grad_low.astype(F32) + scale_two * (d_norm - normed_two * row_mean(d_norm * normed_two))
    d_mid_ref[...] = d_mid
    d_branch = d_mid.astype(BF16)
    d_attended[...] = times_transposed(d_branch, w_out[...]).astype(BF16)
    grad_out = rows_product(attended[...], d_branch)

    @pl.loop(0, 2)
    def _(mb):
        rows = pl.ds(pl.multiple_of(mb * ROWS, ROWS), ROWS)
        key_rows = pl.ds(pl.multiple_of(mb * 512, 512), 512)
        parts = []
        d_keys = []
        d_values = []
        for group in range(KEY_VALUE_HEADS):
            lanes = slice(LANES * group, LANES * group + LANES)
            query_rows = heads_of(queries, rows, group)
            cotangent = heads_of(d_attended, rows, group)
            found = probs[mb, group]
            d_probs = times_transposed(cotangent, values[key_rows, lanes])
            delta = jnp.sum(outs[mb, group] * cotangent.astype(F32), axis=-1, keepdims=True)
            d_scores = (found * (d_probs - delta)).astype(BF16)
            out = product(d_scores, keys[key_rows, lanes]) * HEAD_SIZE ** (-0.5)
            parts += [out[ROWS * k : ROWS * k + ROWS] for k in range(3)]
            d_key = rows_product(d_scores, query_rows)
            d_value = rows_product(found.astype(BF16), cotangent)
            d_keys.append(d_key + half_turn(d_key))
            d_values.append(d_value + half_turn(d_value))
        cosines, sines = cos_pair[0][0, mb], sin_pair[0][0, mb]
        for k, tile in enumerate(tiles_of_heads(parts)):
            d_query[rows, LANES * k : LANES * k + LANES] = rope_back(tile, cosines, sines).astype(BF16)
        low_keys = lower_lanes((512, LANES))
        cosines = jnp.concatenate([at_slot(cos_pair, slot)[mb] for slot in range(4)], axis=0)
        sines = jnp.concatenate([at_slot(sin_pair, slot)[mb] for slot in range(4)], axis=0)
        key_a = rope_back(jnp.where(low_keys, d_keys[0], d_keys[1]), cosines, sines)
        key_b = rope_back(d_keys[2], cosines, sines)
        dkv_all[key_rows, 0:128] = key_a.astype(BF16)
        dkv_all[key_rows, 128:256] = jnp.where(low_keys, d_values[0], d_values[1]).astype(BF16)
        dkv_all[key_rows, 256:384] = jnp.where(low_keys, key_b, d_values[2]).astype(BF16)
        for slot in range(4):
            target = dkv_send if slot % 2 else dkv_keep
            target[slot // 2, mb] = dkv_all[pl.ds(pl.multiple_of(mb * 512 + slot * ROWS, ROWS), ROWS), :]

    dkv = dkv_all[...]
    d_q = d_query[...]
    dq_wq = times_transposed(d_q, w_q[...])
    dq_wq_ref[...] = dq_wq
    bias_q_sum = jnp.sum(d_q.astype(F32), axis=0, keepdims=True)
    bias_kv_sum = jnp.sum(dkv.astype(F32), axis=0, keepdims=True)
    gain_sum = jnp.zeros((1, WIDE), F32)
    for mb in range(2):
        gain_sum += jnp.sum(dq_wq[ROWS * mb : ROWS * mb + ROWS] * normed_all[512 * mb : 512 * mb + ROWS, :], axis=0, keepdims=True)
    for k in range(4):
        part = slice(256 * k, 256 * k + 256)
        gain_sum += jnp.sum(times_transposed(dkv_all[part, :], w_kv[...]) * normed_all[part, :], axis=0, keepdims=True)

    hidden_own = jnp.concatenate([hidden_all[0:ROWS, :], hidden_all[512 : 512 + ROWS, :]], axis=0)
    grad_q = rows_product(hidden_own, d_q)
    grad_kv = rows_product(hidden_all[...], dkv)
    rest = grad_kv[0:576, 256:384]
    low = lower_lanes((288, LANES))
    key_tiles = (grad_kv[0:576, 0:128], jnp.where(low, rest[0:288], half_turn(rest[288:576])))
    value_tiles = (grad_kv[0:576, 128:256], jnp.where(low, half_turn(rest[0:288]), rest[288:576]))
    query_tiles = [tiles_of_rows(grad_q[192 * k : 192 * k + 192]) for k in range(3)]
    out_tiles = [tiles_of_rows(grad_out[192 * k : 192 * k + 192]) for k in range(3)]
    store_rows(0, query_tiles[0], query_tiles[1])
    store_rows(1, query_tiles[2], key_tiles)
    store_rows(2, value_tiles, out_tiles[0])
    store_rows(3, out_tiles[1], out_tiles[2])
    def flat_rows(first, second, third, pair):
        tile = lambda row, k: row[:, LANES * k : LANES * k + LANES]
        low = lower_lanes((1, LANES))
        across_two = lambda one, two: jnp.where(low, half_turn(one), half_turn(two))
        lines = [tile(first, k) for k in range(4)]
        lines.append(side_by_side(tile(first, 4), tile(second, 0)))
        lines += [across_two(tile(second, k), tile(second, k + 1)) for k in range(4)]
        lines += [tile(third, k) for k in range(4)]
        lines.append(side_by_side(tile(third, 4), tile(pair, 0)))
        lines.append(across_two(tile(pair, 0), tile(pair, 2)))
        lines.append(tile(pair, 1))
        lines.append(jnp.where(low, half_turn(tile(pair, 2)), 0.0))
        return lines

    at = FIRST_AT + PART
    for row, line in enumerate(flat_rows(gain_sum, gain_two_sum, bias_q_sum, bias_kv_sum)):
        vector_ref[row : row + 1, :] = line
    vector_ref[17:24, :] = jnp.zeros((7, LANES), F32)
    vector = vector_ref[...]
    high = vector.astype(BF16).astype(F32)
    both = jnp.concatenate([high, vector - high], axis=0).astype(BF16)
    for ref in (send_all, keep_all):
        ref[at : at + 2 * VECTOR_ROWS, :] = both
    last = deliveries(0, 1, 0)
    last.append(pltpu.make_async_copy(send_all.at[pl.ds(at, 2 * VECTOR_ROWS)], parts_out[0].at[pl.ds(PART, 2 * VECTOR_ROWS)], out_sems.at[24]))
    last.append(pltpu.make_async_copy(keep_all.at[pl.ds(at, 2 * VECTOR_ROWS)], parts_out[4].at[pl.ds(PART, 2 * VECTOR_ROWS)], out_sems.at[25]))
    for copy in last:
        copy.start()
    for copy in early + last:
        copy.wait()


def run_layer(slots, heads, tails, *others):
    shape = jax.ShapeDtypeStruct
    vmem = pl.BlockSpec(memory_space=pltpu.VMEM)
    anywhere = pl.BlockSpec(memory_space=pl.ANY)
    scratch = [
        ((BLOCKS, HEAD_ROWS, LANES), BF16),
        ((BLOCKS, TAIL_ROWS, LANES), BF16),
        ((WIDE, WIDE), BF16),
        ((WIDE, WIDE), BF16),
        ((WIDE, FF), BF16),
        ((WIDE, FF), BF16),
        ((FF, WIDE), BF16),
        ((1024, WIDE), F32),
        ((1024, WIDE), BF16),
        ((1024, 384), BF16),
        ((1024, 384), BF16),
        ((256, WIDE), BF16),
        ((2, 3, 384, 512), F32),
        ((256, WIDE), BF16),
        ((256, FF), BF16),
        ((256, WIDE), F32),
        ((256, WIDE), F32),
        ((256, WIDE), BF16),
        ((1024, 384), BF16),
        ((256, WIDE), BF16),
        ((ALL_ROWS, LANES), BF16),
        ((ALL_ROWS, LANES), BF16),
        ((VECTOR_ROWS, LANES), F32),
        ((2, 3, 384, LANES), F32),
    ]
    return pl.pallas_call(
        layer_kernel,
        out_shape=(
            shape((2, MODEL_WIDTH, ROWS), BF16),
            *[shape((count, LANES), BF16) for _, count in SEND_PARTS + KEEP_PARTS],
            shape((2, 2, ROWS, 384), BF16),
            shape((2, 2, ROWS, 384), BF16),
            shape((256, WIDE), F32),
            shape((256, WIDE), F32),
            shape((WIDE, 384), BF16),
        ),
        in_specs=[pl.BlockSpec(memory_space=pltpu.SMEM)] + [anywhere] * 12 + [vmem] * 12,
        out_specs=(vmem,) + (anywhere,) * 10 + (vmem,) * 5,
        scratch_shapes=[pltpu.VMEM(dims, kind) for dims, kind in scratch]
        + [pltpu.SemaphoreType.DMA((48,)), pltpu.SemaphoreType.DMA((26,))],
        compiler_params=pltpu.CompilerParams(vmem_limit_bytes=50 * 1024 * 1024),
        name="layer",
    )(slots, *heads, *tails, *others)


def adamw(param, grad, mom_one, mom_two, rate, decay):
    new_one = BETA_ONE * mom_one + (1.0 - BETA_ONE) * grad
    new_two = BETA_TWO * mom_two + (1.0 - BETA_TWO) * grad * grad
    fixed_one = new_one / (1.0 - BETA_ONE**STEP)
    fixed_two = new_two / (1.0 - BETA_TWO**STEP)
    new_param = param - rate * (fixed_one / (jnp.sqrt(fixed_two) + EPS_ADAM) + decay * param)
    return (new_param, new_one, new_two)


def inner_groups():
    inner = inner_count()
    data_inner = inner // lax.axis_size("ctx")
    data_count = lax.axis_size("dp")
    return [list(range(k, k + data_inner)) for k in range(0, data_count, data_inner)]


def whole_block(flat):
    if inner_count() == 1:
        return flat
    flat = lax.all_gather(flat, "ctx", axis=0, tiled=True)
    return lax.all_gather(flat, "dp", axis=0, tiled=True, axis_index_groups=inner_groups())


def own_slice(block):
    if inner_count() == 1:
        return block
    block = lax.psum_scatter(
        block, "dp", scatter_dimension=0, tiled=True, axis_index_groups=inner_groups()
    )
    return lax.psum_scatter(block, "ctx", scatter_dimension=0, tiled=True)


def bias_tiles(bias_key, bias_value):
    return jnp.concatenate([bias_key[:128], bias_value[:128], bias_key[128:], bias_value[128:]])


def local(tokens_in, places, out_grad, weights, first_moment, second_moment, vectors, vector_first, vector_second):
    kind = kind_of(device_number() // inner_count()).astype(jnp.int32).reshape(1)
    block = whole_block(weights).reshape(BLOCK_ROWS, LANES)
    head, tail = to_tiles(kind, block)

    head, tail, tokens_in, places = together(head, tail, tokens_in, places)
    own_tokens = tokens_in.reshape(2, ROWS, MODEL_WIDTH)
    own_places = places.reshape(2, ROWS)
    marks = jnp.stack([own_places // 16, own_places % 16], axis=-1).astype(BF16)
    packed = jnp.concatenate(
        [own_tokens, marks, jnp.zeros((2, ROWS, WIDE - MODEL_WIDTH - 2), BF16)], axis=-1
    )
    padding = ((0, 0), (0, WIDE - MODEL_WIDTH))
    gains = jnp.pad(vectors[: 2 * MODEL_WIDTH].reshape(2, MODEL_WIDTH), padding)
    bias_q = jnp.pad(vectors[2 * MODEL_WIDTH : 3 * MODEL_WIDTH].reshape(1, MODEL_WIDTH), padding)
    bias_kv = bias_tiles(vectors[1728:1920], vectors[1920:2112]).reshape(1, 384)
    grad = jnp.pad(out_grad.reshape(2 * ROWS, MODEL_WIDTH), padding)
    spare = VECTOR_ROWS * LANES - vectors.shape[0]
    vector_state = [
        jnp.pad(array, (0, spare), constant_values=1.0).reshape(VECTOR_ROWS, LANES)
        for array in (vectors, vector_first, vector_second)
    ]
    table = jnp.concatenate([kind, (coordinates(device_number() // inner_count())["z"]).astype(jnp.int32).reshape(1)])
    others = (slot_table(), gains, bias_q, bias_kv, grad, vector_state, table)
    heads, tails, (near, far), (cosines, sines), others = gather_all(head, tail, packed, others)
    slots, gains, bias_q, bias_kv, grad, vector_state, table = others
    cosines_far, sines_far = place_tables(far)
    place_all = jnp.stack([places_of(near), places_of(far)], axis=1)
    place_q = place_all[0, 0][..., None]
    place_k = jnp.transpose(place_all.reshape(4, 2, ROWS), (1, 0, 2)).reshape(2, 1, 4 * ROWS)

    block_out, *found = run_layer(
        slots, heads, tails, near, far, cosines, cosines_far, sines, sines_far, place_q, place_k, gains, bias_q, bias_kv, grad
    )
    sends, keeps = found[:4], found[4:10]
    dkv_send, dkv_keep, dq_wq, d_mid, w_kv = found[10:]
    parts, pairs = scatter_blocks(sends, keeps, dkv_send, dkv_keep)
    inputs = (near, gains, w_kv, dq_wq, d_mid, *pairs)
    state = (weights, first_moment, second_moment)
    if inner_count() == 1:
        blocks = [array.reshape(BLOCK_ROWS, LANES) for array in state]
        *updated, input_grad = finish(table, parts, inputs, [*vector_state, *blocks])
        new_vector_state = [array.reshape(-1)[: vectors.shape[0]] for array in updated[:3]]
        new_state = [array.reshape(-1) for array in updated[3:]]
    else:
        block_grad, vector, input_grad = finish(table, parts, inputs, [])
        vector = lax.psum(vector, "ctx")
        vector = lax.psum(vector, "dp", axis_index_groups=inner_groups())
        grad_own = own_slice(block_grad.reshape(-1))
        vector_grad = vector.reshape(-1)[: vectors.shape[0]]
        new_state = adamw(weights, grad_own, first_moment, second_moment, RATE_MATRIX, DECAY)
        new_vector_state = adamw(vectors, vector_grad, vector_first, vector_second, RATE_VECTOR, 0.0)
    shape = tokens_in.shape
    return (
        jnp.transpose(block_out, (0, 2, 1)).reshape(shape),
        jnp.transpose(input_grad, (0, 2, 1)).reshape(shape),
        *new_state,
        *new_vector_state,
    )


def solution(mesh):
    in_specs = (
        P(None, "dp", "ctx", None),
        P(None, "dp", "ctx"),
        P(None, "dp", "ctx", None),
        P(("dp", "ctx")),
        P(("dp", "ctx")),
        P(("dp", "ctx")),
        P(),
        P(),
        P(),
    )
    out_specs = (
        P(None, "dp", "ctx", None),
        P(None, "dp", "ctx", None),
        P(("dp", "ctx")),
        P(("dp", "ctx")),
        P(("dp", "ctx")),
        P(),
        P(),
        P(),
    )
    return jax.shard_map(local, mesh=mesh, in_specs=in_specs, out_specs=out_specs, check_vma=False)
```

```python
import jax
import jax.numpy as jnp
from jax import lax
from jax.experimental import pallas as pl
from jax.experimental.pallas import tpu as pltpu
from jax.sharding import PartitionSpec as P

MODEL_WIDTH = 576
QUERY_HEADS = 9
KEY_VALUE_HEADS = 3
HEAD_SIZE = 64
FF = 1536
STEP = 10

EPS_NORM = 1e-05
THETA = 100000.0
BETA_ONE = 0.9
BETA_TWO = 0.95
EPS_ADAM = 1e-08
RATE_MATRIX = 0.06
RATE_VECTOR = 0.3
DECAY = 0.1
MASKED = -1e30

LANES = 128
WIDE = 640
BLOCKS = 32
BLOCK_ROWS = 864
HEAD_ROWS = 576
TAIL_ROWS = BLOCK_ROWS - HEAD_ROWS
VECTOR_ROWS = 24
PART = 4 * HEAD_ROWS
FIRST_AT = 4 * PART
TAIL_AT = FIRST_AT + PART + 2 * VECTOR_ROWS
ALL_ROWS = TAIL_AT + PART
SEND_PARTS = [(FIRST_AT, PART + 2 * VECTOR_ROWS), (TAIL_AT, PART), (0, 3 * PART), (3 * PART, PART)]
KEEP_PARTS = SEND_PARTS[:2] + [(PART * k, PART) for k in range(4)]
SIZES = {"z": 4, "y": 2, "x": 2, "c": 2}
ROWS = 128
HALF = 64
F32 = jnp.float32
BF16 = jnp.bfloat16


def coordinates(number):
    found = {}
    for name in ("c", "x", "y", "z"):
        found[name] = number % SIZES[name]
        number = number // SIZES[name]
    return found


def number_of(found):
    number = 0
    for name in ("z", "y", "x", "c"):
        number = number * SIZES[name] + found[name]
    return number


def device_number():
    return lax.axis_index("dp") * lax.axis_size("ctx") + lax.axis_index("ctx")


def inner_count():
    return lax.axis_size("dp") * lax.axis_size("ctx") // BLOCKS


def moved(buffer, name, shift):
    inner = inner_count()
    pairs = []
    for number in range(BLOCKS):
        found = coordinates(number)
        found[name] = found[name] ^ shift
        target = number_of(found)
        pairs += [(number * inner + k, target * inner + k) for k in range(inner)]
    return lax.ppermute(buffer, ("dp", "ctx"), pairs)


def across(buffer, distance):
    count = lax.axis_size("ctx")
    return lax.ppermute(buffer, "ctx", [(i, i ^ distance) for i in range(count)])


def together(*arrays):
    return lax.optimization_barrier(arrays)


def gather_all(head, tail, packed, others):
    hz = [moved(head, "z", s) for s in (1, 2, 3)]
    tx = moved(tail, "x", 1)
    two = across(packed, 2)
    head, tail, tx, two, *hz = together(head, tail, tx, two, *hz)
    own = jnp.stack([head] + hz)
    pair = jnp.stack([tail, tx])
    ay = moved(own, "y", 1)
    ax = moved(own, "x", 1)
    tz = [moved(pair, "z", s) for s in (1, 2, 3)]
    near = jnp.stack([packed, two])
    tables = place_tables(near)
    own, pair, ay, ax, near, tables, others, *tz = together(own, pair, ay, ax, near, tables, others, *tz)
    eight = jnp.concatenate([pair] + tz)
    far = across(near, 1)
    axy = moved(ay, "x", 1)
    ty = moved(eight, "y", 1)
    ac = moved(own, "c", 1)
    acy = moved(ay, "c", 1)
    acx = moved(ax, "c", 1)
    tc = moved(eight, "c", 1)
    axy, ty, ac, acy, acx, tc, far = together(axy, ty, ac, acy, acx, tc, far)
    acxy = moved(axy, "c", 1)
    tcy = moved(ty, "c", 1)
    heads = [own, ay, ax, axy, ac, acy, acx, acxy]
    return heads, [eight, ty, tc, tcy], (near, far), tables, others


def places_of(tokens):
    found = tokens[..., MODEL_WIDTH : MODEL_WIDTH + 2].astype(F32)
    return found[..., 0] * 16.0 + found[..., 1]


def place_tables(tokens):
    half_dim = HEAD_SIZE // 2
    frequency = THETA ** (-2.0 * jnp.arange(half_dim, dtype=F32) / HEAD_SIZE)
    angles = places_of(tokens)[..., None] * jnp.tile(frequency, 4)
    sign = jnp.where(jnp.arange(LANES) % HEAD_SIZE < half_dim, -1.0, 1.0).astype(F32)
    return jnp.cos(angles), jnp.sin(angles) * sign


def fold(order, relative):
    slot = 0
    for name in order:
        slot = slot * SIZES[name] + relative[name]
    return slot


def head_row(slot, z, _):
    return slot * PART + jnp.where(slot < 3, 0, FIRST_AT - 3 * PART) + z * HEAD_ROWS


def tail_row(slot, z, inside):
    return jnp.where(slot < 1, 3 * PART, TAIL_AT) + (2 * z + inside) * TAIL_ROWS


def slot_table():
    mine = coordinates(device_number() // inner_count())
    entries = []
    for order in (("c", "x", "y", "z"), ("c", "y", "z", "x")):
        for number in range(BLOCKS):
            found = coordinates(number)
            entries.append(fold(order, {n: mine[n] ^ found[n] for n in SIZES}))
    for order, start in ((("x", "y"), head_row), (("y",), tail_row)):
        for number in range(0, BLOCKS, 2):
            found = coordinates(number)
            slot = fold(order, {n: mine[n] ^ found[n] for n in SIZES})
            inside = mine["x"] ^ found["x"]
            entries.append(start(slot, found["z"], inside))
    entries.append(mine["c"])
    entries.append(mine["z"])
    return jnp.stack([jnp.asarray(entry, jnp.int32) for entry in entries])


AT_HEAD, AT_TAIL, TO_HEAD, TO_TAIL = 0, BLOCKS, 2 * BLOCKS, 2 * BLOCKS + 16
MY_CORE, MY_Z = 2 * BLOCKS + 32, 2 * BLOCKS + 33


def summed(*parts):
    total = parts[0].astype(F32)
    for part in parts[1:]:
        total = total + part.astype(F32)
    return total


def summed_vector(mine, other):
    total = summed(mine[:VECTOR_ROWS], other[:VECTOR_ROWS]) + summed(mine[VECTOR_ROWS:], other[VECTOR_ROWS:])
    high = lax.reduce_precision(total, 8, 7)
    return jnp.concatenate([high.astype(BF16), (total - high).astype(BF16)])


def scatter_blocks(sends, keeps, dkv_send, dkv_keep):
    keep_head, keep_tail, keep_low, keep_mid, keep_far, keep_rest = keeps
    got_head, got_tail = moved(sends[0], "c", 1), moved(sends[1], "c", 1)
    got_head, got_tail, rest_head, rest_tail, dkv_send = together(got_head, got_tail, *sends[2:], dkv_send)
    got_rest_head, got_rest_tail = moved(rest_head, "c", 1), moved(rest_tail, "c", 1)
    got_dkv = across(dkv_send, 1)
    vector = summed_vector(keep_head[PART:], got_head[PART:])
    hx = jnp.concatenate([summed(keep_head[:PART], got_head[:PART]).astype(BF16), vector])
    ty = summed(keep_tail, got_tail).astype(BF16)
    got_hx = moved(hx, "x", 1)
    got_ty = moved(ty, "y", 1)
    low, mid, far = [
        summed(keep, got_rest_head[PART * k : PART * k + PART]).astype(BF16)
        for k, keep in enumerate((keep_low, keep_mid, keep_far))
    ]
    tail = summed(keep_rest, got_rest_tail).astype(BF16)
    dkv = summed(dkv_keep, got_dkv).astype(BF16)
    got_hx, got_ty, low, mid, far, tail, dkv, vector = together(got_hx, got_ty, low, mid, far, tail, dkv, vector)
    place = coordinates(device_number() // inner_count())["z"]

    def part_for(array, shift):
        return lax.dynamic_slice_in_dim(array, HEAD_ROWS * (place ^ shift), HEAD_ROWS, 0)

    vector = summed_vector(vector, got_hx[PART:])
    hy = jnp.concatenate([summed(mid, got_hx[:PART]).astype(BF16), vector])
    tz = [summed(part_for(tail, s), part_for(got_ty, s)).astype(BF16) for s in range(4)]
    got_hy = moved(hy, "y", 1)
    got_far = moved(far, "x", 1)
    got_tz = [moved(tz[s], "z", s) for s in (1, 2, 3)]
    got_hy, got_far, low, own_tail, vector, dkv, *got_tz = together(got_hy, got_far, low, tz[0], vector, dkv, *got_tz)
    vector = summed_vector(vector, got_hy[PART:])
    head = [summed(part_for(low, s), part_for(got_far, s), part_for(got_hy, s)) for s in range(4)]
    got_hz = [moved(jnp.concatenate([head[s].astype(BF16), vector]), "z", s) for s in (1, 2, 3)]
    tx = summed(own_tail[TAIL_ROWS:], *[part[TAIL_ROWS:] for part in got_tz]).astype(BF16)
    own_tail = summed(own_tail[:TAIL_ROWS], *[part[:TAIL_ROWS] for part in got_tz])
    got_tx = moved(tx, "x", 1)
    got_dkv = across(dkv[1], 2)
    return (head[0], *got_hz, own_tail, got_tx, vector), (dkv[0], got_dkv)


def lower_lanes(shape):
    return lax.broadcasted_iota(jnp.int32, shape, 1) < HEAD_SIZE


def half_turn(value):
    return pltpu.roll(value, HEAD_SIZE, 1)


def side_by_side(left, right):
    return jnp.where(lower_lanes(left.shape), left, half_turn(right))


def kind_of(block):
    return jnp.where(block >= 24, 1, jnp.where(block >= 8, 0, jnp.where((block == 3) | (block == 4), 2, 1)))


def tile_kernel(kind_ref, flat_ref, head_ref, tail_ref, tiles, narrow):
    kind = kind_ref[0]

    @pl.when(kind == 0)
    def _():
        for j in range(12):
            tiles[72 * j : 72 * j + 72, :] = flat_ref[pl.ds(j, 72, stride=12), :]

    @pl.when(kind == 1)
    def _():
        lines = [flat_ref[pl.ds(t, 96, stride=9), :] for t in range(9)]
        turned = [half_turn(line) for line in lines[4:]]
        low = lower_lanes((96, LANES))
        for j in range(4):
            tiles[pl.ds(192 * j, 96, stride=2), :] = lines[j]
            tiles[pl.ds(192 * j + 1, 96, stride=2), :] = jnp.where(low, turned[j], turned[j + 1])
        narrow[pl.ds(0, 96, stride=2), :] = lines[4]
        narrow[pl.ds(1, 96, stride=2), :] = turned[4]
        tiles[768:864, :] = side_by_side(narrow[0:96, :], narrow[96:192, :])

    @pl.when(kind == 2)
    def _():
        lines = [flat_ref[pl.ds(t, 288, stride=3), :] for t in range(3)]
        first, second = half_turn(lines[1]), half_turn(lines[2])
        tiles[pl.ds(0, 288, stride=2), :] = lines[0]
        tiles[pl.ds(1, 288, stride=2), :] = jnp.where(lower_lanes((288, LANES)), first, second)
        narrow[pl.ds(0, 288, stride=2), :] = lines[1]
        narrow[pl.ds(1, 288, stride=2), :] = second
        tiles[576:864, :] = side_by_side(narrow[0:288, :], narrow[288:576, :])

    head_ref[...] = tiles[0:HEAD_ROWS, :].astype(BF16)
    tail_ref[...] = tiles[HEAD_ROWS:BLOCK_ROWS, :].astype(BF16)


def to_tiles(kind, flat):
    return pl.pallas_call(
        tile_kernel,
        out_shape=(
            jax.ShapeDtypeStruct((HEAD_ROWS, LANES), BF16),
            jax.ShapeDtypeStruct((TAIL_ROWS, LANES), BF16),
        ),
        in_specs=[
            pl.BlockSpec(memory_space=pltpu.SMEM),
            pl.BlockSpec(memory_space=pltpu.VMEM),
        ],
        out_specs=(pl.BlockSpec(memory_space=pltpu.VMEM),) * 2,
        scratch_shapes=[
            pltpu.VMEM((BLOCK_ROWS, LANES), F32),
            pltpu.VMEM((HEAD_ROWS, LANES), F32),
        ],
        name="to_tiles",
    )(kind, flat)


def finish_kernel(table_ref, head_ref, one_ref, two_ref, three_ref, tail_ref, other_ref, mine_ref, *refs):
    kind, place = table_ref[0], table_ref[1]
    tiles, narrow, flat_ref, vector_parts = refs[-4:]
    tokens_ref, gains_ref, w_kv_ref, dq_wq_ref, d_mid_ref, own_dkv, other_dkv = refs[:7]
    states = refs[7:-4]
    tiles[0:HEAD_ROWS, :] = (head_ref[...] + one_ref[0:HEAD_ROWS, :].astype(F32)) + (
        two_ref[0:HEAD_ROWS, :].astype(F32) + three_ref[0:HEAD_ROWS, :].astype(F32)
    )
    tiles[HEAD_ROWS:BLOCK_ROWS, :] = tail_ref[...] + other_ref[...].astype(F32)

    for at, ref in enumerate((mine_ref, one_ref, two_ref, three_ref)):
        rows = ref.shape[0]
        part = ref[rows - 2 * VECTOR_ROWS : rows, :].astype(F32)
        vector_parts[at] = part[:VECTOR_ROWS] + part[VECTOR_ROWS:]
    vector = vector_parts[place]
    for z in (1, 2, 3):
        vector = vector + vector_parts[jnp.bitwise_xor(place, z)]

    lane = lax.broadcasted_iota(jnp.int32, (2 * ROWS, WIDE), 1)
    x = jnp.where(lane < MODEL_WIDTH, tokens_ref[0].astype(F32).reshape(2 * ROWS, WIDE), 0.0)
    normed, scale = normed_rows(x)
    total = summed(own_dkv[...], other_dkv[...]).reshape(2 * ROWS, 384).astype(BF16)
    d_norm = (dq_wq_ref[...] + times_transposed(total, w_kv_ref[...])) * gains_ref[0:1, :]
    d_input = d_mid_ref[...] + scale * (d_norm - normed * row_mean(d_norm * normed))
    out_ref = states[-1]
    for mb in range(2):
        out_ref[mb] = d_input[ROWS * mb : ROWS * mb + ROWS].T[0:MODEL_WIDTH].astype(BF16)

    @pl.when(kind == 0)
    def _():
        for j in range(12):
            flat_ref[pl.ds(j, 72, stride=12), :] = tiles[72 * j : 72 * j + 72, :]

    @pl.when(kind == 1)
    def _():
        low = lower_lanes((96, LANES))
        narrow[0:96, :] = tiles[768:864, :]
        narrow[96:192, :] = half_turn(tiles[768:864, :])
        odd = [half_turn(tiles[pl.ds(192 * j + 1, 96, stride=2), :]) for j in range(4)]
        for j in range(4):
            flat_ref[pl.ds(j, 96, stride=9), :] = tiles[pl.ds(192 * j, 96, stride=2), :]
        flat_ref[pl.ds(4, 96, stride=9), :] = jnp.where(low, narrow[pl.ds(0, 96, stride=2), :], odd[0])
        for j in range(3):
            flat_ref[pl.ds(5 + j, 96, stride=9), :] = jnp.where(low, odd[j], odd[j + 1])
        last = half_turn(narrow[pl.ds(1, 96, stride=2), :])
        flat_ref[pl.ds(8, 96, stride=9), :] = jnp.where(low, odd[3], last)

    @pl.when(kind == 2)
    def _():
        low = lower_lanes((288, LANES))
        narrow[0:288, :] = tiles[576:864, :]
        narrow[288:576, :] = half_turn(tiles[576:864, :])
        odd = half_turn(tiles[pl.ds(1, 288, stride=2), :])
        flat_ref[pl.ds(0, 288, stride=3), :] = tiles[pl.ds(0, 288, stride=2), :]
        flat_ref[pl.ds(1, 288, stride=3), :] = jnp.where(low, narrow[pl.ds(0, 288, stride=2), :], odd)
        last = half_turn(narrow[pl.ds(1, 288, stride=2), :])
        flat_ref[pl.ds(2, 288, stride=3), :] = jnp.where(low, odd, last)


    if len(states) == 3:
        states[0][...], states[1][...] = flat_ref[...], vector
        return
    old_vectors, old_block, new_vectors, new_block = states[0:3], states[3:6], states[6:9], states[9:12]
    found = adamw(old_vectors[0][...], vector, old_vectors[1][...], old_vectors[2][...], RATE_VECTOR, 0.0)
    for ref, value in zip(new_vectors, found):
        ref[...] = value

    @pl.loop(0, 6)
    def _(k):
        rows = pl.ds(pl.multiple_of(k * 144, 8), 144)
        found = adamw(
            old_block[0][rows, :], flat_ref[rows, :], old_block[1][rows, :], old_block[2][rows, :], RATE_MATRIX, DECAY
        )
        for ref, value in zip(new_block, found):
            ref[rows, :] = value


def finish(table, parts, inputs, state):
    vmem = pl.BlockSpec(memory_space=pltpu.VMEM)
    flat = jax.ShapeDtypeStruct((BLOCK_ROWS, LANES), F32)
    vector = jax.ShapeDtypeStruct((VECTOR_ROWS, LANES), F32)
    shapes = (vector,) * 3 + (flat,) * 3 if state else (flat, vector)
    shapes += (jax.ShapeDtypeStruct((2, MODEL_WIDTH, ROWS), BF16),)
    return pl.pallas_call(
        finish_kernel,
        out_shape=shapes,
        in_specs=[pl.BlockSpec(memory_space=pltpu.SMEM)] + [vmem] * (len(parts) + len(inputs) + len(state)),
        out_specs=(vmem,) * len(shapes),
        scratch_shapes=[
            pltpu.VMEM((BLOCK_ROWS, LANES), F32),
            pltpu.VMEM((HEAD_ROWS, LANES), F32),
            pltpu.VMEM((BLOCK_ROWS, LANES), F32),
            pltpu.VMEM((4, VECTOR_ROWS, LANES), F32),
        ],
        name="finish",
    )(table, *parts, *inputs, *state)


def product(left, right):
    return jnp.dot(left, right, preferred_element_type=F32)


def times_transposed(left, right):
    return lax.dot_general(left, right, (((1,), (1,)), ((), ())), preferred_element_type=F32)


def rows_product(left, right):
    return lax.dot_general(left, right, (((0,), (0,)), ((), ())), preferred_element_type=F32)


def swapped(value):
    lane = lax.broadcasted_iota(jnp.int32, value.shape, 1)
    return jnp.where(lane % HEAD_SIZE < HEAD_SIZE // 2, pltpu.roll(value, 96, 1), pltpu.roll(value, 32, 1))


def rope(value, cosines, sines):
    return value * cosines + swapped(value) * sines


def rope_back(value, cosines, sines):
    return value * cosines - swapped(value) * sines


def row_mean(value):
    return jnp.sum(value, axis=-1, keepdims=True) * (1.0 / MODEL_WIDTH)


def normed_rows(value):
    scale = lax.rsqrt(row_mean(value * value) + EPS_NORM)
    return value * scale, scale


def place_rows(ref, head_tile, tail_tile, first):
    for j in range(3):
        ref[first : first + 192, LANES * j : LANES * j + LANES] = head_tile[192 * j : 192 * j + 192, :]
    ref[first : first + 192, 384:512] = tail_tile[0:192, :]
    rest = tail_tile[192:288, :].astype(F32)
    low = lower_lanes(rest.shape)
    ref[first : first + 96, 512:640] = jnp.where(low, rest, 0.0).astype(BF16)
    ref[first + 96 : first + 192, 512:640] = jnp.where(low, half_turn(rest), 0.0).astype(BF16)


def tiles_of_rows(value):
    head = jnp.concatenate([value[:, LANES * j : LANES * j + LANES] for j in range(3)], axis=0)
    rest = side_by_side(value[0:96, 512:640], value[96:192, 512:640])
    return head, jnp.concatenate([value[:, 384:512], rest], axis=0)


def layer_kernel(*refs):
    slots = refs[0]
    head_parts = refs[1:9]
    tail_parts = refs[9:13]
    tokens_pair, cos_pair, sin_pair = refs[13:15], refs[15:17], refs[17:19]
    (place_q_ref, place_k_ref, gains_ref, bias_q_ref, bias_kv_ref, grad_ref) = refs[19:25]
    block_out_ref, parts_out = refs[25], refs[26:36]
    (dkv_send, dkv_keep, dq_wq_ref, d_mid_ref, w_kv) = refs[36:41]
    (raw_head, raw_tail, w_q, w_out, w_gate, w_up, w_down, normed_all, hidden_all, keys, values, queries, probs_low, probs_high, attended, act_all, block_acc, d_hidden, d_attended, dkv_all, d_query, send_all, keep_all, vector_ref, outs, sems, out_sems) = refs[41:]

    place = slots[MY_Z]

    def fetches(shift, sem):
        at = jnp.bitwise_xor(place, shift)
        copies = []
        for k, part in enumerate(head_parts):
            copies.append(pltpu.make_async_copy(part.at[at], raw_head.at[4 * k + at], sems.at[sem + k]))
        for k, part in enumerate(tail_parts):
            rows = pl.ds(2 * at, 2)
            copies.append(pltpu.make_async_copy(part.at[rows], raw_tail.at[pl.ds(8 * k + 2 * at, 2)], sems.at[sem + 8 + k]))
        return copies

    attention_blocks = fetches(0, 0)
    other_blocks = fetches(1, 12) + fetches(2, 24) + fetches(3, 36)
    for copy in attention_blocks + other_blocks:
        copy.start()

    core = slots[MY_CORE]

    def key_rows_of(mb, slot, half):
        return pl.ds(pl.multiple_of(mb * 512 + half * 256 + slot * HALF, HALF), HALF)

    def in_key_order(pair, mb):
        return jnp.concatenate(
            [at_slot(pair, slot)[mb, HALF * half : HALF * half + HALF, :] for half in range(2) for slot in range(4)],
            axis=0,
        )

    def at_slot(pair, slot):
        return pair[slot % 2].at[slot // 2]

    def head_tile(block):
        return raw_head.at[slots[AT_HEAD + block]]

    def tail_tile(block):
        return raw_tail.at[slots[AT_TAIL + block]]

    gain_one = gains_ref[0:1, :]
    gain_two = gains_ref[1:2, :]
    low_rows = lower_lanes((HALF, LANES))

    @pl.loop(0, 2)
    def _(mb):
        lane = lax.broadcasted_iota(jnp.int32, (ROWS, WIDE), 1)
        for slot in range(4):
            x = jnp.where(lane < MODEL_WIDTH, at_slot(tokens_pair, slot)[mb].astype(F32), 0.0)
            normed, _ = normed_rows(x)
            hidden = (normed * gain_one).astype(BF16)
            for half in range(2):
                rows = key_rows_of(mb, slot, half)
                normed_all[rows, :] = normed[HALF * half : HALF * half + HALF]
                hidden_all[rows, :] = hidden[HALF * half : HALF * half + HALF]

    for copy in attention_blocks:
        copy.wait()
    for ref in (w_q, w_out, w_gate, w_up, w_kv):
        ref[576:640, :] = jnp.zeros((64, ref.shape[1]), BF16)
    for k in range(3):
        place_rows(w_q, head_tile(k), tail_tile(k), 192 * k)
        place_rows(w_out, head_tile(5 + k), tail_tile(5 + k), 192 * k)
    w_kv[0:576, 0:128] = head_tile(3)[...]
    w_kv[0:576, 128:256] = head_tile(4)[...]
    rest_key = tail_tile(3)[...].astype(F32)
    rest_value = tail_tile(4)[...].astype(F32)
    low = lower_lanes(rest_key.shape)
    w_kv[0:288, 256:384] = jnp.where(low, rest_key, half_turn(rest_value)).astype(BF16)
    w_kv[288:576, 256:384] = jnp.where(low, half_turn(rest_key), rest_value).astype(BF16)

    @pl.loop(0, 2)
    def _(mb):
        rows = pl.ds(pl.multiple_of(mb * 512, 512), 512)
        pair = product(hidden_all[rows, :], w_kv[...]) + bias_kv_ref[...]
        cosines, sines = in_key_order(cos_pair, mb), in_key_order(sin_pair, mb)
        key_a = rope(pair[:, 0:128], cosines, sines)
        key_b = rope(pair[:, 256:384], cosines, sines)
        value_a, value_b = pair[:, 128:256], pair[:, 256:384]
        low_keys = lower_lanes((512, LANES))
        turned = half_turn(key_a)
        keys[rows, 0:128] = jnp.where(low_keys, key_a, turned).astype(BF16)
        keys[rows, 128:256] = jnp.where(low_keys, turned, key_a).astype(BF16)
        keys[rows, 256:384] = jnp.where(low_keys, key_b, half_turn(key_b)).astype(BF16)
        turned = half_turn(value_a)
        values[rows, 0:128] = jnp.where(low_keys, value_a, turned).astype(BF16)
        values[rows, 128:256] = jnp.where(low_keys, turned, value_a).astype(BF16)
        values[rows, 256:384] = jnp.where(low_keys, half_turn(value_b), value_b).astype(BF16)

    def heads_of(ref, rows, group):
        stacked = []
        for k in range(3):
            number = 3 * group + k
            tile = ref[rows, LANES * (number // 2) : LANES * (number // 2) + LANES]
            keep = low_rows if number % 2 == 0 else jnp.logical_not(low_rows)
            stacked.append(jnp.where(keep, tile.astype(F32), 0.0).astype(BF16))
        return jnp.concatenate(stacked, axis=0)

    def tiles_of_heads(parts):
        found = [jnp.where(low_rows, parts[2 * k], parts[2 * k + 1]) for k in range(4)]
        return found + [jnp.where(low_rows, parts[8], 0.0)]

    @pl.loop(0, 2)
    def _(mb):
        rows = pl.ds(pl.multiple_of(mb * ROWS, ROWS), ROWS)
        key_rows = pl.ds(pl.multiple_of(mb * 512, 512), 512)
        cosines, sines = cos_pair[0][0, mb], sin_pair[0][0, mb]
        hidden = jnp.concatenate([hidden_all[key_rows_of(mb, 0, half), :] for half in range(2)], axis=0)
        made = product(hidden, w_q[...]) + bias_q_ref[...]
        for k in range(5):
            turned = rope(made[:, LANES * k : LANES * k + LANES], cosines, sines)
            queries[rows, LANES * k : LANES * k + LANES] = (turned * HEAD_SIZE ** (-0.5)).astype(BF16)
        place_q, place_k = place_q_ref[mb], place_k_ref[mb]
        for half, probs in enumerate((probs_low, probs_high)):
            count = 256 * (half + 1)
            own = pl.ds(pl.multiple_of(mb * ROWS + HALF * half, HALF), HALF)
            masked = jnp.where(place_q[HALF * half : HALF * half + HALF] >= place_k[:, 0:count], 0.0, MASKED)
            masked = jnp.concatenate([masked] * 3, axis=0)
            seen = pl.ds(pl.multiple_of(mb * 512, 512), count)
            parts = []
            for group in range(KEY_VALUE_HEADS):
                lanes = slice(LANES * group, LANES * group + LANES)
                scores = times_transposed(heads_of(queries, own, group), keys[seen, lanes]) + masked
                top = jnp.max(scores, axis=-1, keepdims=True)
                powers = jnp.exp(scores - top)
                found = powers * (1.0 / jnp.sum(powers, axis=-1, keepdims=True))
                probs[mb, group] = found
                out = product(found.astype(BF16), values[seen, lanes])
                outs[mb, 2 * group + half] = out
                parts += [out[HALF * k : HALF * k + HALF] for k in range(3)]
            for k, tile in enumerate(tiles_of_heads(parts)):
                attended[own, LANES * k : LANES * k + LANES] = tile.astype(BF16)

    for copy in other_blocks:
        copy.wait()
    for k in range(8):
        place_rows(w_down, head_tile(24 + k), tail_tile(24 + k), 192 * k)
    for ref, base in ((w_gate, 8), (w_up, 16)):
        for k in range(4):
            for i in range(6):
                if i < 4:
                    even = head_tile(base + 2 * k)[144 * i : 144 * i + 144, :].astype(F32)
                    odd = head_tile(base + 2 * k + 1)[144 * i : 144 * i + 144, :].astype(F32)
                else:
                    even = tail_tile(base + 2 * k)[144 * (i - 4) : 144 * (i - 4) + 144, :].astype(F32)
                    odd = tail_tile(base + 2 * k + 1)[144 * (i - 4) : 144 * (i - 4) + 144, :].astype(F32)
                ref[144 * k : 144 * k + 144, 256 * i : 256 * i + 128] = jnp.concatenate(
                    [even[0:72], odd[0:72]], axis=0
                ).astype(BF16)
                ref[144 * k : 144 * k + 144, 256 * i + 128 : 256 * i + 256] = jnp.concatenate(
                    [even[72:144], odd[72:144]], axis=0
                ).astype(BF16)

    lane = lax.broadcasted_iota(jnp.int32, (2 * ROWS, WIDE), 1)
    x_own = tokens_pair[0][0].astype(F32).reshape(2 * ROWS, WIDE)
    x_own = jnp.where(lane < MODEL_WIDTH, x_own, 0.0)
    resid_mid = x_own + product(attended[...], w_out[...])
    normed_two, scale_two = normed_rows(resid_mid)
    hidden_two = (normed_two * gain_two).astype(BF16)
    hidden_turned = hidden_two.T
    grad_low = grad_ref[...]
    block_acc[...] = resid_mid
    d_hidden[...] = jnp.zeros_like(d_hidden)

    def store_pair(at, even, odd, table, first):
        rows = pl.ds(pl.multiple_of(slots[table + at] + first, 16), even.shape[0])
        send_all[rows, :] = jnp.where(core == 0, odd, even).astype(BF16)
        keep_all[rows, :] = jnp.where(core == 0, even, odd).astype(BF16)

    def feed_forward(chunk, first, table):
        cols = pl.ds(pl.multiple_of(chunk * 512, 512), 512)
        gate = product(hidden_two, w_gate[:, cols])
        up = product(hidden_two, w_up[:, cols])
        sigma = 1.0 / (1.0 + jnp.exp(-gate))
        act = (gate * sigma * up).astype(BF16)
        act_all[:, cols] = act
        down = w_down[cols, :]
        d_act = times_transposed(grad_low, down)
        block_acc[...] += product(act, down)
        d_up = (d_act * gate * sigma).astype(BF16)
        d_gate = (d_act * up * sigma * (1.0 + gate * (1.0 - sigma))).astype(BF16)
        d_hidden[...] += times_transposed(d_gate, w_gate[:, cols]) + times_transposed(d_up, w_up[:, cols])
        for base, cotangent in ((4, d_gate), (8, d_up)):
            made = product(hidden_turned, cotangent)
            for k in range(4):
                part = made[144 * k : 144 * k + 144, :]
                even = jnp.concatenate([part[0:72, LANES * j : LANES * j + LANES] for j in range(4)], axis=0)
                odd = jnp.concatenate([part[72:144, LANES * j : LANES * j + LANES] for j in range(4)], axis=0)
                store_pair(base + k, even, odd, table, (chunk - first) * 288)

    @pl.loop(0, 2)
    def _(chunk):
        feed_forward(chunk, 0, TO_HEAD)

    feed_forward(2, 2, TO_TAIL)

    def store_rows(at, even, odd):
        even_head, even_tail = even
        odd_head, odd_tail = odd
        store_pair(at, even_head, odd_head, TO_HEAD, 0)
        store_pair(at, even_tail, odd_tail, TO_TAIL, 0)

    @pl.loop(0, 4)
    def _(k):
        made = rows_product(act_all[:, pl.ds(pl.multiple_of(k * 384, 128), 384)], grad_low)
        store_rows(12 + k, tiles_of_rows(made[0:192]), tiles_of_rows(made[192:384]))

    def deliveries(first, count, sem):
        copies = []
        for base, outs_of in ((send_all, parts_out[0:4]), (keep_all, parts_out[4:10])):
            rest = [(outs_of[2], PART * k) for k in range(3)] if len(outs_of) == 4 else [(out, 0) for out in outs_of[2:5]]
            targets = [(outs_of[0], 0, FIRST_AT), (outs_of[1], 0, TAIL_AT)]
            targets += [(out, into, PART * k) for k, (out, into) in enumerate(rest)]
            targets.append((outs_of[-1], 0, 3 * PART))
            for out, into, start in targets:
                rows = HEAD_ROWS * count
                copies.append(
                    pltpu.make_async_copy(
                        base.at[pl.ds(start + HEAD_ROWS * first, rows)],
                        out.at[pl.ds(into + HEAD_ROWS * first, rows)],
                        out_sems.at[sem + len(copies)],
                    )
                )
        return copies

    early = deliveries(1, 3, 12)
    for copy in early:
        copy.start()

    for mb in range(2):
        block_out_ref[mb] = block_acc[ROWS * mb : ROWS * mb + ROWS, :].T[0:MODEL_WIDTH].astype(BF16)

    d_two = d_hidden[...]
    gain_two_sum = jnp.sum(d_two * normed_two, axis=0, keepdims=True)
    d_norm = d_two * gain_two
    d_mid = grad_low.astype(F32) + scale_two * (d_norm - normed_two * row_mean(d_norm * normed_two))
    d_mid_ref[...] = d_mid
    d_branch = d_mid.astype(BF16)
    d_attended[...] = times_transposed(d_branch, w_out[...]).astype(BF16)
    grad_out = rows_product(attended[...], d_branch)

    @pl.loop(0, 2)
    def _(mb):
        rows = pl.ds(pl.multiple_of(mb * ROWS, ROWS), ROWS)
        key_rows = pl.ds(pl.multiple_of(mb * 512, 512), 512)
        d_keys = []
        d_values = []
        parts = ([], [])
        for group in range(KEY_VALUE_HEADS):
            lanes = slice(LANES * group, LANES * group + LANES)
            d_key, d_value = [], []
            for half, probs in enumerate((probs_low, probs_high)):
                own = pl.ds(pl.multiple_of(mb * ROWS + HALF * half, HALF), HALF)
                seen = pl.ds(pl.multiple_of(mb * 512, 512), 256 * (half + 1))
                query_rows = heads_of(queries, own, group)
                cotangent = heads_of(d_attended, own, group)
                found = probs[mb, group]
                d_probs = times_transposed(cotangent, values[seen, lanes])
                delta = jnp.sum(outs[mb, 2 * group + half] * cotangent.astype(F32), axis=-1, keepdims=True)
                d_scores = (found * (d_probs - delta)).astype(BF16)
                out = product(d_scores, keys[seen, lanes]) * HEAD_SIZE ** (-0.5)
                parts[half].extend(out[HALF * k : HALF * k + HALF] for k in range(3))
                d_key.append(rows_product(d_scores, query_rows))
                d_value.append(rows_product(found.astype(BF16), cotangent))
            d_key = jnp.concatenate([d_key[0] + d_key[1][0:256], d_key[1][256:512]], axis=0)
            d_value = jnp.concatenate([d_value[0] + d_value[1][0:256], d_value[1][256:512]], axis=0)
            d_keys.append(d_key + half_turn(d_key))
            d_values.append(d_value + half_turn(d_value))
        for half in range(2):
            own = pl.ds(pl.multiple_of(mb * ROWS + HALF * half, HALF), HALF)
            cosines = cos_pair[0][0, mb, HALF * half : HALF * half + HALF, :]
            sines = sin_pair[0][0, mb, HALF * half : HALF * half + HALF, :]
            for k, tile in enumerate(tiles_of_heads(parts[half])):
                d_query[own, LANES * k : LANES * k + LANES] = rope_back(tile, cosines, sines).astype(BF16)
        low_keys = lower_lanes((512, LANES))
        cosines, sines = in_key_order(cos_pair, mb), in_key_order(sin_pair, mb)
        key_a = rope_back(jnp.where(low_keys, d_keys[0], d_keys[1]), cosines, sines)
        key_b = rope_back(d_keys[2], cosines, sines)
        dkv_all[key_rows, 0:128] = key_a.astype(BF16)
        dkv_all[key_rows, 128:256] = jnp.where(low_keys, d_values[0], d_values[1]).astype(BF16)
        dkv_all[key_rows, 256:384] = jnp.where(low_keys, key_b, d_values[2]).astype(BF16)
        for slot in range(4):
            target = dkv_send if slot % 2 else dkv_keep
            for half in range(2):
                target[slot // 2, mb, HALF * half : HALF * half + HALF, :] = dkv_all[key_rows_of(mb, slot, half), :]

    dkv = dkv_all[...]
    d_q = d_query[...]
    dq_wq = times_transposed(d_q, w_q[...])
    dq_wq_ref[...] = dq_wq
    bias_q_sum = jnp.sum(d_q.astype(F32), axis=0, keepdims=True)
    bias_kv_sum = jnp.sum(dkv.astype(F32), axis=0, keepdims=True)
    gain_sum = jnp.zeros((1, WIDE), F32)
    for at in range(4):
        gain_sum += jnp.sum(
            dq_wq[HALF * at : HALF * at + HALF] * normed_all[256 * at : 256 * at + HALF, :], axis=0, keepdims=True
        )
    for k in range(4):
        part = slice(256 * k, 256 * k + 256)
        gain_sum += jnp.sum(times_transposed(dkv_all[part, :], w_kv[...]) * normed_all[part, :], axis=0, keepdims=True)

    hidden_own = jnp.concatenate([hidden_all[256 * at : 256 * at + HALF, :] for at in range(4)], axis=0)
    grad_q = rows_product(hidden_own, d_q)
    grad_kv = rows_product(hidden_all[...], dkv)
    rest = grad_kv[0:576, 256:384]
    low = lower_lanes((288, LANES))
    key_tiles = (grad_kv[0:576, 0:128], jnp.where(low, rest[0:288], half_turn(rest[288:576])))
    value_tiles = (grad_kv[0:576, 128:256], jnp.where(low, half_turn(rest[0:288]), rest[288:576]))
    query_tiles = [tiles_of_rows(grad_q[192 * k : 192 * k + 192]) for k in range(3)]
    out_tiles = [tiles_of_rows(grad_out[192 * k : 192 * k + 192]) for k in range(3)]
    store_rows(0, query_tiles[0], query_tiles[1])
    store_rows(1, query_tiles[2], key_tiles)
    store_rows(2, value_tiles, out_tiles[0])
    store_rows(3, out_tiles[1], out_tiles[2])
    def flat_rows(first, second, third, pair):
        tile = lambda row, k: row[:, LANES * k : LANES * k + LANES]
        low = lower_lanes((1, LANES))
        across_two = lambda one, two: jnp.where(low, half_turn(one), half_turn(two))
        lines = [tile(first, k) for k in range(4)]
        lines.append(side_by_side(tile(first, 4), tile(second, 0)))
        lines += [across_two(tile(second, k), tile(second, k + 1)) for k in range(4)]
        lines += [tile(third, k) for k in range(4)]
        lines.append(side_by_side(tile(third, 4), tile(pair, 0)))
        lines.append(across_two(tile(pair, 0), tile(pair, 2)))
        lines.append(tile(pair, 1))
        lines.append(jnp.where(low, half_turn(tile(pair, 2)), 0.0))
        return lines

    at = FIRST_AT + PART
    for row, line in enumerate(flat_rows(gain_sum, gain_two_sum, bias_q_sum, bias_kv_sum)):
        vector_ref[row : row + 1, :] = line
    vector_ref[17:24, :] = jnp.zeros((7, LANES), F32)
    vector = vector_ref[...]
    high = vector.astype(BF16).astype(F32)
    both = jnp.concatenate([high, vector - high], axis=0).astype(BF16)
    for ref in (send_all, keep_all):
        ref[at : at + 2 * VECTOR_ROWS, :] = both
    last = deliveries(0, 1, 0)
    last.append(pltpu.make_async_copy(send_all.at[pl.ds(at, 2 * VECTOR_ROWS)], parts_out[0].at[pl.ds(PART, 2 * VECTOR_ROWS)], out_sems.at[24]))
    last.append(pltpu.make_async_copy(keep_all.at[pl.ds(at, 2 * VECTOR_ROWS)], parts_out[4].at[pl.ds(PART, 2 * VECTOR_ROWS)], out_sems.at[25]))
    for copy in last:
        copy.start()
    for copy in early + last:
        copy.wait()


def run_layer(slots, heads, tails, *others):
    shape = jax.ShapeDtypeStruct
    vmem = pl.BlockSpec(memory_space=pltpu.VMEM)
    anywhere = pl.BlockSpec(memory_space=pl.ANY)
    scratch = [
        ((BLOCKS, HEAD_ROWS, LANES), BF16),
        ((BLOCKS, TAIL_ROWS, LANES), BF16),
        ((WIDE, WIDE), BF16),
        ((WIDE, WIDE), BF16),
        ((WIDE, FF), BF16),
        ((WIDE, FF), BF16),
        ((FF, WIDE), BF16),
        ((1024, WIDE), F32),
        ((1024, WIDE), BF16),
        ((1024, 384), BF16),
        ((1024, 384), BF16),
        ((256, WIDE), BF16),
        ((2, 3, 192, 256), F32),
        ((2, 3, 192, 512), F32),
        ((256, WIDE), BF16),
        ((256, FF), BF16),
        ((256, WIDE), F32),
        ((256, WIDE), F32),
        ((256, WIDE), BF16),
        ((1024, 384), BF16),
        ((256, WIDE), BF16),
        ((ALL_ROWS, LANES), BF16),
        ((ALL_ROWS, LANES), BF16),
        ((VECTOR_ROWS, LANES), F32),
        ((2, 6, 192, LANES), F32),
    ]
    return pl.pallas_call(
        layer_kernel,
        out_shape=(
            shape((2, MODEL_WIDTH, ROWS), BF16),
            *[shape((count, LANES), BF16) for _, count in SEND_PARTS + KEEP_PARTS],
            shape((2, 2, ROWS, 384), BF16),
            shape((2, 2, ROWS, 384), BF16),
            shape((256, WIDE), F32),
            shape((256, WIDE), F32),
            shape((WIDE, 384), BF16),
        ),
        in_specs=[pl.BlockSpec(memory_space=pltpu.SMEM)] + [anywhere] * 12 + [vmem] * 12,
        out_specs=(vmem,) + (anywhere,) * 10 + (vmem,) * 5,
        scratch_shapes=[pltpu.VMEM(dims, kind) for dims, kind in scratch]
        + [pltpu.SemaphoreType.DMA((48,)), pltpu.SemaphoreType.DMA((26,))],
        compiler_params=pltpu.CompilerParams(vmem_limit_bytes=50 * 1024 * 1024),
        name="layer",
    )(slots, *heads, *tails, *others)


def adamw(param, grad, mom_one, mom_two, rate, decay):
    new_one = BETA_ONE * mom_one + (1.0 - BETA_ONE) * grad
    new_two = BETA_TWO * mom_two + (1.0 - BETA_TWO) * grad * grad
    fixed_one = new_one / (1.0 - BETA_ONE**STEP)
    fixed_two = new_two / (1.0 - BETA_TWO**STEP)
    new_param = param - rate * (fixed_one / (jnp.sqrt(fixed_two) + EPS_ADAM) + decay * param)
    return (new_param, new_one, new_two)


def inner_groups():
    inner = inner_count()
    data_inner = inner // lax.axis_size("ctx")
    data_count = lax.axis_size("dp")
    return [list(range(k, k + data_inner)) for k in range(0, data_count, data_inner)]


def whole_block(flat):
    if inner_count() == 1:
        return flat
    flat = lax.all_gather(flat, "ctx", axis=0, tiled=True)
    return lax.all_gather(flat, "dp", axis=0, tiled=True, axis_index_groups=inner_groups())


def own_slice(block):
    if inner_count() == 1:
        return block
    block = lax.psum_scatter(
        block, "dp", scatter_dimension=0, tiled=True, axis_index_groups=inner_groups()
    )
    return lax.psum_scatter(block, "ctx", scatter_dimension=0, tiled=True)


def bias_tiles(bias_key, bias_value):
    return jnp.concatenate([bias_key[:128], bias_value[:128], bias_key[128:], bias_value[128:]])


def local(tokens_in, places, out_grad, weights, first_moment, second_moment, vectors, vector_first, vector_second):
    kind = kind_of(device_number() // inner_count()).astype(jnp.int32).reshape(1)
    block = whole_block(weights).reshape(BLOCK_ROWS, LANES)
    head, tail = to_tiles(kind, block)

    head, tail, tokens_in, places = together(head, tail, tokens_in, places)
    own_tokens = tokens_in.reshape(2, ROWS, MODEL_WIDTH)
    own_places = places.reshape(2, ROWS)
    marks = jnp.stack([own_places // 16, own_places % 16], axis=-1).astype(BF16)
    packed = jnp.concatenate(
        [own_tokens, marks, jnp.zeros((2, ROWS, WIDE - MODEL_WIDTH - 2), BF16)], axis=-1
    )
    padding = ((0, 0), (0, WIDE - MODEL_WIDTH))
    gains = jnp.pad(vectors[: 2 * MODEL_WIDTH].reshape(2, MODEL_WIDTH), padding)
    bias_q = jnp.pad(vectors[2 * MODEL_WIDTH : 3 * MODEL_WIDTH].reshape(1, MODEL_WIDTH), padding)
    bias_kv = bias_tiles(vectors[1728:1920], vectors[1920:2112]).reshape(1, 384)
    grad = jnp.pad(out_grad.reshape(2 * ROWS, MODEL_WIDTH), padding)
    spare = VECTOR_ROWS * LANES - vectors.shape[0]
    vector_state = [
        jnp.pad(array, (0, spare), constant_values=1.0).reshape(VECTOR_ROWS, LANES)
        for array in (vectors, vector_first, vector_second)
    ]
    table = jnp.concatenate([kind, (coordinates(device_number() // inner_count())["z"]).astype(jnp.int32).reshape(1)])
    others = (slot_table(), gains, bias_q, bias_kv, grad, vector_state, table)
    heads, tails, (near, far), (cosines, sines), others = gather_all(head, tail, packed, others)
    slots, gains, bias_q, bias_kv, grad, vector_state, table = others
    cosines_far, sines_far = place_tables(far)
    place_all = jnp.stack([places_of(near), places_of(far)], axis=1)
    place_q = place_all[0, 0][..., None]
    place_k = jnp.transpose(place_all.reshape(4, 2, 2, HALF), (1, 2, 0, 3)).reshape(2, 1, 4 * ROWS)

    block_out, *found = run_layer(
        slots, heads, tails, near, far, cosines, cosines_far, sines, sines_far, place_q, place_k, gains, bias_q, bias_kv, grad
    )
    sends, keeps = found[:4], found[4:10]
    dkv_send, dkv_keep, dq_wq, d_mid, w_kv = found[10:]
    parts, pairs = scatter_blocks(sends, keeps, dkv_send, dkv_keep)
    inputs = (near, gains, w_kv, dq_wq, d_mid, *pairs)
    state = (weights, first_moment, second_moment)
    if inner_count() == 1:
        blocks = [array.reshape(BLOCK_ROWS, LANES) for array in state]
        *updated, input_grad = finish(table, parts, inputs, [*vector_state, *blocks])
        new_vector_state = [array.reshape(-1)[: vectors.shape[0]] for array in updated[:3]]
        new_state = [array.reshape(-1) for array in updated[3:]]
    else:
        block_grad, vector, input_grad = finish(table, parts, inputs, [])
        vector = lax.psum(vector, "ctx")
        vector = lax.psum(vector, "dp", axis_index_groups=inner_groups())
        grad_own = own_slice(block_grad.reshape(-1))
        vector_grad = vector.reshape(-1)[: vectors.shape[0]]
        new_state = adamw(weights, grad_own, first_moment, second_moment, RATE_MATRIX, DECAY)
        new_vector_state = adamw(vectors, vector_grad, vector_first, vector_second, RATE_VECTOR, 0.0)
    shape = tokens_in.shape
    return (
        jnp.transpose(block_out, (0, 2, 1)).reshape(shape),
        jnp.transpose(input_grad, (0, 2, 1)).reshape(shape),
        *new_state,
        *new_vector_state,
    )


def solution(mesh):
    in_specs = (
        P(None, "dp", "ctx", None),
        P(None, "dp", "ctx"),
        P(None, "dp", "ctx", None),
        P(("dp", "ctx")),
        P(("dp", "ctx")),
        P(("dp", "ctx")),
        P(),
        P(),
        P(),
    )
    out_specs = (
        P(None, "dp", "ctx", None),
        P(None, "dp", "ctx", None),
        P(("dp", "ctx")),
        P(("dp", "ctx")),
        P(("dp", "ctx")),
        P(),
        P(),
        P(),
    )
    return jax.shard_map(local, mesh=mesh, in_specs=in_specs, out_specs=out_specs, check_vma=False)
```

```python
import jax
import jax.numpy as jnp
from jax import lax
from jax.experimental import pallas as pl
from jax.experimental.pallas import tpu as pltpu
from jax.sharding import PartitionSpec as P

MODEL_WIDTH = 576
QUERY_HEADS = 9
KEY_VALUE_HEADS = 3
HEAD_SIZE = 64
FF = 1536
STEP = 10

EPS_NORM = 1e-05
THETA = 100000.0
BETA_ONE = 0.9
BETA_TWO = 0.95
EPS_ADAM = 1e-08
RATE_MATRIX = 0.06
RATE_VECTOR = 0.3
DECAY = 0.1
MASKED = -1e30

LANES = 128
WIDE = 640
BLOCKS = 32
BLOCK_ROWS = 864
HEAD_ROWS = 576
TAIL_ROWS = BLOCK_ROWS - HEAD_ROWS
VECTOR_ROWS = 24
STEP_ROWS = 432
PART = 4 * HEAD_ROWS
FIRST_AT = 4 * PART
TAIL_AT = FIRST_AT + PART + 2 * VECTOR_ROWS
ALL_ROWS = TAIL_AT + PART
SEND_PARTS = [(FIRST_AT, PART + 2 * VECTOR_ROWS), (TAIL_AT, PART), (0, 3 * PART), (3 * PART, PART)]
KEEP_PARTS = SEND_PARTS[:2] + [(PART * k, PART) for k in range(4)]
SIZES = {"z": 4, "y": 2, "x": 2, "c": 2}
ROWS = 128
F32 = jnp.float32
BF16 = jnp.bfloat16


def coordinates(number):
    found = {}
    for name in ("c", "x", "y", "z"):
        found[name] = number % SIZES[name]
        number = number // SIZES[name]
    return found


def number_of(found):
    number = 0
    for name in ("z", "y", "x", "c"):
        number = number * SIZES[name] + found[name]
    return number


def device_number():
    return lax.axis_index("dp") * lax.axis_size("ctx") + lax.axis_index("ctx")


def inner_count():
    return lax.axis_size("dp") * lax.axis_size("ctx") // BLOCKS


def moved(buffer, name, shift):
    inner = inner_count()
    pairs = []
    for number in range(BLOCKS):
        found = coordinates(number)
        found[name] = (found[name] + shift) % SIZES[name]
        target = number_of(found)
        pairs += [(number * inner + k, target * inner + k) for k in range(inner)]
    return lax.ppermute(buffer, ("dp", "ctx"), pairs)


def across(buffer, distance):
    count = lax.axis_size("ctx")
    return lax.ppermute(buffer, "ctx", [(i, i ^ distance) for i in range(count)])


def together(*arrays):
    return lax.optimization_barrier(arrays)


def gather_at_once(rows):
    if inner_count() == 1:
        return lax.all_gather(rows, ("dp", "ctx"))
    data_count, data_inner = lax.axis_size("dp"), inner_count() // lax.axis_size("ctx")
    groups = [list(range(k, data_count, data_inner)) for k in range(data_inner)]
    return lax.all_gather(rows, "dp", axis_index_groups=groups)


def gather_all(head, tail, packed, others):
    tails = gather_at_once(tail)
    hz = [moved(head, "z", s) for s in (1, 2, 3)]
    two = across(packed, 2)
    head, two, *hz = together(head, two, *hz)
    own = jnp.stack([head] + hz)
    ay = moved(own, "y", 1)
    ax = moved(own, "x", 1)
    ac = moved(own, "c", 1)
    near = jnp.stack([packed, two])
    tables = place_tables(near)
    own, ay, ax, near, tables, others = together(own, ay, ax, near, tables, others)
    far = across(near, 1)
    axy = moved(ay, "x", 1)
    acy = moved(ay, "c", 1)
    acx = moved(ax, "c", 1)
    axy, acy, acx, far = together(axy, acy, acx, far)
    acxy = moved(axy, "c", 1)
    heads = [own, ay, ax, axy, ac, acy, acx, acxy]
    return heads, tails, (near, far), tables, others


def places_of(tokens):
    found = tokens[..., MODEL_WIDTH : MODEL_WIDTH + 2].astype(F32)
    return found[..., 0] * 16.0 + found[..., 1]


def place_tables(tokens):
    half_dim = HEAD_SIZE // 2
    frequency = THETA ** (-2.0 * jnp.arange(half_dim, dtype=F32) / HEAD_SIZE)
    angles = places_of(tokens)[..., None] * jnp.tile(frequency, 4)
    sign = jnp.where(jnp.arange(LANES) % HEAD_SIZE < half_dim, -1.0, 1.0).astype(F32)
    return jnp.cos(angles), jnp.sin(angles) * sign


def fold(order, relative):
    slot = 0
    for name in order:
        slot = slot * SIZES[name] + relative[name]
    return slot


def head_row(slot, z, _):
    return slot * PART + jnp.where(slot < 3, 0, FIRST_AT - 3 * PART) + z * HEAD_ROWS


def tail_row(slot, z, inside):
    return jnp.where(slot < 1, 3 * PART, TAIL_AT) + (2 * z + inside) * TAIL_ROWS


def slot_table():
    mine = coordinates(device_number() // inner_count())
    entries = []
    for number in range(BLOCKS):
        found = coordinates(number)
        entries.append(fold(("c", "x", "y", "z"), {n: (mine[n] - found[n]) % SIZES[n] for n in SIZES}))
    for order, start in ((("x", "y"), head_row), (("y",), tail_row)):
        for number in range(0, BLOCKS, 2):
            found = coordinates(number)
            slot = fold(order, {n: (found[n] - mine[n]) % SIZES[n] for n in SIZES})
            inside = (found["x"] - mine["x"]) % SIZES["x"]
            entries.append(start(slot, found["z"], inside))
    entries.append(mine["c"])
    entries.append(mine["z"])
    return jnp.stack([jnp.asarray(entry, jnp.int32) for entry in entries])


AT_HEAD, TO_HEAD, TO_TAIL, MY_CORE, MY_Z = 0, BLOCKS, BLOCKS + 16, BLOCKS + 32, BLOCKS + 33


def summed(*parts):
    total = parts[0].astype(F32)
    for part in parts[1:]:
        total = total + part.astype(F32)
    return total


def summed_vector(mine, other):
    total = summed(mine[:VECTOR_ROWS], other[:VECTOR_ROWS]) + summed(mine[VECTOR_ROWS:], other[VECTOR_ROWS:])
    high = lax.reduce_precision(total, 8, 7)
    return jnp.concatenate([high.astype(BF16), (total - high).astype(BF16)])


def scatter_blocks(sends, keeps, dkv_send, dkv_keep):
    keep_head, keep_tail, keep_low, keep_mid, keep_far, keep_rest = keeps
    got_head, got_tail = moved(sends[0], "c", 1), moved(sends[1], "c", 1)
    got_head, got_tail, rest_head, rest_tail, dkv_send = together(got_head, got_tail, *sends[2:], dkv_send)
    got_rest_head, got_rest_tail = moved(rest_head, "c", 1), moved(rest_tail, "c", 1)
    got_dkv = across(dkv_send, 1)
    vector = summed_vector(keep_head[PART:], got_head[PART:])
    hx = jnp.concatenate([summed(keep_head[:PART], got_head[:PART]).astype(BF16), vector])
    ty = summed(keep_tail, got_tail).astype(BF16)
    got_hx = moved(hx, "x", 1)
    got_ty = moved(ty, "y", 1)
    low, mid, far = [
        summed(keep, got_rest_head[PART * k : PART * k + PART]).astype(BF16)
        for k, keep in enumerate((keep_low, keep_mid, keep_far))
    ]
    tail = summed(keep_rest, got_rest_tail).astype(BF16)
    dkv = summed(dkv_keep, got_dkv).astype(BF16)
    got_hx, got_ty, low, mid, far, tail, dkv, vector = together(got_hx, got_ty, low, mid, far, tail, dkv, vector)
    place = coordinates(device_number() // inner_count())["z"]

    def part_for(array, shift):
        return lax.dynamic_slice_in_dim(array, HEAD_ROWS * ((place + shift) % SIZES["z"]), HEAD_ROWS, 0)

    vector = summed_vector(vector, got_hx[PART:])
    hy = jnp.concatenate([summed(mid, got_hx[:PART]).astype(BF16), vector])
    tz = [summed(part_for(tail, s), part_for(got_ty, s)).astype(BF16) for s in range(4)]
    got_hy = moved(hy, "y", 1)
    got_far = moved(far, "x", 1)
    got_tz = [moved(tz[s], "z", s) for s in (1, 2, 3)]
    got_hy, got_far, low, own_tail, vector, dkv, *got_tz = together(got_hy, got_far, low, tz[0], vector, dkv, *got_tz)
    vector = summed_vector(vector, got_hy[PART:])
    head = [summed(part_for(low, s), part_for(got_far, s), part_for(got_hy, s)) for s in range(4)]
    got_hz = [moved(jnp.concatenate([head[s].astype(BF16), vector]), "z", s) for s in (1, 2, 3)]
    tx = summed(own_tail[TAIL_ROWS:], *[part[TAIL_ROWS:] for part in got_tz]).astype(BF16)
    own_tail = summed(own_tail[:TAIL_ROWS], *[part[:TAIL_ROWS] for part in got_tz])
    got_tx = moved(tx, "x", 1)
    got_dkv = across(dkv[1], 2)
    return (head[0], *got_hz, own_tail, got_tx, vector), (dkv[0], got_dkv)


def lower_lanes(shape):
    return lax.broadcasted_iota(jnp.int32, shape, 1) < HEAD_SIZE


def half_turn(value):
    return pltpu.roll(value, HEAD_SIZE, 1)


def side_by_side(left, right):
    return jnp.where(lower_lanes(left.shape), left, half_turn(right))


def kind_of(block):
    return jnp.where(block >= 24, 1, jnp.where(block >= 8, 0, jnp.where((block == 3) | (block == 4), 2, 1)))


def tile_kernel(kind_ref, flat_ref, head_ref, tail_ref, tiles, narrow):
    kind = kind_ref[0]

    @pl.when(kind == 0)
    def _():
        for j in range(12):
            tiles[72 * j : 72 * j + 72, :] = flat_ref[pl.ds(j, 72, stride=12), :]

    @pl.when(kind == 1)
    def _():
        lines = [flat_ref[pl.ds(t, 96, stride=9), :] for t in range(9)]
        turned = [half_turn(line) for line in lines[4:]]
        low = lower_lanes((96, LANES))
        for j in range(4):
            tiles[pl.ds(192 * j, 96, stride=2), :] = lines[j]
            tiles[pl.ds(192 * j + 1, 96, stride=2), :] = jnp.where(low, turned[j], turned[j + 1])
        narrow[pl.ds(0, 96, stride=2), :] = lines[4]
        narrow[pl.ds(1, 96, stride=2), :] = turned[4]
        tiles[768:864, :] = side_by_side(narrow[0:96, :], narrow[96:192, :])

    @pl.when(kind == 2)
    def _():
        lines = [flat_ref[pl.ds(t, 288, stride=3), :] for t in range(3)]
        first, second = half_turn(lines[1]), half_turn(lines[2])
        tiles[pl.ds(0, 288, stride=2), :] = lines[0]
        tiles[pl.ds(1, 288, stride=2), :] = jnp.where(lower_lanes((288, LANES)), first, second)
        narrow[pl.ds(0, 288, stride=2), :] = lines[1]
        narrow[pl.ds(1, 288, stride=2), :] = second
        tiles[576:864, :] = side_by_side(narrow[0:288, :], narrow[288:576, :])

    head_ref[...] = tiles[0:STEP_ROWS, :].astype(BF16)
    tail_ref[...] = tiles[STEP_ROWS:BLOCK_ROWS, :].astype(BF16)


def to_tiles(kind, flat):
    return pl.pallas_call(
        tile_kernel,
        out_shape=(
            jax.ShapeDtypeStruct((STEP_ROWS, LANES), BF16),
            jax.ShapeDtypeStruct((BLOCK_ROWS - STEP_ROWS, LANES), BF16),
        ),
        in_specs=[
            pl.BlockSpec(memory_space=pltpu.SMEM),
            pl.BlockSpec(memory_space=pltpu.VMEM),
        ],
        out_specs=(pl.BlockSpec(memory_space=pltpu.VMEM),) * 2,
        scratch_shapes=[
            pltpu.VMEM((BLOCK_ROWS, LANES), F32),
            pltpu.VMEM((HEAD_ROWS, LANES), F32),
        ],
        name="to_tiles",
    )(kind, flat)


def finish_kernel(table_ref, head_ref, one_ref, two_ref, three_ref, tail_ref, other_ref, mine_ref, *refs):
    kind, place = table_ref[0], table_ref[1]
    tiles, narrow, flat_ref, vector_parts = refs[-4:]
    tokens_ref, gains_ref, w_kv_ref, dq_wq_ref, d_mid_ref, own_dkv, other_dkv = refs[:7]
    states = refs[7:-4]
    tiles[0:HEAD_ROWS, :] = (head_ref[...] + one_ref[0:HEAD_ROWS, :].astype(F32)) + (
        two_ref[0:HEAD_ROWS, :].astype(F32) + three_ref[0:HEAD_ROWS, :].astype(F32)
    )
    tiles[HEAD_ROWS:BLOCK_ROWS, :] = tail_ref[...] + other_ref[...].astype(F32)

    for at, ref in enumerate((mine_ref, one_ref, two_ref, three_ref)):
        rows = ref.shape[0]
        part = ref[rows - 2 * VECTOR_ROWS : rows, :].astype(F32)
        vector_parts[at] = part[:VECTOR_ROWS] + part[VECTOR_ROWS:]
    vector = vector_parts[lax.rem(place, 4)]
    for z in (1, 2, 3):
        vector = vector + vector_parts[lax.rem(place + 4 - z, 4)]

    lane = lax.broadcasted_iota(jnp.int32, (2 * ROWS, WIDE), 1)
    x = jnp.where(lane < MODEL_WIDTH, tokens_ref[0].astype(F32).reshape(2 * ROWS, WIDE), 0.0)
    normed, scale = normed_rows(x)
    total = summed(own_dkv[...], other_dkv[...]).reshape(2 * ROWS, 384).astype(BF16)
    d_norm = (dq_wq_ref[...] + times_transposed(total, w_kv_ref[...])) * gains_ref[0:1, :]
    d_input = d_mid_ref[...] + scale * (d_norm - normed * row_mean(d_norm * normed))
    out_ref = states[-1]
    for mb in range(2):
        out_ref[mb] = d_input[ROWS * mb : ROWS * mb + ROWS].T[0:MODEL_WIDTH].astype(BF16)

    @pl.when(kind == 0)
    def _():
        for j in range(12):
            flat_ref[pl.ds(j, 72, stride=12), :] = tiles[72 * j : 72 * j + 72, :]

    @pl.when(kind == 1)
    def _():
        low = lower_lanes((96, LANES))
        narrow[0:96, :] = tiles[768:864, :]
        narrow[96:192, :] = half_turn(tiles[768:864, :])
        odd = [half_turn(tiles[pl.ds(192 * j + 1, 96, stride=2), :]) for j in range(4)]
        for j in range(4):
            flat_ref[pl.ds(j, 96, stride=9), :] = tiles[pl.ds(192 * j, 96, stride=2), :]
        flat_ref[pl.ds(4, 96, stride=9), :] = jnp.where(low, narrow[pl.ds(0, 96, stride=2), :], odd[0])
        for j in range(3):
            flat_ref[pl.ds(5 + j, 96, stride=9), :] = jnp.where(low, odd[j], odd[j + 1])
        last = half_turn(narrow[pl.ds(1, 96, stride=2), :])
        flat_ref[pl.ds(8, 96, stride=9), :] = jnp.where(low, odd[3], last)

    @pl.when(kind == 2)
    def _():
        low = lower_lanes((288, LANES))
        narrow[0:288, :] = tiles[576:864, :]
        narrow[288:576, :] = half_turn(tiles[576:864, :])
        odd = half_turn(tiles[pl.ds(1, 288, stride=2), :])
        flat_ref[pl.ds(0, 288, stride=3), :] = tiles[pl.ds(0, 288, stride=2), :]
        flat_ref[pl.ds(1, 288, stride=3), :] = jnp.where(low, narrow[pl.ds(0, 288, stride=2), :], odd)
        last = half_turn(narrow[pl.ds(1, 288, stride=2), :])
        flat_ref[pl.ds(2, 288, stride=3), :] = jnp.where(low, odd, last)


    if len(states) == 3:
        states[0][...], states[1][...] = flat_ref[...], vector
        return
    old_vectors, old_block, new_vectors, new_block = states[0:3], states[3:6], states[6:9], states[9:12]
    found = adamw(old_vectors[0][...], vector, old_vectors[1][...], old_vectors[2][...], RATE_VECTOR, 0.0)
    for ref, value in zip(new_vectors, found):
        ref[...] = value

    @pl.loop(0, 6)
    def _(k):
        rows = pl.ds(pl.multiple_of(k * 144, 8), 144)
        found = adamw(
            old_block[0][rows, :], flat_ref[rows, :], old_block[1][rows, :], old_block[2][rows, :], RATE_MATRIX, DECAY
        )
        for ref, value in zip(new_block, found):
            ref[rows, :] = value


def finish(table, parts, inputs, state):
    vmem = pl.BlockSpec(memory_space=pltpu.VMEM)
    flat = jax.ShapeDtypeStruct((BLOCK_ROWS, LANES), F32)
    vector = jax.ShapeDtypeStruct((VECTOR_ROWS, LANES), F32)
    shapes = (vector,) * 3 + (flat,) * 3 if state else (flat, vector)
    shapes += (jax.ShapeDtypeStruct((2, MODEL_WIDTH, ROWS), BF16),)
    return pl.pallas_call(
        finish_kernel,
        out_shape=shapes,
        in_specs=[pl.BlockSpec(memory_space=pltpu.SMEM)] + [vmem] * (len(parts) + len(inputs) + len(state)),
        out_specs=(vmem,) * len(shapes),
        scratch_shapes=[
            pltpu.VMEM((BLOCK_ROWS, LANES), F32),
            pltpu.VMEM((HEAD_ROWS, LANES), F32),
            pltpu.VMEM((BLOCK_ROWS, LANES), F32),
            pltpu.VMEM((4, VECTOR_ROWS, LANES), F32),
        ],
        name="finish",
    )(table, *parts, *inputs, *state)


def product(left, right):
    return jnp.dot(left, right, preferred_element_type=F32)


def times_transposed(left, right):
    return lax.dot_general(left, right, (((1,), (1,)), ((), ())), preferred_element_type=F32)


def rows_product(left, right):
    return lax.dot_general(left, right, (((0,), (0,)), ((), ())), preferred_element_type=F32)


def swapped(value):
    lane = lax.broadcasted_iota(jnp.int32, value.shape, 1)
    return jnp.where(lane % HEAD_SIZE < HEAD_SIZE // 2, pltpu.roll(value, 96, 1), pltpu.roll(value, 32, 1))


def rope(value, cosines, sines):
    return value * cosines + swapped(value) * sines


def rope_back(value, cosines, sines):
    return value * cosines - swapped(value) * sines


def row_mean(value):
    return jnp.sum(value, axis=-1, keepdims=True) * (1.0 / MODEL_WIDTH)


def normed_rows(value):
    scale = lax.rsqrt(row_mean(value * value) + EPS_NORM)
    return value * scale, scale


def place_rows(ref, read, first):
    for j in range(4):
        ref[first : first + 192, LANES * j : LANES * j + LANES] = read(192 * j, 192 * j + 192)
    rest = read(768, 864).astype(F32)
    low = lower_lanes(rest.shape)
    ref[first : first + 96, 512:640] = jnp.where(low, rest, 0.0).astype(BF16)
    ref[first + 96 : first + 192, 512:640] = jnp.where(low, half_turn(rest), 0.0).astype(BF16)


def tiles_of_rows(value):
    head = jnp.concatenate([value[:, LANES * j : LANES * j + LANES] for j in range(3)], axis=0)
    rest = side_by_side(value[0:96, 512:640], value[96:192, 512:640])
    return head, jnp.concatenate([value[:, 384:512], rest], axis=0)


def layer_kernel(*refs):
    slots = refs[0]
    head_parts = refs[1:9]
    tail_part = refs[9]
    tokens_pair, cos_pair, sin_pair = refs[10:12], refs[12:14], refs[14:16]
    (place_q_ref, place_k_ref, gains_ref, bias_q_ref, bias_kv_ref, grad_ref) = refs[16:22]
    block_out_ref, parts_out = refs[22], refs[23:33]
    (dkv_send, dkv_keep, dq_wq_ref, d_mid_ref, w_kv) = refs[33:38]
    (raw_head, raw_tail, w_q, w_out, w_gate, w_up, w_down, normed_all, hidden_all, keys, values, queries, probs, attended, act_all, block_acc, d_hidden, d_attended, dkv_all, d_query, send_all, keep_all, vector_ref, outs, sems, out_sems) = refs[38:]

    place = slots[MY_Z]

    def fetches(shift, sem):
        at = lax.rem(place + shift, 4)
        return [
            pltpu.make_async_copy(part.at[at], raw_head.at[4 * k + at], sems.at[sem + k])
            for k, part in enumerate(head_parts)
        ]

    attention_blocks = fetches(0, 0)
    attention_blocks.append(pltpu.make_async_copy(tail_part.at[pl.ds(0, 8)], raw_tail.at[pl.ds(0, 8)], sems.at[32]))
    other_blocks = fetches(1, 8) + fetches(2, 16) + fetches(3, 24)
    other_blocks.append(pltpu.make_async_copy(tail_part.at[pl.ds(8, 24)], raw_tail.at[pl.ds(8, 24)], sems.at[33]))
    for copy in attention_blocks + other_blocks:
        copy.start()

    core = slots[MY_CORE]

    def at_slot(pair, slot):
        return pair[slot % 2].at[slot // 2]

    def reader(block):
        def read(first, last):
            parts = []
            if first < STEP_ROWS:
                parts.append(raw_head[slots[AT_HEAD + block], first : min(last, STEP_ROWS), :])
            if last > STEP_ROWS:
                parts.append(raw_tail[block, max(first, STEP_ROWS) - STEP_ROWS : last - STEP_ROWS, :])
            return parts[0] if len(parts) == 1 else jnp.concatenate(parts, axis=0)

        return read

    gain_one = gains_ref[0:1, :]
    gain_two = gains_ref[1:2, :]
    low_rows = lower_lanes((ROWS, LANES))

    @pl.loop(0, 2)
    def _(mb):
        lane = lax.broadcasted_iota(jnp.int32, (ROWS, WIDE), 1)
        for slot in range(4):
            rows = pl.ds(pl.multiple_of(mb * 512 + slot * ROWS, ROWS), ROWS)
            x = jnp.where(lane < MODEL_WIDTH, at_slot(tokens_pair, slot)[mb].astype(F32), 0.0)
            normed, _ = normed_rows(x)
            normed_all[rows, :] = normed
            hidden_all[rows, :] = (normed * gain_one).astype(BF16)

    for copy in attention_blocks:
        copy.wait()
    for ref in (w_q, w_out, w_gate, w_up, w_kv):
        ref[576:640, :] = jnp.zeros((64, ref.shape[1]), BF16)
    for k in range(3):
        place_rows(w_q, reader(k), 192 * k)
        place_rows(w_out, reader(5 + k), 192 * k)
    for at in range(0, 576, 144):
        w_kv[at : at + 144, 0:128] = reader(3)(at, at + 144)
        w_kv[at : at + 144, 128:256] = reader(4)(at, at + 144)
    rest_key = reader(3)(576, 864).astype(F32)
    rest_value = reader(4)(576, 864).astype(F32)
    low = lower_lanes(rest_key.shape)
    w_kv[0:288, 256:384] = jnp.where(low, rest_key, half_turn(rest_value)).astype(BF16)
    w_kv[288:576, 256:384] = jnp.where(low, half_turn(rest_key), rest_value).astype(BF16)

    @pl.loop(0, 2)
    def _(mb):
        rows = pl.ds(pl.multiple_of(mb * 512, 512), 512)
        pair = product(hidden_all[rows, :], w_kv[...]) + bias_kv_ref[...]
        cosines = jnp.concatenate([at_slot(cos_pair, slot)[mb] for slot in range(4)], axis=0)
        sines = jnp.concatenate([at_slot(sin_pair, slot)[mb] for slot in range(4)], axis=0)
        key_a = rope(pair[:, 0:128], cosines, sines)
        key_b = rope(pair[:, 256:384], cosines, sines)
        value_a, value_b = pair[:, 128:256], pair[:, 256:384]
        low_keys = lower_lanes((512, LANES))
        turned = half_turn(key_a)
        keys[rows, 0:128] = jnp.where(low_keys, key_a, turned).astype(BF16)
        keys[rows, 128:256] = jnp.where(low_keys, turned, key_a).astype(BF16)
        keys[rows, 256:384] = jnp.where(low_keys, key_b, half_turn(key_b)).astype(BF16)
        turned = half_turn(value_a)
        values[rows, 0:128] = jnp.where(low_keys, value_a, turned).astype(BF16)
        values[rows, 128:256] = jnp.where(low_keys, turned, value_a).astype(BF16)
        values[rows, 256:384] = jnp.where(low_keys, half_turn(value_b), value_b).astype(BF16)

    def heads_of(ref, rows, group):
        stacked = []
        for k in range(3):
            number = 3 * group + k
            tile = ref[rows, LANES * (number // 2) : LANES * (number // 2) + LANES]
            keep = low_rows if number % 2 == 0 else jnp.logical_not(low_rows)
            stacked.append(jnp.where(keep, tile.astype(F32), 0.0).astype(BF16))
        return jnp.concatenate(stacked, axis=0)

    def tiles_of_heads(parts):
        found = [jnp.where(low_rows, parts[2 * k], parts[2 * k + 1]) for k in range(4)]
        return found + [jnp.where(low_rows, parts[8], 0.0)]

    @pl.loop(0, 2)
    def _(mb):
        rows = pl.ds(pl.multiple_of(mb * ROWS, ROWS), ROWS)
        key_rows = pl.ds(pl.multiple_of(mb * 512, 512), 512)
        cosines, sines = cos_pair[0][0, mb], sin_pair[0][0, mb]
        made = product(hidden_all[pl.ds(pl.multiple_of(mb * 512, 512), ROWS), :], w_q[...]) + bias_q_ref[...]
        for k in range(5):
            turned = rope(made[:, LANES * k : LANES * k + LANES], cosines, sines)
            queries[rows, LANES * k : LANES * k + LANES] = (turned * HEAD_SIZE ** (-0.5)).astype(BF16)
        masked = jnp.where(place_q_ref[mb] >= place_k_ref[mb], 0.0, MASKED)
        masked = jnp.concatenate([masked] * 3, axis=0)
        parts = []
        for group in range(KEY_VALUE_HEADS):
            lanes = slice(LANES * group, LANES * group + LANES)
            scores = times_transposed(heads_of(queries, rows, group), keys[key_rows, lanes])
            scores = scores + masked
            top = jnp.max(scores, axis=-1, keepdims=True)
            powers = jnp.exp(scores - top)
            found = powers * (1.0 / jnp.sum(powers, axis=-1, keepdims=True))
            probs[mb, group] = found
            out = product(found.astype(BF16), values[key_rows, lanes])
            outs[mb, group] = out
            parts += [out[ROWS * k : ROWS * k + ROWS] for k in range(3)]
        for k, tile in enumerate(tiles_of_heads(parts)):
            attended[rows, LANES * k : LANES * k + LANES] = tile.astype(BF16)

    for copy in other_blocks:
        copy.wait()
    for k in range(8):
        place_rows(w_down, reader(24 + k), 192 * k)
    for ref, base in ((w_gate, 8), (w_up, 16)):
        for k in range(4):
            for i in range(6):
                even = reader(base + 2 * k)(144 * i, 144 * i + 144).astype(F32)
                odd = reader(base + 2 * k + 1)(144 * i, 144 * i + 144).astype(F32)
                ref[144 * k : 144 * k + 144, 256 * i : 256 * i + 128] = jnp.concatenate(
                    [even[0:72], odd[0:72]], axis=0
                ).astype(BF16)
                ref[144 * k : 144 * k + 144, 256 * i + 128 : 256 * i + 256] = jnp.concatenate(
                    [even[72:144], odd[72:144]], axis=0
                ).astype(BF16)

    lane = lax.broadcasted_iota(jnp.int32, (2 * ROWS, WIDE), 1)
    x_own = tokens_pair[0][0].astype(F32).reshape(2 * ROWS, WIDE)
    x_own = jnp.where(lane < MODEL_WIDTH, x_own, 0.0)
    resid_mid = x_own + product(attended[...], w_out[...])
    normed_two, scale_two = normed_rows(resid_mid)
    hidden_two = (normed_two * gain_two).astype(BF16)
    hidden_turned = hidden_two.T
    grad_low = grad_ref[...]
    block_acc[...] = resid_mid
    d_hidden[...] = jnp.zeros_like(d_hidden)

    def store_pair(at, even, odd, table, first):
        rows = pl.ds(pl.multiple_of(slots[table + at] + first, 16), even.shape[0])
        send_all[rows, :] = jnp.where(core == 0, odd, even).astype(BF16)
        keep_all[rows, :] = jnp.where(core == 0, even, odd).astype(BF16)

    def feed_forward(chunk, first, table):
        cols = pl.ds(pl.multiple_of(chunk * 512, 512), 512)
        gate = product(hidden_two, w_gate[:, cols])
        up = product(hidden_two, w_up[:, cols])
        sigma = 1.0 / (1.0 + jnp.exp(-gate))
        act = (gate * sigma * up).astype(BF16)
        act_all[:, cols] = act
        down = w_down[cols, :]
        d_act = times_transposed(grad_low, down)
        block_acc[...] += product(act, down)
        d_up = (d_act * gate * sigma).astype(BF16)
        d_gate = (d_act * up * sigma * (1.0 + gate * (1.0 - sigma))).astype(BF16)
        d_hidden[...] += times_transposed(d_gate, w_gate[:, cols]) + times_transposed(d_up, w_up[:, cols])
        for base, cotangent in ((4, d_gate), (8, d_up)):
            made = product(hidden_turned, cotangent)
            for k in range(4):
                part = made[144 * k : 144 * k + 144, :]
                even = jnp.concatenate([part[0:72, LANES * j : LANES * j + LANES] for j in range(4)], axis=0)
                odd = jnp.concatenate([part[72:144, LANES * j : LANES * j + LANES] for j in range(4)], axis=0)
                store_pair(base + k, even, odd, table, (chunk - first) * 288)

    @pl.loop(0, 2)
    def _(chunk):
        feed_forward(chunk, 0, TO_HEAD)

    feed_forward(2, 2, TO_TAIL)

    def store_rows(at, even, odd):
        even_head, even_tail = even
        odd_head, odd_tail = odd
        store_pair(at, even_head, odd_head, TO_HEAD, 0)
        store_pair(at, even_tail, odd_tail, TO_TAIL, 0)

    @pl.loop(0, 4)
    def _(k):
        made = rows_product(act_all[:, pl.ds(pl.multiple_of(k * 384, 128), 384)], grad_low)
        store_rows(12 + k, tiles_of_rows(made[0:192]), tiles_of_rows(made[192:384]))

    def deliveries(first, count, sem):
        copies = []
        for base, outs_of in ((send_all, parts_out[0:4]), (keep_all, parts_out[4:10])):
            rest = [(outs_of[2], PART * k) for k in range(3)] if len(outs_of) == 4 else [(out, 0) for out in outs_of[2:5]]
            targets = [(outs_of[0], 0, FIRST_AT), (outs_of[1], 0, TAIL_AT)]
            targets += [(out, into, PART * k) for k, (out, into) in enumerate(rest)]
            targets.append((outs_of[-1], 0, 3 * PART))
            for out, into, start in targets:
                rows = HEAD_ROWS * count
                copies.append(
                    pltpu.make_async_copy(
                        base.at[pl.ds(start + HEAD_ROWS * first, rows)],
                        out.at[pl.ds(into + HEAD_ROWS * first, rows)],
                        out_sems.at[sem + len(copies)],
                    )
                )
        return copies

    early = deliveries(1, 3, 12)
    for copy in early:
        copy.start()

    for mb in range(2):
        block_out_ref[mb] = block_acc[ROWS * mb : ROWS * mb + ROWS, :].T[0:MODEL_WIDTH].astype(BF16)

    d_two = d_hidden[...]
    gain_two_sum = jnp.sum(d_two * normed_two, axis=0, keepdims=True)
    d_norm = d_two * gain_two
    d_mid = grad_low.astype(F32) + scale_two * (d_norm - normed_two * row_mean(d_norm * normed_two))
    d_mid_ref[...] = d_mid
    d_branch = d_mid.astype(BF16)
    d_attended[...] = times_transposed(d_branch, w_out[...]).astype(BF16)
    grad_out = rows_product(attended[...], d_branch)

    @pl.loop(0, 2)
    def _(mb):
        rows = pl.ds(pl.multiple_of(mb * ROWS, ROWS), ROWS)
        key_rows = pl.ds(pl.multiple_of(mb * 512, 512), 512)
        parts = []
        d_keys = []
        d_values = []
        for group in range(KEY_VALUE_HEADS):
            lanes = slice(LANES * group, LANES * group + LANES)
            query_rows = heads_of(queries, rows, group)
            cotangent = heads_of(d_attended, rows, group)
            found = probs[mb, group]
            d_probs = times_transposed(cotangent, values[key_rows, lanes])
            delta = jnp.sum(outs[mb, group] * cotangent.astype(F32), axis=-1, keepdims=True)
            d_scores = (found * (d_probs - delta)).astype(BF16)
            out = product(d_scores, keys[key_rows, lanes]) * HEAD_SIZE ** (-0.5)
            parts += [out[ROWS * k : ROWS * k + ROWS] for k in range(3)]
            d_key = rows_product(d_scores, query_rows)
            d_value = rows_product(found.astype(BF16), cotangent)
            d_keys.append(d_key + half_turn(d_key))
            d_values.append(d_value + half_turn(d_value))
        cosines, sines = cos_pair[0][0, mb], sin_pair[0][0, mb]
        for k, tile in enumerate(tiles_of_heads(parts)):
            d_query[rows, LANES * k : LANES * k + LANES] = rope_back(tile, cosines, sines).astype(BF16)
        low_keys = lower_lanes((512, LANES))
        cosines = jnp.concatenate([at_slot(cos_pair, slot)[mb] for slot in range(4)], axis=0)
        sines = jnp.concatenate([at_slot(sin_pair, slot)[mb] for slot in range(4)], axis=0)
        key_a = rope_back(jnp.where(low_keys, d_keys[0], d_keys[1]), cosines, sines)
        key_b = rope_back(d_keys[2], cosines, sines)
        dkv_all[key_rows, 0:128] = key_a.astype(BF16)
        dkv_all[key_rows, 128:256] = jnp.where(low_keys, d_values[0], d_values[1]).astype(BF16)
        dkv_all[key_rows, 256:384] = jnp.where(low_keys, key_b, d_values[2]).astype(BF16)
        for slot in range(4):
            target = dkv_send if slot % 2 else dkv_keep
            target[slot // 2, mb] = dkv_all[pl.ds(pl.multiple_of(mb * 512 + slot * ROWS, ROWS), ROWS), :]

    dkv = dkv_all[...]
    d_q = d_query[...]
    dq_wq = times_transposed(d_q, w_q[...])
    dq_wq_ref[...] = dq_wq
    bias_q_sum = jnp.sum(d_q.astype(F32), axis=0, keepdims=True)
    bias_kv_sum = jnp.sum(dkv.astype(F32), axis=0, keepdims=True)
    gain_sum = jnp.zeros((1, WIDE), F32)
    for mb in range(2):
        gain_sum += jnp.sum(dq_wq[ROWS * mb : ROWS * mb + ROWS] * normed_all[512 * mb : 512 * mb + ROWS, :], axis=0, keepdims=True)
    for k in range(4):
        part = slice(256 * k, 256 * k + 256)
        gain_sum += jnp.sum(times_transposed(dkv_all[part, :], w_kv[...]) * normed_all[part, :], axis=0, keepdims=True)

    hidden_own = jnp.concatenate([hidden_all[0:ROWS, :], hidden_all[512 : 512 + ROWS, :]], axis=0)
    grad_q = rows_product(hidden_own, d_q)
    grad_kv = rows_product(hidden_all[...], dkv)
    rest = grad_kv[0:576, 256:384]
    low = lower_lanes((288, LANES))
    key_tiles = (grad_kv[0:576, 0:128], jnp.where(low, rest[0:288], half_turn(rest[288:576])))
    value_tiles = (grad_kv[0:576, 128:256], jnp.where(low, half_turn(rest[0:288]), rest[288:576]))
    query_tiles = [tiles_of_rows(grad_q[192 * k : 192 * k + 192]) for k in range(3)]
    out_tiles = [tiles_of_rows(grad_out[192 * k : 192 * k + 192]) for k in range(3)]
    store_rows(0, query_tiles[0], query_tiles[1])
    store_rows(1, query_tiles[2], key_tiles)
    store_rows(2, value_tiles, out_tiles[0])
    store_rows(3, out_tiles[1], out_tiles[2])
    def flat_rows(first, second, third, pair):
        tile = lambda row, k: row[:, LANES * k : LANES * k + LANES]
        low = lower_lanes((1, LANES))
        across_two = lambda one, two: jnp.where(low, half_turn(one), half_turn(two))
        lines = [tile(first, k) for k in range(4)]
        lines.append(side_by_side(tile(first, 4), tile(second, 0)))
        lines += [across_two(tile(second, k), tile(second, k + 1)) for k in range(4)]
        lines += [tile(third, k) for k in range(4)]
        lines.append(side_by_side(tile(third, 4), tile(pair, 0)))
        lines.append(across_two(tile(pair, 0), tile(pair, 2)))
        lines.append(tile(pair, 1))
        lines.append(jnp.where(low, half_turn(tile(pair, 2)), 0.0))
        return lines

    at = FIRST_AT + PART
    for row, line in enumerate(flat_rows(gain_sum, gain_two_sum, bias_q_sum, bias_kv_sum)):
        vector_ref[row : row + 1, :] = line
    vector_ref[17:24, :] = jnp.zeros((7, LANES), F32)
    vector = vector_ref[...]
    high = vector.astype(BF16).astype(F32)
    both = jnp.concatenate([high, vector - high], axis=0).astype(BF16)
    for ref in (send_all, keep_all):
        ref[at : at + 2 * VECTOR_ROWS, :] = both
    last = deliveries(0, 1, 0)
    last.append(pltpu.make_async_copy(send_all.at[pl.ds(at, 2 * VECTOR_ROWS)], parts_out[0].at[pl.ds(PART, 2 * VECTOR_ROWS)], out_sems.at[24]))
    last.append(pltpu.make_async_copy(keep_all.at[pl.ds(at, 2 * VECTOR_ROWS)], parts_out[4].at[pl.ds(PART, 2 * VECTOR_ROWS)], out_sems.at[25]))
    for copy in last:
        copy.start()
    for copy in early + last:
        copy.wait()


def run_layer(slots, heads, tails, *others):
    shape = jax.ShapeDtypeStruct
    vmem = pl.BlockSpec(memory_space=pltpu.VMEM)
    anywhere = pl.BlockSpec(memory_space=pl.ANY)
    scratch = [
        ((BLOCKS, STEP_ROWS, LANES), BF16),
        ((BLOCKS, BLOCK_ROWS - STEP_ROWS, LANES), BF16),
        ((WIDE, WIDE), BF16),
        ((WIDE, WIDE), BF16),
        ((WIDE, FF), BF16),
        ((WIDE, FF), BF16),
        ((FF, WIDE), BF16),
        ((1024, WIDE), F32),
        ((1024, WIDE), BF16),
        ((1024, 384), BF16),
        ((1024, 384), BF16),
        ((256, WIDE), BF16),
        ((2, 3, 384, 512), F32),
        ((256, WIDE), BF16),
        ((256, FF), BF16),
        ((256, WIDE), F32),
        ((256, WIDE), F32),
        ((256, WIDE), BF16),
        ((1024, 384), BF16),
        ((256, WIDE), BF16),
        ((ALL_ROWS, LANES), BF16),
        ((ALL_ROWS, LANES), BF16),
        ((VECTOR_ROWS, LANES), F32),
        ((2, 3, 384, LANES), F32),
    ]
    return pl.pallas_call(
        layer_kernel,
        out_shape=(
            shape((2, MODEL_WIDTH, ROWS), BF16),
            *[shape((count, LANES), BF16) for _, count in SEND_PARTS + KEEP_PARTS],
            shape((2, 2, ROWS, 384), BF16),
            shape((2, 2, ROWS, 384), BF16),
            shape((256, WIDE), F32),
            shape((256, WIDE), F32),
            shape((WIDE, 384), BF16),
        ),
        in_specs=[pl.BlockSpec(memory_space=pltpu.SMEM)] + [anywhere] * 9 + [vmem] * 12,
        out_specs=(vmem,) + (anywhere,) * 10 + (vmem,) * 5,
        scratch_shapes=[pltpu.VMEM(dims, kind) for dims, kind in scratch]
        + [pltpu.SemaphoreType.DMA((48,)), pltpu.SemaphoreType.DMA((26,))],
        compiler_params=pltpu.CompilerParams(vmem_limit_bytes=50 * 1024 * 1024),
        name="layer",
    )(slots, *heads, tails, *others)


def adamw(param, grad, mom_one, mom_two, rate, decay):
    new_one = BETA_ONE * mom_one + (1.0 - BETA_ONE) * grad
    new_two = BETA_TWO * mom_two + (1.0 - BETA_TWO) * grad * grad
    fixed_one = new_one / (1.0 - BETA_ONE**STEP)
    fixed_two = new_two / (1.0 - BETA_TWO**STEP)
    new_param = param - rate * (fixed_one / (jnp.sqrt(fixed_two) + EPS_ADAM) + decay * param)
    return (new_param, new_one, new_two)


def inner_groups():
    inner = inner_count()
    data_inner = inner // lax.axis_size("ctx")
    data_count = lax.axis_size("dp")
    return [list(range(k, k + data_inner)) for k in range(0, data_count, data_inner)]


def whole_block(flat):
    if inner_count() == 1:
        return flat
    flat = lax.all_gather(flat, "ctx", axis=0, tiled=True)
    return lax.all_gather(flat, "dp", axis=0, tiled=True, axis_index_groups=inner_groups())


def own_slice(block):
    if inner_count() == 1:
        return block
    block = lax.psum_scatter(
        block, "dp", scatter_dimension=0, tiled=True, axis_index_groups=inner_groups()
    )
    return lax.psum_scatter(block, "ctx", scatter_dimension=0, tiled=True)


def bias_tiles(bias_key, bias_value):
    return jnp.concatenate([bias_key[:128], bias_value[:128], bias_key[128:], bias_value[128:]])


def local(tokens_in, places, out_grad, weights, first_moment, second_moment, vectors, vector_first, vector_second):
    kind = kind_of(device_number() // inner_count()).astype(jnp.int32).reshape(1)
    block = whole_block(weights).reshape(BLOCK_ROWS, LANES)
    head, tail = to_tiles(kind, block)

    head, tail, tokens_in, places = together(head, tail, tokens_in, places)
    own_tokens = tokens_in.reshape(2, ROWS, MODEL_WIDTH)
    own_places = places.reshape(2, ROWS)
    marks = jnp.stack([own_places // 16, own_places % 16], axis=-1).astype(BF16)
    packed = jnp.concatenate(
        [own_tokens, marks, jnp.zeros((2, ROWS, WIDE - MODEL_WIDTH - 2), BF16)], axis=-1
    )
    padding = ((0, 0), (0, WIDE - MODEL_WIDTH))
    gains = jnp.pad(vectors[: 2 * MODEL_WIDTH].reshape(2, MODEL_WIDTH), padding)
    bias_q = jnp.pad(vectors[2 * MODEL_WIDTH : 3 * MODEL_WIDTH].reshape(1, MODEL_WIDTH), padding)
    bias_kv = bias_tiles(vectors[1728:1920], vectors[1920:2112]).reshape(1, 384)
    grad = jnp.pad(out_grad.reshape(2 * ROWS, MODEL_WIDTH), padding)
    spare = VECTOR_ROWS * LANES - vectors.shape[0]
    vector_state = [
        jnp.pad(array, (0, spare), constant_values=1.0).reshape(VECTOR_ROWS, LANES)
        for array in (vectors, vector_first, vector_second)
    ]
    table = jnp.concatenate([kind, (coordinates(device_number() // inner_count())["z"]).astype(jnp.int32).reshape(1)])
    others = (slot_table(), gains, bias_q, bias_kv, grad, vector_state, table)
    heads, tails, (near, far), (cosines, sines), others = gather_all(head, tail, packed, others)
    slots, gains, bias_q, bias_kv, grad, vector_state, table = others
    cosines_far, sines_far = place_tables(far)
    place_all = jnp.stack([places_of(near), places_of(far)], axis=1)
    place_q = place_all[0, 0][..., None]
    place_k = jnp.transpose(place_all.reshape(4, 2, ROWS), (1, 0, 2)).reshape(2, 1, 4 * ROWS)

    block_out, *found = run_layer(
        slots, heads, tails, near, far, cosines, cosines_far, sines, sines_far, place_q, place_k, gains, bias_q, bias_kv, grad
    )
    sends, keeps = found[:4], found[4:10]
    dkv_send, dkv_keep, dq_wq, d_mid, w_kv = found[10:]
    parts, pairs = scatter_blocks(sends, keeps, dkv_send, dkv_keep)
    inputs = (near, gains, w_kv, dq_wq, d_mid, *pairs)
    state = (weights, first_moment, second_moment)
    if inner_count() == 1:
        blocks = [array.reshape(BLOCK_ROWS, LANES) for array in state]
        *updated, input_grad = finish(table, parts, inputs, [*vector_state, *blocks])
        new_vector_state = [array.reshape(-1)[: vectors.shape[0]] for array in updated[:3]]
        new_state = [array.reshape(-1) for array in updated[3:]]
    else:
        block_grad, vector, input_grad = finish(table, parts, inputs, [])
        vector = lax.psum(vector, "ctx")
        vector = lax.psum(vector, "dp", axis_index_groups=inner_groups())
        grad_own = own_slice(block_grad.reshape(-1))
        vector_grad = vector.reshape(-1)[: vectors.shape[0]]
        new_state = adamw(weights, grad_own, first_moment, second_moment, RATE_MATRIX, DECAY)
        new_vector_state = adamw(vectors, vector_grad, vector_first, vector_second, RATE_VECTOR, 0.0)
    shape = tokens_in.shape
    return (
        jnp.transpose(block_out, (0, 2, 1)).reshape(shape),
        jnp.transpose(input_grad, (0, 2, 1)).reshape(shape),
        *new_state,
        *new_vector_state,
    )


def solution(mesh):
    in_specs = (
        P(None, "dp", "ctx", None),
        P(None, "dp", "ctx"),
        P(None, "dp", "ctx", None),
        P(("dp", "ctx")),
        P(("dp", "ctx")),
        P(("dp", "ctx")),
        P(),
        P(),
        P(),
    )
    out_specs = (
        P(None, "dp", "ctx", None),
        P(None, "dp", "ctx", None),
        P(("dp", "ctx")),
        P(("dp", "ctx")),
        P(("dp", "ctx")),
        P(),
        P(),
        P(),
    )
    return jax.shard_map(local, mesh=mesh, in_specs=in_specs, out_specs=out_specs, check_vma=False)
```

```python
import jax
import jax.numpy as jnp
from jax import lax
from jax.experimental import pallas as pl
from jax.experimental.pallas import tpu as pltpu
from jax.sharding import PartitionSpec as P

MODEL_WIDTH = 576
QUERY_HEADS = 9
KEY_VALUE_HEADS = 3
HEAD_SIZE = 64
FF = 1536
STEP = 10

EPS_NORM = 1e-05
THETA = 100000.0
BETA_ONE = 0.9
BETA_TWO = 0.95
EPS_ADAM = 1e-08
RATE_MATRIX = 0.06
RATE_VECTOR = 0.3
DECAY = 0.1
MASKED = -1e30

LANES = 128
WIDE = 640
BLOCKS = 32
BLOCK_ROWS = 864
HEAD_ROWS = 576
TAIL_ROWS = BLOCK_ROWS - HEAD_ROWS
VECTOR_ROWS = 24
PART = 4 * HEAD_ROWS
FIRST_AT = 4 * PART
TAIL_AT = FIRST_AT + PART + 2 * VECTOR_ROWS
ALL_ROWS = TAIL_AT + PART
SEND_PARTS = [(FIRST_AT, PART + 2 * VECTOR_ROWS), (TAIL_AT, PART), (0, 3 * PART), (3 * PART, PART)]
KEEP_PARTS = SEND_PARTS[:2] + [(PART * k, PART) for k in range(4)]
SIZES = {"z": 4, "y": 2, "x": 2, "c": 2}
ROWS = 128
F32 = jnp.float32
BF16 = jnp.bfloat16


def coordinates(number):
    found = {}
    for name in ("c", "x", "y", "z"):
        found[name] = number % SIZES[name]
        number = number // SIZES[name]
    return found


def number_of(found):
    number = 0
    for name in ("z", "y", "x", "c"):
        number = number * SIZES[name] + found[name]
    return number


def device_number():
    return lax.axis_index("dp") * lax.axis_size("ctx") + lax.axis_index("ctx")


def inner_count():
    return lax.axis_size("dp") * lax.axis_size("ctx") // BLOCKS


def moved(buffer, name, shift):
    inner = inner_count()
    pairs = []
    for number in range(BLOCKS):
        found = coordinates(number)
        found[name] = (found[name] + shift) % SIZES[name]
        target = number_of(found)
        pairs += [(number * inner + k, target * inner + k) for k in range(inner)]
    return lax.ppermute(buffer, ("dp", "ctx"), pairs)


def across(buffer, distance):
    count = lax.axis_size("ctx")
    return lax.ppermute(buffer, "ctx", [(i, i ^ distance) for i in range(count)])


def together(*arrays):
    return lax.optimization_barrier(arrays)


def gather_all(head, tail, packed, others):
    hz = [moved(head, "z", s) for s in (1, 2, 3)]
    tx = moved(tail, "x", 1)
    two = across(packed, 2)
    head, tail, tx, two, *hz = together(head, tail, tx, two, *hz)
    own = jnp.stack([head] + hz)
    pair = jnp.stack([tail, tx])
    ay = moved(own, "y", 1)
    ax = moved(own, "x", 1)
    tz = [moved(pair, "z", s) for s in (1, 2, 3)]
    near = jnp.stack([packed, two])
    tables = place_tables(near)
    own, pair, ay, ax, near, tables, others, *tz = together(own, pair, ay, ax, near, tables, others, *tz)
    eight = jnp.concatenate([pair] + tz)
    far = across(near, 1)
    axy = moved(ay, "x", 1)
    ty = moved(eight, "y", 1)
    ac = moved(own, "c", 1)
    acy = moved(ay, "c", 1)
    acx = moved(ax, "c", 1)
    tc = moved(eight, "c", 1)
    axy, ty, ac, acy, acx, tc, far = together(axy, ty, ac, acy, acx, tc, far)
    acxy = moved(axy, "c", 1)
    tcy = moved(ty, "c", 1)
    heads = [own, ay, ax, axy, ac, acy, acx, acxy]
    return heads, [eight, ty, tc, tcy], (near, far), tables, others


def places_of(tokens):
    found = tokens[..., MODEL_WIDTH : MODEL_WIDTH + 2].astype(F32)
    return found[..., 0] * 16.0 + found[..., 1]


def place_tables(tokens):
    half_dim = HEAD_SIZE // 2
    frequency = THETA ** (-2.0 * jnp.arange(half_dim, dtype=F32) / HEAD_SIZE)
    angles = places_of(tokens)[..., None] * jnp.tile(frequency, 4)
    sign = jnp.where(jnp.arange(LANES) % HEAD_SIZE < half_dim, -1.0, 1.0).astype(F32)
    return jnp.cos(angles), jnp.sin(angles) * sign


def fold(order, relative):
    slot = 0
    for name in order:
        slot = slot * SIZES[name] + relative[name]
    return slot


def head_row(slot, z, _):
    return slot * PART + jnp.where(slot < 3, 0, FIRST_AT - 3 * PART) + z * HEAD_ROWS


def tail_row(slot, z, inside):
    return jnp.where(slot < 1, 3 * PART, TAIL_AT) + (2 * z + inside) * TAIL_ROWS


def slot_table():
    mine = coordinates(device_number() // inner_count())
    entries = []
    for order in (("c", "x", "y", "z"), ("c", "y", "z", "x")):
        for number in range(BLOCKS):
            found = coordinates(number)
            entries.append(fold(order, {n: (mine[n] - found[n]) % SIZES[n] for n in SIZES}))
    for order, start in ((("x", "y"), head_row), (("y",), tail_row)):
        for number in range(0, BLOCKS, 2):
            found = coordinates(number)
            slot = fold(order, {n: (found[n] - mine[n]) % SIZES[n] for n in SIZES})
            inside = (found["x"] - mine["x"]) % SIZES["x"]
            entries.append(start(slot, found["z"], inside))
    entries.append(mine["c"])
    entries.append(mine["z"])
    return jnp.stack([jnp.asarray(entry, jnp.int32) for entry in entries])


AT_HEAD, AT_TAIL, TO_HEAD, TO_TAIL = 0, BLOCKS, 2 * BLOCKS, 2 * BLOCKS + 16
MY_CORE, MY_Z = 2 * BLOCKS + 32, 2 * BLOCKS + 33


def summed(*parts):
    total = parts[0].astype(F32)
    for part in parts[1:]:
        total = total + part.astype(F32)
    return total


def summed_vector(mine, other):
    total = summed(mine[:VECTOR_ROWS], other[:VECTOR_ROWS]) + summed(mine[VECTOR_ROWS:], other[VECTOR_ROWS:])
    high = lax.reduce_precision(total, 8, 7)
    return jnp.concatenate([high.astype(BF16), (total - high).astype(BF16)])


def scatter_blocks(sends, keeps, dkv_send, dkv_keep):
    keep_head, keep_tail, keep_low, keep_mid, keep_far, keep_rest = keeps
    got_head, got_tail = moved(sends[0], "c", 1), moved(sends[1], "c", 1)
    got_head, got_tail, rest_head, rest_tail, dkv_send = together(got_head, got_tail, *sends[2:], dkv_send)
    got_rest_head, got_rest_tail = moved(rest_head, "c", 1), moved(rest_tail, "c", 1)
    got_dkv = across(dkv_send, 1)
    vector = summed_vector(keep_head[PART:], got_head[PART:])
    hx = jnp.concatenate([summed(keep_head[:PART], got_head[:PART]).astype(BF16), vector])
    ty = summed(keep_tail, got_tail).astype(BF16)
    got_hx = moved(hx, "x", 1)
    got_ty = moved(ty, "y", 1)
    low, mid, far = [
        summed(keep, got_rest_head[PART * k : PART * k + PART]).astype(BF16)
        for k, keep in enumerate((keep_low, keep_mid, keep_far))
    ]
    tail = summed(keep_rest, got_rest_tail).astype(BF16)
    dkv = summed(dkv_keep, got_dkv).astype(BF16)
    got_hx, got_ty, low, mid, far, tail, dkv, vector = together(got_hx, got_ty, low, mid, far, tail, dkv, vector)
    place = coordinates(device_number() // inner_count())["z"]

    def part_for(array, shift):
        return lax.dynamic_slice_in_dim(array, HEAD_ROWS * ((place + shift) % SIZES["z"]), HEAD_ROWS, 0)

    vector = summed_vector(vector, got_hx[PART:])
    hy = jnp.concatenate([summed(mid, got_hx[:PART]).astype(BF16), vector])
    tz = [summed(part_for(tail, s), part_for(got_ty, s)).astype(BF16) for s in range(4)]
    got_hy = moved(hy, "y", 1)
    got_far = moved(far, "x", 1)
    got_tz = [moved(tz[s], "z", s) for s in (1, 2, 3)]
    got_hy, got_far, low, own_tail, vector, dkv, *got_tz = together(got_hy, got_far, low, tz[0], vector, dkv, *got_tz)
    vector = summed_vector(vector, got_hy[PART:])
    head = [summed(part_for(low, s), part_for(got_far, s), part_for(got_hy, s)) for s in range(4)]
    got_hz = [moved(jnp.concatenate([head[s].astype(BF16), vector]), "z", s) for s in (1, 2, 3)]
    tx = summed(own_tail[TAIL_ROWS:], *[part[TAIL_ROWS:] for part in got_tz]).astype(BF16)
    own_tail = summed(own_tail[:TAIL_ROWS], *[part[:TAIL_ROWS] for part in got_tz])
    got_tx = moved(tx, "x", 1)
    got_dkv = across(dkv[1], 2)
    return (head[0], *got_hz, own_tail, got_tx, vector), (dkv[0], got_dkv)


def lower_lanes(shape):
    return lax.broadcasted_iota(jnp.int32, shape, 1) < HEAD_SIZE


def half_turn(value):
    return pltpu.roll(value, HEAD_SIZE, 1)


def side_by_side(left, right):
    return jnp.where(lower_lanes(left.shape), left, half_turn(right))


def kind_of(block):
    return jnp.where(block >= 24, 1, jnp.where(block >= 8, 0, jnp.where((block == 3) | (block == 4), 2, 1)))


def tile_kernel(kind_ref, flat_ref, head_ref, tail_ref, tiles, narrow):
    kind = kind_ref[0]

    @pl.when(kind == 0)
    def _():
        for j in range(12):
            tiles[72 * j : 72 * j + 72, :] = flat_ref[pl.ds(j, 72, stride=12), :]

    @pl.when(kind == 1)
    def _():
        lines = [flat_ref[pl.ds(t, 96, stride=9), :] for t in range(9)]
        turned = [half_turn(line) for line in lines[4:]]
        low = lower_lanes((96, LANES))
        for j in range(4):
            tiles[pl.ds(192 * j, 96, stride=2), :] = lines[j]
            tiles[pl.ds(192 * j + 1, 96, stride=2), :] = jnp.where(low, turned[j], turned[j + 1])
        narrow[pl.ds(0, 96, stride=2), :] = lines[4]
        narrow[pl.ds(1, 96, stride=2), :] = turned[4]
        tiles[768:864, :] = side_by_side(narrow[0:96, :], narrow[96:192, :])

    @pl.when(kind == 2)
    def _():
        lines = [flat_ref[pl.ds(t, 288, stride=3), :] for t in range(3)]
        first, second = half_turn(lines[1]), half_turn(lines[2])
        tiles[pl.ds(0, 288, stride=2), :] = lines[0]
        tiles[pl.ds(1, 288, stride=2), :] = jnp.where(lower_lanes((288, LANES)), first, second)
        narrow[pl.ds(0, 288, stride=2), :] = lines[1]
        narrow[pl.ds(1, 288, stride=2), :] = second
        tiles[576:864, :] = side_by_side(narrow[0:288, :], narrow[288:576, :])

    head_ref[...] = tiles[0:HEAD_ROWS, :].astype(BF16)
    tail_ref[...] = tiles[HEAD_ROWS:BLOCK_ROWS, :].astype(BF16)


def to_tiles(kind, flat):
    return pl.pallas_call(
        tile_kernel,
        out_shape=(
            jax.ShapeDtypeStruct((HEAD_ROWS, LANES), BF16),
            jax.ShapeDtypeStruct((TAIL_ROWS, LANES), BF16),
        ),
        in_specs=[
            pl.BlockSpec(memory_space=pltpu.SMEM),
            pl.BlockSpec(memory_space=pltpu.VMEM),
        ],
        out_specs=(pl.BlockSpec(memory_space=pltpu.VMEM),) * 2,
        scratch_shapes=[
            pltpu.VMEM((BLOCK_ROWS, LANES), F32),
            pltpu.VMEM((HEAD_ROWS, LANES), F32),
        ],
        name="to_tiles",
    )(kind, flat)


def finish_kernel(table_ref, head_ref, one_ref, two_ref, three_ref, tail_ref, other_ref, mine_ref, *refs):
    kind, place = table_ref[0], table_ref[1]
    tiles, narrow, flat_ref, vector_parts = refs[-4:]
    tokens_ref, gains_ref, w_kv_ref, base_ref, own_dkv, other_dkv = refs[:6]
    states = refs[6:-4]
    tiles[0:HEAD_ROWS, :] = (head_ref[...] + one_ref[0:HEAD_ROWS, :].astype(F32)) + (
        two_ref[0:HEAD_ROWS, :].astype(F32) + three_ref[0:HEAD_ROWS, :].astype(F32)
    )
    tiles[HEAD_ROWS:BLOCK_ROWS, :] = tail_ref[...] + other_ref[...].astype(F32)

    for at, ref in enumerate((mine_ref, one_ref, two_ref, three_ref)):
        rows = ref.shape[0]
        part = ref[rows - 2 * VECTOR_ROWS : rows, :].astype(F32)
        vector_parts[at] = part[:VECTOR_ROWS] + part[VECTOR_ROWS:]
    vector = vector_parts[lax.rem(place, 4)]
    for z in (1, 2, 3):
        vector = vector + vector_parts[lax.rem(place + 4 - z, 4)]

    lane = lax.broadcasted_iota(jnp.int32, (2 * ROWS, WIDE), 1)
    x = jnp.where(lane < MODEL_WIDTH, tokens_ref[...].astype(F32).reshape(2 * ROWS, WIDE), 0.0)
    normed, scale = normed_rows(x)
    total = summed(own_dkv[...], other_dkv[...]).reshape(2 * ROWS, 384).astype(BF16)
    d_norm = times_transposed(total, w_kv_ref[...]) * gains_ref[0:1, :]
    d_input = base_ref[...] + scale * (d_norm - normed * row_mean(d_norm * normed))
    out_ref = states[-1]
    for mb in range(2):
        out_ref[mb] = d_input[ROWS * mb : ROWS * mb + ROWS].T[0:MODEL_WIDTH].astype(BF16)

    @pl.when(kind == 0)
    def _():
        for j in range(12):
            flat_ref[pl.ds(j, 72, stride=12), :] = tiles[72 * j : 72 * j + 72, :]

    @pl.when(kind == 1)
    def _():
        low = lower_lanes((96, LANES))
        narrow[0:96, :] = tiles[768:864, :]
        narrow[96:192, :] = half_turn(tiles[768:864, :])
        odd = [half_turn(tiles[pl.ds(192 * j + 1, 96, stride=2), :]) for j in range(4)]
        for j in range(4):
            flat_ref[pl.ds(j, 96, stride=9), :] = tiles[pl.ds(192 * j, 96, stride=2), :]
        flat_ref[pl.ds(4, 96, stride=9), :] = jnp.where(low, narrow[pl.ds(0, 96, stride=2), :], odd[0])
        for j in range(3):
            flat_ref[pl.ds(5 + j, 96, stride=9), :] = jnp.where(low, odd[j], odd[j + 1])
        last = half_turn(narrow[pl.ds(1, 96, stride=2), :])
        flat_ref[pl.ds(8, 96, stride=9), :] = jnp.where(low, odd[3], last)

    @pl.when(kind == 2)
    def _():
        low = lower_lanes((288, LANES))
        narrow[0:288, :] = tiles[576:864, :]
        narrow[288:576, :] = half_turn(tiles[576:864, :])
        odd = half_turn(tiles[pl.ds(1, 288, stride=2), :])
        flat_ref[pl.ds(0, 288, stride=3), :] = tiles[pl.ds(0, 288, stride=2), :]
        flat_ref[pl.ds(1, 288, stride=3), :] = jnp.where(low, narrow[pl.ds(0, 288, stride=2), :], odd)
        last = half_turn(narrow[pl.ds(1, 288, stride=2), :])
        flat_ref[pl.ds(2, 288, stride=3), :] = jnp.where(low, odd, last)


    if len(states) == 3:
        states[0][...], states[1][...] = flat_ref[...], vector
        return
    old_vectors, old_block, new_vectors, new_block = states[0:3], states[3:6], states[6:9], states[9:12]
    found = adamw(old_vectors[0][...], vector, old_vectors[1][...], old_vectors[2][...], RATE_VECTOR, 0.0)
    for ref, value in zip(new_vectors, found):
        ref[...] = value

    @pl.loop(0, 6)
    def _(k):
        rows = pl.ds(pl.multiple_of(k * 144, 8), 144)
        found = adamw(
            old_block[0][rows, :], flat_ref[rows, :], old_block[1][rows, :], old_block[2][rows, :], RATE_MATRIX, DECAY
        )
        for ref, value in zip(new_block, found):
            ref[rows, :] = value


def finish(table, parts, inputs, state):
    vmem = pl.BlockSpec(memory_space=pltpu.VMEM)
    flat = jax.ShapeDtypeStruct((BLOCK_ROWS, LANES), F32)
    vector = jax.ShapeDtypeStruct((VECTOR_ROWS, LANES), F32)
    shapes = (vector,) * 3 + (flat,) * 3 if state else (flat, vector)
    shapes += (jax.ShapeDtypeStruct((2, MODEL_WIDTH, ROWS), BF16),)
    return pl.pallas_call(
        finish_kernel,
        out_shape=shapes,
        in_specs=[pl.BlockSpec(memory_space=pltpu.SMEM)] + [vmem] * (len(parts) + len(inputs) + len(state)),
        out_specs=(vmem,) * len(shapes),
        scratch_shapes=[
            pltpu.VMEM((BLOCK_ROWS, LANES), F32),
            pltpu.VMEM((HEAD_ROWS, LANES), F32),
            pltpu.VMEM((BLOCK_ROWS, LANES), F32),
            pltpu.VMEM((4, VECTOR_ROWS, LANES), F32),
        ],
        name="finish",
    )(table, *parts, *inputs, *state)


def product(left, right):
    return jnp.dot(left, right, preferred_element_type=F32)


def times_transposed(left, right):
    return lax.dot_general(left, right, (((1,), (1,)), ((), ())), preferred_element_type=F32)


def rows_product(left, right):
    return lax.dot_general(left, right, (((0,), (0,)), ((), ())), preferred_element_type=F32)


def swapped(value):
    lane = lax.broadcasted_iota(jnp.int32, value.shape, 1)
    return jnp.where(lane % HEAD_SIZE < HEAD_SIZE // 2, pltpu.roll(value, 96, 1), pltpu.roll(value, 32, 1))


def rope(value, cosines, sines):
    return value * cosines + swapped(value) * sines


def rope_back(value, cosines, sines):
    return value * cosines - swapped(value) * sines


def row_mean(value):
    return jnp.sum(value, axis=-1, keepdims=True) * (1.0 / MODEL_WIDTH)


def normed_rows(value):
    scale = lax.rsqrt(row_mean(value * value) + EPS_NORM)
    return value * scale, scale


def place_rows(ref, head_tile, tail_tile, first):
    for j in range(3):
        ref[first : first + 192, LANES * j : LANES * j + LANES] = head_tile[192 * j : 192 * j + 192, :]
    ref[first : first + 192, 384:512] = tail_tile[0:192, :]
    rest = tail_tile[192:288, :].astype(F32)
    low = lower_lanes(rest.shape)
    ref[first : first + 96, 512:640] = jnp.where(low, rest, 0.0).astype(BF16)
    ref[first + 96 : first + 192, 512:640] = jnp.where(low, half_turn(rest), 0.0).astype(BF16)


def tiles_of_rows(value):
    head = jnp.concatenate([value[:, LANES * j : LANES * j + LANES] for j in range(3)], axis=0)
    rest = side_by_side(value[0:96, 512:640], value[96:192, 512:640])
    return head, jnp.concatenate([value[:, 384:512], rest], axis=0)


def layer_kernel(*refs):
    slots = refs[0]
    head_parts = refs[1:9]
    tail_parts = refs[9:13]
    tokens_pair, cos_pair, sin_pair = refs[13:15], refs[15:17], refs[17:19]
    (place_q_ref, place_k_ref, gains_ref, bias_q_ref, bias_kv_ref, grad_ref) = refs[19:25]
    block_out_ref, parts_out = refs[25], refs[26:36]
    (dkv_send, dkv_keep, base_ref, w_kv) = refs[36:40]
    (raw_head, raw_tail, w_q, w_out, w_gate, w_up, w_down, normed_all, hidden_all, keys, values, queries, probs, attended, act_all, block_acc, d_hidden, d_attended, dkv_all, d_query, both_all, vector_ref, outs, sems, out_sems) = refs[40:]

    place = slots[MY_Z]

    def fetches(shift, sem):
        at = lax.rem(place + shift, 4)
        copies = []
        for k, part in enumerate(head_parts):
            copies.append(pltpu.make_async_copy(part.at[at], raw_head.at[4 * k + at], sems.at[sem + k]))
        for k, part in enumerate(tail_parts):
            rows = pl.ds(2 * at, 2)
            copies.append(pltpu.make_async_copy(part.at[rows], raw_tail.at[pl.ds(8 * k + 2 * at, 2)], sems.at[sem + 8 + k]))
        return copies

    attention_blocks = fetches(0, 0)
    other_blocks = fetches(1, 12) + fetches(2, 24) + fetches(3, 36)
    for copy in attention_blocks + other_blocks:
        copy.start()

    core = slots[MY_CORE]

    def at_slot(pair, slot):
        return pair[slot % 2].at[slot // 2]

    def head_tile(block):
        return raw_head.at[slots[AT_HEAD + block]]

    def tail_tile(block):
        return raw_tail.at[slots[AT_TAIL + block]]

    gain_one = gains_ref[0:1, :]
    gain_two = gains_ref[1:2, :]
    low_rows = lower_lanes((ROWS, LANES))

    @pl.loop(0, 2)
    def _(mb):
        lane = lax.broadcasted_iota(jnp.int32, (ROWS, WIDE), 1)
        for slot in range(4):
            rows = pl.ds(pl.multiple_of(mb * 512 + slot * ROWS, ROWS), ROWS)
            x = jnp.where(lane < MODEL_WIDTH, at_slot(tokens_pair, slot)[mb].astype(F32), 0.0)
            normed, _ = normed_rows(x)
            normed_all[rows, :] = normed
            hidden_all[rows, :] = (normed * gain_one).astype(BF16)

    for copy in attention_blocks:
        copy.wait()
    for ref in (w_q, w_out, w_gate, w_up, w_kv):
        ref[576:640, :] = jnp.zeros((64, ref.shape[1]), BF16)
    for k in range(3):
        place_rows(w_q, head_tile(k), tail_tile(k), 192 * k)
        place_rows(w_out, head_tile(5 + k), tail_tile(5 + k), 192 * k)
    w_kv[0:576, 0:128] = head_tile(3)[...]
    w_kv[0:576, 128:256] = head_tile(4)[...]
    rest_key = tail_tile(3)[...].astype(F32)
    rest_value = tail_tile(4)[...].astype(F32)
    low = lower_lanes(rest_key.shape)
    w_kv[0:288, 256:384] = jnp.where(low, rest_key, half_turn(rest_value)).astype(BF16)
    w_kv[288:576, 256:384] = jnp.where(low, half_turn(rest_key), rest_value).astype(BF16)

    @pl.loop(0, 2)
    def _(mb):
        rows = pl.ds(pl.multiple_of(mb * 512, 512), 512)
        pair = product(hidden_all[rows, :], w_kv[...]) + bias_kv_ref[...]
        cosines = jnp.concatenate([at_slot(cos_pair, slot)[mb] for slot in range(4)], axis=0)
        sines = jnp.concatenate([at_slot(sin_pair, slot)[mb] for slot in range(4)], axis=0)
        key_a = rope(pair[:, 0:128], cosines, sines)
        key_b = rope(pair[:, 256:384], cosines, sines)
        value_a, value_b = pair[:, 128:256], pair[:, 256:384]
        low_keys = lower_lanes((512, LANES))
        turned = half_turn(key_a)
        keys[rows, 0:128] = jnp.where(low_keys, key_a, turned).astype(BF16)
        keys[rows, 128:256] = jnp.where(low_keys, turned, key_a).astype(BF16)
        keys[rows, 256:384] = jnp.where(low_keys, key_b, half_turn(key_b)).astype(BF16)
        turned = half_turn(value_a)
        values[rows, 0:128] = jnp.where(low_keys, value_a, turned).astype(BF16)
        values[rows, 128:256] = jnp.where(low_keys, turned, value_a).astype(BF16)
        values[rows, 256:384] = jnp.where(low_keys, half_turn(value_b), value_b).astype(BF16)

    def heads_of(ref, rows, group):
        stacked = []
        for k in range(3):
            number = 3 * group + k
            tile = ref[rows, LANES * (number // 2) : LANES * (number // 2) + LANES]
            keep = low_rows if number % 2 == 0 else jnp.logical_not(low_rows)
            stacked.append(jnp.where(keep, tile.astype(F32), 0.0).astype(BF16))
        return jnp.concatenate(stacked, axis=0)

    def tiles_of_heads(parts):
        found = [jnp.where(low_rows, parts[2 * k], parts[2 * k + 1]) for k in range(4)]
        return found + [jnp.where(low_rows, parts[8], 0.0)]

    @pl.loop(0, 2)
    def _(mb):
        rows = pl.ds(pl.multiple_of(mb * ROWS, ROWS), ROWS)
        key_rows = pl.ds(pl.multiple_of(mb * 512, 512), 512)
        cosines, sines = cos_pair[0][0, mb], sin_pair[0][0, mb]
        made = product(hidden_all[pl.ds(pl.multiple_of(mb * 512, 512), ROWS), :], w_q[...]) + bias_q_ref[...]
        for k in range(5):
            turned = rope(made[:, LANES * k : LANES * k + LANES], cosines, sines)
            queries[rows, LANES * k : LANES * k + LANES] = (turned * HEAD_SIZE ** (-0.5)).astype(BF16)
        masked = jnp.where(place_q_ref[mb] >= place_k_ref[mb], 0.0, MASKED)
        masked = jnp.concatenate([masked] * 3, axis=0)
        parts = []
        for group in range(KEY_VALUE_HEADS):
            lanes = slice(LANES * group, LANES * group + LANES)
            scores = times_transposed(heads_of(queries, rows, group), keys[key_rows, lanes])
            scores = scores + masked
            top = jnp.max(scores, axis=-1, keepdims=True)
            powers = jnp.exp(scores - top)
            found = powers * (1.0 / jnp.sum(powers, axis=-1, keepdims=True))
            probs[mb, group] = found
            out = product(found.astype(BF16), values[key_rows, lanes])
            outs[mb, group] = out
            parts += [out[ROWS * k : ROWS * k + ROWS] for k in range(3)]
        for k, tile in enumerate(tiles_of_heads(parts)):
            attended[rows, LANES * k : LANES * k + LANES] = tile.astype(BF16)

    for copy in other_blocks:
        copy.wait()
    for k in range(8):
        place_rows(w_down, head_tile(24 + k), tail_tile(24 + k), 192 * k)
    for ref, base in ((w_gate, 8), (w_up, 16)):
        for k in range(4):
            for i in range(6):
                if i < 4:
                    even = head_tile(base + 2 * k)[144 * i : 144 * i + 144, :].astype(F32)
                    odd = head_tile(base + 2 * k + 1)[144 * i : 144 * i + 144, :].astype(F32)
                else:
                    even = tail_tile(base + 2 * k)[144 * (i - 4) : 144 * (i - 4) + 144, :].astype(F32)
                    odd = tail_tile(base + 2 * k + 1)[144 * (i - 4) : 144 * (i - 4) + 144, :].astype(F32)
                ref[144 * k : 144 * k + 144, 256 * i : 256 * i + 128] = jnp.concatenate(
                    [even[0:72], odd[0:72]], axis=0
                ).astype(BF16)
                ref[144 * k : 144 * k + 144, 256 * i + 128 : 256 * i + 256] = jnp.concatenate(
                    [even[72:144], odd[72:144]], axis=0
                ).astype(BF16)

    lane = lax.broadcasted_iota(jnp.int32, (2 * ROWS, WIDE), 1)
    x_own = tokens_pair[0][0].astype(F32).reshape(2 * ROWS, WIDE)
    x_own = jnp.where(lane < MODEL_WIDTH, x_own, 0.0)
    resid_mid = x_own + product(attended[...], w_out[...])
    normed_two, scale_two = normed_rows(resid_mid)
    hidden_two = (normed_two * gain_two).astype(BF16)
    hidden_turned = hidden_two.T
    grad_low = grad_ref[...]
    block_acc[...] = resid_mid
    d_hidden[...] = jnp.zeros_like(d_hidden)

    def store_pair(at, even, odd, table, first):
        rows = pl.ds(pl.multiple_of(slots[table + at] + first, 16), even.shape[0])
        both_all[1 - core, rows, :] = even.astype(BF16)
        both_all[core, rows, :] = odd.astype(BF16)

    def feed_forward(chunk, first, table):
        cols = slice(chunk * 512, chunk * 512 + 512)
        gate = product(hidden_two, w_gate[:, cols])
        up = product(hidden_two, w_up[:, cols])
        sigma = 1.0 / (1.0 + jnp.exp(-gate))
        act = (gate * sigma * up).astype(BF16)
        act_all[:, cols] = act
        down = w_down[cols, :]
        d_act = times_transposed(grad_low, down)
        block_acc[...] += product(act, down)
        d_up = (d_act * gate * sigma).astype(BF16)
        d_gate = (d_act * up * sigma * (1.0 + gate * (1.0 - sigma))).astype(BF16)
        d_hidden[...] += times_transposed(d_gate, w_gate[:, cols]) + times_transposed(d_up, w_up[:, cols])
        for base, cotangent in ((4, d_gate), (8, d_up)):
            made = product(hidden_turned, cotangent)
            for k in range(4):
                part = made[144 * k : 144 * k + 144, :]
                even = jnp.concatenate([part[0:72, LANES * j : LANES * j + LANES] for j in range(4)], axis=0)
                odd = jnp.concatenate([part[72:144, LANES * j : LANES * j + LANES] for j in range(4)], axis=0)
                store_pair(base + k, even, odd, table, (chunk - first) * 288)

    feed_forward(0, 0, TO_HEAD)
    feed_forward(1, 0, TO_HEAD)
    feed_forward(2, 2, TO_TAIL)

    def store_rows(at, even, odd):
        even_head, even_tail = even
        odd_head, odd_tail = odd
        store_pair(at, even_head, odd_head, TO_HEAD, 0)
        store_pair(at, even_tail, odd_tail, TO_TAIL, 0)

    @pl.loop(0, 4)
    def _(k):
        made = rows_product(act_all[:, pl.ds(pl.multiple_of(k * 384, 128), 384)], grad_low)
        store_rows(12 + k, tiles_of_rows(made[0:192]), tiles_of_rows(made[192:384]))

    def deliveries(first, count, sem):
        copies = []
        for base, outs_of in ((both_all.at[0], parts_out[0:4]), (both_all.at[1], parts_out[4:10])):
            rest = [(outs_of[2], PART * k) for k in range(3)] if len(outs_of) == 4 else [(out, 0) for out in outs_of[2:5]]
            targets = [(outs_of[0], 0, FIRST_AT), (outs_of[1], 0, TAIL_AT)]
            targets += [(out, into, PART * k) for k, (out, into) in enumerate(rest)]
            targets.append((outs_of[-1], 0, 3 * PART))
            for out, into, start in targets:
                rows = HEAD_ROWS * count
                copies.append(
                    pltpu.make_async_copy(
                        base.at[pl.ds(start + HEAD_ROWS * first, rows)],
                        out.at[pl.ds(into + HEAD_ROWS * first, rows)],
                        out_sems.at[sem + len(copies)],
                    )
                )
        return copies

    early = deliveries(1, 3, 12)
    for copy in early:
        copy.start()

    for mb in range(2):
        block_out_ref[mb] = block_acc[ROWS * mb : ROWS * mb + ROWS, :].T[0:MODEL_WIDTH].astype(BF16)

    d_two = d_hidden[...]
    gain_two_sum = jnp.sum(d_two * normed_two, axis=0, keepdims=True)
    d_norm = d_two * gain_two
    d_mid = grad_low.astype(F32) + scale_two * (d_norm - normed_two * row_mean(d_norm * normed_two))
    d_branch = d_mid.astype(BF16)
    d_attended[...] = times_transposed(d_branch, w_out[...]).astype(BF16)
    grad_out = rows_product(attended[...], d_branch)

    @pl.loop(0, 2)
    def _(mb):
        rows = pl.ds(pl.multiple_of(mb * ROWS, ROWS), ROWS)
        key_rows = pl.ds(pl.multiple_of(mb * 512, 512), 512)
        parts = []
        d_keys = []
        d_values = []
        for group in range(KEY_VALUE_HEADS):
            lanes = slice(LANES * group, LANES * group + LANES)
            query_rows = heads_of(queries, rows, group)
            cotangent = heads_of(d_attended, rows, group)
            found = probs[mb, group]
            d_probs = times_transposed(cotangent, values[key_rows, lanes])
            delta = jnp.sum(outs[mb, group] * cotangent.astype(F32), axis=-1, keepdims=True)
            d_scores = (found * (d_probs - delta)).astype(BF16)
            out = product(d_scores, keys[key_rows, lanes]) * HEAD_SIZE ** (-0.5)
            parts += [out[ROWS * k : ROWS * k + ROWS] for k in range(3)]
            d_key = rows_product(d_scores, query_rows)
            d_value = rows_product(found.astype(BF16), cotangent)
            d_keys.append(d_key + half_turn(d_key))
            d_values.append(d_value + half_turn(d_value))
        cosines, sines = cos_pair[0][0, mb], sin_pair[0][0, mb]
        for k, tile in enumerate(tiles_of_heads(parts)):
            d_query[rows, LANES * k : LANES * k + LANES] = rope_back(tile, cosines, sines).astype(BF16)
        low_keys = lower_lanes((512, LANES))
        cosines = jnp.concatenate([at_slot(cos_pair, slot)[mb] for slot in range(4)], axis=0)
        sines = jnp.concatenate([at_slot(sin_pair, slot)[mb] for slot in range(4)], axis=0)
        key_a = rope_back(jnp.where(low_keys, d_keys[0], d_keys[1]), cosines, sines)
        key_b = rope_back(d_keys[2], cosines, sines)
        dkv_all[key_rows, 0:128] = key_a.astype(BF16)
        dkv_all[key_rows, 128:256] = jnp.where(low_keys, d_values[0], d_values[1]).astype(BF16)
        dkv_all[key_rows, 256:384] = jnp.where(low_keys, key_b, d_values[2]).astype(BF16)
        for slot in range(4):
            target = dkv_send if slot % 2 else dkv_keep
            target[slot // 2, mb] = dkv_all[pl.ds(pl.multiple_of(mb * 512 + slot * ROWS, ROWS), ROWS), :]

    dkv = dkv_all[...]
    d_q = d_query[...]
    dq_wq = times_transposed(d_q, w_q[...])
    normed = jnp.concatenate([normed_all[512 * mb : 512 * mb + ROWS, :] for mb in range(2)], axis=0)
    scale = lax.rsqrt(row_mean(x_own * x_own) + EPS_NORM)
    d_norm = dq_wq * gain_one
    base_ref[...] = d_mid + scale * (d_norm - normed * row_mean(d_norm * normed))
    bias_q_sum = jnp.sum(d_q.astype(F32), axis=0, keepdims=True)
    bias_kv_sum = jnp.sum(dkv.astype(F32), axis=0, keepdims=True)
    gain_sum = jnp.zeros((1, WIDE), F32)
    for mb in range(2):
        gain_sum += jnp.sum(dq_wq[ROWS * mb : ROWS * mb + ROWS] * normed_all[512 * mb : 512 * mb + ROWS, :], axis=0, keepdims=True)
    for k in range(4):
        part = slice(256 * k, 256 * k + 256)
        gain_sum += jnp.sum(times_transposed(dkv_all[part, :], w_kv[...]) * normed_all[part, :], axis=0, keepdims=True)

    hidden_own = jnp.concatenate([hidden_all[0:ROWS, :], hidden_all[512 : 512 + ROWS, :]], axis=0)
    grad_q = rows_product(hidden_own, d_q)
    grad_kv = rows_product(hidden_all[...], dkv)
    rest = grad_kv[0:576, 256:384]
    low = lower_lanes((288, LANES))
    key_tiles = (grad_kv[0:576, 0:128], jnp.where(low, rest[0:288], half_turn(rest[288:576])))
    value_tiles = (grad_kv[0:576, 128:256], jnp.where(low, half_turn(rest[0:288]), rest[288:576]))
    query_tiles = [tiles_of_rows(grad_q[192 * k : 192 * k + 192]) for k in range(3)]
    out_tiles = [tiles_of_rows(grad_out[192 * k : 192 * k + 192]) for k in range(3)]
    store_rows(0, query_tiles[0], query_tiles[1])
    store_rows(1, query_tiles[2], key_tiles)
    store_rows(2, value_tiles, out_tiles[0])
    store_rows(3, out_tiles[1], out_tiles[2])
    def flat_rows(first, second, third, pair):
        tile = lambda row, k: row[:, LANES * k : LANES * k + LANES]
        low = lower_lanes((1, LANES))
        across_two = lambda one, two: jnp.where(low, half_turn(one), half_turn(two))
        lines = [tile(first, k) for k in range(4)]
        lines.append(side_by_side(tile(first, 4), tile(second, 0)))
        lines += [across_two(tile(second, k), tile(second, k + 1)) for k in range(4)]
        lines += [tile(third, k) for k in range(4)]
        lines.append(side_by_side(tile(third, 4), tile(pair, 0)))
        lines.append(across_two(tile(pair, 0), tile(pair, 2)))
        lines.append(tile(pair, 1))
        lines.append(jnp.where(low, half_turn(tile(pair, 2)), 0.0))
        return lines

    at = FIRST_AT + PART
    for row, line in enumerate(flat_rows(gain_sum, gain_two_sum, bias_q_sum, bias_kv_sum)):
        vector_ref[row : row + 1, :] = line
    vector_ref[17:24, :] = jnp.zeros((7, LANES), F32)
    vector = vector_ref[...]
    high = vector.astype(BF16).astype(F32)
    both = jnp.concatenate([high, vector - high], axis=0).astype(BF16)
    for k in range(2):
        both_all[k, at : at + 2 * VECTOR_ROWS, :] = both
    last = deliveries(0, 1, 0)
    last.append(pltpu.make_async_copy(both_all.at[0, pl.ds(at, 2 * VECTOR_ROWS)], parts_out[0].at[pl.ds(PART, 2 * VECTOR_ROWS)], out_sems.at[24]))
    last.append(pltpu.make_async_copy(both_all.at[1, pl.ds(at, 2 * VECTOR_ROWS)], parts_out[4].at[pl.ds(PART, 2 * VECTOR_ROWS)], out_sems.at[25]))
    for copy in last:
        copy.start()
    for copy in early + last:
        copy.wait()


def run_layer(slots, heads, tails, *others):
    shape = jax.ShapeDtypeStruct
    vmem = pl.BlockSpec(memory_space=pltpu.VMEM)
    anywhere = pl.BlockSpec(memory_space=pl.ANY)
    scratch = [
        ((BLOCKS, HEAD_ROWS, LANES), BF16),
        ((BLOCKS, TAIL_ROWS, LANES), BF16),
        ((WIDE, WIDE), BF16),
        ((WIDE, WIDE), BF16),
        ((WIDE, FF), BF16),
        ((WIDE, FF), BF16),
        ((FF, WIDE), BF16),
        ((1024, WIDE), F32),
        ((1024, WIDE), BF16),
        ((1024, 384), BF16),
        ((1024, 384), BF16),
        ((256, WIDE), BF16),
        ((2, 3, 384, 512), F32),
        ((256, WIDE), BF16),
        ((256, FF), BF16),
        ((256, WIDE), F32),
        ((256, WIDE), F32),
        ((256, WIDE), BF16),
        ((1024, 384), BF16),
        ((256, WIDE), BF16),
        ((2, ALL_ROWS, LANES), BF16),
        ((VECTOR_ROWS, LANES), F32),
        ((2, 3, 384, LANES), F32),
    ]
    return pl.pallas_call(
        layer_kernel,
        out_shape=(
            shape((2, MODEL_WIDTH, ROWS), BF16),
            *[shape((count, LANES), BF16) for _, count in SEND_PARTS + KEEP_PARTS],
            shape((2, 2, ROWS, 384), BF16),
            shape((2, 2, ROWS, 384), BF16),
            shape((256, WIDE), F32),
            shape((WIDE, 384), BF16),
        ),
        in_specs=[pl.BlockSpec(memory_space=pltpu.SMEM)] + [anywhere] * 12 + [vmem] * 12,
        out_specs=(vmem,) + (anywhere,) * 10 + (vmem,) * 4,
        scratch_shapes=[pltpu.VMEM(dims, kind) for dims, kind in scratch]
        + [pltpu.SemaphoreType.DMA((48,)), pltpu.SemaphoreType.DMA((26,))],
        compiler_params=pltpu.CompilerParams(vmem_limit_bytes=50 * 1024 * 1024),
        name="layer",
    )(slots, *heads, *tails, *others)


def adamw(param, grad, mom_one, mom_two, rate, decay):
    new_one = BETA_ONE * mom_one + (1.0 - BETA_ONE) * grad
    new_two = BETA_TWO * mom_two + (1.0 - BETA_TWO) * grad * grad
    fixed_one = new_one / (1.0 - BETA_ONE**STEP)
    fixed_two = new_two / (1.0 - BETA_TWO**STEP)
    new_param = param - rate * (fixed_one / (jnp.sqrt(fixed_two) + EPS_ADAM) + decay * param)
    return (new_param, new_one, new_two)


def inner_groups():
    inner = inner_count()
    data_inner = inner // lax.axis_size("ctx")
    data_count = lax.axis_size("dp")
    return [list(range(k, k + data_inner)) for k in range(0, data_count, data_inner)]


def whole_block(flat):
    if inner_count() == 1:
        return flat
    flat = lax.all_gather(flat, "ctx", axis=0, tiled=True)
    return lax.all_gather(flat, "dp", axis=0, tiled=True, axis_index_groups=inner_groups())


def own_slice(block):
    if inner_count() == 1:
        return block
    block = lax.psum_scatter(
        block, "dp", scatter_dimension=0, tiled=True, axis_index_groups=inner_groups()
    )
    return lax.psum_scatter(block, "ctx", scatter_dimension=0, tiled=True)


def bias_tiles(bias_key, bias_value):
    return jnp.concatenate([bias_key[:128], bias_value[:128], bias_key[128:], bias_value[128:]])


def local(tokens_in, places, out_grad, weights, first_moment, second_moment, vectors, vector_first, vector_second):
    kind = kind_of(device_number() // inner_count()).astype(jnp.int32).reshape(1)
    block = whole_block(weights).reshape(BLOCK_ROWS, LANES)
    head, tail = to_tiles(kind, block)

    head, tail, tokens_in, places = together(head, tail, tokens_in, places)
    own_tokens = tokens_in.reshape(2, ROWS, MODEL_WIDTH)
    own_places = places.reshape(2, ROWS)
    marks = jnp.stack([own_places // 16, own_places % 16], axis=-1).astype(BF16)
    packed = jnp.concatenate(
        [own_tokens, marks, jnp.zeros((2, ROWS, WIDE - MODEL_WIDTH - 2), BF16)], axis=-1
    )
    padding = ((0, 0), (0, WIDE - MODEL_WIDTH))
    gains = jnp.pad(vectors[: 2 * MODEL_WIDTH].reshape(2, MODEL_WIDTH), padding)
    bias_q = jnp.pad(vectors[2 * MODEL_WIDTH : 3 * MODEL_WIDTH].reshape(1, MODEL_WIDTH), padding)
    bias_kv = bias_tiles(vectors[1728:1920], vectors[1920:2112]).reshape(1, 384)
    grad = jnp.pad(out_grad.reshape(2 * ROWS, MODEL_WIDTH), padding)
    spare = VECTOR_ROWS * LANES - vectors.shape[0]
    vector_state = [
        jnp.pad(array, (0, spare), constant_values=1.0).reshape(VECTOR_ROWS, LANES)
        for array in (vectors, vector_first, vector_second)
    ]
    table = jnp.concatenate([kind, (coordinates(device_number() // inner_count())["z"]).astype(jnp.int32).reshape(1)])
    others = (slot_table(), gains, bias_q, bias_kv, grad, vector_state, table)
    heads, tails, (near, far), (cosines, sines), others = gather_all(head, tail, packed, others)
    slots, gains, bias_q, bias_kv, grad, vector_state, table = others
    cosines_far, sines_far = place_tables(far)
    place_all = jnp.stack([places_of(near), places_of(far)], axis=1)
    place_q = place_all[0, 0][..., None]
    place_k = jnp.transpose(place_all.reshape(4, 2, ROWS), (1, 0, 2)).reshape(2, 1, 4 * ROWS)

    block_out, *found = run_layer(
        slots, heads, tails, near, far, cosines, cosines_far, sines, sines_far, place_q, place_k, gains, bias_q, bias_kv, grad
    )
    sends, keeps = found[:4], found[4:10]
    dkv_send, dkv_keep, base, w_kv = found[10:]
    parts, pairs = scatter_blocks(sends, keeps, dkv_send, dkv_keep)
    inputs = (packed, gains, w_kv, base, *pairs)
    state = (weights, first_moment, second_moment)
    if inner_count() == 1:
        blocks = [array.reshape(BLOCK_ROWS, LANES) for array in state]
        *updated, input_grad = finish(table, parts, inputs, [*vector_state, *blocks])
        new_vector_state = [array.reshape(-1)[: vectors.shape[0]] for array in updated[:3]]
        new_state = [array.reshape(-1) for array in updated[3:]]
    else:
        block_grad, vector, input_grad = finish(table, parts, inputs, [])
        vector = lax.psum(vector, "ctx")
        vector = lax.psum(vector, "dp", axis_index_groups=inner_groups())
        grad_own = own_slice(block_grad.reshape(-1))
        vector_grad = vector.reshape(-1)[: vectors.shape[0]]
        new_state = adamw(weights, grad_own, first_moment, second_moment, RATE_MATRIX, DECAY)
        new_vector_state = adamw(vectors, vector_grad, vector_first, vector_second, RATE_VECTOR, 0.0)
    shape = tokens_in.shape
    return (
        jnp.transpose(block_out, (0, 2, 1)).reshape(shape),
        jnp.transpose(input_grad, (0, 2, 1)).reshape(shape),
        *new_state,
        *new_vector_state,
    )


def solution(mesh):
    in_specs = (
        P(None, "dp", "ctx", None),
        P(None, "dp", "ctx"),
        P(None, "dp", "ctx", None),
        P(("dp", "ctx")),
        P(("dp", "ctx")),
        P(("dp", "ctx")),
        P(),
        P(),
        P(),
    )
    out_specs = (
        P(None, "dp", "ctx", None),
        P(None, "dp", "ctx", None),
        P(("dp", "ctx")),
        P(("dp", "ctx")),
        P(("dp", "ctx")),
        P(),
        P(),
        P(),
    )
    return jax.shard_map(local, mesh=mesh, in_specs=in_specs, out_specs=out_specs, check_vma=False)
```

```python
import jax
import jax.numpy as jnp
from jax import lax
from jax.experimental import pallas as pl
from jax.experimental.pallas import tpu as pltpu
from jax.sharding import PartitionSpec as P

MODEL_WIDTH = 576
QUERY_HEADS = 9
KEY_VALUE_HEADS = 3
HEAD_SIZE = 64
FF = 1536
STEP = 10

EPS_NORM = 1e-05
THETA = 100000.0
BETA_ONE = 0.9
BETA_TWO = 0.95
EPS_ADAM = 1e-08
RATE_MATRIX = 0.06
RATE_VECTOR = 0.3
DECAY = 0.1
MASKED = -1e30

LANES = 128
WIDE = 640
BLOCKS = 32
BLOCK_ROWS = 864
HEAD_ROWS = 576
TAIL_ROWS = BLOCK_ROWS - HEAD_ROWS
VECTOR_ROWS = 24
PART = 4 * HEAD_ROWS
FIRST_AT = 4 * PART
TAIL_AT = FIRST_AT + PART + 2 * VECTOR_ROWS
ALL_ROWS = TAIL_AT + PART
SEND_PARTS = [(FIRST_AT, PART + 2 * VECTOR_ROWS), (TAIL_AT, PART), (0, 3 * PART), (3 * PART, PART)]
KEEP_PARTS = SEND_PARTS[:2] + [(PART * k, PART) for k in range(4)]
SIZES = {"z": 4, "y": 2, "x": 2, "c": 2}
ROWS = 128
F32 = jnp.float32
BF16 = jnp.bfloat16


def coordinates(number):
    found = {}
    for name in ("c", "x", "y", "z"):
        found[name] = number % SIZES[name]
        number = number // SIZES[name]
    return found


def number_of(found):
    number = 0
    for name in ("z", "y", "x", "c"):
        number = number * SIZES[name] + found[name]
    return number


def device_number():
    return lax.axis_index("dp") * lax.axis_size("ctx") + lax.axis_index("ctx")


def inner_count():
    return lax.axis_size("dp") * lax.axis_size("ctx") // BLOCKS


def moved(buffer, name, shift):
    inner = inner_count()
    pairs = []
    for number in range(BLOCKS):
        found = coordinates(number)
        found[name] = (found[name] + shift) % SIZES[name]
        target = number_of(found)
        pairs += [(number * inner + k, target * inner + k) for k in range(inner)]
    return lax.ppermute(buffer, ("dp", "ctx"), pairs)


def across(buffer, distance):
    count = lax.axis_size("ctx")
    return lax.ppermute(buffer, "ctx", [(i, i ^ distance) for i in range(count)])


def together(*arrays):
    return lax.optimization_barrier(arrays)


def gather_all(head, tail, packed, others):
    hz = [moved(head, "z", s) for s in (1, 2, 3)]
    tx = moved(tail, "x", 1)
    two = across(packed, 2)
    head, tail, tx, two, *hz = together(head, tail, tx, two, *hz)
    own = jnp.stack([head] + hz)
    pair = jnp.stack([tail, tx])
    ay = moved(own, "y", 1)
    ax = moved(own, "x", 1)
    tz = [moved(pair, "z", s) for s in (1, 2, 3)]
    near = jnp.stack([packed, two])
    tables = place_tables(near)
    own, pair, ay, ax, near, tables, others, *tz = together(own, pair, ay, ax, near, tables, others, *tz)
    eight = jnp.concatenate([pair] + tz)
    far = across(near, 1)
    axy = moved(ay, "x", 1)
    ty = moved(eight, "y", 1)
    ac = moved(own, "c", 1)
    acy = moved(ay, "c", 1)
    acx = moved(ax, "c", 1)
    tc = moved(eight, "c", 1)
    axy, ty, ac, acy, acx, tc, far = together(axy, ty, ac, acy, acx, tc, far)
    acxy = moved(axy, "c", 1)
    tcy = moved(ty, "c", 1)
    heads = [own, ay, ax, axy, ac, acy, acx, acxy]
    return heads, [eight, ty, tc, tcy], (near, far), tables, others


def places_of(tokens):
    found = tokens[..., MODEL_WIDTH : MODEL_WIDTH + 2].astype(F32)
    return found[..., 0] * 16.0 + found[..., 1]


def place_tables(tokens):
    half_dim = HEAD_SIZE // 2
    frequency = THETA ** (-2.0 * jnp.arange(half_dim, dtype=F32) / HEAD_SIZE)
    angles = places_of(tokens)[..., None] * jnp.tile(frequency, 4)
    sign = jnp.where(jnp.arange(LANES) % HEAD_SIZE < half_dim, -1.0, 1.0).astype(F32)
    return jnp.cos(angles), jnp.sin(angles) * sign


def fold(order, relative):
    slot = 0
    for name in order:
        slot = slot * SIZES[name] + relative[name]
    return slot


def head_row(slot, z, _):
    return slot * PART + jnp.where(slot < 3, 0, FIRST_AT - 3 * PART) + z * HEAD_ROWS


def tail_row(slot, z, inside):
    return jnp.where(slot < 1, 3 * PART, TAIL_AT) + (2 * z + inside) * TAIL_ROWS


def slot_table():
    mine = coordinates(device_number() // inner_count())
    entries = []
    for order in (("c", "x", "y", "z"), ("c", "y", "z", "x")):
        for number in range(BLOCKS):
            found = coordinates(number)
            entries.append(fold(order, {n: (mine[n] - found[n]) % SIZES[n] for n in SIZES}))
    for order, start in ((("x", "y"), head_row), (("y",), tail_row)):
        for number in range(0, BLOCKS, 2):
            found = coordinates(number)
            slot = fold(order, {n: (found[n] - mine[n]) % SIZES[n] for n in SIZES})
            inside = (found["x"] - mine["x"]) % SIZES["x"]
            entries.append(start(slot, (found["z"] - mine["z"]) % SIZES["z"], inside))
    entries.append(mine["c"])
    entries.append(mine["z"])
    return jnp.stack([jnp.asarray(entry, jnp.int32) for entry in entries])


AT_HEAD, AT_TAIL, TO_HEAD, TO_TAIL = 0, BLOCKS, 2 * BLOCKS, 2 * BLOCKS + 16
MY_CORE, MY_Z = 2 * BLOCKS + 32, 2 * BLOCKS + 33


def summed(*parts):
    total = parts[0].astype(F32)
    for part in parts[1:]:
        total = total + part.astype(F32)
    return total


def summed_vector(mine, other):
    total = summed(mine[:VECTOR_ROWS], other[:VECTOR_ROWS]) + summed(mine[VECTOR_ROWS:], other[VECTOR_ROWS:])
    high = lax.reduce_precision(total, 8, 7)
    return jnp.concatenate([high.astype(BF16), (total - high).astype(BF16)])


def scatter_blocks(sends, keeps, dkv_send, dkv_keep):
    keep_head, keep_tail, keep_low, keep_mid, keep_far, keep_rest = keeps
    got_head, got_tail = moved(sends[0], "c", 1), moved(sends[1], "c", 1)
    got_head, got_tail, rest_head, rest_tail, dkv_send = together(got_head, got_tail, *sends[2:], dkv_send)
    got_rest_head, got_rest_tail = moved(rest_head, "c", 1), moved(rest_tail, "c", 1)
    got_dkv = across(dkv_send, 1)
    vector = summed_vector(keep_head[PART:], got_head[PART:])
    hx = jnp.concatenate([summed(keep_head[:PART], got_head[:PART]).astype(BF16), vector])
    ty = summed(keep_tail, got_tail).astype(BF16)
    got_hx = moved(hx, "x", 1)
    got_ty = moved(ty, "y", 1)
    low, mid, far = [
        summed(keep, got_rest_head[PART * k : PART * k + PART]).astype(BF16)
        for k, keep in enumerate((keep_low, keep_mid, keep_far))
    ]
    tail = summed(keep_rest, got_rest_tail).astype(BF16)
    dkv = summed(dkv_keep, got_dkv).astype(BF16)
    got_hx, got_ty, low, mid, far, tail, dkv, vector = together(got_hx, got_ty, low, mid, far, tail, dkv, vector)

    def part_for(array, shift):
        return array[HEAD_ROWS * shift : HEAD_ROWS * shift + HEAD_ROWS]

    vector = summed_vector(vector, got_hx[PART:])
    hy = jnp.concatenate([summed(mid, got_hx[:PART]).astype(BF16), vector])
    tz = [summed(part_for(tail, s), part_for(got_ty, s)).astype(BF16) for s in range(4)]
    got_hy = moved(hy, "y", 1)
    got_far = moved(far, "x", 1)
    got_tz = [moved(tz[s], "z", s) for s in (1, 2, 3)]
    got_hy, got_far, low, own_tail, vector, dkv, *got_tz = together(got_hy, got_far, low, tz[0], vector, dkv, *got_tz)
    vector = summed_vector(vector, got_hy[PART:])
    head = [summed(part_for(low, s), part_for(got_far, s), part_for(got_hy, s)) for s in range(4)]
    got_hz = [moved(jnp.concatenate([head[s].astype(BF16), vector]), "z", s) for s in (1, 2, 3)]
    tx = summed(own_tail[TAIL_ROWS:], *[part[TAIL_ROWS:] for part in got_tz]).astype(BF16)
    own_tail = summed(own_tail[:TAIL_ROWS], *[part[:TAIL_ROWS] for part in got_tz])
    got_tx = moved(tx, "x", 1)
    got_dkv = across(dkv[1], 2)
    return (head[0], *got_hz, own_tail, got_tx, vector), (dkv[0], got_dkv)


def lower_lanes(shape):
    return lax.broadcasted_iota(jnp.int32, shape, 1) < HEAD_SIZE


def half_turn(value):
    return pltpu.roll(value, HEAD_SIZE, 1)


def side_by_side(left, right):
    return jnp.where(lower_lanes(left.shape), left, half_turn(right))


def kind_of(block):
    return jnp.where(block >= 24, 1, jnp.where(block >= 8, 0, jnp.where((block == 3) | (block == 4), 2, 1)))


def tile_kernel(kind_ref, flat_ref, head_ref, tail_ref, tiles, narrow):
    kind = kind_ref[0]

    @pl.when(kind == 0)
    def _():
        for j in range(12):
            tiles[72 * j : 72 * j + 72, :] = flat_ref[pl.ds(j, 72, stride=12), :]

    @pl.when(kind == 1)
    def _():
        lines = [flat_ref[pl.ds(t, 96, stride=9), :] for t in range(9)]
        turned = [half_turn(line) for line in lines[4:]]
        low = lower_lanes((96, LANES))
        for j in range(4):
            tiles[pl.ds(192 * j, 96, stride=2), :] = lines[j]
            tiles[pl.ds(192 * j + 1, 96, stride=2), :] = jnp.where(low, turned[j], turned[j + 1])
        narrow[pl.ds(0, 96, stride=2), :] = lines[4]
        narrow[pl.ds(1, 96, stride=2), :] = turned[4]
        tiles[768:864, :] = side_by_side(narrow[0:96, :], narrow[96:192, :])

    @pl.when(kind == 2)
    def _():
        lines = [flat_ref[pl.ds(t, 288, stride=3), :] for t in range(3)]
        first, second = half_turn(lines[1]), half_turn(lines[2])
        tiles[pl.ds(0, 288, stride=2), :] = lines[0]
        tiles[pl.ds(1, 288, stride=2), :] = jnp.where(lower_lanes((288, LANES)), first, second)
        narrow[pl.ds(0, 288, stride=2), :] = lines[1]
        narrow[pl.ds(1, 288, stride=2), :] = second
        tiles[576:864, :] = side_by_side(narrow[0:288, :], narrow[288:576, :])

    head_ref[...] = tiles[0:HEAD_ROWS, :].astype(BF16)
    tail_ref[...] = tiles[HEAD_ROWS:BLOCK_ROWS, :].astype(BF16)


def to_tiles(kind, flat):
    return pl.pallas_call(
        tile_kernel,
        out_shape=(
            jax.ShapeDtypeStruct((HEAD_ROWS, LANES), BF16),
            jax.ShapeDtypeStruct((TAIL_ROWS, LANES), BF16),
        ),
        in_specs=[
            pl.BlockSpec(memory_space=pltpu.SMEM),
            pl.BlockSpec(memory_space=pltpu.VMEM),
        ],
        out_specs=(pl.BlockSpec(memory_space=pltpu.VMEM),) * 2,
        scratch_shapes=[
            pltpu.VMEM((BLOCK_ROWS, LANES), F32),
            pltpu.VMEM((HEAD_ROWS, LANES), F32),
        ],
        name="to_tiles",
    )(kind, flat)


def finish_kernel(table_ref, head_ref, one_ref, two_ref, three_ref, tail_ref, other_ref, mine_ref, *refs):
    kind, place = table_ref[0], table_ref[1]
    tiles, narrow, flat_ref, vector_parts = refs[-4:]
    tokens_ref, gains_ref, w_kv_ref, base_ref, own_dkv, other_dkv = refs[:6]
    states = refs[6:-4]
    tiles[0:HEAD_ROWS, :] = (head_ref[...] + one_ref[0:HEAD_ROWS, :].astype(F32)) + (
        two_ref[0:HEAD_ROWS, :].astype(F32) + three_ref[0:HEAD_ROWS, :].astype(F32)
    )
    tiles[HEAD_ROWS:BLOCK_ROWS, :] = tail_ref[...] + other_ref[...].astype(F32)

    for at, ref in enumerate((mine_ref, one_ref, two_ref, three_ref)):
        rows = ref.shape[0]
        part = ref[rows - 2 * VECTOR_ROWS : rows, :].astype(F32)
        vector_parts[at] = part[:VECTOR_ROWS] + part[VECTOR_ROWS:]
    vector = vector_parts[lax.rem(place, 4)]
    for z in (1, 2, 3):
        vector = vector + vector_parts[lax.rem(place + 4 - z, 4)]

    lane = lax.broadcasted_iota(jnp.int32, (2 * ROWS, WIDE), 1)
    x = jnp.where(lane < MODEL_WIDTH, tokens_ref[...].astype(F32).reshape(2 * ROWS, WIDE), 0.0)
    normed, scale = normed_rows(x)
    total = summed(own_dkv[...], other_dkv[...]).reshape(2 * ROWS, 384).astype(BF16)
    d_norm = times_transposed(total, w_kv_ref[...]) * gains_ref[0:1, :]
    d_input = base_ref[...] + scale * (d_norm - normed * row_mean(d_norm * normed))
    out_ref = states[-1]
    for mb in range(2):
        out_ref[mb] = d_input[ROWS * mb : ROWS * mb + ROWS].T[0:MODEL_WIDTH].astype(BF16)

    @pl.when(kind == 0)
    def _():
        for j in range(12):
            flat_ref[pl.ds(j, 72, stride=12), :] = tiles[72 * j : 72 * j + 72, :]

    @pl.when(kind == 1)
    def _():
        low = lower_lanes((96, LANES))
        narrow[0:96, :] = tiles[768:864, :]
        narrow[96:192, :] = half_turn(tiles[768:864, :])
        odd = [half_turn(tiles[pl.ds(192 * j + 1, 96, stride=2), :]) for j in range(4)]
        for j in range(4):
            flat_ref[pl.ds(j, 96, stride=9), :] = tiles[pl.ds(192 * j, 96, stride=2), :]
        flat_ref[pl.ds(4, 96, stride=9), :] = jnp.where(low, narrow[pl.ds(0, 96, stride=2), :], odd[0])
        for j in range(3):
            flat_ref[pl.ds(5 + j, 96, stride=9), :] = jnp.where(low, odd[j], odd[j + 1])
        last = half_turn(narrow[pl.ds(1, 96, stride=2), :])
        flat_ref[pl.ds(8, 96, stride=9), :] = jnp.where(low, odd[3], last)

    @pl.when(kind == 2)
    def _():
        low = lower_lanes((288, LANES))
        narrow[0:288, :] = tiles[576:864, :]
        narrow[288:576, :] = half_turn(tiles[576:864, :])
        odd = half_turn(tiles[pl.ds(1, 288, stride=2), :])
        flat_ref[pl.ds(0, 288, stride=3), :] = tiles[pl.ds(0, 288, stride=2), :]
        flat_ref[pl.ds(1, 288, stride=3), :] = jnp.where(low, narrow[pl.ds(0, 288, stride=2), :], odd)
        last = half_turn(narrow[pl.ds(1, 288, stride=2), :])
        flat_ref[pl.ds(2, 288, stride=3), :] = jnp.where(low, odd, last)


    if len(states) == 3:
        states[0][...], states[1][...] = flat_ref[...], vector
        return
    old_vectors, old_block, new_vectors, new_block = states[0:3], states[3:6], states[6:9], states[9:12]
    found = adamw(old_vectors[0][...], vector, old_vectors[1][...], old_vectors[2][...], RATE_VECTOR, 0.0)
    for ref, value in zip(new_vectors, found):
        ref[...] = value

    @pl.loop(0, 6)
    def _(k):
        rows = pl.ds(pl.multiple_of(k * 144, 8), 144)
        found = adamw(
            old_block[0][rows, :], flat_ref[rows, :], old_block[1][rows, :], old_block[2][rows, :], RATE_MATRIX, DECAY
        )
        for ref, value in zip(new_block, found):
            ref[rows, :] = value


def finish(table, parts, inputs, state):
    vmem = pl.BlockSpec(memory_space=pltpu.VMEM)
    flat = jax.ShapeDtypeStruct((BLOCK_ROWS, LANES), F32)
    vector = jax.ShapeDtypeStruct((VECTOR_ROWS, LANES), F32)
    shapes = (vector,) * 3 + (flat,) * 3 if state else (flat, vector)
    shapes += (jax.ShapeDtypeStruct((2, MODEL_WIDTH, ROWS), BF16),)
    return pl.pallas_call(
        finish_kernel,
        out_shape=shapes,
        in_specs=[pl.BlockSpec(memory_space=pltpu.SMEM)] + [vmem] * (len(parts) + len(inputs) + len(state)),
        out_specs=(vmem,) * len(shapes),
        scratch_shapes=[
            pltpu.VMEM((BLOCK_ROWS, LANES), F32),
            pltpu.VMEM((HEAD_ROWS, LANES), F32),
            pltpu.VMEM((BLOCK_ROWS, LANES), F32),
            pltpu.VMEM((4, VECTOR_ROWS, LANES), F32),
        ],
        name="finish",
    )(table, *parts, *inputs, *state)


def product(left, right):
    return jnp.dot(left, right, preferred_element_type=F32)


def times_transposed(left, right):
    return lax.dot_general(left, right, (((1,), (1,)), ((), ())), preferred_element_type=F32)


def rows_product(left, right):
    return lax.dot_general(left, right, (((0,), (0,)), ((), ())), preferred_element_type=F32)


def swapped(value):
    lane = lax.broadcasted_iota(jnp.int32, value.shape, 1)
    return jnp.where(lane % HEAD_SIZE < HEAD_SIZE // 2, pltpu.roll(value, 96, 1), pltpu.roll(value, 32, 1))


def rope(value, cosines, sines):
    return value * cosines + swapped(value) * sines


def rope_back(value, cosines, sines):
    return value * cosines - swapped(value) * sines


def row_mean(value):
    return jnp.sum(value, axis=-1, keepdims=True) * (1.0 / MODEL_WIDTH)


def normed_rows(value):
    scale = lax.rsqrt(row_mean(value * value) + EPS_NORM)
    return value * scale, scale


def place_rows(ref, head_tile, tail_tile, first):
    for j in range(3):
        ref[first : first + 192, LANES * j : LANES * j + LANES] = head_tile[192 * j : 192 * j + 192, :]
    ref[first : first + 192, 384:512] = tail_tile[0:192, :]
    rest = tail_tile[192:288, :].astype(F32)
    low = lower_lanes(rest.shape)
    ref[first : first + 96, 512:640] = jnp.where(low, rest, 0.0).astype(BF16)
    ref[first + 96 : first + 192, 512:640] = jnp.where(low, half_turn(rest), 0.0).astype(BF16)


def tiles_of_rows(value):
    head = jnp.concatenate([value[:, LANES * j : LANES * j + LANES] for j in range(3)], axis=0)
    rest = side_by_side(value[0:96, 512:640], value[96:192, 512:640])
    return head, jnp.concatenate([value[:, 384:512], rest], axis=0)


def layer_kernel(*refs):
    slots = refs[0]
    head_parts = refs[1:9]
    tail_parts = refs[9:13]
    tokens_pair, cos_pair, sin_pair = refs[13:15], refs[15:17], refs[17:19]
    (place_q_ref, place_k_ref, gains_ref, bias_q_ref, bias_kv_ref, grad_ref) = refs[19:25]
    block_out_ref, parts_out = refs[25], refs[26:36]
    (dkv_send, dkv_keep, base_ref, w_kv) = refs[36:40]
    (raw_head, raw_tail, w_q, w_out, w_gate, w_up, w_down, normed_all, hidden_all, keys, values, queries, probs, attended, act_all, block_acc, d_hidden, d_attended, dkv_all, d_query, both_all, vector_ref, outs, sems, out_sems) = refs[40:]

    place = slots[MY_Z]

    def fetches(shift, sem):
        at = lax.rem(place + shift, 4)
        copies = []
        for k, part in enumerate(head_parts):
            copies.append(pltpu.make_async_copy(part.at[at], raw_head.at[4 * k + at], sems.at[sem + k]))
        for k, part in enumerate(tail_parts):
            rows = pl.ds(2 * at, 2)
            copies.append(pltpu.make_async_copy(part.at[rows], raw_tail.at[pl.ds(8 * k + 2 * at, 2)], sems.at[sem + 8 + k]))
        return copies

    attention_blocks = fetches(0, 0)
    other_blocks = fetches(1, 12) + fetches(2, 24) + fetches(3, 36)
    for copy in attention_blocks + other_blocks:
        copy.start()

    core = slots[MY_CORE]

    def at_slot(pair, slot):
        return pair[slot % 2].at[slot // 2]

    def head_tile(block):
        return raw_head.at[slots[AT_HEAD + block]]

    def tail_tile(block):
        return raw_tail.at[slots[AT_TAIL + block]]

    gain_one = gains_ref[0:1, :]
    gain_two = gains_ref[1:2, :]
    low_rows = lower_lanes((ROWS, LANES))

    for mb in range(0, 2):
        lane = lax.broadcasted_iota(jnp.int32, (ROWS, WIDE), 1)
        for slot in range(4):
            rows = pl.ds(mb * 512 + slot * ROWS, ROWS)
            x = jnp.where(lane < MODEL_WIDTH, at_slot(tokens_pair, slot)[mb].astype(F32), 0.0)
            normed, _ = normed_rows(x)
            normed_all[rows, :] = normed
            hidden_all[rows, :] = (normed * gain_one).astype(BF16)

    for copy in attention_blocks:
        copy.wait()
    for ref in (w_q, w_out, w_gate, w_up, w_kv):
        ref[576:640, :] = jnp.zeros((64, ref.shape[1]), BF16)
    for k in range(3):
        place_rows(w_q, head_tile(k), tail_tile(k), 192 * k)
        place_rows(w_out, head_tile(5 + k), tail_tile(5 + k), 192 * k)
    w_kv[0:576, 0:128] = head_tile(3)[...]
    w_kv[0:576, 128:256] = head_tile(4)[...]
    rest_key = tail_tile(3)[...].astype(F32)
    rest_value = tail_tile(4)[...].astype(F32)
    low = lower_lanes(rest_key.shape)
    w_kv[0:288, 256:384] = jnp.where(low, rest_key, half_turn(rest_value)).astype(BF16)
    w_kv[288:576, 256:384] = jnp.where(low, half_turn(rest_key), rest_value).astype(BF16)

    for mb in range(0, 2):
        rows = pl.ds(mb * 512, 512)
        pair = product(hidden_all[rows, :], w_kv[...]) + bias_kv_ref[...]
        cosines = jnp.concatenate([at_slot(cos_pair, slot)[mb] for slot in range(4)], axis=0)
        sines = jnp.concatenate([at_slot(sin_pair, slot)[mb] for slot in range(4)], axis=0)
        key_a = rope(pair[:, 0:128], cosines, sines)
        key_b = rope(pair[:, 256:384], cosines, sines)
        value_a, value_b = pair[:, 128:256], pair[:, 256:384]
        low_keys = lower_lanes((512, LANES))
        turned = half_turn(key_a)
        keys[rows, 0:128] = jnp.where(low_keys, key_a, turned).astype(BF16)
        keys[rows, 128:256] = jnp.where(low_keys, turned, key_a).astype(BF16)
        keys[rows, 256:384] = jnp.where(low_keys, key_b, half_turn(key_b)).astype(BF16)
        turned = half_turn(value_a)
        values[rows, 0:128] = jnp.where(low_keys, value_a, turned).astype(BF16)
        values[rows, 128:256] = jnp.where(low_keys, turned, value_a).astype(BF16)
        values[rows, 256:384] = jnp.where(low_keys, half_turn(value_b), value_b).astype(BF16)

    def heads_of(ref, rows, group):
        stacked = []
        for k in range(3):
            number = 3 * group + k
            tile = ref[rows, LANES * (number // 2) : LANES * (number // 2) + LANES]
            keep = low_rows if number % 2 == 0 else jnp.logical_not(low_rows)
            stacked.append(jnp.where(keep, tile.astype(F32), 0.0).astype(BF16))
        return jnp.concatenate(stacked, axis=0)

    def tiles_of_heads(parts):
        found = [jnp.where(low_rows, parts[2 * k], parts[2 * k + 1]) for k in range(4)]
        return found + [jnp.where(low_rows, parts[8], 0.0)]

    for mb in range(0, 2):
        rows = pl.ds(mb * ROWS, ROWS)
        key_rows = pl.ds(mb * 512, 512)
        cosines, sines = cos_pair[0][0, mb], sin_pair[0][0, mb]
        made = product(hidden_all[pl.ds(mb * 512, ROWS), :], w_q[...]) + bias_q_ref[...]
        for k in range(5):
            turned = rope(made[:, LANES * k : LANES * k + LANES], cosines, sines)
            queries[rows, LANES * k : LANES * k + LANES] = (turned * HEAD_SIZE ** (-0.5)).astype(BF16)
        masked = jnp.where(place_q_ref[mb] >= place_k_ref[mb], 0.0, MASKED)
        masked = jnp.concatenate([masked] * 3, axis=0)
        parts = []
        for group in range(KEY_VALUE_HEADS):
            lanes = slice(LANES * group, LANES * group + LANES)
            scores = times_transposed(heads_of(queries, rows, group), keys[key_rows, lanes])
            scores = scores + masked
            top = jnp.max(scores, axis=-1, keepdims=True)
            powers = jnp.exp(scores - top)
            found = powers * (1.0 / jnp.sum(powers, axis=-1, keepdims=True))
            probs[mb, group] = found
            out = product(found.astype(BF16), values[key_rows, lanes])
            outs[mb, group] = out
            parts += [out[ROWS * k : ROWS * k + ROWS] for k in range(3)]
        for k, tile in enumerate(tiles_of_heads(parts)):
            attended[rows, LANES * k : LANES * k + LANES] = tile.astype(BF16)

    for copy in other_blocks:
        copy.wait()
    for k in range(8):
        place_rows(w_down, head_tile(24 + k), tail_tile(24 + k), 192 * k)
    for ref, base in ((w_gate, 8), (w_up, 16)):
        for k in range(4):
            for i in range(6):
                if i < 4:
                    even = head_tile(base + 2 * k)[144 * i : 144 * i + 144, :].astype(F32)
                    odd = head_tile(base + 2 * k + 1)[144 * i : 144 * i + 144, :].astype(F32)
                else:
                    even = tail_tile(base + 2 * k)[144 * (i - 4) : 144 * (i - 4) + 144, :].astype(F32)
                    odd = tail_tile(base + 2 * k + 1)[144 * (i - 4) : 144 * (i - 4) + 144, :].astype(F32)
                ref[144 * k : 144 * k + 144, 256 * i : 256 * i + 128] = jnp.concatenate(
                    [even[0:72], odd[0:72]], axis=0
                ).astype(BF16)
                ref[144 * k : 144 * k + 144, 256 * i + 128 : 256 * i + 256] = jnp.concatenate(
                    [even[72:144], odd[72:144]], axis=0
                ).astype(BF16)

    lane = lax.broadcasted_iota(jnp.int32, (2 * ROWS, WIDE), 1)
    x_own = tokens_pair[0][0].astype(F32).reshape(2 * ROWS, WIDE)
    x_own = jnp.where(lane < MODEL_WIDTH, x_own, 0.0)
    resid_mid = x_own + product(attended[...], w_out[...])
    normed_two, scale_two = normed_rows(resid_mid)
    hidden_two = (normed_two * gain_two).astype(BF16)
    hidden_turned = hidden_two.T
    grad_low = grad_ref[...]
    block_acc[...] = resid_mid
    d_hidden[...] = jnp.zeros_like(d_hidden)

    def store_pair(at, even, odd, table, first):
        rows = pl.ds(pl.multiple_of(slots[table + at] + first, 16), even.shape[0])
        both_all[1 - core, rows, :] = even.astype(BF16)
        both_all[core, rows, :] = odd.astype(BF16)

    def feed_forward(chunk, first, table):
        cols = slice(chunk * 512, chunk * 512 + 512)
        gate = product(hidden_two, w_gate[:, cols])
        up = product(hidden_two, w_up[:, cols])
        sigma = 1.0 / (1.0 + jnp.exp(-gate))
        act = (gate * sigma * up).astype(BF16)
        act_all[:, cols] = act
        down = w_down[cols, :]
        d_act = times_transposed(grad_low, down)
        block_acc[...] += product(act, down)
        d_up = (d_act * gate * sigma).astype(BF16)
        d_gate = (d_act * up * sigma * (1.0 + gate * (1.0 - sigma))).astype(BF16)
        d_hidden[...] += times_transposed(d_gate, w_gate[:, cols]) + times_transposed(d_up, w_up[:, cols])
        for base, cotangent in ((4, d_gate), (8, d_up)):
            made = product(hidden_turned, cotangent)
            for k in range(4):
                part = made[144 * k : 144 * k + 144, :]
                even = jnp.concatenate([part[0:72, LANES * j : LANES * j + LANES] for j in range(4)], axis=0)
                odd = jnp.concatenate([part[72:144, LANES * j : LANES * j + LANES] for j in range(4)], axis=0)
                store_pair(base + k, even, odd, table, (chunk - first) * 288)

    feed_forward(0, 0, TO_HEAD)
    feed_forward(1, 0, TO_HEAD)
    feed_forward(2, 2, TO_TAIL)

    def store_rows(at, even, odd):
        even_head, even_tail = even
        odd_head, odd_tail = odd
        store_pair(at, even_head, odd_head, TO_HEAD, 0)
        store_pair(at, even_tail, odd_tail, TO_TAIL, 0)

    for k in range(0, 4):
        made = rows_product(act_all[:, pl.ds(k * 384, 384)], grad_low)
        store_rows(12 + k, tiles_of_rows(made[0:192]), tiles_of_rows(made[192:384]))

    def deliveries(z, sem):
        copies = []
        inside = pl.multiple_of(HEAD_ROWS * lax.rem(z + 4 - place, 4), HEAD_ROWS)
        for base, outs_of in ((both_all.at[0], parts_out[0:4]), (both_all.at[1], parts_out[4:10])):
            rest = [(outs_of[2], PART * k) for k in range(3)] if len(outs_of) == 4 else [(out, 0) for out in outs_of[2:5]]
            targets = [(outs_of[0], 0, FIRST_AT), (outs_of[1], 0, TAIL_AT)]
            targets += [(out, into, PART * k) for k, (out, into) in enumerate(rest)]
            targets.append((outs_of[-1], 0, 3 * PART))
            for out, into, start in targets:
                copies.append(
                    pltpu.make_async_copy(
                        base.at[pl.ds(pl.multiple_of(start + inside, 16), HEAD_ROWS)],
                        out.at[pl.ds(pl.multiple_of(into + inside, 16), HEAD_ROWS)],
                        out_sems.at[sem + len(copies)],
                    )
                )
        return copies

    early = deliveries(1, 12) + deliveries(2, 24) + deliveries(3, 36)
    for copy in early:
        copy.start()

    for mb in range(2):
        block_out_ref[mb] = block_acc[ROWS * mb : ROWS * mb + ROWS, :].T[0:MODEL_WIDTH].astype(BF16)

    d_two = d_hidden[...]
    gain_two_sum = jnp.sum(d_two * normed_two, axis=0, keepdims=True)
    d_norm = d_two * gain_two
    d_mid = grad_low.astype(F32) + scale_two * (d_norm - normed_two * row_mean(d_norm * normed_two))
    d_branch = d_mid.astype(BF16)
    d_attended[...] = times_transposed(d_branch, w_out[...]).astype(BF16)
    grad_out = rows_product(attended[...], d_branch)

    for mb in range(0, 2):
        rows = pl.ds(mb * ROWS, ROWS)
        key_rows = pl.ds(mb * 512, 512)
        parts = []
        d_keys = []
        d_values = []
        for group in range(KEY_VALUE_HEADS):
            lanes = slice(LANES * group, LANES * group + LANES)
            query_rows = heads_of(queries, rows, group)
            cotangent = heads_of(d_attended, rows, group)
            found = probs[mb, group]
            d_probs = times_transposed(cotangent, values[key_rows, lanes])
            delta = jnp.sum(outs[mb, group] * cotangent.astype(F32), axis=-1, keepdims=True)
            d_scores = (found * (d_probs - delta)).astype(BF16)
            out = product(d_scores, keys[key_rows, lanes]) * HEAD_SIZE ** (-0.5)
            parts += [out[ROWS * k : ROWS * k + ROWS] for k in range(3)]
            d_key = rows_product(d_scores, query_rows)
            d_value = rows_product(found.astype(BF16), cotangent)
            d_keys.append(d_key + half_turn(d_key))
            d_values.append(d_value + half_turn(d_value))
        cosines, sines = cos_pair[0][0, mb], sin_pair[0][0, mb]
        for k, tile in enumerate(tiles_of_heads(parts)):
            d_query[rows, LANES * k : LANES * k + LANES] = rope_back(tile, cosines, sines).astype(BF16)
        low_keys = lower_lanes((512, LANES))
        cosines = jnp.concatenate([at_slot(cos_pair, slot)[mb] for slot in range(4)], axis=0)
        sines = jnp.concatenate([at_slot(sin_pair, slot)[mb] for slot in range(4)], axis=0)
        key_a = rope_back(jnp.where(low_keys, d_keys[0], d_keys[1]), cosines, sines)
        key_b = rope_back(d_keys[2], cosines, sines)
        dkv_all[key_rows, 0:128] = key_a.astype(BF16)
        dkv_all[key_rows, 128:256] = jnp.where(low_keys, d_values[0], d_values[1]).astype(BF16)
        dkv_all[key_rows, 256:384] = jnp.where(low_keys, key_b, d_values[2]).astype(BF16)
        for slot in range(4):
            target = dkv_send if slot % 2 else dkv_keep
            target[slot // 2, mb] = dkv_all[pl.ds(mb * 512 + slot * ROWS, ROWS), :]

    dkv = dkv_all[...]
    d_q = d_query[...]
    dq_wq = times_transposed(d_q, w_q[...])
    normed = jnp.concatenate([normed_all[512 * mb : 512 * mb + ROWS, :] for mb in range(2)], axis=0)
    scale = lax.rsqrt(row_mean(x_own * x_own) + EPS_NORM)
    d_norm = dq_wq * gain_one
    base_ref[...] = d_mid + scale * (d_norm - normed * row_mean(d_norm * normed))
    bias_q_sum = jnp.sum(d_q.astype(F32), axis=0, keepdims=True)
    bias_kv_sum = jnp.sum(dkv.astype(F32), axis=0, keepdims=True)
    gain_sum = jnp.zeros((1, WIDE), F32)
    for mb in range(2):
        gain_sum += jnp.sum(dq_wq[ROWS * mb : ROWS * mb + ROWS] * normed_all[512 * mb : 512 * mb + ROWS, :], axis=0, keepdims=True)
    for k in range(4):
        part = slice(256 * k, 256 * k + 256)
        gain_sum += jnp.sum(times_transposed(dkv_all[part, :], w_kv[...]) * normed_all[part, :], axis=0, keepdims=True)

    hidden_own = jnp.concatenate([hidden_all[0:ROWS, :], hidden_all[512 : 512 + ROWS, :]], axis=0)
    grad_q = rows_product(hidden_own, d_q)
    grad_kv = rows_product(hidden_all[...], dkv)
    rest = grad_kv[0:576, 256:384]
    low = lower_lanes((288, LANES))
    key_tiles = (grad_kv[0:576, 0:128], jnp.where(low, rest[0:288], half_turn(rest[288:576])))
    value_tiles = (grad_kv[0:576, 128:256], jnp.where(low, half_turn(rest[0:288]), rest[288:576]))
    query_tiles = [tiles_of_rows(grad_q[192 * k : 192 * k + 192]) for k in range(3)]
    out_tiles = [tiles_of_rows(grad_out[192 * k : 192 * k + 192]) for k in range(3)]
    store_rows(0, query_tiles[0], query_tiles[1])
    store_rows(1, query_tiles[2], key_tiles)
    store_rows(2, value_tiles, out_tiles[0])
    store_rows(3, out_tiles[1], out_tiles[2])
    def flat_rows(first, second, third, pair):
        tile = lambda row, k: row[:, LANES * k : LANES * k + LANES]
        low = lower_lanes((1, LANES))
        across_two = lambda one, two: jnp.where(low, half_turn(one), half_turn(two))
        lines = [tile(first, k) for k in range(4)]
        lines.append(side_by_side(tile(first, 4), tile(second, 0)))
        lines += [across_two(tile(second, k), tile(second, k + 1)) for k in range(4)]
        lines += [tile(third, k) for k in range(4)]
        lines.append(side_by_side(tile(third, 4), tile(pair, 0)))
        lines.append(across_two(tile(pair, 0), tile(pair, 2)))
        lines.append(tile(pair, 1))
        lines.append(jnp.where(low, half_turn(tile(pair, 2)), 0.0))
        return lines

    at = FIRST_AT + PART
    for row, line in enumerate(flat_rows(gain_sum, gain_two_sum, bias_q_sum, bias_kv_sum)):
        vector_ref[row : row + 1, :] = line
    vector_ref[17:24, :] = jnp.zeros((7, LANES), F32)
    vector = vector_ref[...]
    high = vector.astype(BF16).astype(F32)
    both = jnp.concatenate([high, vector - high], axis=0).astype(BF16)
    for k in range(2):
        both_all[k, at : at + 2 * VECTOR_ROWS, :] = both
    last = deliveries(0, 0)
    last.append(pltpu.make_async_copy(both_all.at[0, pl.ds(at, 2 * VECTOR_ROWS)], parts_out[0].at[pl.ds(PART, 2 * VECTOR_ROWS)], out_sems.at[48]))
    last.append(pltpu.make_async_copy(both_all.at[1, pl.ds(at, 2 * VECTOR_ROWS)], parts_out[4].at[pl.ds(PART, 2 * VECTOR_ROWS)], out_sems.at[49]))
    for copy in last:
        copy.start()
    for copy in early + last:
        copy.wait()


def run_layer(slots, heads, tails, *others):
    shape = jax.ShapeDtypeStruct
    vmem = pl.BlockSpec(memory_space=pltpu.VMEM)
    anywhere = pl.BlockSpec(memory_space=pl.ANY)
    scratch = [
        ((BLOCKS, HEAD_ROWS, LANES), BF16),
        ((BLOCKS, TAIL_ROWS, LANES), BF16),
        ((WIDE, WIDE), BF16),
        ((WIDE, WIDE), BF16),
        ((WIDE, FF), BF16),
        ((WIDE, FF), BF16),
        ((FF, WIDE), BF16),
        ((1024, WIDE), F32),
        ((1024, WIDE), BF16),
        ((1024, 384), BF16),
        ((1024, 384), BF16),
        ((256, WIDE), BF16),
        ((2, 3, 384, 512), F32),
        ((256, WIDE), BF16),
        ((256, FF), BF16),
        ((256, WIDE), F32),
        ((256, WIDE), F32),
        ((256, WIDE), BF16),
        ((1024, 384), BF16),
        ((256, WIDE), BF16),
        ((2, ALL_ROWS, LANES), BF16),
        ((VECTOR_ROWS, LANES), F32),
        ((2, 3, 384, LANES), F32),
    ]
    return pl.pallas_call(
        layer_kernel,
        out_shape=(
            shape((2, MODEL_WIDTH, ROWS), BF16),
            *[shape((count, LANES), BF16) for _, count in SEND_PARTS + KEEP_PARTS],
            shape((2, 2, ROWS, 384), BF16),
            shape((2, 2, ROWS, 384), BF16),
            shape((256, WIDE), F32),
            shape((WIDE, 384), BF16),
        ),
        in_specs=[pl.BlockSpec(memory_space=pltpu.SMEM)] + [anywhere] * 12 + [vmem] * 12,
        out_specs=(vmem,) + (anywhere,) * 10 + (vmem,) * 4,
        scratch_shapes=[pltpu.VMEM(dims, kind) for dims, kind in scratch]
        + [pltpu.SemaphoreType.DMA((48,)), pltpu.SemaphoreType.DMA((50,))],
        compiler_params=pltpu.CompilerParams(vmem_limit_bytes=50 * 1024 * 1024),
        name="layer",
    )(slots, *heads, *tails, *others)


def adamw(param, grad, mom_one, mom_two, rate, decay):
    new_one = BETA_ONE * mom_one + (1.0 - BETA_ONE) * grad
    new_two = BETA_TWO * mom_two + (1.0 - BETA_TWO) * grad * grad
    fixed_one = new_one / (1.0 - BETA_ONE**STEP)
    fixed_two = new_two / (1.0 - BETA_TWO**STEP)
    new_param = param - rate * (fixed_one / (jnp.sqrt(fixed_two) + EPS_ADAM) + decay * param)
    return (new_param, new_one, new_two)


def inner_groups():
    inner = inner_count()
    data_inner = inner // lax.axis_size("ctx")
    data_count = lax.axis_size("dp")
    return [list(range(k, k + data_inner)) for k in range(0, data_count, data_inner)]


def whole_block(flat):
    if inner_count() == 1:
        return flat
    flat = lax.all_gather(flat, "ctx", axis=0, tiled=True)
    return lax.all_gather(flat, "dp", axis=0, tiled=True, axis_index_groups=inner_groups())


def own_slice(block):
    if inner_count() == 1:
        return block
    block = lax.psum_scatter(
        block, "dp", scatter_dimension=0, tiled=True, axis_index_groups=inner_groups()
    )
    return lax.psum_scatter(block, "ctx", scatter_dimension=0, tiled=True)


def bias_tiles(bias_key, bias_value):
    return jnp.concatenate([bias_key[:128], bias_value[:128], bias_key[128:], bias_value[128:]])


def local(tokens_in, places, out_grad, weights, first_moment, second_moment, vectors, vector_first, vector_second):
    kind = kind_of(device_number() // inner_count()).astype(jnp.int32).reshape(1)
    block = whole_block(weights).reshape(BLOCK_ROWS, LANES)
    head, tail = to_tiles(kind, block)

    head, tail, tokens_in, places = together(head, tail, tokens_in, places)
    own_tokens = tokens_in.reshape(2, ROWS, MODEL_WIDTH)
    own_places = places.reshape(2, ROWS)
    marks = jnp.stack([own_places // 16, own_places % 16], axis=-1).astype(BF16)
    packed = jnp.concatenate(
        [own_tokens, marks, jnp.zeros((2, ROWS, WIDE - MODEL_WIDTH - 2), BF16)], axis=-1
    )
    padding = ((0, 0), (0, WIDE - MODEL_WIDTH))
    gains = jnp.pad(vectors[: 2 * MODEL_WIDTH].reshape(2, MODEL_WIDTH), padding)
    bias_q = jnp.pad(vectors[2 * MODEL_WIDTH : 3 * MODEL_WIDTH].reshape(1, MODEL_WIDTH), padding)
    bias_kv = bias_tiles(vectors[1728:1920], vectors[1920:2112]).reshape(1, 384)
    grad = jnp.pad(out_grad.reshape(2 * ROWS, MODEL_WIDTH), padding)
    spare = VECTOR_ROWS * LANES - vectors.shape[0]
    vector_state = [
        jnp.pad(array, (0, spare), constant_values=1.0).reshape(VECTOR_ROWS, LANES)
        for array in (vectors, vector_first, vector_second)
    ]
    table = jnp.concatenate([kind, (coordinates(device_number() // inner_count())["z"]).astype(jnp.int32).reshape(1)])
    others = (slot_table(), gains, bias_q, bias_kv, grad, vector_state, table)
    heads, tails, (near, far), (cosines, sines), others = gather_all(head, tail, packed, others)
    slots, gains, bias_q, bias_kv, grad, vector_state, table = others
    cosines_far, sines_far = place_tables(far)
    place_all = jnp.stack([places_of(near), places_of(far)], axis=1)
    place_q = place_all[0, 0][..., None]
    place_k = jnp.transpose(place_all.reshape(4, 2, ROWS), (1, 0, 2)).reshape(2, 1, 4 * ROWS)

    block_out, *found = run_layer(
        slots, heads, tails, near, far, cosines, cosines_far, sines, sines_far, place_q, place_k, gains, bias_q, bias_kv, grad
    )
    sends, keeps = found[:4], found[4:10]
    dkv_send, dkv_keep, base, w_kv = found[10:]
    parts, pairs = scatter_blocks(sends, keeps, dkv_send, dkv_keep)
    inputs = (packed, gains, w_kv, base, *pairs)
    state = (weights, first_moment, second_moment)
    if inner_count() == 1:
        blocks = [array.reshape(BLOCK_ROWS, LANES) for array in state]
        *updated, input_grad = finish(table, parts, inputs, [*vector_state, *blocks])
        new_vector_state = [array.reshape(-1)[: vectors.shape[0]] for array in updated[:3]]
        new_state = [array.reshape(-1) for array in updated[3:]]
    else:
        block_grad, vector, input_grad = finish(table, parts, inputs, [])
        vector = lax.psum(vector, "ctx")
        vector = lax.psum(vector, "dp", axis_index_groups=inner_groups())
        grad_own = own_slice(block_grad.reshape(-1))
        vector_grad = vector.reshape(-1)[: vectors.shape[0]]
        new_state = adamw(weights, grad_own, first_moment, second_moment, RATE_MATRIX, DECAY)
        new_vector_state = adamw(vectors, vector_grad, vector_first, vector_second, RATE_VECTOR, 0.0)
    shape = tokens_in.shape
    return (
        jnp.transpose(block_out, (0, 2, 1)).reshape(shape),
        jnp.transpose(input_grad, (0, 2, 1)).reshape(shape),
        *new_state,
        *new_vector_state,
    )


def solution(mesh):
    in_specs = (
        P(None, "dp", "ctx", None),
        P(None, "dp", "ctx"),
        P(None, "dp", "ctx", None),
        P(("dp", "ctx")),
        P(("dp", "ctx")),
        P(("dp", "ctx")),
        P(),
        P(),
        P(),
    )
    out_specs = (
        P(None, "dp", "ctx", None),
        P(None, "dp", "ctx", None),
        P(("dp", "ctx")),
        P(("dp", "ctx")),
        P(("dp", "ctx")),
        P(),
        P(),
        P(),
    )
    return jax.shard_map(local, mesh=mesh, in_specs=in_specs, out_specs=out_specs, check_vma=False)
```

```python
import jax
import jax.numpy as jnp
from jax import lax
from jax.experimental import pallas as pl
from jax.experimental.pallas import tpu as pltpu
from jax.sharding import PartitionSpec as P

MODEL_WIDTH = 576
QUERY_HEADS = 9
KEY_VALUE_HEADS = 3
HEAD_SIZE = 64
FF = 1536
STEP = 10

EPS_NORM = 1e-05
THETA = 100000.0
BETA_ONE = 0.9
BETA_TWO = 0.95
EPS_ADAM = 1e-08
RATE_MATRIX = 0.06
RATE_VECTOR = 0.3
DECAY = 0.1
MASKED = -1e30

LANES = 128
WIDE = 640
BLOCKS = 32
BLOCK_ROWS = 864
HEAD_ROWS = 576
TAIL_ROWS = BLOCK_ROWS - HEAD_ROWS
VECTOR_ROWS = 24
PART = 4 * HEAD_ROWS
FIRST_AT = 4 * PART
TAIL_AT = FIRST_AT + PART + 2 * VECTOR_ROWS
ALL_ROWS = TAIL_AT + PART
SEND_PARTS = [(FIRST_AT, PART + 2 * VECTOR_ROWS), (TAIL_AT, PART), (0, 3 * PART), (3 * PART, PART)]
KEEP_PARTS = SEND_PARTS[:2] + [(PART * k, PART) for k in range(4)]
SIZES = {"z": 4, "y": 2, "x": 2, "c": 2}
ROWS = 128
F32 = jnp.float32
BF16 = jnp.bfloat16


def coordinates(number):
    found = {}
    for name in ("c", "x", "y", "z"):
        found[name] = number % SIZES[name]
        number = number // SIZES[name]
    return found


def number_of(found):
    number = 0
    for name in ("z", "y", "x", "c"):
        number = number * SIZES[name] + found[name]
    return number


def device_number():
    return lax.axis_index("dp") * lax.axis_size("ctx") + lax.axis_index("ctx")


def inner_count():
    return lax.axis_size("dp") * lax.axis_size("ctx") // BLOCKS


def moved(buffer, name, shift):
    inner = inner_count()
    pairs = []
    for number in range(BLOCKS):
        found = coordinates(number)
        found[name] = (found[name] + shift) % SIZES[name]
        target = number_of(found)
        pairs += [(number * inner + k, target * inner + k) for k in range(inner)]
    return lax.ppermute(buffer, ("dp", "ctx"), pairs)


def across(buffer, distance):
    count = lax.axis_size("ctx")
    return lax.ppermute(buffer, "ctx", [(i, i ^ distance) for i in range(count)])


def together(*arrays):
    return lax.optimization_barrier(arrays)


def gather_all(head, tail, packed, others):
    hz = [moved(head, "z", s) for s in (1, 2, 3)]
    tx = moved(tail, "x", 1)
    two = across(packed, 2)
    head, tail, tx, two, *hz = together(head, tail, tx, two, *hz)
    own = jnp.stack([head] + hz)
    pair = jnp.stack([tail, tx])
    ay = moved(own, "y", 1)
    ax = moved(own, "x", 1)
    near = jnp.stack([packed, two])
    tables = place_tables(near)
    pair, *tables = together(pair, *tables)
    tz = [moved(pair, "z", s) for s in (1, 2, 3)]
    own, pair, ay, ax, near, tables, others, *tz = together(own, pair, ay, ax, near, tables, others, *tz)
    eight = jnp.concatenate([pair] + tz)
    far = across(near, 1)
    axy = moved(ay, "x", 1)
    ty = moved(eight, "y", 1)
    ac = moved(own, "c", 1)
    acy = moved(ay, "c", 1)
    acx = moved(ax, "c", 1)
    tc = moved(eight, "c", 1)
    tc, acx, acy, ac, far, ty, axy = together(tc, acx, acy, ac, far, ty, axy)
    acxy = moved(axy, "c", 1)
    tcy = moved(ty, "c", 1)
    heads = [own, ay, ax, axy, ac, acy, acx, acxy]
    return heads, [eight, ty, tc, tcy], (near, far), tables, others


def places_of(tokens):
    found = tokens[..., MODEL_WIDTH : MODEL_WIDTH + 2].astype(F32)
    return found[..., 0] * 16.0 + found[..., 1]


def place_tables(tokens):
    half_dim = HEAD_SIZE // 2
    frequency = THETA ** (-2.0 * jnp.arange(half_dim, dtype=F32) / HEAD_SIZE)
    angles = places_of(tokens)[..., None] * jnp.tile(frequency, 4)
    sign = jnp.where(jnp.arange(LANES) % HEAD_SIZE < half_dim, -1.0, 1.0).astype(F32)
    return jnp.cos(angles), jnp.sin(angles) * sign


def fold(order, relative):
    slot = 0
    for name in order:
        slot = slot * SIZES[name] + relative[name]
    return slot


def head_row(slot, z, _):
    return slot * PART + jnp.where(slot < 3, 0, FIRST_AT - 3 * PART) + z * HEAD_ROWS


def tail_row(slot, z, inside):
    return jnp.where(slot < 1, 3 * PART, TAIL_AT) + (2 * z + inside) * TAIL_ROWS


def slot_table():
    mine = coordinates(device_number() // inner_count())
    entries = []
    for order in (("c", "x", "y", "z"), ("c", "y", "z", "x")):
        for number in range(BLOCKS):
            found = coordinates(number)
            entries.append(fold(order, {n: (mine[n] - found[n]) % SIZES[n] for n in SIZES}))
    for order, start in ((("x", "y"), head_row), (("y",), tail_row)):
        for number in range(0, BLOCKS, 2):
            found = coordinates(number)
            slot = fold(order, {n: (found[n] - mine[n]) % SIZES[n] for n in SIZES})
            inside = (found["x"] - mine["x"]) % SIZES["x"]
            entries.append(start(slot, (found["z"] - mine["z"]) % SIZES["z"], inside))
    entries.append(mine["c"])
    entries.append(mine["z"])
    return jnp.stack([jnp.asarray(entry, jnp.int32) for entry in entries])


AT_HEAD, AT_TAIL, TO_HEAD, TO_TAIL = 0, BLOCKS, 2 * BLOCKS, 2 * BLOCKS + 16
MY_CORE, MY_Z = 2 * BLOCKS + 32, 2 * BLOCKS + 33


def summed(*parts):
    total = parts[0].astype(F32)
    for part in parts[1:]:
        total = total + part.astype(F32)
    return total


def summed_vector(mine, other):
    total = summed(mine[:VECTOR_ROWS], other[:VECTOR_ROWS]) + summed(mine[VECTOR_ROWS:], other[VECTOR_ROWS:])
    high = lax.reduce_precision(total, 8, 7)
    return jnp.concatenate([high.astype(BF16), (total - high).astype(BF16)])


def scatter_blocks(sends, keeps, dkv_send, dkv_keep):
    keep_head, keep_tail, keep_low, keep_mid, keep_far, keep_rest = keeps
    got_head, got_tail = moved(sends[0], "c", 1), moved(sends[1], "c", 1)
    got_head, got_tail, rest_head, rest_tail, dkv_send = together(got_head, got_tail, *sends[2:], dkv_send)
    got_rest_head, got_rest_tail = moved(rest_head, "c", 1), moved(rest_tail, "c", 1)
    got_dkv = across(dkv_send, 1)
    vector = summed_vector(keep_head[PART:], got_head[PART:])
    hx = jnp.concatenate([summed(keep_head[:PART], got_head[:PART]).astype(BF16), vector])
    ty = summed(keep_tail, got_tail).astype(BF16)
    got_hx = moved(hx, "x", 1)
    got_ty = moved(ty, "y", 1)
    low, mid, far = [
        summed(keep, got_rest_head[PART * k : PART * k + PART]).astype(BF16)
        for k, keep in enumerate((keep_low, keep_mid, keep_far))
    ]
    tail = summed(keep_rest, got_rest_tail).astype(BF16)
    dkv = summed(dkv_keep, got_dkv).astype(BF16)
    got_hx, got_ty, low, mid, far, tail, dkv, vector = together(got_hx, got_ty, low, mid, far, tail, dkv, vector)

    def part_for(array, shift):
        return array[HEAD_ROWS * shift : HEAD_ROWS * shift + HEAD_ROWS]

    vector = summed_vector(vector, got_hx[PART:])
    hy = jnp.concatenate([summed(mid, got_hx[:PART]).astype(BF16), vector])
    tz = [summed(part_for(tail, s), part_for(got_ty, s)).astype(BF16) for s in range(4)]
    got_hy = moved(hy, "y", 1)
    got_far = moved(far, "x", 1)
    got_tz = [moved(tz[s], "z", s) for s in (1, 2, 3)]
    got_hy, got_far, low, own_tail, vector, dkv, *got_tz = together(got_hy, got_far, low, tz[0], vector, dkv, *got_tz)
    vector = summed_vector(vector, got_hy[PART:])
    head = [summed(part_for(low, s), part_for(got_far, s), part_for(got_hy, s)) for s in range(4)]
    got_hz = [moved(jnp.concatenate([head[s].astype(BF16), vector]), "z", s) for s in (1, 2, 3)]
    tx = summed(own_tail[TAIL_ROWS:], *[part[TAIL_ROWS:] for part in got_tz]).astype(BF16)
    own_tail = summed(own_tail[:TAIL_ROWS], *[part[:TAIL_ROWS] for part in got_tz])
    got_tx = moved(tx, "x", 1)
    got_dkv = across(dkv[1], 2)
    return (head[0], *got_hz, own_tail, got_tx, vector), (dkv[0], got_dkv)


def lower_lanes(shape):
    return lax.broadcasted_iota(jnp.int32, shape, 1) < HEAD_SIZE


def half_turn(value):
    return pltpu.roll(value, HEAD_SIZE, 1)


def side_by_side(left, right):
    return jnp.where(lower_lanes(left.shape), left, half_turn(right))


def kind_of(block):
    return jnp.where(block >= 24, 1, jnp.where(block >= 8, 0, jnp.where((block == 3) | (block == 4), 2, 1)))


def tile_kernel(kind_ref, flat_ref, head_ref, tail_ref, tiles, narrow):
    kind = kind_ref[0]

    @pl.when(kind == 0)
    def _():
        for j in range(12):
            tiles[72 * j : 72 * j + 72, :] = flat_ref[pl.ds(j, 72, stride=12), :]

    @pl.when(kind == 1)
    def _():
        lines = [flat_ref[pl.ds(t, 96, stride=9), :] for t in range(9)]
        turned = [half_turn(line) for line in lines[4:]]
        low = lower_lanes((96, LANES))
        for j in range(4):
            tiles[pl.ds(192 * j, 96, stride=2), :] = lines[j]
            tiles[pl.ds(192 * j + 1, 96, stride=2), :] = jnp.where(low, turned[j], turned[j + 1])
        narrow[pl.ds(0, 96, stride=2), :] = lines[4]
        narrow[pl.ds(1, 96, stride=2), :] = turned[4]
        tiles[768:864, :] = side_by_side(narrow[0:96, :], narrow[96:192, :])

    @pl.when(kind == 2)
    def _():
        lines = [flat_ref[pl.ds(t, 288, stride=3), :] for t in range(3)]
        first, second = half_turn(lines[1]), half_turn(lines[2])
        tiles[pl.ds(0, 288, stride=2), :] = lines[0]
        tiles[pl.ds(1, 288, stride=2), :] = jnp.where(lower_lanes((288, LANES)), first, second)
        narrow[pl.ds(0, 288, stride=2), :] = lines[1]
        narrow[pl.ds(1, 288, stride=2), :] = second
        tiles[576:864, :] = side_by_side(narrow[0:288, :], narrow[288:576, :])

    head_ref[...] = tiles[0:HEAD_ROWS, :].astype(BF16)
    tail_ref[...] = tiles[HEAD_ROWS:BLOCK_ROWS, :].astype(BF16)


def to_tiles(kind, flat):
    return pl.pallas_call(
        tile_kernel,
        out_shape=(
            jax.ShapeDtypeStruct((HEAD_ROWS, LANES), BF16),
            jax.ShapeDtypeStruct((TAIL_ROWS, LANES), BF16),
        ),
        in_specs=[
            pl.BlockSpec(memory_space=pltpu.SMEM),
            pl.BlockSpec(memory_space=pltpu.VMEM),
        ],
        out_specs=(pl.BlockSpec(memory_space=pltpu.VMEM),) * 2,
        scratch_shapes=[
            pltpu.VMEM((BLOCK_ROWS, LANES), F32),
            pltpu.VMEM((HEAD_ROWS, LANES), F32),
        ],
        name="to_tiles",
    )(kind, flat)


def finish_kernel(table_ref, head_ref, one_ref, two_ref, three_ref, tail_ref, other_ref, mine_ref, *refs):
    kind, place = table_ref[0], table_ref[1]
    tiles, narrow, flat_ref, vector_parts = refs[-4:]
    tokens_ref, gains_ref, w_kv_ref, base_ref, own_dkv, other_dkv = refs[:6]
    states = refs[6:-4]
    tiles[0:HEAD_ROWS, :] = (head_ref[...] + one_ref[0:HEAD_ROWS, :].astype(F32)) + (
        two_ref[0:HEAD_ROWS, :].astype(F32) + three_ref[0:HEAD_ROWS, :].astype(F32)
    )
    tiles[HEAD_ROWS:BLOCK_ROWS, :] = tail_ref[...] + other_ref[...].astype(F32)

    for at, ref in enumerate((mine_ref, one_ref, two_ref, three_ref)):
        rows = ref.shape[0]
        part = ref[rows - 2 * VECTOR_ROWS : rows, :].astype(F32)
        vector_parts[at] = part[:VECTOR_ROWS] + part[VECTOR_ROWS:]
    vector = vector_parts[lax.rem(place, 4)]
    for z in (1, 2, 3):
        vector = vector + vector_parts[lax.rem(place + 4 - z, 4)]

    lane = lax.broadcasted_iota(jnp.int32, (2 * ROWS, WIDE), 1)
    x = jnp.where(lane < MODEL_WIDTH, tokens_ref[...].astype(F32).reshape(2 * ROWS, WIDE), 0.0)
    normed, scale = normed_rows(x)
    total = summed(own_dkv[...], other_dkv[...]).reshape(2 * ROWS, 384).astype(BF16)
    d_norm = times_transposed(total, w_kv_ref[...]) * gains_ref[0:1, :]
    d_input = base_ref[...] + scale * (d_norm - normed * row_mean(d_norm * normed))
    out_ref = states[-1]
    for mb in range(2):
        out_ref[mb] = d_input[ROWS * mb : ROWS * mb + ROWS].T[0:MODEL_WIDTH].astype(BF16)

    @pl.when(kind == 0)
    def _():
        for j in range(12):
            flat_ref[pl.ds(j, 72, stride=12), :] = tiles[72 * j : 72 * j + 72, :]

    @pl.when(kind == 1)
    def _():
        low = lower_lanes((96, LANES))
        narrow[0:96, :] = tiles[768:864, :]
        narrow[96:192, :] = half_turn(tiles[768:864, :])
        odd = [half_turn(tiles[pl.ds(192 * j + 1, 96, stride=2), :]) for j in range(4)]
        for j in range(4):
            flat_ref[pl.ds(j, 96, stride=9), :] = tiles[pl.ds(192 * j, 96, stride=2), :]
        flat_ref[pl.ds(4, 96, stride=9), :] = jnp.where(low, narrow[pl.ds(0, 96, stride=2), :], odd[0])
        for j in range(3):
            flat_ref[pl.ds(5 + j, 96, stride=9), :] = jnp.where(low, odd[j], odd[j + 1])
        last = half_turn(narrow[pl.ds(1, 96, stride=2), :])
        flat_ref[pl.ds(8, 96, stride=9), :] = jnp.where(low, odd[3], last)

    @pl.when(kind == 2)
    def _():
        low = lower_lanes((288, LANES))
        narrow[0:288, :] = tiles[576:864, :]
        narrow[288:576, :] = half_turn(tiles[576:864, :])
        odd = half_turn(tiles[pl.ds(1, 288, stride=2), :])
        flat_ref[pl.ds(0, 288, stride=3), :] = tiles[pl.ds(0, 288, stride=2), :]
        flat_ref[pl.ds(1, 288, stride=3), :] = jnp.where(low, narrow[pl.ds(0, 288, stride=2), :], odd)
        last = half_turn(narrow[pl.ds(1, 288, stride=2), :])
        flat_ref[pl.ds(2, 288, stride=3), :] = jnp.where(low, odd, last)


    if len(states) == 3:
        states[0][...], states[1][...] = flat_ref[...], vector
        return
    old_vectors, old_block, new_vectors, new_block = states[0:3], states[3:6], states[6:9], states[9:12]
    found = adamw(old_vectors[0][...], vector, old_vectors[1][...], old_vectors[2][...], RATE_VECTOR, 0.0)
    for ref, value in zip(new_vectors, found):
        ref[...] = value

    @pl.loop(0, 6)
    def _(k):
        rows = pl.ds(pl.multiple_of(k * 144, 8), 144)
        found = adamw(
            old_block[0][rows, :], flat_ref[rows, :], old_block[1][rows, :], old_block[2][rows, :], RATE_MATRIX, DECAY
        )
        for ref, value in zip(new_block, found):
            ref[rows, :] = value


def finish(table, parts, inputs, state):
    vmem = pl.BlockSpec(memory_space=pltpu.VMEM)
    flat = jax.ShapeDtypeStruct((BLOCK_ROWS, LANES), F32)
    vector = jax.ShapeDtypeStruct((VECTOR_ROWS, LANES), F32)
    shapes = (vector,) * 3 + (flat,) * 3 if state else (flat, vector)
    shapes += (jax.ShapeDtypeStruct((2, MODEL_WIDTH, ROWS), BF16),)
    return pl.pallas_call(
        finish_kernel,
        out_shape=shapes,
        in_specs=[pl.BlockSpec(memory_space=pltpu.SMEM)] + [vmem] * (len(parts) + len(inputs) + len(state)),
        out_specs=(vmem,) * len(shapes),
        scratch_shapes=[
            pltpu.VMEM((BLOCK_ROWS, LANES), F32),
            pltpu.VMEM((HEAD_ROWS, LANES), F32),
            pltpu.VMEM((BLOCK_ROWS, LANES), F32),
            pltpu.VMEM((4, VECTOR_ROWS, LANES), F32),
        ],
        name="finish",
    )(table, *parts, *inputs, *state)


def product(left, right):
    return jnp.dot(left, right, preferred_element_type=F32)


def times_transposed(left, right):
    return lax.dot_general(left, right, (((1,), (1,)), ((), ())), preferred_element_type=F32)


def rows_product(left, right):
    return lax.dot_general(left, right, (((0,), (0,)), ((), ())), preferred_element_type=F32)


def swapped(value):
    lane = lax.broadcasted_iota(jnp.int32, value.shape, 1)
    return jnp.where(lane % HEAD_SIZE < HEAD_SIZE // 2, pltpu.roll(value, 96, 1), pltpu.roll(value, 32, 1))


def rope(value, cosines, sines):
    return value * cosines + swapped(value) * sines


def rope_back(value, cosines, sines):
    return value * cosines - swapped(value) * sines


def row_mean(value):
    return jnp.sum(value, axis=-1, keepdims=True) * (1.0 / MODEL_WIDTH)


def normed_rows(value):
    scale = lax.rsqrt(row_mean(value * value) + EPS_NORM)
    return value * scale, scale


def place_rows(ref, head_tile, tail_tile, first):
    for j in range(3):
        ref[first : first + 192, LANES * j : LANES * j + LANES] = head_tile[192 * j : 192 * j + 192, :]
    ref[first : first + 192, 384:512] = tail_tile[0:192, :]
    rest = tail_tile[192:288, :].astype(F32)
    low = lower_lanes(rest.shape)
    ref[first : first + 96, 512:640] = jnp.where(low, rest, 0.0).astype(BF16)
    ref[first + 96 : first + 192, 512:640] = jnp.where(low, half_turn(rest), 0.0).astype(BF16)


def tiles_of_rows(value):
    head = jnp.concatenate([value[:, LANES * j : LANES * j + LANES] for j in range(3)], axis=0)
    rest = side_by_side(value[0:96, 512:640], value[96:192, 512:640])
    return head, jnp.concatenate([value[:, 384:512], rest], axis=0)


def layer_kernel(*refs):
    slots = refs[0]
    head_parts = refs[1:9]
    tail_parts = refs[9:13]
    tokens_pair, cos_pair, sin_pair = refs[13:15], refs[15:17], refs[17:19]
    (place_q_ref, place_k_ref, gains_ref, bias_q_ref, bias_kv_ref, grad_ref) = refs[19:25]
    block_out_ref, parts_out = refs[25], refs[26:36]
    (dkv_send, dkv_keep, base_ref, w_kv) = refs[36:40]
    (raw_head, raw_tail, w_q, w_out, w_gate, w_up, w_down, normed_all, hidden_all, keys, values, queries, probs, attended, act_all, block_acc, d_hidden, d_attended, dkv_all, d_query, both_all, vector_ref, outs, sems, out_sems) = refs[40:]

    place = slots[MY_Z]

    def fetches(shift, sem):
        at = lax.rem(place + shift, 4)
        copies = []
        for k, part in enumerate(head_parts):
            copies.append(pltpu.make_async_copy(part.at[at], raw_head.at[4 * k + at], sems.at[sem + k]))
        for k, part in enumerate(tail_parts):
            rows = pl.ds(2 * at, 2)
            copies.append(pltpu.make_async_copy(part.at[rows], raw_tail.at[pl.ds(8 * k + 2 * at, 2)], sems.at[sem + 8 + k]))
        return copies

    attention_blocks = fetches(0, 0)
    other_blocks = fetches(1, 12) + fetches(2, 24) + fetches(3, 36)
    for copy in attention_blocks + other_blocks:
        copy.start()

    core = slots[MY_CORE]

    def at_slot(pair, slot):
        return pair[slot % 2].at[slot // 2]

    def head_tile(block):
        return raw_head.at[slots[AT_HEAD + block]]

    def tail_tile(block):
        return raw_tail.at[slots[AT_TAIL + block]]

    gain_one = gains_ref[0:1, :]
    gain_two = gains_ref[1:2, :]
    low_rows = lower_lanes((ROWS, LANES))

    for mb in range(0, 2):
        lane = lax.broadcasted_iota(jnp.int32, (ROWS, WIDE), 1)
        for slot in range(4):
            rows = pl.ds(mb * 512 + slot * ROWS, ROWS)
            x = jnp.where(lane < MODEL_WIDTH, at_slot(tokens_pair, slot)[mb].astype(F32), 0.0)
            normed, _ = normed_rows(x)
            normed_all[rows, :] = normed
            hidden_all[rows, :] = (normed * gain_one).astype(BF16)

    for copy in attention_blocks:
        copy.wait()
    for ref in (w_q, w_out, w_gate, w_up, w_kv):
        ref[576:640, :] = jnp.zeros((64, ref.shape[1]), BF16)
    for k in range(3):
        place_rows(w_q, head_tile(k), tail_tile(k), 192 * k)
        place_rows(w_out, head_tile(5 + k), tail_tile(5 + k), 192 * k)
    w_kv[0:576, 0:128] = head_tile(3)[...]
    w_kv[0:576, 128:256] = head_tile(4)[...]
    rest_key = tail_tile(3)[...].astype(F32)
    rest_value = tail_tile(4)[...].astype(F32)
    low = lower_lanes(rest_key.shape)
    w_kv[0:288, 256:384] = jnp.where(low, rest_key, half_turn(rest_value)).astype(BF16)
    w_kv[288:576, 256:384] = jnp.where(low, half_turn(rest_key), rest_value).astype(BF16)

    for mb in range(0, 2):
        rows = pl.ds(mb * 512, 512)
        pair = product(hidden_all[rows, :], w_kv[...]) + bias_kv_ref[...]
        cosines = jnp.concatenate([at_slot(cos_pair, slot)[mb] for slot in range(4)], axis=0)
        sines = jnp.concatenate([at_slot(sin_pair, slot)[mb] for slot in range(4)], axis=0)
        key_a = rope(pair[:, 0:128], cosines, sines)
        key_b = rope(pair[:, 256:384], cosines, sines)
        value_a, value_b = pair[:, 128:256], pair[:, 256:384]
        low_keys = lower_lanes((512, LANES))
        turned = half_turn(key_a)
        keys[rows, 0:128] = jnp.where(low_keys, key_a, turned).astype(BF16)
        keys[rows, 128:256] = jnp.where(low_keys, turned, key_a).astype(BF16)
        keys[rows, 256:384] = jnp.where(low_keys, key_b, half_turn(key_b)).astype(BF16)
        turned = half_turn(value_a)
        values[rows, 0:128] = jnp.where(low_keys, value_a, turned).astype(BF16)
        values[rows, 128:256] = jnp.where(low_keys, turned, value_a).astype(BF16)
        values[rows, 256:384] = jnp.where(low_keys, half_turn(value_b), value_b).astype(BF16)

    def heads_of(ref, rows, group):
        stacked = []
        for k in range(3):
            number = 3 * group + k
            tile = ref[rows, LANES * (number // 2) : LANES * (number // 2) + LANES]
            keep = low_rows if number % 2 == 0 else jnp.logical_not(low_rows)
            stacked.append(jnp.where(keep, tile.astype(F32), 0.0).astype(BF16))
        return jnp.concatenate(stacked, axis=0)

    def tiles_of_heads(parts):
        found = [jnp.where(low_rows, parts[2 * k], parts[2 * k + 1]) for k in range(4)]
        return found + [jnp.where(low_rows, parts[8], 0.0)]

    for mb in range(0, 2):
        rows = pl.ds(mb * ROWS, ROWS)
        key_rows = pl.ds(mb * 512, 512)
        cosines, sines = cos_pair[0][0, mb], sin_pair[0][0, mb]
        made = product(hidden_all[pl.ds(mb * 512, ROWS), :], w_q[...]) + bias_q_ref[...]
        for k in range(5):
            turned = rope(made[:, LANES * k : LANES * k + LANES], cosines, sines)
            queries[rows, LANES * k : LANES * k + LANES] = (turned * HEAD_SIZE ** (-0.5)).astype(BF16)
        masked = jnp.where(place_q_ref[mb] >= place_k_ref[mb], 0.0, MASKED)
        masked = jnp.concatenate([masked] * 3, axis=0)
        parts = []
        for group in range(KEY_VALUE_HEADS):
            lanes = slice(LANES * group, LANES * group + LANES)
            scores = times_transposed(heads_of(queries, rows, group), keys[key_rows, lanes])
            scores = scores + masked
            top = jnp.max(scores, axis=-1, keepdims=True)
            powers = jnp.exp(scores - top)
            found = powers * (1.0 / jnp.sum(powers, axis=-1, keepdims=True))
            probs[mb, group] = found
            out = product(found.astype(BF16), values[key_rows, lanes])
            outs[mb, group] = out
            parts += [out[ROWS * k : ROWS * k + ROWS] for k in range(3)]
        for k, tile in enumerate(tiles_of_heads(parts)):
            attended[rows, LANES * k : LANES * k + LANES] = tile.astype(BF16)

    for copy in other_blocks:
        copy.wait()
    for k in range(8):
        place_rows(w_down, head_tile(24 + k), tail_tile(24 + k), 192 * k)
    for ref, base in ((w_gate, 8), (w_up, 16)):
        for k in range(4):
            for i in range(6):
                if i < 4:
                    even = head_tile(base + 2 * k)[144 * i : 144 * i + 144, :].astype(F32)
                    odd = head_tile(base + 2 * k + 1)[144 * i : 144 * i + 144, :].astype(F32)
                else:
                    even = tail_tile(base + 2 * k)[144 * (i - 4) : 144 * (i - 4) + 144, :].astype(F32)
                    odd = tail_tile(base + 2 * k + 1)[144 * (i - 4) : 144 * (i - 4) + 144, :].astype(F32)
                ref[144 * k : 144 * k + 144, 256 * i : 256 * i + 128] = jnp.concatenate(
                    [even[0:72], odd[0:72]], axis=0
                ).astype(BF16)
                ref[144 * k : 144 * k + 144, 256 * i + 128 : 256 * i + 256] = jnp.concatenate(
                    [even[72:144], odd[72:144]], axis=0
                ).astype(BF16)

    lane = lax.broadcasted_iota(jnp.int32, (2 * ROWS, WIDE), 1)
    x_own = tokens_pair[0][0].astype(F32).reshape(2 * ROWS, WIDE)
    x_own = jnp.where(lane < MODEL_WIDTH, x_own, 0.0)
    resid_mid = x_own + product(attended[...], w_out[...])
    normed_two, scale_two = normed_rows(resid_mid)
    hidden_two = (normed_two * gain_two).astype(BF16)
    hidden_turned = hidden_two.T
    grad_low = grad_ref[...]
    block_acc[...] = resid_mid
    d_hidden[...] = jnp.zeros_like(d_hidden)

    def store_pair(at, even, odd, table, first):
        rows = pl.ds(pl.multiple_of(slots[table + at] + first, 16), even.shape[0])
        both_all[1 - core, rows, :] = even.astype(BF16)
        both_all[core, rows, :] = odd.astype(BF16)

    def feed_forward(chunk, first, table):
        cols = slice(chunk * 512, chunk * 512 + 512)
        gate = product(hidden_two, w_gate[:, cols])
        up = product(hidden_two, w_up[:, cols])
        sigma = 1.0 / (1.0 + jnp.exp(-gate))
        act = (gate * sigma * up).astype(BF16)
        act_all[:, cols] = act
        down = w_down[cols, :]
        d_act = times_transposed(grad_low, down)
        block_acc[...] += product(act, down)
        d_up = (d_act * gate * sigma).astype(BF16)
        d_gate = (d_act * up * sigma * (1.0 + gate * (1.0 - sigma))).astype(BF16)
        d_hidden[...] += times_transposed(d_gate, w_gate[:, cols]) + times_transposed(d_up, w_up[:, cols])
        for base, cotangent in ((4, d_gate), (8, d_up)):
            made = product(hidden_turned, cotangent)
            for k in range(4):
                part = made[144 * k : 144 * k + 144, :]
                even = jnp.concatenate([part[0:72, LANES * j : LANES * j + LANES] for j in range(4)], axis=0)
                odd = jnp.concatenate([part[72:144, LANES * j : LANES * j + LANES] for j in range(4)], axis=0)
                store_pair(base + k, even, odd, table, (chunk - first) * 288)

    feed_forward(0, 0, TO_HEAD)
    feed_forward(1, 0, TO_HEAD)
    feed_forward(2, 2, TO_TAIL)

    def store_rows(at, even, odd):
        even_head, even_tail = even
        odd_head, odd_tail = odd
        store_pair(at, even_head, odd_head, TO_HEAD, 0)
        store_pair(at, even_tail, odd_tail, TO_TAIL, 0)

    for k in range(0, 4):
        made = rows_product(act_all[:, pl.ds(k * 384, 384)], grad_low)
        store_rows(12 + k, tiles_of_rows(made[0:192]), tiles_of_rows(made[192:384]))

    def deliveries(z, sem):
        copies = []
        inside = pl.multiple_of(HEAD_ROWS * lax.rem(z + 4 - place, 4), HEAD_ROWS)
        for base, outs_of in ((both_all.at[0], parts_out[0:4]), (both_all.at[1], parts_out[4:10])):
            rest = [(outs_of[2], PART * k) for k in range(3)] if len(outs_of) == 4 else [(out, 0) for out in outs_of[2:5]]
            targets = [(outs_of[0], 0, FIRST_AT), (outs_of[1], 0, TAIL_AT)]
            targets += [(out, into, PART * k) for k, (out, into) in enumerate(rest)]
            targets.append((outs_of[-1], 0, 3 * PART))
            for out, into, start in targets:
                copies.append(
                    pltpu.make_async_copy(
                        base.at[pl.ds(pl.multiple_of(start + inside, 16), HEAD_ROWS)],
                        out.at[pl.ds(pl.multiple_of(into + inside, 16), HEAD_ROWS)],
                        out_sems.at[sem + len(copies)],
                    )
                )
        return copies

    early = deliveries(1, 12) + deliveries(2, 24) + deliveries(3, 36)
    for copy in early:
        copy.start()

    for mb in range(2):
        block_out_ref[mb] = block_acc[ROWS * mb : ROWS * mb + ROWS, :].T[0:MODEL_WIDTH].astype(BF16)

    d_two = d_hidden[...]
    gain_two_sum = jnp.sum(d_two * normed_two, axis=0, keepdims=True)
    d_norm = d_two * gain_two
    d_mid = grad_low.astype(F32) + scale_two * (d_norm - normed_two * row_mean(d_norm * normed_two))
    d_branch = d_mid.astype(BF16)
    d_attended[...] = times_transposed(d_branch, w_out[...]).astype(BF16)
    grad_out = rows_product(attended[...], d_branch)

    for mb in range(0, 2):
        rows = pl.ds(mb * ROWS, ROWS)
        key_rows = pl.ds(mb * 512, 512)
        parts = []
        d_keys = []
        d_values = []
        for group in range(KEY_VALUE_HEADS):
            lanes = slice(LANES * group, LANES * group + LANES)
            query_rows = heads_of(queries, rows, group)
            cotangent = heads_of(d_attended, rows, group)
            found = probs[mb, group]
            d_probs = times_transposed(cotangent, values[key_rows, lanes])
            delta = jnp.sum(outs[mb, group] * cotangent.astype(F32), axis=-1, keepdims=True)
            d_scores = (found * (d_probs - delta)).astype(BF16)
            out = product(d_scores, keys[key_rows, lanes]) * HEAD_SIZE ** (-0.5)
            parts += [out[ROWS * k : ROWS * k + ROWS] for k in range(3)]
            d_key = rows_product(d_scores, query_rows)
            d_value = rows_product(found.astype(BF16), cotangent)
            d_keys.append(d_key + half_turn(d_key))
            d_values.append(d_value + half_turn(d_value))
        cosines, sines = cos_pair[0][0, mb], sin_pair[0][0, mb]
        for k, tile in enumerate(tiles_of_heads(parts)):
            d_query[rows, LANES * k : LANES * k + LANES] = rope_back(tile, cosines, sines).astype(BF16)
        low_keys = lower_lanes((512, LANES))
        cosines = jnp.concatenate([at_slot(cos_pair, slot)[mb] for slot in range(4)], axis=0)
        sines = jnp.concatenate([at_slot(sin_pair, slot)[mb] for slot in range(4)], axis=0)
        key_a = rope_back(jnp.where(low_keys, d_keys[0], d_keys[1]), cosines, sines)
        key_b = rope_back(d_keys[2], cosines, sines)
        dkv_all[key_rows, 0:128] = key_a.astype(BF16)
        dkv_all[key_rows, 128:256] = jnp.where(low_keys, d_values[0], d_values[1]).astype(BF16)
        dkv_all[key_rows, 256:384] = jnp.where(low_keys, key_b, d_values[2]).astype(BF16)
        for slot in range(4):
            target = dkv_send if slot % 2 else dkv_keep
            target[slot // 2, mb] = dkv_all[pl.ds(mb * 512 + slot * ROWS, ROWS), :]

    dkv = dkv_all[...]
    d_q = d_query[...]
    dq_wq = times_transposed(d_q, w_q[...])
    normed = jnp.concatenate([normed_all[512 * mb : 512 * mb + ROWS, :] for mb in range(2)], axis=0)
    scale = lax.rsqrt(row_mean(x_own * x_own) + EPS_NORM)
    d_norm = dq_wq * gain_one
    base_ref[...] = d_mid + scale * (d_norm - normed * row_mean(d_norm * normed))
    bias_q_sum = jnp.sum(d_q.astype(F32), axis=0, keepdims=True)
    bias_kv_sum = jnp.sum(dkv.astype(F32), axis=0, keepdims=True)
    gain_sum = jnp.zeros((1, WIDE), F32)
    for mb in range(2):
        gain_sum += jnp.sum(dq_wq[ROWS * mb : ROWS * mb + ROWS] * normed_all[512 * mb : 512 * mb + ROWS, :], axis=0, keepdims=True)
    for k in range(4):
        part = slice(256 * k, 256 * k + 256)
        gain_sum += jnp.sum(times_transposed(dkv_all[part, :], w_kv[...]) * normed_all[part, :], axis=0, keepdims=True)

    hidden_own = jnp.concatenate([hidden_all[0:ROWS, :], hidden_all[512 : 512 + ROWS, :]], axis=0)
    grad_q = rows_product(hidden_own, d_q)
    grad_kv = rows_product(hidden_all[...], dkv)
    rest = grad_kv[0:576, 256:384]
    low = lower_lanes((288, LANES))
    key_tiles = (grad_kv[0:576, 0:128], jnp.where(low, rest[0:288], half_turn(rest[288:576])))
    value_tiles = (grad_kv[0:576, 128:256], jnp.where(low, half_turn(rest[0:288]), rest[288:576]))
    query_tiles = [tiles_of_rows(grad_q[192 * k : 192 * k + 192]) for k in range(3)]
    out_tiles = [tiles_of_rows(grad_out[192 * k : 192 * k + 192]) for k in range(3)]
    store_rows(0, query_tiles[0], query_tiles[1])
    store_rows(1, query_tiles[2], key_tiles)
    store_rows(2, value_tiles, out_tiles[0])
    store_rows(3, out_tiles[1], out_tiles[2])
    def flat_rows(first, second, third, pair):
        tile = lambda row, k: row[:, LANES * k : LANES * k + LANES]
        low = lower_lanes((1, LANES))
        across_two = lambda one, two: jnp.where(low, half_turn(one), half_turn(two))
        lines = [tile(first, k) for k in range(4)]
        lines.append(side_by_side(tile(first, 4), tile(second, 0)))
        lines += [across_two(tile(second, k), tile(second, k + 1)) for k in range(4)]
        lines += [tile(third, k) for k in range(4)]
        lines.append(side_by_side(tile(third, 4), tile(pair, 0)))
        lines.append(across_two(tile(pair, 0), tile(pair, 2)))
        lines.append(tile(pair, 1))
        lines.append(jnp.where(low, half_turn(tile(pair, 2)), 0.0))
        return lines

    at = FIRST_AT + PART
    for row, line in enumerate(flat_rows(gain_sum, gain_two_sum, bias_q_sum, bias_kv_sum)):
        vector_ref[row : row + 1, :] = line
    vector_ref[17:24, :] = jnp.zeros((7, LANES), F32)
    vector = vector_ref[...]
    high = vector.astype(BF16).astype(F32)
    both = jnp.concatenate([high, vector - high], axis=0).astype(BF16)
    for k in range(2):
        both_all[k, at : at + 2 * VECTOR_ROWS, :] = both
    last = deliveries(0, 0)
    last.append(pltpu.make_async_copy(both_all.at[0, pl.ds(at, 2 * VECTOR_ROWS)], parts_out[0].at[pl.ds(PART, 2 * VECTOR_ROWS)], out_sems.at[48]))
    last.append(pltpu.make_async_copy(both_all.at[1, pl.ds(at, 2 * VECTOR_ROWS)], parts_out[4].at[pl.ds(PART, 2 * VECTOR_ROWS)], out_sems.at[49]))
    for copy in last:
        copy.start()
    for copy in early + last:
        copy.wait()


def run_layer(slots, heads, tails, *others):
    shape = jax.ShapeDtypeStruct
    vmem = pl.BlockSpec(memory_space=pltpu.VMEM)
    anywhere = pl.BlockSpec(memory_space=pl.ANY)
    scratch = [
        ((BLOCKS, HEAD_ROWS, LANES), BF16),
        ((BLOCKS, TAIL_ROWS, LANES), BF16),
        ((WIDE, WIDE), BF16),
        ((WIDE, WIDE), BF16),
        ((WIDE, FF), BF16),
        ((WIDE, FF), BF16),
        ((FF, WIDE), BF16),
        ((1024, WIDE), F32),
        ((1024, WIDE), BF16),
        ((1024, 384), BF16),
        ((1024, 384), BF16),
        ((256, WIDE), BF16),
        ((2, 3, 384, 512), F32),
        ((256, WIDE), BF16),
        ((256, FF), BF16),
        ((256, WIDE), F32),
        ((256, WIDE), F32),
        ((256, WIDE), BF16),
        ((1024, 384), BF16),
        ((256, WIDE), BF16),
        ((2, ALL_ROWS, LANES), BF16),
        ((VECTOR_ROWS, LANES), F32),
        ((2, 3, 384, LANES), F32),
    ]
    return pl.pallas_call(
        layer_kernel,
        out_shape=(
            shape((2, MODEL_WIDTH, ROWS), BF16),
            *[shape((count, LANES), BF16) for _, count in SEND_PARTS + KEEP_PARTS],
            shape((2, 2, ROWS, 384), BF16),
            shape((2, 2, ROWS, 384), BF16),
            shape((256, WIDE), F32),
            shape((WIDE, 384), BF16),
        ),
        in_specs=[pl.BlockSpec(memory_space=pltpu.SMEM)] + [anywhere] * 12 + [vmem] * 12,
        out_specs=(vmem,) + (anywhere,) * 10 + (vmem,) * 4,
        scratch_shapes=[pltpu.VMEM(dims, kind) for dims, kind in scratch]
        + [pltpu.SemaphoreType.DMA((48,)), pltpu.SemaphoreType.DMA((50,))],
        compiler_params=pltpu.CompilerParams(vmem_limit_bytes=50 * 1024 * 1024),
        name="layer",
    )(slots, *heads, *tails, *others)


def adamw(param, grad, mom_one, mom_two, rate, decay):
    new_one = BETA_ONE * mom_one + (1.0 - BETA_ONE) * grad
    new_two = BETA_TWO * mom_two + (1.0 - BETA_TWO) * grad * grad
    fixed_one = new_one / (1.0 - BETA_ONE**STEP)
    fixed_two = new_two / (1.0 - BETA_TWO**STEP)
    new_param = param - rate * (fixed_one / (jnp.sqrt(fixed_two) + EPS_ADAM) + decay * param)
    return (new_param, new_one, new_two)


def inner_groups():
    inner = inner_count()
    data_inner = inner // lax.axis_size("ctx")
    data_count = lax.axis_size("dp")
    return [list(range(k, k + data_inner)) for k in range(0, data_count, data_inner)]


def whole_block(flat):
    if inner_count() == 1:
        return flat
    flat = lax.all_gather(flat, "ctx", axis=0, tiled=True)
    return lax.all_gather(flat, "dp", axis=0, tiled=True, axis_index_groups=inner_groups())


def own_slice(block):
    if inner_count() == 1:
        return block
    block = lax.psum_scatter(
        block, "dp", scatter_dimension=0, tiled=True, axis_index_groups=inner_groups()
    )
    return lax.psum_scatter(block, "ctx", scatter_dimension=0, tiled=True)


def bias_tiles(bias_key, bias_value):
    return jnp.concatenate([bias_key[:128], bias_value[:128], bias_key[128:], bias_value[128:]])


def local(tokens_in, places, out_grad, weights, first_moment, second_moment, vectors, vector_first, vector_second):
    kind = kind_of(device_number() // inner_count()).astype(jnp.int32).reshape(1)
    block = whole_block(weights).reshape(BLOCK_ROWS, LANES)
    head, tail = to_tiles(kind, block)

    head, tail, tokens_in, places = together(head, tail, tokens_in, places)
    own_tokens = tokens_in.reshape(2, ROWS, MODEL_WIDTH)
    own_places = places.reshape(2, ROWS)
    marks = jnp.stack([own_places // 16, own_places % 16], axis=-1).astype(BF16)
    packed = jnp.concatenate(
        [own_tokens, marks, jnp.zeros((2, ROWS, WIDE - MODEL_WIDTH - 2), BF16)], axis=-1
    )
    padding = ((0, 0), (0, WIDE - MODEL_WIDTH))
    gains = jnp.pad(vectors[: 2 * MODEL_WIDTH].reshape(2, MODEL_WIDTH), padding)
    bias_q = jnp.pad(vectors[2 * MODEL_WIDTH : 3 * MODEL_WIDTH].reshape(1, MODEL_WIDTH), padding)
    bias_kv = bias_tiles(vectors[1728:1920], vectors[1920:2112]).reshape(1, 384)
    grad = jnp.pad(out_grad.reshape(2 * ROWS, MODEL_WIDTH), padding)
    spare = VECTOR_ROWS * LANES - vectors.shape[0]
    vector_state = [
        jnp.pad(array, (0, spare), constant_values=1.0).reshape(VECTOR_ROWS, LANES)
        for array in (vectors, vector_first, vector_second)
    ]
    table = jnp.concatenate([kind, (coordinates(device_number() // inner_count())["z"]).astype(jnp.int32).reshape(1)])
    others = (slot_table(), gains, bias_q, bias_kv, grad, vector_state, table)
    heads, tails, (near, far), (cosines, sines), others = gather_all(head, tail, packed, others)
    slots, gains, bias_q, bias_kv, grad, vector_state, table = others
    cosines_far, sines_far = place_tables(far)
    place_all = jnp.stack([places_of(near), places_of(far)], axis=1)
    place_q = place_all[0, 0][..., None]
    place_k = jnp.transpose(place_all.reshape(4, 2, ROWS), (1, 0, 2)).reshape(2, 1, 4 * ROWS)

    block_out, *found = run_layer(
        slots, heads, tails, near, far, cosines, cosines_far, sines, sines_far, place_q, place_k, gains, bias_q, bias_kv, grad
    )
    sends, keeps = found[:4], found[4:10]
    dkv_send, dkv_keep, base, w_kv = found[10:]
    parts, pairs = scatter_blocks(sends, keeps, dkv_send, dkv_keep)
    inputs = (packed, gains, w_kv, base, *pairs)
    state = (weights, first_moment, second_moment)
    if inner_count() == 1:
        blocks = [array.reshape(BLOCK_ROWS, LANES) for array in state]
        *updated, input_grad = finish(table, parts, inputs, [*vector_state, *blocks])
        new_vector_state = [array.reshape(-1)[: vectors.shape[0]] for array in updated[:3]]
        new_state = [array.reshape(-1) for array in updated[3:]]
    else:
        block_grad, vector, input_grad = finish(table, parts, inputs, [])
        vector = lax.psum(vector, "ctx")
        vector = lax.psum(vector, "dp", axis_index_groups=inner_groups())
        grad_own = own_slice(block_grad.reshape(-1))
        vector_grad = vector.reshape(-1)[: vectors.shape[0]]
        new_state = adamw(weights, grad_own, first_moment, second_moment, RATE_MATRIX, DECAY)
        new_vector_state = adamw(vectors, vector_grad, vector_first, vector_second, RATE_VECTOR, 0.0)
    shape = tokens_in.shape
    return (
        jnp.transpose(block_out, (0, 2, 1)).reshape(shape),
        jnp.transpose(input_grad, (0, 2, 1)).reshape(shape),
        *new_state,
        *new_vector_state,
    )


def solution(mesh):
    in_specs = (
        P(None, "dp", "ctx", None),
        P(None, "dp", "ctx"),
        P(None, "dp", "ctx", None),
        P(("dp", "ctx")),
        P(("dp", "ctx")),
        P(("dp", "ctx")),
        P(),
        P(),
        P(),
    )
    out_specs = (
        P(None, "dp", "ctx", None),
        P(None, "dp", "ctx", None),
        P(("dp", "ctx")),
        P(("dp", "ctx")),
        P(("dp", "ctx")),
        P(),
        P(),
        P(),
    )
    return jax.shard_map(local, mesh=mesh, in_specs=in_specs, out_specs=out_specs, check_vma=False)
```

```python
import jax
import jax.numpy as jnp
from jax import lax
from jax.experimental import pallas as pl
from jax.experimental.pallas import tpu as pltpu
from jax.sharding import PartitionSpec as P

MODEL_WIDTH = 576
QUERY_HEADS = 9
KEY_VALUE_HEADS = 3
HEAD_SIZE = 64
FF = 1536
STEP = 10

EPS_NORM = 1e-05
THETA = 100000.0
BETA_ONE = 0.9
BETA_TWO = 0.95
EPS_ADAM = 1e-08
RATE_MATRIX = 0.06
RATE_VECTOR = 0.3
DECAY = 0.1
MASKED = -1e30

LANES = 128
WIDE = 640
BLOCKS = 32
BLOCK_ROWS = 864
HEAD_ROWS = 576
TAIL_ROWS = BLOCK_ROWS - HEAD_ROWS
VECTOR_ROWS = 24
PART = 4 * HEAD_ROWS
FIRST_AT = 4 * PART
TAIL_AT = FIRST_AT + PART + 2 * VECTOR_ROWS
ALL_ROWS = TAIL_AT + PART
SEND_PARTS = [(FIRST_AT, PART + 2 * VECTOR_ROWS), (TAIL_AT, PART), (0, 3 * PART), (3 * PART, PART)]
KEEP_PARTS = SEND_PARTS[:2] + [(PART * k, PART) for k in range(4)]
SIZES = {"z": 4, "y": 2, "x": 2, "c": 2}
ROWS = 128
F32 = jnp.float32
BF16 = jnp.bfloat16


def coordinates(number):
    found = {}
    for name in ("c", "x", "y", "z"):
        found[name] = number % SIZES[name]
        number = number // SIZES[name]
    return found


def number_of(found):
    number = 0
    for name in ("z", "y", "x", "c"):
        number = number * SIZES[name] + found[name]
    return number


def device_number():
    return lax.axis_index("dp") * lax.axis_size("ctx") + lax.axis_index("ctx")


def inner_count():
    return lax.axis_size("dp") * lax.axis_size("ctx") // BLOCKS


def moved(buffer, name, shift):
    inner = inner_count()
    pairs = []
    for number in range(BLOCKS):
        found = coordinates(number)
        found[name] = (found[name] + shift) % SIZES[name]
        target = number_of(found)
        pairs += [(number * inner + k, target * inner + k) for k in range(inner)]
    return lax.ppermute(buffer, ("dp", "ctx"), pairs)


def across(buffer, distance):
    count = lax.axis_size("ctx")
    return lax.ppermute(buffer, "ctx", [(i, i ^ distance) for i in range(count)])


def together(*arrays):
    return lax.optimization_barrier(arrays)


def gather_all(head, tail, packed, others):
    hz = [moved(head, "z", s) for s in (1, 2, 3)]
    tx = moved(tail, "x", 1)
    two = across(packed, 2)
    hz, head, tail, tx, two = together(hz[::-1], head, tail, tx, two)
    hz = hz[::-1]
    own = jnp.stack([head] + hz)
    pair = jnp.stack([tail, tx])
    ay = moved(own, "y", 1)
    ax = moved(own, "x", 1)
    near = jnp.stack([packed, two])
    tables = place_tables(near)
    pair, near = together(pair, near)
    tz = [moved(pair, "z", s) for s in (1, 2, 3)]
    own, pair, tz, ax, ay, near, tables, others = together(own, pair, tz[::-1], ax, ay, near, tables, others)
    tz = tz[::-1]
    eight = jnp.concatenate([pair] + tz)
    far = across(near, 1)
    axy = moved(ay, "x", 1)
    ty = moved(eight, "y", 1)
    ac = moved(own, "c", 1)
    acy = moved(ay, "c", 1)
    acx = moved(ax, "c", 1)
    tc = moved(eight, "c", 1)
    tc, acx, acy, ac, far, ty, axy = together(tc, acx, acy, ac, far, ty, axy)
    acxy = moved(axy, "c", 1)
    tcy = moved(ty, "c", 1)
    heads = [own, ay, ax, axy, ac, acy, acx, acxy]
    return heads, [eight, ty, tc, tcy], (near, far), tables, others


def places_of(tokens):
    found = tokens[..., MODEL_WIDTH : MODEL_WIDTH + 2].astype(F32)
    return found[..., 0] * 16.0 + found[..., 1]


def place_tables(tokens):
    half_dim = HEAD_SIZE // 2
    frequency = THETA ** (-2.0 * jnp.arange(half_dim, dtype=F32) / HEAD_SIZE)
    angles = places_of(tokens)[..., None] * jnp.tile(frequency, 4)
    sign = jnp.where(jnp.arange(LANES) % HEAD_SIZE < half_dim, -1.0, 1.0).astype(F32)
    return jnp.cos(angles), jnp.sin(angles) * sign


def fold(order, relative):
    slot = 0
    for name in order:
        slot = slot * SIZES[name] + relative[name]
    return slot


def head_row(slot, z, _):
    return slot * PART + jnp.where(slot < 3, 0, FIRST_AT - 3 * PART) + z * HEAD_ROWS


def tail_row(slot, z, inside):
    return jnp.where(slot < 1, 3 * PART, TAIL_AT) + (2 * z + inside) * TAIL_ROWS


def slot_table():
    mine = coordinates(device_number() // inner_count())
    entries = []
    for order in (("c", "x", "y", "z"), ("c", "y", "z", "x")):
        for number in range(BLOCKS):
            found = coordinates(number)
            entries.append(fold(order, {n: (mine[n] - found[n]) % SIZES[n] for n in SIZES}))
    for order, start in ((("x", "y"), head_row), (("y",), tail_row)):
        for number in range(0, BLOCKS, 2):
            found = coordinates(number)
            slot = fold(order, {n: (found[n] - mine[n]) % SIZES[n] for n in SIZES})
            inside = (found["x"] - mine["x"]) % SIZES["x"]
            entries.append(start(slot, (found["z"] - mine["z"]) % SIZES["z"], inside))
    entries.append(mine["c"])
    entries.append(mine["z"])
    return jnp.stack([jnp.asarray(entry, jnp.int32) for entry in entries])


AT_HEAD, AT_TAIL, TO_HEAD, TO_TAIL = 0, BLOCKS, 2 * BLOCKS, 2 * BLOCKS + 16
MY_CORE, MY_Z = 2 * BLOCKS + 32, 2 * BLOCKS + 33


def summed(*parts):
    total = parts[0].astype(F32)
    for part in parts[1:]:
        total = total + part.astype(F32)
    return total


def summed_vector(mine, other):
    total = summed(mine[:VECTOR_ROWS], other[:VECTOR_ROWS]) + summed(mine[VECTOR_ROWS:], other[VECTOR_ROWS:])
    high = lax.reduce_precision(total, 8, 7)
    return jnp.concatenate([high.astype(BF16), (total - high).astype(BF16)])


def scatter_blocks(sends, keeps, dkv_send, dkv_keep):
    keep_head, keep_tail, keep_low, keep_mid, keep_far, keep_rest = keeps
    got_head, got_tail = moved(sends[0], "c", 1), moved(sends[1], "c", 1)
    got_head, got_tail, rest_head, rest_tail, dkv_send = together(got_head, got_tail, *sends[2:], dkv_send)
    got_rest_head, got_rest_tail = moved(rest_head, "c", 1), moved(rest_tail, "c", 1)
    got_dkv = across(dkv_send, 1)
    vector = summed_vector(keep_head[PART:], got_head[PART:])
    hx = jnp.concatenate([summed(keep_head[:PART], got_head[:PART]).astype(BF16), vector])
    ty = summed(keep_tail, got_tail).astype(BF16)
    got_hx = moved(hx, "x", 1)
    got_ty = moved(ty, "y", 1)
    low, mid, far = [
        summed(keep, got_rest_head[PART * k : PART * k + PART]).astype(BF16)
        for k, keep in enumerate((keep_low, keep_mid, keep_far))
    ]
    tail = summed(keep_rest, got_rest_tail).astype(BF16)
    dkv = summed(dkv_keep, got_dkv).astype(BF16)
    got_hx, got_ty, low, mid, far, tail, dkv, vector = together(got_hx, got_ty, low, mid, far, tail, dkv, vector)

    def part_for(array, shift):
        return array[HEAD_ROWS * shift : HEAD_ROWS * shift + HEAD_ROWS]

    vector = summed_vector(vector, got_hx[PART:])
    hy = jnp.concatenate([summed(mid, got_hx[:PART]).astype(BF16), vector])
    tz = [summed(part_for(tail, s), part_for(got_ty, s)).astype(BF16) for s in range(4)]
    got_hy = moved(hy, "y", 1)
    got_far = moved(far, "x", 1)
    got_tz = [moved(tz[s], "z", s) for s in (1, 2, 3)]
    got_tz, got_far, got_hy, low, own_tail, vector, dkv = together(got_tz[::-1], got_far, got_hy, low, tz[0], vector, dkv)
    got_tz = got_tz[::-1]
    vector = summed_vector(vector, got_hy[PART:])
    head = [summed(part_for(low, s), part_for(got_far, s), part_for(got_hy, s)) for s in range(4)]
    got_hz = [moved(jnp.concatenate([head[s].astype(BF16), vector]), "z", s) for s in (1, 2, 3)]
    tx = summed(own_tail[TAIL_ROWS:], *[part[TAIL_ROWS:] for part in got_tz]).astype(BF16)
    own_tail = summed(own_tail[:TAIL_ROWS], *[part[:TAIL_ROWS] for part in got_tz])
    got_tx = moved(tx, "x", 1)
    got_dkv = across(dkv[1], 2)
    return (head[0], *got_hz[::-1], own_tail, got_tx, vector), (dkv[0], got_dkv)


def lower_lanes(shape):
    return lax.broadcasted_iota(jnp.int32, shape, 1) < HEAD_SIZE


def half_turn(value):
    return pltpu.roll(value, HEAD_SIZE, 1)


def side_by_side(left, right):
    return jnp.where(lower_lanes(left.shape), left, half_turn(right))


def kind_of(block):
    return jnp.where(block >= 24, 1, jnp.where(block >= 8, 0, jnp.where((block == 3) | (block == 4), 2, 1)))


def tile_kernel(kind_ref, flat_ref, head_ref, tail_ref, tiles, narrow):
    kind = kind_ref[0]

    @pl.when(kind == 0)
    def _():
        for j in range(12):
            tiles[72 * j : 72 * j + 72, :] = flat_ref[pl.ds(j, 72, stride=12), :]

    @pl.when(kind == 1)
    def _():
        lines = [flat_ref[pl.ds(t, 96, stride=9), :] for t in range(9)]
        turned = [half_turn(line) for line in lines[4:]]
        low = lower_lanes((96, LANES))
        for j in range(4):
            tiles[pl.ds(192 * j, 96, stride=2), :] = lines[j]
            tiles[pl.ds(192 * j + 1, 96, stride=2), :] = jnp.where(low, turned[j], turned[j + 1])
        narrow[pl.ds(0, 96, stride=2), :] = lines[4]
        narrow[pl.ds(1, 96, stride=2), :] = turned[4]
        tiles[768:864, :] = side_by_side(narrow[0:96, :], narrow[96:192, :])

    @pl.when(kind == 2)
    def _():
        lines = [flat_ref[pl.ds(t, 288, stride=3), :] for t in range(3)]
        first, second = half_turn(lines[1]), half_turn(lines[2])
        tiles[pl.ds(0, 288, stride=2), :] = lines[0]
        tiles[pl.ds(1, 288, stride=2), :] = jnp.where(lower_lanes((288, LANES)), first, second)
        narrow[pl.ds(0, 288, stride=2), :] = lines[1]
        narrow[pl.ds(1, 288, stride=2), :] = second
        tiles[576:864, :] = side_by_side(narrow[0:288, :], narrow[288:576, :])

    head_ref[...] = tiles[0:HEAD_ROWS, :].astype(BF16)
    tail_ref[...] = tiles[HEAD_ROWS:BLOCK_ROWS, :].astype(BF16)


def to_tiles(kind, flat):
    return pl.pallas_call(
        tile_kernel,
        out_shape=(
            jax.ShapeDtypeStruct((HEAD_ROWS, LANES), BF16),
            jax.ShapeDtypeStruct((TAIL_ROWS, LANES), BF16),
        ),
        in_specs=[
            pl.BlockSpec(memory_space=pltpu.SMEM),
            pl.BlockSpec(memory_space=pltpu.VMEM),
        ],
        out_specs=(pl.BlockSpec(memory_space=pltpu.VMEM),) * 2,
        scratch_shapes=[
            pltpu.VMEM((BLOCK_ROWS, LANES), F32),
            pltpu.VMEM((HEAD_ROWS, LANES), F32),
        ],
        name="to_tiles",
    )(kind, flat)


def finish_kernel(table_ref, head_ref, three_ref, two_ref, one_ref, tail_ref, other_ref, mine_ref, *refs):
    kind, place = table_ref[0], table_ref[1]
    tiles, narrow, flat_ref, vector_parts = refs[-4:]
    tokens_ref, gains_ref, w_kv_ref, base_ref, own_dkv, other_dkv = refs[:6]
    states = refs[6:-4]
    tiles[0:HEAD_ROWS, :] = (head_ref[...] + one_ref[0:HEAD_ROWS, :].astype(F32)) + (
        two_ref[0:HEAD_ROWS, :].astype(F32) + three_ref[0:HEAD_ROWS, :].astype(F32)
    )
    tiles[HEAD_ROWS:BLOCK_ROWS, :] = tail_ref[...] + other_ref[...].astype(F32)

    for at, ref in enumerate((mine_ref, one_ref, two_ref, three_ref)):
        rows = ref.shape[0]
        part = ref[rows - 2 * VECTOR_ROWS : rows, :].astype(F32)
        vector_parts[at] = part[:VECTOR_ROWS] + part[VECTOR_ROWS:]
    vector = vector_parts[lax.rem(place, 4)]
    for z in (1, 2, 3):
        vector = vector + vector_parts[lax.rem(place + 4 - z, 4)]

    lane = lax.broadcasted_iota(jnp.int32, (2 * ROWS, WIDE), 1)
    x = jnp.where(lane < MODEL_WIDTH, tokens_ref[...].astype(F32).reshape(2 * ROWS, WIDE), 0.0)
    normed, scale = normed_rows(x)
    total = summed(own_dkv[...], other_dkv[...]).reshape(2 * ROWS, 384).astype(BF16)
    d_norm = times_transposed(total, w_kv_ref[...]) * gains_ref[0:1, :]
    d_input = base_ref[...] + scale * (d_norm - normed * row_mean(d_norm * normed))
    out_ref = states[-1]
    for mb in range(2):
        out_ref[mb] = d_input[ROWS * mb : ROWS * mb + ROWS].T[0:MODEL_WIDTH].astype(BF16)

    @pl.when(kind == 0)
    def _():
        for j in range(12):
            flat_ref[pl.ds(j, 72, stride=12), :] = tiles[72 * j : 72 * j + 72, :]

    @pl.when(kind == 1)
    def _():
        low = lower_lanes((96, LANES))
        narrow[0:96, :] = tiles[768:864, :]
        narrow[96:192, :] = half_turn(tiles[768:864, :])
        odd = [half_turn(tiles[pl.ds(192 * j + 1, 96, stride=2), :]) for j in range(4)]
        for j in range(4):
            flat_ref[pl.ds(j, 96, stride=9), :] = tiles[pl.ds(192 * j, 96, stride=2), :]
        flat_ref[pl.ds(4, 96, stride=9), :] = jnp.where(low, narrow[pl.ds(0, 96, stride=2), :], odd[0])
        for j in range(3):
            flat_ref[pl.ds(5 + j, 96, stride=9), :] = jnp.where(low, odd[j], odd[j + 1])
        last = half_turn(narrow[pl.ds(1, 96, stride=2), :])
        flat_ref[pl.ds(8, 96, stride=9), :] = jnp.where(low, odd[3], last)

    @pl.when(kind == 2)
    def _():
        low = lower_lanes((288, LANES))
        narrow[0:288, :] = tiles[576:864, :]
        narrow[288:576, :] = half_turn(tiles[576:864, :])
        odd = half_turn(tiles[pl.ds(1, 288, stride=2), :])
        flat_ref[pl.ds(0, 288, stride=3), :] = tiles[pl.ds(0, 288, stride=2), :]
        flat_ref[pl.ds(1, 288, stride=3), :] = jnp.where(low, narrow[pl.ds(0, 288, stride=2), :], odd)
        last = half_turn(narrow[pl.ds(1, 288, stride=2), :])
        flat_ref[pl.ds(2, 288, stride=3), :] = jnp.where(low, odd, last)


    if len(states) == 3:
        states[0][...], states[1][...] = flat_ref[...], vector
        return
    old_vectors, old_block, new_vectors, new_block = states[0:3], states[3:6], states[6:9], states[9:12]
    found = adamw(old_vectors[0][...], vector, old_vectors[1][...], old_vectors[2][...], RATE_VECTOR, 0.0)
    for ref, value in zip(new_vectors, found):
        ref[...] = value

    @pl.loop(0, 6)
    def _(k):
        rows = pl.ds(pl.multiple_of(k * 144, 8), 144)
        found = adamw(
            old_block[0][rows, :], flat_ref[rows, :], old_block[1][rows, :], old_block[2][rows, :], RATE_MATRIX, DECAY
        )
        for ref, value in zip(new_block, found):
            ref[rows, :] = value


def finish(table, parts, inputs, state):
    vmem = pl.BlockSpec(memory_space=pltpu.VMEM)
    flat = jax.ShapeDtypeStruct((BLOCK_ROWS, LANES), F32)
    vector = jax.ShapeDtypeStruct((VECTOR_ROWS, LANES), F32)
    shapes = (vector,) * 3 + (flat,) * 3 if state else (flat, vector)
    shapes += (jax.ShapeDtypeStruct((2, MODEL_WIDTH, ROWS), BF16),)
    return pl.pallas_call(
        finish_kernel,
        out_shape=shapes,
        in_specs=[pl.BlockSpec(memory_space=pltpu.SMEM)] + [vmem] * (len(parts) + len(inputs) + len(state)),
        out_specs=(vmem,) * len(shapes),
        scratch_shapes=[
            pltpu.VMEM((BLOCK_ROWS, LANES), F32),
            pltpu.VMEM((HEAD_ROWS, LANES), F32),
            pltpu.VMEM((BLOCK_ROWS, LANES), F32),
            pltpu.VMEM((4, VECTOR_ROWS, LANES), F32),
        ],
        name="finish",
    )(table, *parts, *inputs, *state)


def product(left, right):
    return jnp.dot(left, right, preferred_element_type=F32)


def times_transposed(left, right):
    return lax.dot_general(left, right, (((1,), (1,)), ((), ())), preferred_element_type=F32)


def rows_product(left, right):
    return lax.dot_general(left, right, (((0,), (0,)), ((), ())), preferred_element_type=F32)


def swapped(value):
    lane = lax.broadcasted_iota(jnp.int32, value.shape, 1)
    return jnp.where(lane % HEAD_SIZE < HEAD_SIZE // 2, pltpu.roll(value, 96, 1), pltpu.roll(value, 32, 1))


def rope(value, cosines, sines):
    return value * cosines + swapped(value) * sines


def rope_back(value, cosines, sines):
    return value * cosines - swapped(value) * sines


def row_mean(value):
    return jnp.sum(value, axis=-1, keepdims=True) * (1.0 / MODEL_WIDTH)


def normed_rows(value):
    scale = lax.rsqrt(row_mean(value * value) + EPS_NORM)
    return value * scale, scale


def place_rows(ref, head_tile, tail_tile, first):
    for j in range(3):
        ref[first : first + 192, LANES * j : LANES * j + LANES] = head_tile[192 * j : 192 * j + 192, :]
    ref[first : first + 192, 384:512] = tail_tile[0:192, :]
    rest = tail_tile[192:288, :].astype(F32)
    low = lower_lanes(rest.shape)
    ref[first : first + 96, 512:640] = jnp.where(low, rest, 0.0).astype(BF16)
    ref[first + 96 : first + 192, 512:640] = jnp.where(low, half_turn(rest), 0.0).astype(BF16)


def tiles_of_rows(value):
    head = jnp.concatenate([value[:, LANES * j : LANES * j + LANES] for j in range(3)], axis=0)
    rest = side_by_side(value[0:96, 512:640], value[96:192, 512:640])
    return head, jnp.concatenate([value[:, 384:512], rest], axis=0)


def layer_kernel(*refs):
    slots = refs[0]
    head_parts = refs[1:9]
    tail_parts = refs[9:13]
    tokens_pair, cos_pair, sin_pair = refs[13:15], refs[15:17], refs[17:19]
    (place_q_ref, place_k_ref, gains_ref, bias_q_ref, bias_kv_ref, grad_ref) = refs[19:25]
    block_out_ref, parts_out = refs[25], refs[26:36]
    (dkv_send, dkv_keep, base_ref, w_kv) = refs[36:40]
    (raw_head, raw_tail, w_q, w_out, w_gate, w_up, w_down, normed_all, hidden_all, keys, values, queries, probs, attended, act_all, block_acc, d_hidden, d_attended, dkv_all, d_query, both_all, vector_ref, outs, sems, out_sems) = refs[40:]

    place = slots[MY_Z]

    def fetches(shift, sem):
        at = lax.rem(place + shift, 4)
        copies = []
        for k, part in enumerate(head_parts):
            copies.append(pltpu.make_async_copy(part.at[at], raw_head.at[4 * k + at], sems.at[sem + k]))
        for k, part in enumerate(tail_parts):
            rows = pl.ds(2 * at, 2)
            copies.append(pltpu.make_async_copy(part.at[rows], raw_tail.at[pl.ds(8 * k + 2 * at, 2)], sems.at[sem + 8 + k]))
        return copies

    attention_blocks = fetches(0, 0)
    other_blocks = fetches(1, 12) + fetches(2, 24) + fetches(3, 36)
    for copy in attention_blocks + other_blocks:
        copy.start()

    core = slots[MY_CORE]

    def at_slot(pair, slot):
        return pair[slot % 2].at[slot // 2]

    def head_tile(block):
        return raw_head.at[slots[AT_HEAD + block]]

    def tail_tile(block):
        return raw_tail.at[slots[AT_TAIL + block]]

    gain_one = gains_ref[0:1, :]
    gain_two = gains_ref[1:2, :]
    low_rows = lower_lanes((ROWS, LANES))

    for mb in range(0, 2):
        lane = lax.broadcasted_iota(jnp.int32, (ROWS, WIDE), 1)
        for slot in range(4):
            rows = pl.ds(mb * 512 + slot * ROWS, ROWS)
            x = jnp.where(lane < MODEL_WIDTH, at_slot(tokens_pair, slot)[mb].astype(F32), 0.0)
            normed, _ = normed_rows(x)
            normed_all[rows, :] = normed
            hidden_all[rows, :] = (normed * gain_one).astype(BF16)

    for copy in attention_blocks:
        copy.wait()
    for ref in (w_q, w_out, w_gate, w_up, w_kv):
        ref[576:640, :] = jnp.zeros((64, ref.shape[1]), BF16)
    for k in range(3):
        place_rows(w_q, head_tile(k), tail_tile(k), 192 * k)
        place_rows(w_out, head_tile(5 + k), tail_tile(5 + k), 192 * k)
    w_kv[0:576, 0:128] = head_tile(3)[...]
    w_kv[0:576, 128:256] = head_tile(4)[...]
    rest_key = tail_tile(3)[...].astype(F32)
    rest_value = tail_tile(4)[...].astype(F32)
    low = lower_lanes(rest_key.shape)
    w_kv[0:288, 256:384] = jnp.where(low, rest_key, half_turn(rest_value)).astype(BF16)
    w_kv[288:576, 256:384] = jnp.where(low, half_turn(rest_key), rest_value).astype(BF16)

    for mb in range(0, 2):
        rows = pl.ds(mb * 512, 512)
        pair = product(hidden_all[rows, :], w_kv[...]) + bias_kv_ref[...]
        cosines = jnp.concatenate([at_slot(cos_pair, slot)[mb] for slot in range(4)], axis=0)
        sines = jnp.concatenate([at_slot(sin_pair, slot)[mb] for slot in range(4)], axis=0)
        key_a = rope(pair[:, 0:128], cosines, sines)
        key_b = rope(pair[:, 256:384], cosines, sines)
        value_a, value_b = pair[:, 128:256], pair[:, 256:384]
        low_keys = lower_lanes((512, LANES))
        turned = half_turn(key_a)
        keys[rows, 0:128] = jnp.where(low_keys, key_a, turned).astype(BF16)
        keys[rows, 128:256] = jnp.where(low_keys, turned, key_a).astype(BF16)
        keys[rows, 256:384] = jnp.where(low_keys, key_b, half_turn(key_b)).astype(BF16)
        turned = half_turn(value_a)
        values[rows, 0:128] = jnp.where(low_keys, value_a, turned).astype(BF16)
        values[rows, 128:256] = jnp.where(low_keys, turned, value_a).astype(BF16)
        values[rows, 256:384] = jnp.where(low_keys, half_turn(value_b), value_b).astype(BF16)

    def heads_of(ref, rows, group):
        stacked = []
        for k in range(3):
            number = 3 * group + k
            tile = ref[rows, LANES * (number // 2) : LANES * (number // 2) + LANES]
            keep = low_rows if number % 2 == 0 else jnp.logical_not(low_rows)
            stacked.append(jnp.where(keep, tile.astype(F32), 0.0).astype(BF16))
        return jnp.concatenate(stacked, axis=0)

    def tiles_of_heads(parts):
        found = [jnp.where(low_rows, parts[2 * k], parts[2 * k + 1]) for k in range(4)]
        return found + [jnp.where(low_rows, parts[8], 0.0)]

    for mb in range(0, 2):
        rows = pl.ds(mb * ROWS, ROWS)
        key_rows = pl.ds(mb * 512, 512)
        cosines, sines = cos_pair[0][0, mb], sin_pair[0][0, mb]
        made = product(hidden_all[pl.ds(mb * 512, ROWS), :], w_q[...]) + bias_q_ref[...]
        for k in range(5):
            turned = rope(made[:, LANES * k : LANES * k + LANES], cosines, sines)
            queries[rows, LANES * k : LANES * k + LANES] = (turned * HEAD_SIZE ** (-0.5)).astype(BF16)
        masked = jnp.where(place_q_ref[mb] >= place_k_ref[mb], 0.0, MASKED)
        masked = jnp.concatenate([masked] * 3, axis=0)
        parts = []
        for group in range(KEY_VALUE_HEADS):
            lanes = slice(LANES * group, LANES * group + LANES)
            scores = times_transposed(heads_of(queries, rows, group), keys[key_rows, lanes])
            scores = scores + masked
            top = jnp.max(scores, axis=-1, keepdims=True)
            powers = jnp.exp(scores - top)
            found = powers * (1.0 / jnp.sum(powers, axis=-1, keepdims=True))
            probs[mb, group] = found
            out = product(found.astype(BF16), values[key_rows, lanes])
            outs[mb, group] = out
            parts += [out[ROWS * k : ROWS * k + ROWS] for k in range(3)]
        for k, tile in enumerate(tiles_of_heads(parts)):
            attended[rows, LANES * k : LANES * k + LANES] = tile.astype(BF16)

    for copy in other_blocks:
        copy.wait()
    for k in range(8):
        place_rows(w_down, head_tile(24 + k), tail_tile(24 + k), 192 * k)
    for ref, base in ((w_gate, 8), (w_up, 16)):
        for k in range(4):
            for i in range(6):
                if i < 4:
                    even = head_tile(base + 2 * k)[144 * i : 144 * i + 144, :].astype(F32)
                    odd = head_tile(base + 2 * k + 1)[144 * i : 144 * i + 144, :].astype(F32)
                else:
                    even = tail_tile(base + 2 * k)[144 * (i - 4) : 144 * (i - 4) + 144, :].astype(F32)
                    odd = tail_tile(base + 2 * k + 1)[144 * (i - 4) : 144 * (i - 4) + 144, :].astype(F32)
                ref[144 * k : 144 * k + 144, 256 * i : 256 * i + 128] = jnp.concatenate(
                    [even[0:72], odd[0:72]], axis=0
                ).astype(BF16)
                ref[144 * k : 144 * k + 144, 256 * i + 128 : 256 * i + 256] = jnp.concatenate(
                    [even[72:144], odd[72:144]], axis=0
                ).astype(BF16)

    lane = lax.broadcasted_iota(jnp.int32, (2 * ROWS, WIDE), 1)
    x_own = tokens_pair[0][0].astype(F32).reshape(2 * ROWS, WIDE)
    x_own = jnp.where(lane < MODEL_WIDTH, x_own, 0.0)
    resid_mid = x_own + product(attended[...], w_out[...])
    normed_two, scale_two = normed_rows(resid_mid)
    hidden_two = (normed_two * gain_two).astype(BF16)
    hidden_turned = hidden_two.T
    grad_low = grad_ref[...]
    block_acc[...] = resid_mid
    d_hidden[...] = jnp.zeros_like(d_hidden)

    def store_pair(at, even, odd, table, first):
        rows = pl.ds(pl.multiple_of(slots[table + at] + first, 16), even.shape[0])
        both_all[1 - core, rows, :] = even.astype(BF16)
        both_all[core, rows, :] = odd.astype(BF16)

    def feed_forward(chunk, first, table):
        cols = slice(chunk * 512, chunk * 512 + 512)
        gate = product(hidden_two, w_gate[:, cols])
        up = product(hidden_two, w_up[:, cols])
        sigma = 1.0 / (1.0 + jnp.exp(-gate))
        act = (gate * sigma * up).astype(BF16)
        act_all[:, cols] = act
        down = w_down[cols, :]
        d_act = times_transposed(grad_low, down)
        block_acc[...] += product(act, down)
        d_up = (d_act * gate * sigma).astype(BF16)
        d_gate = (d_act * up * sigma * (1.0 + gate * (1.0 - sigma))).astype(BF16)
        d_hidden[...] += times_transposed(d_gate, w_gate[:, cols]) + times_transposed(d_up, w_up[:, cols])
        for base, cotangent in ((4, d_gate), (8, d_up)):
            made = product(hidden_turned, cotangent)
            for k in range(4):
                part = made[144 * k : 144 * k + 144, :]
                even = jnp.concatenate([part[0:72, LANES * j : LANES * j + LANES] for j in range(4)], axis=0)
                odd = jnp.concatenate([part[72:144, LANES * j : LANES * j + LANES] for j in range(4)], axis=0)
                store_pair(base + k, even, odd, table, (chunk - first) * 288)

    feed_forward(0, 0, TO_HEAD)
    feed_forward(1, 0, TO_HEAD)
    feed_forward(2, 2, TO_TAIL)

    def store_rows(at, even, odd):
        even_head, even_tail = even
        odd_head, odd_tail = odd
        store_pair(at, even_head, odd_head, TO_HEAD, 0)
        store_pair(at, even_tail, odd_tail, TO_TAIL, 0)

    for k in range(0, 4):
        made = rows_product(act_all[:, pl.ds(k * 384, 384)], grad_low)
        store_rows(12 + k, tiles_of_rows(made[0:192]), tiles_of_rows(made[192:384]))

    def deliveries(z, sem):
        copies = []
        inside = pl.multiple_of(HEAD_ROWS * lax.rem(z + 4 - place, 4), HEAD_ROWS)
        for base, outs_of in ((both_all.at[0], parts_out[0:4]), (both_all.at[1], parts_out[4:10])):
            rest = [(outs_of[2], PART * k) for k in range(3)] if len(outs_of) == 4 else [(out, 0) for out in outs_of[2:5]]
            targets = [(outs_of[0], 0, FIRST_AT), (outs_of[1], 0, TAIL_AT)]
            targets += [(out, into, PART * k) for k, (out, into) in enumerate(rest)]
            targets.append((outs_of[-1], 0, 3 * PART))
            for out, into, start in targets:
                copies.append(
                    pltpu.make_async_copy(
                        base.at[pl.ds(pl.multiple_of(start + inside, 16), HEAD_ROWS)],
                        out.at[pl.ds(pl.multiple_of(into + inside, 16), HEAD_ROWS)],
                        out_sems.at[sem + len(copies)],
                    )
                )
        return copies

    early = deliveries(1, 12) + deliveries(2, 24) + deliveries(3, 36)
    for copy in early:
        copy.start()

    for mb in range(2):
        block_out_ref[mb] = block_acc[ROWS * mb : ROWS * mb + ROWS, :].T[0:MODEL_WIDTH].astype(BF16)

    d_two = d_hidden[...]
    gain_two_sum = jnp.sum(d_two * normed_two, axis=0, keepdims=True)
    d_norm = d_two * gain_two
    d_mid = grad_low.astype(F32) + scale_two * (d_norm - normed_two * row_mean(d_norm * normed_two))
    d_branch = d_mid.astype(BF16)
    d_attended[...] = times_transposed(d_branch, w_out[...]).astype(BF16)
    grad_out = rows_product(attended[...], d_branch)

    for mb in range(0, 2):
        rows = pl.ds(mb * ROWS, ROWS)
        key_rows = pl.ds(mb * 512, 512)
        parts = []
        d_keys = []
        d_values = []
        for group in range(KEY_VALUE_HEADS):
            lanes = slice(LANES * group, LANES * group + LANES)
            query_rows = heads_of(queries, rows, group)
            cotangent = heads_of(d_attended, rows, group)
            found = probs[mb, group]
            d_probs = times_transposed(cotangent, values[key_rows, lanes])
            delta = jnp.sum(outs[mb, group] * cotangent.astype(F32), axis=-1, keepdims=True)
            d_scores = (found * (d_probs - delta)).astype(BF16)
            out = product(d_scores, keys[key_rows, lanes]) * HEAD_SIZE ** (-0.5)
            parts += [out[ROWS * k : ROWS * k + ROWS] for k in range(3)]
            d_key = rows_product(d_scores, query_rows)
            d_value = rows_product(found.astype(BF16), cotangent)
            d_keys.append(d_key + half_turn(d_key))
            d_values.append(d_value + half_turn(d_value))
        cosines, sines = cos_pair[0][0, mb], sin_pair[0][0, mb]
        for k, tile in enumerate(tiles_of_heads(parts)):
            d_query[rows, LANES * k : LANES * k + LANES] = rope_back(tile, cosines, sines).astype(BF16)
        low_keys = lower_lanes((512, LANES))
        cosines = jnp.concatenate([at_slot(cos_pair, slot)[mb] for slot in range(4)], axis=0)
        sines = jnp.concatenate([at_slot(sin_pair, slot)[mb] for slot in range(4)], axis=0)
        key_a = rope_back(jnp.where(low_keys, d_keys[0], d_keys[1]), cosines, sines)
        key_b = rope_back(d_keys[2], cosines, sines)
        dkv_all[key_rows, 0:128] = key_a.astype(BF16)
        dkv_all[key_rows, 128:256] = jnp.where(low_keys, d_values[0], d_values[1]).astype(BF16)
        dkv_all[key_rows, 256:384] = jnp.where(low_keys, key_b, d_values[2]).astype(BF16)
        for slot in range(4):
            target = dkv_send if slot % 2 else dkv_keep
            target[slot // 2, mb] = dkv_all[pl.ds(mb * 512 + slot * ROWS, ROWS), :]

    dkv = dkv_all[...]
    d_q = d_query[...]
    dq_wq = times_transposed(d_q, w_q[...])
    normed = jnp.concatenate([normed_all[512 * mb : 512 * mb + ROWS, :] for mb in range(2)], axis=0)
    scale = lax.rsqrt(row_mean(x_own * x_own) + EPS_NORM)
    d_norm = dq_wq * gain_one
    base_ref[...] = d_mid + scale * (d_norm - normed * row_mean(d_norm * normed))
    bias_q_sum = jnp.sum(d_q.astype(F32), axis=0, keepdims=True)
    bias_kv_sum = jnp.sum(dkv.astype(F32), axis=0, keepdims=True)
    gain_sum = jnp.zeros((1, WIDE), F32)
    for mb in range(2):
        gain_sum += jnp.sum(dq_wq[ROWS * mb : ROWS * mb + ROWS] * normed_all[512 * mb : 512 * mb + ROWS, :], axis=0, keepdims=True)
    for k in range(4):
        part = slice(256 * k, 256 * k + 256)
        gain_sum += jnp.sum(times_transposed(dkv_all[part, :], w_kv[...]) * normed_all[part, :], axis=0, keepdims=True)

    hidden_own = jnp.concatenate([hidden_all[0:ROWS, :], hidden_all[512 : 512 + ROWS, :]], axis=0)
    grad_q = rows_product(hidden_own, d_q)
    grad_kv = rows_product(hidden_all[...], dkv)
    rest = grad_kv[0:576, 256:384]
    low = lower_lanes((288, LANES))
    key_tiles = (grad_kv[0:576, 0:128], jnp.where(low, rest[0:288], half_turn(rest[288:576])))
    value_tiles = (grad_kv[0:576, 128:256], jnp.where(low, half_turn(rest[0:288]), rest[288:576]))
    query_tiles = [tiles_of_rows(grad_q[192 * k : 192 * k + 192]) for k in range(3)]
    out_tiles = [tiles_of_rows(grad_out[192 * k : 192 * k + 192]) for k in range(3)]
    store_rows(0, query_tiles[0], query_tiles[1])
    store_rows(1, query_tiles[2], key_tiles)
    store_rows(2, value_tiles, out_tiles[0])
    store_rows(3, out_tiles[1], out_tiles[2])
    def flat_rows(first, second, third, pair):
        tile = lambda row, k: row[:, LANES * k : LANES * k + LANES]
        low = lower_lanes((1, LANES))
        across_two = lambda one, two: jnp.where(low, half_turn(one), half_turn(two))
        lines = [tile(first, k) for k in range(4)]
        lines.append(side_by_side(tile(first, 4), tile(second, 0)))
        lines += [across_two(tile(second, k), tile(second, k + 1)) for k in range(4)]
        lines += [tile(third, k) for k in range(4)]
        lines.append(side_by_side(tile(third, 4), tile(pair, 0)))
        lines.append(across_two(tile(pair, 0), tile(pair, 2)))
        lines.append(tile(pair, 1))
        lines.append(jnp.where(low, half_turn(tile(pair, 2)), 0.0))
        return lines

    at = FIRST_AT + PART
    for row, line in enumerate(flat_rows(gain_sum, gain_two_sum, bias_q_sum, bias_kv_sum)):
        vector_ref[row : row + 1, :] = line
    vector_ref[17:24, :] = jnp.zeros((7, LANES), F32)
    vector = vector_ref[...]
    high = vector.astype(BF16).astype(F32)
    both = jnp.concatenate([high, vector - high], axis=0).astype(BF16)
    for k in range(2):
        both_all[k, at : at + 2 * VECTOR_ROWS, :] = both
    last = deliveries(0, 0)
    last.append(pltpu.make_async_copy(both_all.at[0, pl.ds(at, 2 * VECTOR_ROWS)], parts_out[0].at[pl.ds(PART, 2 * VECTOR_ROWS)], out_sems.at[48]))
    last.append(pltpu.make_async_copy(both_all.at[1, pl.ds(at, 2 * VECTOR_ROWS)], parts_out[4].at[pl.ds(PART, 2 * VECTOR_ROWS)], out_sems.at[49]))
    for copy in last:
        copy.start()
    for copy in early + last:
        copy.wait()


def run_layer(slots, heads, tails, *others):
    shape = jax.ShapeDtypeStruct
    vmem = pl.BlockSpec(memory_space=pltpu.VMEM)
    anywhere = pl.BlockSpec(memory_space=pl.ANY)
    scratch = [
        ((BLOCKS, HEAD_ROWS, LANES), BF16),
        ((BLOCKS, TAIL_ROWS, LANES), BF16),
        ((WIDE, WIDE), BF16),
        ((WIDE, WIDE), BF16),
        ((WIDE, FF), BF16),
        ((WIDE, FF), BF16),
        ((FF, WIDE), BF16),
        ((1024, WIDE), F32),
        ((1024, WIDE), BF16),
        ((1024, 384), BF16),
        ((1024, 384), BF16),
        ((256, WIDE), BF16),
        ((2, 3, 384, 512), F32),
        ((256, WIDE), BF16),
        ((256, FF), BF16),
        ((256, WIDE), F32),
        ((256, WIDE), F32),
        ((256, WIDE), BF16),
        ((1024, 384), BF16),
        ((256, WIDE), BF16),
        ((2, ALL_ROWS, LANES), BF16),
        ((VECTOR_ROWS, LANES), F32),
        ((2, 3, 384, LANES), F32),
    ]
    return pl.pallas_call(
        layer_kernel,
        out_shape=(
            shape((2, MODEL_WIDTH, ROWS), BF16),
            *[shape((count, LANES), BF16) for _, count in SEND_PARTS + KEEP_PARTS],
            shape((2, 2, ROWS, 384), BF16),
            shape((2, 2, ROWS, 384), BF16),
            shape((256, WIDE), F32),
            shape((WIDE, 384), BF16),
        ),
        in_specs=[pl.BlockSpec(memory_space=pltpu.SMEM)] + [anywhere] * 12 + [vmem] * 12,
        out_specs=(vmem,) + (anywhere,) * 10 + (vmem,) * 4,
        scratch_shapes=[pltpu.VMEM(dims, kind) for dims, kind in scratch]
        + [pltpu.SemaphoreType.DMA((48,)), pltpu.SemaphoreType.DMA((50,))],
        compiler_params=pltpu.CompilerParams(vmem_limit_bytes=50 * 1024 * 1024),
        name="layer",
    )(slots, *heads, *tails, *others)


def adamw(param, grad, mom_one, mom_two, rate, decay):
    new_one = BETA_ONE * mom_one + (1.0 - BETA_ONE) * grad
    new_two = BETA_TWO * mom_two + (1.0 - BETA_TWO) * grad * grad
    fixed_one = new_one / (1.0 - BETA_ONE**STEP)
    fixed_two = new_two / (1.0 - BETA_TWO**STEP)
    new_param = param - rate * (fixed_one / (jnp.sqrt(fixed_two) + EPS_ADAM) + decay * param)
    return (new_param, new_one, new_two)


def inner_groups():
    inner = inner_count()
    data_inner = inner // lax.axis_size("ctx")
    data_count = lax.axis_size("dp")
    return [list(range(k, k + data_inner)) for k in range(0, data_count, data_inner)]


def whole_block(flat):
    if inner_count() == 1:
        return flat
    flat = lax.all_gather(flat, "ctx", axis=0, tiled=True)
    return lax.all_gather(flat, "dp", axis=0, tiled=True, axis_index_groups=inner_groups())


def own_slice(block):
    if inner_count() == 1:
        return block
    block = lax.psum_scatter(
        block, "dp", scatter_dimension=0, tiled=True, axis_index_groups=inner_groups()
    )
    return lax.psum_scatter(block, "ctx", scatter_dimension=0, tiled=True)


def bias_tiles(bias_key, bias_value):
    return jnp.concatenate([bias_key[:128], bias_value[:128], bias_key[128:], bias_value[128:]])


def local(tokens_in, places, out_grad, weights, first_moment, second_moment, vectors, vector_first, vector_second):
    kind = kind_of(device_number() // inner_count()).astype(jnp.int32).reshape(1)
    block = whole_block(weights).reshape(BLOCK_ROWS, LANES)
    head, tail = to_tiles(kind, block)

    head, tail, tokens_in, places = together(head, tail, tokens_in, places)
    own_tokens = tokens_in.reshape(2, ROWS, MODEL_WIDTH)
    own_places = places.reshape(2, ROWS)
    marks = jnp.stack([own_places // 16, own_places % 16], axis=-1).astype(BF16)
    packed = jnp.concatenate(
        [own_tokens, marks, jnp.zeros((2, ROWS, WIDE - MODEL_WIDTH - 2), BF16)], axis=-1
    )
    padding = ((0, 0), (0, WIDE - MODEL_WIDTH))
    gains = jnp.pad(vectors[: 2 * MODEL_WIDTH].reshape(2, MODEL_WIDTH), padding)
    bias_q = jnp.pad(vectors[2 * MODEL_WIDTH : 3 * MODEL_WIDTH].reshape(1, MODEL_WIDTH), padding)
    bias_kv = bias_tiles(vectors[1728:1920], vectors[1920:2112]).reshape(1, 384)
    grad = jnp.pad(out_grad.reshape(2 * ROWS, MODEL_WIDTH), padding)
    spare = VECTOR_ROWS * LANES - vectors.shape[0]
    vector_state = [
        jnp.pad(array, (0, spare), constant_values=1.0).reshape(VECTOR_ROWS, LANES)
        for array in (vectors, vector_first, vector_second)
    ]
    table = jnp.concatenate([kind, (coordinates(device_number() // inner_count())["z"]).astype(jnp.int32).reshape(1)])
    others = (slot_table(), gains, bias_q, bias_kv, grad, vector_state, table)
    heads, tails, (near, far), (cosines, sines), others = gather_all(head, tail, packed, others)
    slots, gains, bias_q, bias_kv, grad, vector_state, table = others
    cosines_far, sines_far = place_tables(far)
    place_all = jnp.stack([places_of(near), places_of(far)], axis=1)
    place_q = place_all[0, 0][..., None]
    place_k = jnp.transpose(place_all.reshape(4, 2, ROWS), (1, 0, 2)).reshape(2, 1, 4 * ROWS)

    block_out, *found = run_layer(
        slots, heads, tails, near, far, cosines, cosines_far, sines, sines_far, place_q, place_k, gains, bias_q, bias_kv, grad
    )
    sends, keeps = found[:4], found[4:10]
    dkv_send, dkv_keep, base, w_kv = found[10:]
    parts, pairs = scatter_blocks(sends, keeps, dkv_send, dkv_keep)
    inputs = (packed, gains, w_kv, base, *pairs)
    state = (weights, first_moment, second_moment)
    if inner_count() == 1:
        blocks = [array.reshape(BLOCK_ROWS, LANES) for array in state]
        *updated, input_grad = finish(table, parts, inputs, [*vector_state, *blocks])
        new_vector_state = [array.reshape(-1)[: vectors.shape[0]] for array in updated[:3]]
        new_state = [array.reshape(-1) for array in updated[3:]]
    else:
        block_grad, vector, input_grad = finish(table, parts, inputs, [])
        vector = lax.psum(vector, "ctx")
        vector = lax.psum(vector, "dp", axis_index_groups=inner_groups())
        grad_own = own_slice(block_grad.reshape(-1))
        vector_grad = vector.reshape(-1)[: vectors.shape[0]]
        new_state = adamw(weights, grad_own, first_moment, second_moment, RATE_MATRIX, DECAY)
        new_vector_state = adamw(vectors, vector_grad, vector_first, vector_second, RATE_VECTOR, 0.0)
    shape = tokens_in.shape
    return (
        jnp.transpose(block_out, (0, 2, 1)).reshape(shape),
        jnp.transpose(input_grad, (0, 2, 1)).reshape(shape),
        *new_state,
        *new_vector_state,
    )


def solution(mesh):
    in_specs = (
        P(None, "dp", "ctx", None),
        P(None, "dp", "ctx"),
        P(None, "dp", "ctx", None),
        P(("dp", "ctx")),
        P(("dp", "ctx")),
        P(("dp", "ctx")),
        P(),
        P(),
        P(),
    )
    out_specs = (
        P(None, "dp", "ctx", None),
        P(None, "dp", "ctx", None),
        P(("dp", "ctx")),
        P(("dp", "ctx")),
        P(("dp", "ctx")),
        P(),
        P(),
        P(),
    )
    return jax.shard_map(local, mesh=mesh, in_specs=in_specs, out_specs=out_specs, check_vma=False)
```

```python
import jax
import jax.numpy as jnp
from jax import lax
from jax.experimental import pallas as pl
from jax.experimental.pallas import tpu as pltpu
from jax.sharding import PartitionSpec as P

MODEL_WIDTH = 576
QUERY_HEADS = 9
KEY_VALUE_HEADS = 3
HEAD_SIZE = 64
FF = 1536
STEP = 10

EPS_NORM = 1e-05
THETA = 100000.0
BETA_ONE = 0.9
BETA_TWO = 0.95
EPS_ADAM = 1e-08
RATE_MATRIX = 0.06
RATE_VECTOR = 0.3
DECAY = 0.1
MASKED = -1e30

LANES = 128
WIDE = 640
BLOCKS = 32
BLOCK_ROWS = 864
HEAD_ROWS = 576
TAIL_ROWS = BLOCK_ROWS - HEAD_ROWS
VECTOR_ROWS = 24
PART = 4 * HEAD_ROWS
FIRST_AT = 4 * PART
TAIL_AT = FIRST_AT + PART + 2 * VECTOR_ROWS
ALL_ROWS = TAIL_AT + PART
SEND_PARTS = [(FIRST_AT, PART + 2 * VECTOR_ROWS), (TAIL_AT, PART), (0, 3 * PART), (3 * PART, PART)]
KEEP_PARTS = SEND_PARTS[:2] + [(PART * k, PART) for k in range(4)]
SIZES = {"z": 4, "y": 2, "x": 2, "c": 2}
ROWS = 128
F32 = jnp.float32
BF16 = jnp.bfloat16


def coordinates(number):
    found = {}
    for name in ("c", "x", "y", "z"):
        found[name] = number % SIZES[name]
        number = number // SIZES[name]
    return found


def number_of(found):
    number = 0
    for name in ("z", "y", "x", "c"):
        number = number * SIZES[name] + found[name]
    return number


def device_number():
    return lax.axis_index("dp") * lax.axis_size("ctx") + lax.axis_index("ctx")


def inner_count():
    return lax.axis_size("dp") * lax.axis_size("ctx") // BLOCKS


def moved(buffer, name, shift):
    inner = inner_count()
    pairs = []
    for number in range(BLOCKS):
        found = coordinates(number)
        found[name] = (found[name] + shift) % SIZES[name]
        target = number_of(found)
        pairs += [(number * inner + k, target * inner + k) for k in range(inner)]
    return lax.ppermute(buffer, ("dp", "ctx"), pairs)


def across(buffer, distance):
    count = lax.axis_size("ctx")
    return lax.ppermute(buffer, "ctx", [(i, i ^ distance) for i in range(count)])


def together(*arrays):
    return lax.optimization_barrier(arrays)


def gather_all(head, tail, packed, others):
    head, tail, packed = together(head, tail, packed)
    hz = [moved(head, "z", s) for s in (1, 2, 3)]
    tx = moved(tail, "x", 1)
    two = across(packed, 2)
    hz, head, tail, tx, two = together(hz[::-1], head, tail, tx, two)
    hz = hz[::-1]
    own = jnp.stack([head] + hz)
    pair = jnp.stack([tail, tx])
    ay = moved(own, "y", 1)
    ax = moved(own, "x", 1)
    near = jnp.stack([packed, two])
    tables = place_tables(near)
    pair, near = together(pair, near)
    tz = [moved(pair, "z", s) for s in (1, 2, 3)]
    own, pair, tz, ax, ay, near, tables, others = together(own, pair, tz[::-1], ax, ay, near, tables, others)
    tz = tz[::-1]
    eight = jnp.concatenate([pair] + tz)
    far = across(near, 1)
    axy = moved(ay, "x", 1)
    ty = moved(eight, "y", 1)
    ac = moved(own, "c", 1)
    acy = moved(ay, "c", 1)
    acx = moved(ax, "c", 1)
    tc = moved(eight, "c", 1)
    tc, acx, acy, ac, far, ty, axy = together(tc, acx, acy, ac, far, ty, axy)
    acxy = moved(axy, "c", 1)
    tcy = moved(ty, "c", 1)
    heads = [own, ay, ax, axy, ac, acy, acx, acxy]
    return heads, [eight, ty, tc, tcy], (near, far), tables, others


def places_of(tokens):
    found = tokens[..., MODEL_WIDTH : MODEL_WIDTH + 2].astype(F32)
    return found[..., 0] * 16.0 + found[..., 1]


def place_tables(tokens):
    half_dim = HEAD_SIZE // 2
    frequency = THETA ** (-2.0 * jnp.arange(half_dim, dtype=F32) / HEAD_SIZE)
    angles = places_of(tokens)[..., None] * jnp.tile(frequency, 4)
    sign = jnp.where(jnp.arange(LANES) % HEAD_SIZE < half_dim, -1.0, 1.0).astype(F32)
    return jnp.cos(angles), jnp.sin(angles) * sign


def fold(order, relative):
    slot = 0
    for name in order:
        slot = slot * SIZES[name] + relative[name]
    return slot


def head_row(slot, z, _):
    return slot * PART + jnp.where(slot < 3, 0, FIRST_AT - 3 * PART) + z * HEAD_ROWS


def tail_row(slot, z, inside):
    return jnp.where(slot < 1, 3 * PART, TAIL_AT) + (2 * z + inside) * TAIL_ROWS


def slot_table():
    mine = coordinates(device_number() // inner_count())
    entries = []
    for order in (("c", "x", "y", "z"), ("c", "y", "z", "x")):
        for number in range(BLOCKS):
            found = coordinates(number)
            entries.append(fold(order, {n: (mine[n] - found[n]) % SIZES[n] for n in SIZES}))
    for order, start in ((("x", "y"), head_row), (("y",), tail_row)):
        for number in range(0, BLOCKS, 2):
            found = coordinates(number)
            slot = fold(order, {n: (found[n] - mine[n]) % SIZES[n] for n in SIZES})
            inside = (found["x"] - mine["x"]) % SIZES["x"]
            entries.append(start(slot, (found["z"] - mine["z"]) % SIZES["z"], inside))
    entries.append(mine["c"])
    entries.append(mine["z"])
    return jnp.stack([jnp.asarray(entry, jnp.int32) for entry in entries])


AT_HEAD, AT_TAIL, TO_HEAD, TO_TAIL = 0, BLOCKS, 2 * BLOCKS, 2 * BLOCKS + 16
MY_CORE, MY_Z = 2 * BLOCKS + 32, 2 * BLOCKS + 33


def summed(*parts):
    total = parts[0].astype(F32)
    for part in parts[1:]:
        total = total + part.astype(F32)
    return total


def summed_vector(mine, other):
    total = summed(mine[:VECTOR_ROWS], other[:VECTOR_ROWS]) + summed(mine[VECTOR_ROWS:], other[VECTOR_ROWS:])
    high = lax.reduce_precision(total, 8, 7)
    return jnp.concatenate([high.astype(BF16), (total - high).astype(BF16)])


def scatter_blocks(sends, keeps, dkv_send, dkv_keep):
    keep_head, keep_tail, keep_low, keep_mid, keep_far, keep_rest = keeps
    got_head, got_tail = moved(sends[0], "c", 1), moved(sends[1], "c", 1)
    got_head, got_tail, rest_head, rest_tail, dkv_send = together(got_head, got_tail, *sends[2:], dkv_send)
    got_rest_head, got_rest_tail = moved(rest_head, "c", 1), moved(rest_tail, "c", 1)
    got_dkv = across(dkv_send, 1)
    vector = summed_vector(keep_head[PART:], got_head[PART:])
    hx = jnp.concatenate([summed(keep_head[:PART], got_head[:PART]).astype(BF16), vector])
    ty = summed(keep_tail, got_tail).astype(BF16)
    got_hx = moved(hx, "x", 1)
    got_ty = moved(ty, "y", 1)
    low, mid, far = [
        summed(keep, got_rest_head[PART * k : PART * k + PART]).astype(BF16)
        for k, keep in enumerate((keep_low, keep_mid, keep_far))
    ]
    tail = summed(keep_rest, got_rest_tail).astype(BF16)
    dkv = summed(dkv_keep, got_dkv).astype(BF16)
    got_hx, got_ty, low, mid, far, tail, dkv, vector = together(got_hx, got_ty, low, mid, far, tail, dkv, vector)

    def part_for(array, shift):
        return array[HEAD_ROWS * shift : HEAD_ROWS * shift + HEAD_ROWS]

    vector = summed_vector(vector, got_hx[PART:])
    hy = jnp.concatenate([summed(mid, got_hx[:PART]).astype(BF16), vector])
    tz = [summed(part_for(tail, s), part_for(got_ty, s)).astype(BF16) for s in range(4)]
    got_hy = moved(hy, "y", 1)
    got_far = moved(far, "x", 1)
    got_tz = [moved(tz[s], "z", s) for s in (1, 2, 3)]
    got_tz, got_far, got_hy, low, own_tail, vector, dkv = together(got_tz[::-1], got_far, got_hy, low, tz[0], vector, dkv)
    got_tz = got_tz[::-1]
    vector = summed_vector(vector, got_hy[PART:])
    head = [summed(part_for(low, s), part_for(got_far, s), part_for(got_hy, s)) for s in range(4)]
    got_hz = [moved(jnp.concatenate([head[s].astype(BF16), vector]), "z", s) for s in (1, 2, 3)]
    tx = summed(own_tail[TAIL_ROWS:], *[part[TAIL_ROWS:] for part in got_tz]).astype(BF16)
    own_tail = summed(own_tail[:TAIL_ROWS], *[part[:TAIL_ROWS] for part in got_tz])
    got_tx = moved(tx, "x", 1)
    got_dkv = across(dkv[1], 2)
    return (head[0], *got_hz[::-1], own_tail, got_tx, vector), (dkv[0], got_dkv)


def lower_lanes(shape):
    return lax.broadcasted_iota(jnp.int32, shape, 1) < HEAD_SIZE


def half_turn(value):
    return pltpu.roll(value, HEAD_SIZE, 1)


def side_by_side(left, right):
    return jnp.where(lower_lanes(left.shape), left, half_turn(right))


def kind_of(block):
    return jnp.where(block >= 24, 1, jnp.where(block >= 8, 0, jnp.where((block == 3) | (block == 4), 2, 1)))


def tile_kernel(kind_ref, flat_ref, head_ref, tail_ref, tiles, narrow):
    kind = kind_ref[0]

    @pl.when(kind == 0)
    def _():
        for j in range(12):
            tiles[72 * j : 72 * j + 72, :] = flat_ref[pl.ds(j, 72, stride=12), :]

    @pl.when(kind == 1)
    def _():
        lines = [flat_ref[pl.ds(t, 96, stride=9), :] for t in range(9)]
        turned = [half_turn(line) for line in lines[4:]]
        low = lower_lanes((96, LANES))
        for j in range(4):
            tiles[pl.ds(192 * j, 96, stride=2), :] = lines[j]
            tiles[pl.ds(192 * j + 1, 96, stride=2), :] = jnp.where(low, turned[j], turned[j + 1])
        narrow[pl.ds(0, 96, stride=2), :] = lines[4]
        narrow[pl.ds(1, 96, stride=2), :] = turned[4]
        tiles[768:864, :] = side_by_side(narrow[0:96, :], narrow[96:192, :])

    @pl.when(kind == 2)
    def _():
        lines = [flat_ref[pl.ds(t, 288, stride=3), :] for t in range(3)]
        first, second = half_turn(lines[1]), half_turn(lines[2])
        tiles[pl.ds(0, 288, stride=2), :] = lines[0]
        tiles[pl.ds(1, 288, stride=2), :] = jnp.where(lower_lanes((288, LANES)), first, second)
        narrow[pl.ds(0, 288, stride=2), :] = lines[1]
        narrow[pl.ds(1, 288, stride=2), :] = second
        tiles[576:864, :] = side_by_side(narrow[0:288, :], narrow[288:576, :])

    head_ref[...] = tiles[0:HEAD_ROWS, :].astype(BF16)
    tail_ref[...] = tiles[HEAD_ROWS:BLOCK_ROWS, :].astype(BF16)


def to_tiles(kind, flat):
    return pl.pallas_call(
        tile_kernel,
        out_shape=(
            jax.ShapeDtypeStruct((HEAD_ROWS, LANES), BF16),
            jax.ShapeDtypeStruct((TAIL_ROWS, LANES), BF16),
        ),
        in_specs=[
            pl.BlockSpec(memory_space=pltpu.SMEM),
            pl.BlockSpec(memory_space=pltpu.VMEM),
        ],
        out_specs=(pl.BlockSpec(memory_space=pltpu.VMEM),) * 2,
        scratch_shapes=[
            pltpu.VMEM((BLOCK_ROWS, LANES), F32),
            pltpu.VMEM((HEAD_ROWS, LANES), F32),
        ],
        name="to_tiles",
    )(kind, flat)


def finish_kernel(table_ref, head_ref, three_ref, two_ref, one_ref, tail_ref, other_ref, mine_ref, *refs):
    kind, place = table_ref[0], table_ref[1]
    tiles, narrow, flat_ref, vector_parts = refs[-4:]
    tokens_ref, gains_ref, w_kv_ref, base_ref, own_dkv, other_dkv = refs[:6]
    states = refs[6:-4]
    tiles[0:HEAD_ROWS, :] = (head_ref[...] + one_ref[0:HEAD_ROWS, :].astype(F32)) + (
        two_ref[0:HEAD_ROWS, :].astype(F32) + three_ref[0:HEAD_ROWS, :].astype(F32)
    )
    tiles[HEAD_ROWS:BLOCK_ROWS, :] = tail_ref[...] + other_ref[...].astype(F32)

    for at, ref in enumerate((mine_ref, one_ref, two_ref, three_ref)):
        rows = ref.shape[0]
        part = ref[rows - 2 * VECTOR_ROWS : rows, :].astype(F32)
        vector_parts[at] = part[:VECTOR_ROWS] + part[VECTOR_ROWS:]
    vector = vector_parts[lax.rem(place, 4)]
    for z in (1, 2, 3):
        vector = vector + vector_parts[lax.rem(place + 4 - z, 4)]

    lane = lax.broadcasted_iota(jnp.int32, (2 * ROWS, WIDE), 1)
    x = jnp.where(lane < MODEL_WIDTH, tokens_ref[...].astype(F32).reshape(2 * ROWS, WIDE), 0.0)
    normed, scale = normed_rows(x)
    total = summed(own_dkv[...], other_dkv[...]).reshape(2 * ROWS, 384).astype(BF16)
    d_norm = times_transposed(total, w_kv_ref[...]) * gains_ref[0:1, :]
    d_input = base_ref[...] + scale * (d_norm - normed * row_mean(d_norm * normed))
    out_ref = states[-1]
    for mb in range(2):
        out_ref[mb] = d_input[ROWS * mb : ROWS * mb + ROWS].T[0:MODEL_WIDTH].astype(BF16)

    @pl.when(kind == 0)
    def _():
        for j in range(12):
            flat_ref[pl.ds(j, 72, stride=12), :] = tiles[72 * j : 72 * j + 72, :]

    @pl.when(kind == 1)
    def _():
        low = lower_lanes((96, LANES))
        narrow[0:96, :] = tiles[768:864, :]
        narrow[96:192, :] = half_turn(tiles[768:864, :])
        odd = [half_turn(tiles[pl.ds(192 * j + 1, 96, stride=2), :]) for j in range(4)]
        for j in range(4):
            flat_ref[pl.ds(j, 96, stride=9), :] = tiles[pl.ds(192 * j, 96, stride=2), :]
        flat_ref[pl.ds(4, 96, stride=9), :] = jnp.where(low, narrow[pl.ds(0, 96, stride=2), :], odd[0])
        for j in range(3):
            flat_ref[pl.ds(5 + j, 96, stride=9), :] = jnp.where(low, odd[j], odd[j + 1])
        last = half_turn(narrow[pl.ds(1, 96, stride=2), :])
        flat_ref[pl.ds(8, 96, stride=9), :] = jnp.where(low, odd[3], last)

    @pl.when(kind == 2)
    def _():
        low = lower_lanes((288, LANES))
        narrow[0:288, :] = tiles[576:864, :]
        narrow[288:576, :] = half_turn(tiles[576:864, :])
        odd = half_turn(tiles[pl.ds(1, 288, stride=2), :])
        flat_ref[pl.ds(0, 288, stride=3), :] = tiles[pl.ds(0, 288, stride=2), :]
        flat_ref[pl.ds(1, 288, stride=3), :] = jnp.where(low, narrow[pl.ds(0, 288, stride=2), :], odd)
        last = half_turn(narrow[pl.ds(1, 288, stride=2), :])
        flat_ref[pl.ds(2, 288, stride=3), :] = jnp.where(low, odd, last)


    if len(states) == 3:
        states[0][...], states[1][...] = flat_ref[...], vector
        return
    old_vectors, old_block, new_vectors, new_block = states[0:3], states[3:6], states[6:9], states[9:12]
    found = adamw(old_vectors[0][...], vector, old_vectors[1][...], old_vectors[2][...], RATE_VECTOR, 0.0)
    for ref, value in zip(new_vectors, found):
        ref[...] = value

    @pl.loop(0, 6)
    def _(k):
        rows = pl.ds(pl.multiple_of(k * 144, 8), 144)
        found = adamw(
            old_block[0][rows, :], flat_ref[rows, :], old_block[1][rows, :], old_block[2][rows, :], RATE_MATRIX, DECAY
        )
        for ref, value in zip(new_block, found):
            ref[rows, :] = value


def finish(table, parts, inputs, state):
    vmem = pl.BlockSpec(memory_space=pltpu.VMEM)
    flat = jax.ShapeDtypeStruct((BLOCK_ROWS, LANES), F32)
    vector = jax.ShapeDtypeStruct((VECTOR_ROWS, LANES), F32)
    shapes = (vector,) * 3 + (flat,) * 3 if state else (flat, vector)
    shapes += (jax.ShapeDtypeStruct((2, MODEL_WIDTH, ROWS), BF16),)
    return pl.pallas_call(
        finish_kernel,
        out_shape=shapes,
        in_specs=[pl.BlockSpec(memory_space=pltpu.SMEM)] + [vmem] * (len(parts) + len(inputs) + len(state)),
        out_specs=(vmem,) * len(shapes),
        scratch_shapes=[
            pltpu.VMEM((BLOCK_ROWS, LANES), F32),
            pltpu.VMEM((HEAD_ROWS, LANES), F32),
            pltpu.VMEM((BLOCK_ROWS, LANES), F32),
            pltpu.VMEM((4, VECTOR_ROWS, LANES), F32),
        ],
        name="finish",
    )(table, *parts, *inputs, *state)


def product(left, right):
    return jnp.dot(left, right, preferred_element_type=F32)


def times_transposed(left, right):
    return lax.dot_general(left, right, (((1,), (1,)), ((), ())), preferred_element_type=F32)


def rows_product(left, right):
    return lax.dot_general(left, right, (((0,), (0,)), ((), ())), preferred_element_type=F32)


def swapped(value):
    lane = lax.broadcasted_iota(jnp.int32, value.shape, 1)
    return jnp.where(lane % HEAD_SIZE < HEAD_SIZE // 2, pltpu.roll(value, 96, 1), pltpu.roll(value, 32, 1))


def rope(value, cosines, sines):
    return value * cosines + swapped(value) * sines


def rope_back(value, cosines, sines):
    return value * cosines - swapped(value) * sines


def row_mean(value):
    return jnp.sum(value, axis=-1, keepdims=True) * (1.0 / MODEL_WIDTH)


def normed_rows(value):
    scale = lax.rsqrt(row_mean(value * value) + EPS_NORM)
    return value * scale, scale


def place_rows(ref, head_tile, tail_tile, first):
    for j in range(3):
        ref[first : first + 192, LANES * j : LANES * j + LANES] = head_tile[192 * j : 192 * j + 192, :]
    ref[first : first + 192, 384:512] = tail_tile[0:192, :]
    rest = tail_tile[192:288, :].astype(F32)
    low = lower_lanes(rest.shape)
    ref[first : first + 96, 512:640] = jnp.where(low, rest, 0.0).astype(BF16)
    ref[first + 96 : first + 192, 512:640] = jnp.where(low, half_turn(rest), 0.0).astype(BF16)


def tiles_of_rows(value):
    head = jnp.concatenate([value[:, LANES * j : LANES * j + LANES] for j in range(3)], axis=0)
    rest = side_by_side(value[0:96, 512:640], value[96:192, 512:640])
    return head, jnp.concatenate([value[:, 384:512], rest], axis=0)


def layer_kernel(*refs):
    slots = refs[0]
    head_parts = refs[1:9]
    tail_parts = refs[9:13]
    tokens_pair, cos_pair, sin_pair = refs[13:15], refs[15:17], refs[17:19]
    (place_q_ref, place_k_ref, gains_ref, bias_q_ref, bias_kv_ref, grad_ref) = refs[19:25]
    block_out_ref, parts_out = refs[25], refs[26:36]
    (dkv_send, dkv_keep, base_ref, w_kv) = refs[36:40]
    (raw_head, raw_tail, w_q, w_out, w_gate, w_up, w_down, normed_all, hidden_all, keys, values, queries, probs, attended, act_all, block_acc, d_hidden, d_attended, dkv_all, d_query, both_all, vector_ref, outs, sems, out_sems) = refs[40:]

    place = slots[MY_Z]

    def fetches(shift, sem):
        at = lax.rem(place + shift, 4)
        copies = []
        for k, part in enumerate(head_parts):
            copies.append(pltpu.make_async_copy(part.at[at], raw_head.at[4 * k + at], sems.at[sem + k]))
        for k, part in enumerate(tail_parts):
            rows = pl.ds(2 * at, 2)
            copies.append(pltpu.make_async_copy(part.at[rows], raw_tail.at[pl.ds(8 * k + 2 * at, 2)], sems.at[sem + 8 + k]))
        return copies

    attention_blocks = fetches(0, 0)
    other_blocks = fetches(1, 12) + fetches(2, 24) + fetches(3, 36)
    for copy in attention_blocks + other_blocks:
        copy.start()

    core = slots[MY_CORE]

    def at_slot(pair, slot):
        return pair[slot % 2].at[slot // 2]

    def head_tile(block):
        return raw_head.at[slots[AT_HEAD + block]]

    def tail_tile(block):
        return raw_tail.at[slots[AT_TAIL + block]]

    gain_one = gains_ref[0:1, :]
    gain_two = gains_ref[1:2, :]
    low_rows = lower_lanes((ROWS, LANES))

    for mb in range(0, 2):
        lane = lax.broadcasted_iota(jnp.int32, (ROWS, WIDE), 1)
        for slot in range(4):
            rows = pl.ds(mb * 512 + slot * ROWS, ROWS)
            x = jnp.where(lane < MODEL_WIDTH, at_slot(tokens_pair, slot)[mb].astype(F32), 0.0)
            normed, _ = normed_rows(x)
            normed_all[rows, :] = normed
            hidden_all[rows, :] = (normed * gain_one).astype(BF16)

    for copy in attention_blocks:
        copy.wait()
    for ref in (w_q, w_out, w_gate, w_up, w_kv):
        ref[576:640, :] = jnp.zeros((64, ref.shape[1]), BF16)
    for k in range(3):
        place_rows(w_q, head_tile(k), tail_tile(k), 192 * k)
        place_rows(w_out, head_tile(5 + k), tail_tile(5 + k), 192 * k)
    w_kv[0:576, 0:128] = head_tile(3)[...]
    w_kv[0:576, 128:256] = head_tile(4)[...]
    rest_key = tail_tile(3)[...].astype(F32)
    rest_value = tail_tile(4)[...].astype(F32)
    low = lower_lanes(rest_key.shape)
    w_kv[0:288, 256:384] = jnp.where(low, rest_key, half_turn(rest_value)).astype(BF16)
    w_kv[288:576, 256:384] = jnp.where(low, half_turn(rest_key), rest_value).astype(BF16)

    for mb in range(0, 2):
        rows = pl.ds(mb * 512, 512)
        pair = product(hidden_all[rows, :], w_kv[...]) + bias_kv_ref[...]
        cosines = jnp.concatenate([at_slot(cos_pair, slot)[mb] for slot in range(4)], axis=0)
        sines = jnp.concatenate([at_slot(sin_pair, slot)[mb] for slot in range(4)], axis=0)
        key_a = rope(pair[:, 0:128], cosines, sines)
        key_b = rope(pair[:, 256:384], cosines, sines)
        value_a, value_b = pair[:, 128:256], pair[:, 256:384]
        low_keys = lower_lanes((512, LANES))
        turned = half_turn(key_a)
        keys[rows, 0:128] = jnp.where(low_keys, key_a, turned).astype(BF16)
        keys[rows, 128:256] = jnp.where(low_keys, turned, key_a).astype(BF16)
        keys[rows, 256:384] = jnp.where(low_keys, key_b, half_turn(key_b)).astype(BF16)
        turned = half_turn(value_a)
        values[rows, 0:128] = jnp.where(low_keys, value_a, turned).astype(BF16)
        values[rows, 128:256] = jnp.where(low_keys, turned, value_a).astype(BF16)
        values[rows, 256:384] = jnp.where(low_keys, half_turn(value_b), value_b).astype(BF16)

    def heads_of(ref, rows, group):
        stacked = []
        for k in range(3):
            number = 3 * group + k
            tile = ref[rows, LANES * (number // 2) : LANES * (number // 2) + LANES]
            keep = low_rows if number % 2 == 0 else jnp.logical_not(low_rows)
            stacked.append(jnp.where(keep, tile.astype(F32), 0.0).astype(BF16))
        return jnp.concatenate(stacked, axis=0)

    def tiles_of_heads(parts):
        found = [jnp.where(low_rows, parts[2 * k], parts[2 * k + 1]) for k in range(4)]
        return found + [jnp.where(low_rows, parts[8], 0.0)]

    for mb in range(0, 2):
        rows = pl.ds(mb * ROWS, ROWS)
        key_rows = pl.ds(mb * 512, 512)
        cosines, sines = cos_pair[0][0, mb], sin_pair[0][0, mb]
        made = product(hidden_all[pl.ds(mb * 512, ROWS), :], w_q[...]) + bias_q_ref[...]
        for k in range(5):
            turned = rope(made[:, LANES * k : LANES * k + LANES], cosines, sines)
            queries[rows, LANES * k : LANES * k + LANES] = (turned * HEAD_SIZE ** (-0.5)).astype(BF16)
        masked = jnp.where(place_q_ref[mb] >= place_k_ref[mb], 0.0, MASKED)
        masked = jnp.concatenate([masked] * 3, axis=0)
        parts = []
        for group in range(KEY_VALUE_HEADS):
            lanes = slice(LANES * group, LANES * group + LANES)
            scores = times_transposed(heads_of(queries, rows, group), keys[key_rows, lanes])
            scores = scores + masked
            top = jnp.max(scores, axis=-1, keepdims=True)
            powers = jnp.exp(scores - top)
            found = powers * (1.0 / jnp.sum(powers, axis=-1, keepdims=True))
            probs[mb, group] = found
            out = product(found.astype(BF16), values[key_rows, lanes])
            outs[mb, group] = out
            parts += [out[ROWS * k : ROWS * k + ROWS] for k in range(3)]
        for k, tile in enumerate(tiles_of_heads(parts)):
            attended[rows, LANES * k : LANES * k + LANES] = tile.astype(BF16)

    for copy in other_blocks:
        copy.wait()
    for k in range(8):
        place_rows(w_down, head_tile(24 + k), tail_tile(24 + k), 192 * k)
    for ref, base in ((w_gate, 8), (w_up, 16)):
        for k in range(4):
            for i in range(6):
                if i < 4:
                    even = head_tile(base + 2 * k)[144 * i : 144 * i + 144, :].astype(F32)
                    odd = head_tile(base + 2 * k + 1)[144 * i : 144 * i + 144, :].astype(F32)
                else:
                    even = tail_tile(base + 2 * k)[144 * (i - 4) : 144 * (i - 4) + 144, :].astype(F32)
                    odd = tail_tile(base + 2 * k + 1)[144 * (i - 4) : 144 * (i - 4) + 144, :].astype(F32)
                ref[144 * k : 144 * k + 144, 256 * i : 256 * i + 128] = jnp.concatenate(
                    [even[0:72], odd[0:72]], axis=0
                ).astype(BF16)
                ref[144 * k : 144 * k + 144, 256 * i + 128 : 256 * i + 256] = jnp.concatenate(
                    [even[72:144], odd[72:144]], axis=0
                ).astype(BF16)

    lane = lax.broadcasted_iota(jnp.int32, (2 * ROWS, WIDE), 1)
    x_own = tokens_pair[0][0].astype(F32).reshape(2 * ROWS, WIDE)
    x_own = jnp.where(lane < MODEL_WIDTH, x_own, 0.0)
    resid_mid = x_own + product(attended[...], w_out[...])
    normed_two, scale_two = normed_rows(resid_mid)
    hidden_two = (normed_two * gain_two).astype(BF16)
    hidden_turned = hidden_two.T
    grad_low = grad_ref[...]
    block_acc[...] = resid_mid
    d_hidden[...] = jnp.zeros_like(d_hidden)

    def store_pair(at, even, odd, table, first):
        rows = pl.ds(pl.multiple_of(slots[table + at] + first, 16), even.shape[0])
        both_all[1 - core, rows, :] = even.astype(BF16)
        both_all[core, rows, :] = odd.astype(BF16)

    def feed_forward(chunk, first, table):
        cols = slice(chunk * 512, chunk * 512 + 512)
        gate = product(hidden_two, w_gate[:, cols])
        up = product(hidden_two, w_up[:, cols])
        sigma = 1.0 / (1.0 + jnp.exp(-gate))
        act = (gate * sigma * up).astype(BF16)
        act_all[:, cols] = act
        down = w_down[cols, :]
        d_act = times_transposed(grad_low, down)
        block_acc[...] += product(act, down)
        d_up = (d_act * gate * sigma).astype(BF16)
        d_gate = (d_act * up * sigma * (1.0 + gate * (1.0 - sigma))).astype(BF16)
        d_hidden[...] += times_transposed(d_gate, w_gate[:, cols]) + times_transposed(d_up, w_up[:, cols])
        for base, cotangent in ((4, d_gate), (8, d_up)):
            made = product(hidden_turned, cotangent)
            for k in range(4):
                part = made[144 * k : 144 * k + 144, :]
                even = jnp.concatenate([part[0:72, LANES * j : LANES * j + LANES] for j in range(4)], axis=0)
                odd = jnp.concatenate([part[72:144, LANES * j : LANES * j + LANES] for j in range(4)], axis=0)
                store_pair(base + k, even, odd, table, (chunk - first) * 288)

    feed_forward(0, 0, TO_HEAD)
    feed_forward(1, 0, TO_HEAD)
    feed_forward(2, 2, TO_TAIL)

    def store_rows(at, even, odd):
        even_head, even_tail = even
        odd_head, odd_tail = odd
        store_pair(at, even_head, odd_head, TO_HEAD, 0)
        store_pair(at, even_tail, odd_tail, TO_TAIL, 0)

    for k in range(0, 4):
        made = rows_product(act_all[:, pl.ds(k * 384, 384)], grad_low)
        store_rows(12 + k, tiles_of_rows(made[0:192]), tiles_of_rows(made[192:384]))

    def deliveries(z, sem):
        copies = []
        inside = pl.multiple_of(HEAD_ROWS * lax.rem(z + 4 - place, 4), HEAD_ROWS)
        for base, outs_of in ((both_all.at[0], parts_out[0:4]), (both_all.at[1], parts_out[4:10])):
            rest = [(outs_of[2], PART * k) for k in range(3)] if len(outs_of) == 4 else [(out, 0) for out in outs_of[2:5]]
            targets = [(outs_of[0], 0, FIRST_AT), (outs_of[1], 0, TAIL_AT)]
            targets += [(out, into, PART * k) for k, (out, into) in enumerate(rest)]
            targets.append((outs_of[-1], 0, 3 * PART))
            for out, into, start in targets:
                copies.append(
                    pltpu.make_async_copy(
                        base.at[pl.ds(pl.multiple_of(start + inside, 16), HEAD_ROWS)],
                        out.at[pl.ds(pl.multiple_of(into + inside, 16), HEAD_ROWS)],
                        out_sems.at[sem + len(copies)],
                    )
                )
        return copies

    early = deliveries(1, 12) + deliveries(2, 24) + deliveries(3, 36)
    for copy in early:
        copy.start()

    for mb in range(2):
        block_out_ref[mb] = block_acc[ROWS * mb : ROWS * mb + ROWS, :].T[0:MODEL_WIDTH].astype(BF16)

    d_two = d_hidden[...]
    gain_two_sum = jnp.sum(d_two * normed_two, axis=0, keepdims=True)
    d_norm = d_two * gain_two
    d_mid = grad_low.astype(F32) + scale_two * (d_norm - normed_two * row_mean(d_norm * normed_two))
    d_branch = d_mid.astype(BF16)
    d_attended[...] = times_transposed(d_branch, w_out[...]).astype(BF16)
    grad_out = rows_product(attended[...], d_branch)

    for mb in range(0, 2):
        rows = pl.ds(mb * ROWS, ROWS)
        key_rows = pl.ds(mb * 512, 512)
        parts = []
        d_keys = []
        d_values = []
        for group in range(KEY_VALUE_HEADS):
            lanes = slice(LANES * group, LANES * group + LANES)
            query_rows = heads_of(queries, rows, group)
            cotangent = heads_of(d_attended, rows, group)
            found = probs[mb, group]
            d_probs = times_transposed(cotangent, values[key_rows, lanes])
            delta = jnp.sum(outs[mb, group] * cotangent.astype(F32), axis=-1, keepdims=True)
            d_scores = (found * (d_probs - delta)).astype(BF16)
            out = product(d_scores, keys[key_rows, lanes]) * HEAD_SIZE ** (-0.5)
            parts += [out[ROWS * k : ROWS * k + ROWS] for k in range(3)]
            d_key = rows_product(d_scores, query_rows)
            d_value = rows_product(found.astype(BF16), cotangent)
            d_keys.append(d_key + half_turn(d_key))
            d_values.append(d_value + half_turn(d_value))
        cosines, sines = cos_pair[0][0, mb], sin_pair[0][0, mb]
        for k, tile in enumerate(tiles_of_heads(parts)):
            d_query[rows, LANES * k : LANES * k + LANES] = rope_back(tile, cosines, sines).astype(BF16)
        low_keys = lower_lanes((512, LANES))
        cosines = jnp.concatenate([at_slot(cos_pair, slot)[mb] for slot in range(4)], axis=0)
        sines = jnp.concatenate([at_slot(sin_pair, slot)[mb] for slot in range(4)], axis=0)
        key_a = rope_back(jnp.where(low_keys, d_keys[0], d_keys[1]), cosines, sines)
        key_b = rope_back(d_keys[2], cosines, sines)
        dkv_all[key_rows, 0:128] = key_a.astype(BF16)
        dkv_all[key_rows, 128:256] = jnp.where(low_keys, d_values[0], d_values[1]).astype(BF16)
        dkv_all[key_rows, 256:384] = jnp.where(low_keys, key_b, d_values[2]).astype(BF16)
        for slot in range(4):
            target = dkv_send if slot % 2 else dkv_keep
            target[slot // 2, mb] = dkv_all[pl.ds(mb * 512 + slot * ROWS, ROWS), :]

    dkv = dkv_all[...]
    d_q = d_query[...]
    dq_wq = times_transposed(d_q, w_q[...])
    normed = jnp.concatenate([normed_all[512 * mb : 512 * mb + ROWS, :] for mb in range(2)], axis=0)
    scale = lax.rsqrt(row_mean(x_own * x_own) + EPS_NORM)
    d_norm = dq_wq * gain_one
    base_ref[...] = d_mid + scale * (d_norm - normed * row_mean(d_norm * normed))
    bias_q_sum = jnp.sum(d_q.astype(F32), axis=0, keepdims=True)
    bias_kv_sum = jnp.sum(dkv.astype(F32), axis=0, keepdims=True)
    gain_sum = jnp.zeros((1, WIDE), F32)
    for mb in range(2):
        gain_sum += jnp.sum(dq_wq[ROWS * mb : ROWS * mb + ROWS] * normed_all[512 * mb : 512 * mb + ROWS, :], axis=0, keepdims=True)
    for k in range(4):
        part = slice(256 * k, 256 * k + 256)
        gain_sum += jnp.sum(times_transposed(dkv_all[part, :], w_kv[...]) * normed_all[part, :], axis=0, keepdims=True)

    hidden_own = jnp.concatenate([hidden_all[0:ROWS, :], hidden_all[512 : 512 + ROWS, :]], axis=0)
    grad_q = rows_product(hidden_own, d_q)
    grad_kv = rows_product(hidden_all[...], dkv)
    rest = grad_kv[0:576, 256:384]
    low = lower_lanes((288, LANES))
    key_tiles = (grad_kv[0:576, 0:128], jnp.where(low, rest[0:288], half_turn(rest[288:576])))
    value_tiles = (grad_kv[0:576, 128:256], jnp.where(low, half_turn(rest[0:288]), rest[288:576]))
    query_tiles = [tiles_of_rows(grad_q[192 * k : 192 * k + 192]) for k in range(3)]
    out_tiles = [tiles_of_rows(grad_out[192 * k : 192 * k + 192]) for k in range(3)]
    store_rows(0, query_tiles[0], query_tiles[1])
    store_rows(1, query_tiles[2], key_tiles)
    store_rows(2, value_tiles, out_tiles[0])
    store_rows(3, out_tiles[1], out_tiles[2])
    def flat_rows(first, second, third, pair):
        tile = lambda row, k: row[:, LANES * k : LANES * k + LANES]
        low = lower_lanes((1, LANES))
        across_two = lambda one, two: jnp.where(low, half_turn(one), half_turn(two))
        lines = [tile(first, k) for k in range(4)]
        lines.append(side_by_side(tile(first, 4), tile(second, 0)))
        lines += [across_two(tile(second, k), tile(second, k + 1)) for k in range(4)]
        lines += [tile(third, k) for k in range(4)]
        lines.append(side_by_side(tile(third, 4), tile(pair, 0)))
        lines.append(across_two(tile(pair, 0), tile(pair, 2)))
        lines.append(tile(pair, 1))
        lines.append(jnp.where(low, half_turn(tile(pair, 2)), 0.0))
        return lines

    at = FIRST_AT + PART
    for row, line in enumerate(flat_rows(gain_sum, gain_two_sum, bias_q_sum, bias_kv_sum)):
        vector_ref[row : row + 1, :] = line
    vector_ref[17:24, :] = jnp.zeros((7, LANES), F32)
    vector = vector_ref[...]
    high = vector.astype(BF16).astype(F32)
    both = jnp.concatenate([high, vector - high], axis=0).astype(BF16)
    for k in range(2):
        both_all[k, at : at + 2 * VECTOR_ROWS, :] = both
    last = deliveries(0, 0)
    last.append(pltpu.make_async_copy(both_all.at[0, pl.ds(at, 2 * VECTOR_ROWS)], parts_out[0].at[pl.ds(PART, 2 * VECTOR_ROWS)], out_sems.at[48]))
    last.append(pltpu.make_async_copy(both_all.at[1, pl.ds(at, 2 * VECTOR_ROWS)], parts_out[4].at[pl.ds(PART, 2 * VECTOR_ROWS)], out_sems.at[49]))
    for copy in last:
        copy.start()
    for copy in early + last:
        copy.wait()


def run_layer(slots, heads, tails, *others):
    shape = jax.ShapeDtypeStruct
    vmem = pl.BlockSpec(memory_space=pltpu.VMEM)
    anywhere = pl.BlockSpec(memory_space=pl.ANY)
    scratch = [
        ((BLOCKS, HEAD_ROWS, LANES), BF16),
        ((BLOCKS, TAIL_ROWS, LANES), BF16),
        ((WIDE, WIDE), BF16),
        ((WIDE, WIDE), BF16),
        ((WIDE, FF), BF16),
        ((WIDE, FF), BF16),
        ((FF, WIDE), BF16),
        ((1024, WIDE), F32),
        ((1024, WIDE), BF16),
        ((1024, 384), BF16),
        ((1024, 384), BF16),
        ((256, WIDE), BF16),
        ((2, 3, 384, 512), F32),
        ((256, WIDE), BF16),
        ((256, FF), BF16),
        ((256, WIDE), F32),
        ((256, WIDE), F32),
        ((256, WIDE), BF16),
        ((1024, 384), BF16),
        ((256, WIDE), BF16),
        ((2, ALL_ROWS, LANES), BF16),
        ((VECTOR_ROWS, LANES), F32),
        ((2, 3, 384, LANES), F32),
    ]
    return pl.pallas_call(
        layer_kernel,
        out_shape=(
            shape((2, MODEL_WIDTH, ROWS), BF16),
            *[shape((count, LANES), BF16) for _, count in SEND_PARTS + KEEP_PARTS],
            shape((2, 2, ROWS, 384), BF16),
            shape((2, 2, ROWS, 384), BF16),
            shape((256, WIDE), F32),
            shape((WIDE, 384), BF16),
        ),
        in_specs=[pl.BlockSpec(memory_space=pltpu.SMEM)] + [anywhere] * 12 + [vmem] * 12,
        out_specs=(vmem,) + (anywhere,) * 10 + (vmem,) * 4,
        scratch_shapes=[pltpu.VMEM(dims, kind) for dims, kind in scratch]
        + [pltpu.SemaphoreType.DMA((48,)), pltpu.SemaphoreType.DMA((50,))],
        compiler_params=pltpu.CompilerParams(vmem_limit_bytes=50 * 1024 * 1024),
        name="layer",
    )(slots, *heads, *tails, *others)


def adamw(param, grad, mom_one, mom_two, rate, decay):
    new_one = BETA_ONE * mom_one + (1.0 - BETA_ONE) * grad
    new_two = BETA_TWO * mom_two + (1.0 - BETA_TWO) * grad * grad
    fixed_one = new_one / (1.0 - BETA_ONE**STEP)
    fixed_two = new_two / (1.0 - BETA_TWO**STEP)
    new_param = param - rate * (fixed_one / (jnp.sqrt(fixed_two) + EPS_ADAM) + decay * param)
    return (new_param, new_one, new_two)


def inner_groups():
    inner = inner_count()
    data_inner = inner // lax.axis_size("ctx")
    data_count = lax.axis_size("dp")
    return [list(range(k, k + data_inner)) for k in range(0, data_count, data_inner)]


def whole_block(flat):
    if inner_count() == 1:
        return flat
    flat = lax.all_gather(flat, "ctx", axis=0, tiled=True)
    return lax.all_gather(flat, "dp", axis=0, tiled=True, axis_index_groups=inner_groups())


def own_slice(block):
    if inner_count() == 1:
        return block
    block = lax.psum_scatter(
        block, "dp", scatter_dimension=0, tiled=True, axis_index_groups=inner_groups()
    )
    return lax.psum_scatter(block, "ctx", scatter_dimension=0, tiled=True)


def bias_tiles(bias_key, bias_value):
    return jnp.concatenate([bias_key[:128], bias_value[:128], bias_key[128:], bias_value[128:]])


def local(tokens_in, places, out_grad, weights, first_moment, second_moment, vectors, vector_first, vector_second):
    kind = kind_of(device_number() // inner_count()).astype(jnp.int32).reshape(1)
    block = whole_block(weights).reshape(BLOCK_ROWS, LANES)
    head, tail = to_tiles(kind, block)

    head, tail, tokens_in, places = together(head, tail, tokens_in, places)
    own_tokens = tokens_in.reshape(2, ROWS, MODEL_WIDTH)
    own_places = places.reshape(2, ROWS)
    marks = jnp.stack([own_places // 16, own_places % 16], axis=-1).astype(BF16)
    packed = jnp.concatenate(
        [own_tokens, marks, jnp.zeros((2, ROWS, WIDE - MODEL_WIDTH - 2), BF16)], axis=-1
    )
    padding = ((0, 0), (0, WIDE - MODEL_WIDTH))
    gains = jnp.pad(vectors[: 2 * MODEL_WIDTH].reshape(2, MODEL_WIDTH), padding)
    bias_q = jnp.pad(vectors[2 * MODEL_WIDTH : 3 * MODEL_WIDTH].reshape(1, MODEL_WIDTH), padding)
    bias_kv = bias_tiles(vectors[1728:1920], vectors[1920:2112]).reshape(1, 384)
    grad = jnp.pad(out_grad.reshape(2 * ROWS, MODEL_WIDTH), padding)
    spare = VECTOR_ROWS * LANES - vectors.shape[0]
    vector_state = [
        jnp.pad(array, (0, spare), constant_values=1.0).reshape(VECTOR_ROWS, LANES)
        for array in (vectors, vector_first, vector_second)
    ]
    table = jnp.concatenate([kind, (coordinates(device_number() // inner_count())["z"]).astype(jnp.int32).reshape(1)])
    others = (slot_table(), gains, bias_q, bias_kv, grad, vector_state, table)
    heads, tails, (near, far), (cosines, sines), others = gather_all(head, tail, packed, others)
    slots, gains, bias_q, bias_kv, grad, vector_state, table = others
    cosines_far, sines_far = place_tables(far)
    place_all = jnp.stack([places_of(near), places_of(far)], axis=1)
    place_q = place_all[0, 0][..., None]
    place_k = jnp.transpose(place_all.reshape(4, 2, ROWS), (1, 0, 2)).reshape(2, 1, 4 * ROWS)

    block_out, *found = run_layer(
        slots, heads, tails, near, far, cosines, cosines_far, sines, sines_far, place_q, place_k, gains, bias_q, bias_kv, grad
    )
    sends, keeps = found[:4], found[4:10]
    dkv_send, dkv_keep, base, w_kv = found[10:]
    parts, pairs = scatter_blocks(sends, keeps, dkv_send, dkv_keep)
    inputs = (packed, gains, w_kv, base, *pairs)
    state = (weights, first_moment, second_moment)
    if inner_count() == 1:
        blocks = [array.reshape(BLOCK_ROWS, LANES) for array in state]
        *updated, input_grad = finish(table, parts, inputs, [*vector_state, *blocks])
        new_vector_state = [array.reshape(-1)[: vectors.shape[0]] for array in updated[:3]]
        new_state = [array.reshape(-1) for array in updated[3:]]
    else:
        block_grad, vector, input_grad = finish(table, parts, inputs, [])
        vector = lax.psum(vector, "ctx")
        vector = lax.psum(vector, "dp", axis_index_groups=inner_groups())
        grad_own = own_slice(block_grad.reshape(-1))
        vector_grad = vector.reshape(-1)[: vectors.shape[0]]
        new_state = adamw(weights, grad_own, first_moment, second_moment, RATE_MATRIX, DECAY)
        new_vector_state = adamw(vectors, vector_grad, vector_first, vector_second, RATE_VECTOR, 0.0)
    shape = tokens_in.shape
    return (
        jnp.transpose(block_out, (0, 2, 1)).reshape(shape),
        jnp.transpose(input_grad, (0, 2, 1)).reshape(shape),
        *new_state,
        *new_vector_state,
    )


def solution(mesh):
    in_specs = (
        P(None, "dp", "ctx", None),
        P(None, "dp", "ctx"),
        P(None, "dp", "ctx", None),
        P(("dp", "ctx")),
        P(("dp", "ctx")),
        P(("dp", "ctx")),
        P(),
        P(),
        P(),
    )
    out_specs = (
        P(None, "dp", "ctx", None),
        P(None, "dp", "ctx", None),
        P(("dp", "ctx")),
        P(("dp", "ctx")),
        P(("dp", "ctx")),
        P(),
        P(),
        P(),
    )
    return jax.shard_map(local, mesh=mesh, in_specs=in_specs, out_specs=out_specs, check_vma=False)
```

```python
import jax
import jax.numpy as jnp
from jax import lax
from jax.experimental import pallas as pl
from jax.experimental.pallas import tpu as pltpu
from jax.sharding import PartitionSpec as P

MODEL_WIDTH = 576
QUERY_HEADS = 9
KEY_VALUE_HEADS = 3
HEAD_SIZE = 64
FF = 1536
STEP = 10

EPS_NORM = 1e-05
THETA = 100000.0
BETA_ONE = 0.9
BETA_TWO = 0.95
EPS_ADAM = 1e-08
RATE_MATRIX = 0.06
RATE_VECTOR = 0.3
DECAY = 0.1
MASKED = -1e30

LANES = 128
WIDE = 640
BLOCKS = 32
BLOCK_ROWS = 864
HEAD_ROWS = 576
TAIL_ROWS = BLOCK_ROWS - HEAD_ROWS
VECTOR_ROWS = 24
PART = 4 * HEAD_ROWS
FIRST_AT = 4 * PART
TAIL_AT = FIRST_AT + PART + 2 * VECTOR_ROWS
ALL_ROWS = TAIL_AT + PART
SEND_PARTS = [(FIRST_AT, PART + 2 * VECTOR_ROWS), (TAIL_AT, PART), (0, 3 * PART), (3 * PART, PART)]
KEEP_PARTS = SEND_PARTS[:2] + [(PART * k, PART) for k in range(4)]
SIZES = {"z": 4, "y": 2, "x": 2, "c": 2}
ROWS = 128
F32 = jnp.float32
BF16 = jnp.bfloat16


def coordinates(number):
    found = {}
    for name in ("c", "x", "y", "z"):
        found[name] = number % SIZES[name]
        number = number // SIZES[name]
    return found


def number_of(found):
    number = 0
    for name in ("z", "y", "x", "c"):
        number = number * SIZES[name] + found[name]
    return number


def device_number():
    return lax.axis_index("dp") * lax.axis_size("ctx") + lax.axis_index("ctx")


def inner_count():
    return lax.axis_size("dp") * lax.axis_size("ctx") // BLOCKS


def moved(buffer, name, shift):
    inner = inner_count()
    pairs = []
    for number in range(BLOCKS):
        found = coordinates(number)
        found[name] = (found[name] + shift) % SIZES[name]
        target = number_of(found)
        pairs += [(number * inner + k, target * inner + k) for k in range(inner)]
    return lax.ppermute(buffer, ("dp", "ctx"), pairs)


def across(buffer, distance):
    count = lax.axis_size("ctx")
    return lax.ppermute(buffer, "ctx", [(i, i ^ distance) for i in range(count)])


def together(*arrays):
    return lax.optimization_barrier(arrays)


def gather_all(head, tail, packed, others):
    hz = [moved(head, "z", s) for s in (1, 2, 3)]
    tx = moved(tail, "x", 1)
    two = across(packed, 2)
    hz, head, tail, tx, two = together(hz[::-1], head, tail, tx, two)
    hz = hz[::-1]
    own = jnp.stack([head] + hz)
    pair = jnp.stack([tail, tx])
    ay = moved(own, "y", 1)
    ax = moved(own, "x", 1)
    near = jnp.stack([packed, two])
    tables = place_tables(near)
    pair, near = together(pair, near)
    tz = [moved(pair, "z", s) for s in (1, 2, 3)]
    own, pair, tz, ax, ay, near, tables, others = together(own, pair, tz[::-1], ax, ay, near, tables, others)
    tz = tz[::-1]
    eight = jnp.concatenate([pair] + tz)
    far = across(near, 1)
    axy = moved(ay, "x", 1)
    ty = moved(eight, "y", 1)
    ac = moved(own, "c", 1)
    acy = moved(ay, "c", 1)
    acx = moved(ax, "c", 1)
    tc = moved(eight, "c", 1)
    tc, acx, acy, ac, far, ty, axy = together(tc, acx, acy, ac, far, ty, axy)
    acxy = moved(axy, "c", 1)
    tcy = moved(ty, "c", 1)
    heads = [own, ay, ax, axy, ac, acy, acx, acxy]
    return heads, [eight, ty, tc, tcy], (near, far), tables, others


def places_of(tokens):
    found = tokens[..., MODEL_WIDTH : MODEL_WIDTH + 2].astype(F32)
    return found[..., 0] * 16.0 + found[..., 1]


def place_tables(tokens):
    half_dim = HEAD_SIZE // 2
    frequency = THETA ** (-2.0 * jnp.arange(half_dim, dtype=F32) / HEAD_SIZE)
    angles = places_of(tokens)[..., None] * jnp.tile(frequency, 4)
    sign = jnp.where(jnp.arange(LANES) % HEAD_SIZE < half_dim, -1.0, 1.0).astype(F32)
    return jnp.cos(angles), jnp.sin(angles) * sign


def fold(order, relative):
    slot = 0
    for name in order:
        slot = slot * SIZES[name] + relative[name]
    return slot


def head_row(slot, z, _):
    return slot * PART + jnp.where(slot < 3, 0, FIRST_AT - 3 * PART) + z * HEAD_ROWS


def tail_row(slot, z, inside):
    return jnp.where(slot < 1, 3 * PART, TAIL_AT) + (2 * z + inside) * TAIL_ROWS


def slot_table():
    mine = coordinates(device_number() // inner_count())
    entries = []
    for order in (("c", "x", "y", "z"), ("c", "y", "z", "x")):
        for number in range(BLOCKS):
            found = coordinates(number)
            entries.append(fold(order, {n: (mine[n] - found[n]) % SIZES[n] for n in SIZES}))
    for order, start in ((("x", "y"), head_row), (("y",), tail_row)):
        for number in range(0, BLOCKS, 2):
            found = coordinates(number)
            slot = fold(order, {n: (found[n] - mine[n]) % SIZES[n] for n in SIZES})
            inside = (found["x"] - mine["x"]) % SIZES["x"]
            entries.append(start(slot, (found["z"] - mine["z"]) % SIZES["z"], inside))
    entries.append(mine["c"])
    entries.append(mine["z"])
    return jnp.stack([jnp.asarray(entry, jnp.int32) for entry in entries])


AT_HEAD, AT_TAIL, TO_HEAD, TO_TAIL = 0, BLOCKS, 2 * BLOCKS, 2 * BLOCKS + 16
MY_CORE, MY_Z = 2 * BLOCKS + 32, 2 * BLOCKS + 33


def summed(*parts):
    total = parts[0].astype(F32)
    for part in parts[1:]:
        total = total + part.astype(F32)
    return total


def summed_vector(mine, other):
    total = summed(mine[:VECTOR_ROWS], other[:VECTOR_ROWS]) + summed(mine[VECTOR_ROWS:], other[VECTOR_ROWS:])
    high = lax.reduce_precision(total, 8, 7)
    return jnp.concatenate([high.astype(BF16), (total - high).astype(BF16)])


def scatter_blocks(sends, keeps, dkv_send, dkv_keep):
    keep_head, keep_tail, keep_low, keep_mid, keep_far, keep_rest = keeps
    got_head, got_tail = moved(sends[0], "c", 1), moved(sends[1], "c", 1)
    got_head, got_tail, rest_head, rest_tail, dkv_send = together(got_head, got_tail, *sends[2:], dkv_send)
    got_rest_head, got_rest_tail = moved(rest_head, "c", 1), moved(rest_tail, "c", 1)
    got_dkv = across(dkv_send, 1)
    vector = summed_vector(keep_head[PART:], got_head[PART:])
    hx = jnp.concatenate([summed(keep_head[:PART], got_head[:PART]).astype(BF16), vector])
    ty = summed(keep_tail, got_tail).astype(BF16)
    got_hx = moved(hx, "x", 1)
    got_ty = moved(ty, "y", 1)
    low, mid, far = [
        summed(keep, got_rest_head[PART * k : PART * k + PART]).astype(BF16)
        for k, keep in enumerate((keep_low, keep_mid, keep_far))
    ]
    tail = summed(keep_rest, got_rest_tail).astype(BF16)
    dkv = summed(dkv_keep, got_dkv).astype(BF16)
    got_hx, got_ty, low, mid, far, tail, dkv, vector = together(got_hx, got_ty, low, mid, far, tail, dkv, vector)

    def part_for(array, shift):
        return array[HEAD_ROWS * shift : HEAD_ROWS * shift + HEAD_ROWS]

    vector = summed_vector(vector, got_hx[PART:])
    hy = jnp.concatenate([summed(mid, got_hx[:PART]).astype(BF16), vector])
    tz = [summed(part_for(tail, s), part_for(got_ty, s)).astype(BF16) for s in range(4)]
    got_hy = moved(hy, "y", 1)
    got_far = moved(far, "x", 1)
    got_tz = [moved(tz[s], "z", s) for s in (1, 2, 3)]
    got_tz, got_far, got_hy, low, own_tail, vector, dkv = together(got_tz[::-1], got_far, got_hy, low, tz[0], vector, dkv)
    got_tz = got_tz[::-1]
    vector = summed_vector(vector, got_hy[PART:])
    head = [summed(part_for(low, s), part_for(got_far, s), part_for(got_hy, s)) for s in range(4)]
    got_hz = [moved(jnp.concatenate([head[s].astype(BF16), vector]), "z", s) for s in (1, 2, 3)]
    tx = summed(own_tail[TAIL_ROWS:], *[part[TAIL_ROWS:] for part in got_tz]).astype(BF16)
    own_tail = summed(own_tail[:TAIL_ROWS], *[part[:TAIL_ROWS] for part in got_tz])
    got_tx = moved(tx, "x", 1)
    got_dkv = across(dkv[1], 2)
    return (head[0], *got_hz[::-1], own_tail, got_tx, vector), (dkv[0], got_dkv)


def lower_lanes(shape):
    return lax.broadcasted_iota(jnp.int32, shape, 1) < HEAD_SIZE


def half_turn(value):
    return pltpu.roll(value, HEAD_SIZE, 1)


def side_by_side(left, right):
    return jnp.where(lower_lanes(left.shape), left, half_turn(right))


def kind_of(block):
    return jnp.where(block >= 24, 1, jnp.where(block >= 8, 0, jnp.where((block == 3) | (block == 4), 2, 1)))


def tile_kernel(kind_ref, flat_ref, head_ref, tail_ref, tiles, narrow):
    kind = kind_ref[0]

    @pl.when(kind == 0)
    def _():
        for j in range(12):
            tiles[72 * j : 72 * j + 72, :] = flat_ref[pl.ds(j, 72, stride=12), :]

    @pl.when(kind == 1)
    def _():
        lines = [flat_ref[pl.ds(t, 96, stride=9), :] for t in range(9)]
        turned = [half_turn(line) for line in lines[4:]]
        low = lower_lanes((96, LANES))
        for j in range(4):
            tiles[pl.ds(192 * j, 96, stride=2), :] = lines[j]
            tiles[pl.ds(192 * j + 1, 96, stride=2), :] = jnp.where(low, turned[j], turned[j + 1])
        narrow[pl.ds(0, 96, stride=2), :] = lines[4]
        narrow[pl.ds(1, 96, stride=2), :] = turned[4]
        tiles[768:864, :] = side_by_side(narrow[0:96, :], narrow[96:192, :])

    @pl.when(kind == 2)
    def _():
        lines = [flat_ref[pl.ds(t, 288, stride=3), :] for t in range(3)]
        first, second = half_turn(lines[1]), half_turn(lines[2])
        tiles[pl.ds(0, 288, stride=2), :] = lines[0]
        tiles[pl.ds(1, 288, stride=2), :] = jnp.where(lower_lanes((288, LANES)), first, second)
        narrow[pl.ds(0, 288, stride=2), :] = lines[1]
        narrow[pl.ds(1, 288, stride=2), :] = second
        tiles[576:864, :] = side_by_side(narrow[0:288, :], narrow[288:576, :])

    head_ref[...] = tiles[0:HEAD_ROWS, :].astype(BF16)
    tail_ref[...] = tiles[HEAD_ROWS:BLOCK_ROWS, :].astype(BF16)


def to_tiles(kind, flat):
    return pl.pallas_call(
        tile_kernel,
        out_shape=(
            jax.ShapeDtypeStruct((HEAD_ROWS, LANES), BF16),
            jax.ShapeDtypeStruct((TAIL_ROWS, LANES), BF16),
        ),
        in_specs=[
            pl.BlockSpec(memory_space=pltpu.SMEM),
            pl.BlockSpec(memory_space=pltpu.VMEM),
        ],
        out_specs=(pl.BlockSpec(memory_space=pltpu.VMEM),) * 2,
        scratch_shapes=[
            pltpu.VMEM((BLOCK_ROWS, LANES), F32),
            pltpu.VMEM((HEAD_ROWS, LANES), F32),
        ],
        name="to_tiles",
    )(kind, flat)


def finish_kernel(table_ref, head_ref, three_ref, two_ref, one_ref, tail_ref, other_ref, mine_ref, *refs):
    kind, place = table_ref[0], table_ref[1]
    tiles, narrow, flat_ref, vector_parts = refs[-4:]
    tokens_ref, gains_ref, w_kv_ref, base_ref, own_dkv, other_dkv = refs[:6]
    states = refs[6:-4]
    tiles[0:HEAD_ROWS, :] = (head_ref[...] + one_ref[0:HEAD_ROWS, :].astype(F32)) + (
        two_ref[0:HEAD_ROWS, :].astype(F32) + three_ref[0:HEAD_ROWS, :].astype(F32)
    )
    tiles[HEAD_ROWS:BLOCK_ROWS, :] = tail_ref[...] + other_ref[...].astype(F32)

    for at, ref in enumerate((mine_ref, one_ref, two_ref, three_ref)):
        rows = ref.shape[0]
        part = ref[rows - 2 * VECTOR_ROWS : rows, :].astype(F32)
        vector_parts[at] = part[:VECTOR_ROWS] + part[VECTOR_ROWS:]
    vector = vector_parts[lax.rem(place, 4)]
    for z in (1, 2, 3):
        vector = vector + vector_parts[lax.rem(place + 4 - z, 4)]

    lane = lax.broadcasted_iota(jnp.int32, (2 * ROWS, WIDE), 1)
    x = jnp.where(lane < MODEL_WIDTH, tokens_ref[...].astype(F32).reshape(2 * ROWS, WIDE), 0.0)
    normed, scale = normed_rows(x)
    total = summed(own_dkv[...], other_dkv[...]).reshape(2 * ROWS, 384).astype(BF16)
    d_norm = times_transposed(total, w_kv_ref[...]) * gains_ref[0:1, :]
    d_input = base_ref[...] + scale * (d_norm - normed * row_mean(d_norm * normed))
    out_ref = states[-1]
    for mb in range(2):
        out_ref[mb] = d_input[ROWS * mb : ROWS * mb + ROWS].T[0:MODEL_WIDTH].astype(BF16)

    @pl.when(kind == 0)
    def _():
        for j in range(12):
            flat_ref[pl.ds(j, 72, stride=12), :] = tiles[72 * j : 72 * j + 72, :]

    @pl.when(kind == 1)
    def _():
        low = lower_lanes((96, LANES))
        narrow[0:96, :] = tiles[768:864, :]
        narrow[96:192, :] = half_turn(tiles[768:864, :])
        odd = [half_turn(tiles[pl.ds(192 * j + 1, 96, stride=2), :]) for j in range(4)]
        for j in range(4):
            flat_ref[pl.ds(j, 96, stride=9), :] = tiles[pl.ds(192 * j, 96, stride=2), :]
        flat_ref[pl.ds(4, 96, stride=9), :] = jnp.where(low, narrow[pl.ds(0, 96, stride=2), :], odd[0])
        for j in range(3):
            flat_ref[pl.ds(5 + j, 96, stride=9), :] = jnp.where(low, odd[j], odd[j + 1])
        last = half_turn(narrow[pl.ds(1, 96, stride=2), :])
        flat_ref[pl.ds(8, 96, stride=9), :] = jnp.where(low, odd[3], last)

    @pl.when(kind == 2)
    def _():
        low = lower_lanes((288, LANES))
        narrow[0:288, :] = tiles[576:864, :]
        narrow[288:576, :] = half_turn(tiles[576:864, :])
        odd = half_turn(tiles[pl.ds(1, 288, stride=2), :])
        flat_ref[pl.ds(0, 288, stride=3), :] = tiles[pl.ds(0, 288, stride=2), :]
        flat_ref[pl.ds(1, 288, stride=3), :] = jnp.where(low, narrow[pl.ds(0, 288, stride=2), :], odd)
        last = half_turn(narrow[pl.ds(1, 288, stride=2), :])
        flat_ref[pl.ds(2, 288, stride=3), :] = jnp.where(low, odd, last)


    if len(states) == 3:
        states[0][...], states[1][...] = flat_ref[...], vector
        return
    old_vectors, old_block, new_vectors, new_block = states[0:3], states[3:6], states[6:9], states[9:12]
    found = adamw(old_vectors[0][...], vector, old_vectors[1][...], old_vectors[2][...], RATE_VECTOR, 0.0)
    for ref, value in zip(new_vectors, found):
        ref[...] = value

    @pl.loop(0, 6)
    def _(k):
        rows = pl.ds(pl.multiple_of(k * 144, 8), 144)
        found = adamw(
            old_block[0][rows, :], flat_ref[rows, :], old_block[1][rows, :], old_block[2][rows, :], RATE_MATRIX, DECAY
        )
        for ref, value in zip(new_block, found):
            ref[rows, :] = value


def finish(table, parts, inputs, state):
    vmem = pl.BlockSpec(memory_space=pltpu.VMEM)
    flat = jax.ShapeDtypeStruct((BLOCK_ROWS, LANES), F32)
    vector = jax.ShapeDtypeStruct((VECTOR_ROWS, LANES), F32)
    shapes = (vector,) * 3 + (flat,) * 3 if state else (flat, vector)
    shapes += (jax.ShapeDtypeStruct((2, MODEL_WIDTH, ROWS), BF16),)
    return pl.pallas_call(
        finish_kernel,
        out_shape=shapes,
        in_specs=[pl.BlockSpec(memory_space=pltpu.SMEM)] + [vmem] * (len(parts) + len(inputs) + len(state)),
        out_specs=(vmem,) * len(shapes),
        scratch_shapes=[
            pltpu.VMEM((BLOCK_ROWS, LANES), F32),
            pltpu.VMEM((HEAD_ROWS, LANES), F32),
            pltpu.VMEM((BLOCK_ROWS, LANES), F32),
            pltpu.VMEM((4, VECTOR_ROWS, LANES), F32),
        ],
        name="finish",
    )(table, *parts, *inputs, *state)


def product(left, right):
    return jnp.dot(left, right, preferred_element_type=F32)


def times_transposed(left, right):
    return lax.dot_general(left, right, (((1,), (1,)), ((), ())), preferred_element_type=F32)


def rows_product(left, right):
    return lax.dot_general(left, right, (((0,), (0,)), ((), ())), preferred_element_type=F32)


def swapped(value):
    lane = lax.broadcasted_iota(jnp.int32, value.shape, 1)
    return jnp.where(lane % HEAD_SIZE < HEAD_SIZE // 2, pltpu.roll(value, 96, 1), pltpu.roll(value, 32, 1))


def rope(value, cosines, sines):
    return value * cosines + swapped(value) * sines


def rope_back(value, cosines, sines):
    return value * cosines - swapped(value) * sines


def row_mean(value):
    return jnp.sum(value, axis=-1, keepdims=True) * (1.0 / MODEL_WIDTH)


def normed_rows(value):
    scale = lax.rsqrt(row_mean(value * value) + EPS_NORM)
    return value * scale, scale


def place_rows(ref, head_tile, tail_tile, first):
    for j in range(3):
        ref[first : first + 192, LANES * j : LANES * j + LANES] = head_tile[192 * j : 192 * j + 192, :]
    ref[first : first + 192, 384:512] = tail_tile[0:192, :]
    rest = tail_tile[192:288, :].astype(F32)
    low = lower_lanes(rest.shape)
    ref[first : first + 96, 512:640] = jnp.where(low, rest, 0.0).astype(BF16)
    ref[first + 96 : first + 192, 512:640] = jnp.where(low, half_turn(rest), 0.0).astype(BF16)


def tiles_of_rows(value):
    head = jnp.concatenate([value[:, LANES * j : LANES * j + LANES] for j in range(3)], axis=0)
    rest = side_by_side(value[0:96, 512:640], value[96:192, 512:640])
    return head, jnp.concatenate([value[:, 384:512], rest], axis=0)


def layer_kernel(*refs):
    slots = refs[0]
    head_parts = refs[1:9]
    tail_parts = refs[9:13]
    tokens_pair, cos_pair, sin_pair = refs[13:15], refs[15:17], refs[17:19]
    (place_q_ref, place_k_ref, gains_ref, bias_q_ref, bias_kv_ref, grad_ref) = refs[19:25]
    block_out_ref, parts_out = refs[25], refs[26:36]
    (dkv_send, dkv_keep, base_ref, w_kv) = refs[36:40]
    (raw_head, raw_tail, w_q, w_out, w_gate, w_up, w_down, normed_all, hidden_all, keys, values, queries, probs, attended, act_all, block_acc, d_hidden, d_attended, dkv_all, d_query, both_all, vector_ref, outs, sems, out_sems) = refs[40:]

    place = slots[MY_Z]

    def fetches(shift, sem):
        at = lax.rem(place + shift, 4)
        copies = []
        for k, part in enumerate(head_parts):
            copies.append(pltpu.make_async_copy(part.at[at], raw_head.at[4 * k + at], sems.at[sem + k]))
        for k, part in enumerate(tail_parts):
            rows = pl.ds(2 * at, 2)
            copies.append(pltpu.make_async_copy(part.at[rows], raw_tail.at[pl.ds(8 * k + 2 * at, 2)], sems.at[sem + 8 + k]))
        return copies

    attention_blocks = fetches(0, 0)
    other_blocks = fetches(1, 12) + fetches(2, 24) + fetches(3, 36)
    for copy in attention_blocks + other_blocks:
        copy.start()

    core = slots[MY_CORE]

    def at_slot(pair, slot):
        return pair[slot % 2].at[slot // 2]

    def head_tile(block):
        return raw_head.at[slots[AT_HEAD + block]]

    def tail_tile(block):
        return raw_tail.at[slots[AT_TAIL + block]]

    gain_one = gains_ref[0:1, :]
    gain_two = gains_ref[1:2, :]
    low_rows = lower_lanes((ROWS, LANES))

    for mb in range(0, 2):
        lane = lax.broadcasted_iota(jnp.int32, (ROWS, WIDE), 1)
        for slot in range(4):
            rows = pl.ds(mb * 512 + slot * ROWS, ROWS)
            x = jnp.where(lane < MODEL_WIDTH, at_slot(tokens_pair, slot)[mb].astype(F32), 0.0)
            normed, _ = normed_rows(x)
            normed_all[rows, :] = normed
            hidden_all[rows, :] = (normed * gain_one).astype(BF16)

    for copy in attention_blocks:
        copy.wait()
    for ref in (w_q, w_out, w_gate, w_up, w_kv):
        ref[576:640, :] = jnp.zeros((64, ref.shape[1]), BF16)
    for k in range(3):
        place_rows(w_q, head_tile(k), tail_tile(k), 192 * k)
        place_rows(w_out, head_tile(5 + k), tail_tile(5 + k), 192 * k)
    w_kv[0:576, 0:128] = head_tile(3)[...]
    w_kv[0:576, 128:256] = head_tile(4)[...]
    rest_key = tail_tile(3)[...].astype(F32)
    rest_value = tail_tile(4)[...].astype(F32)
    low = lower_lanes(rest_key.shape)
    w_kv[0:288, 256:384] = jnp.where(low, rest_key, half_turn(rest_value)).astype(BF16)
    w_kv[288:576, 256:384] = jnp.where(low, half_turn(rest_key), rest_value).astype(BF16)

    for mb in range(0, 2):
        rows = pl.ds(mb * 512, 512)
        pair = product(hidden_all[rows, :], w_kv[...]) + bias_kv_ref[...]
        cosines = jnp.concatenate([at_slot(cos_pair, slot)[mb] for slot in range(4)], axis=0)
        sines = jnp.concatenate([at_slot(sin_pair, slot)[mb] for slot in range(4)], axis=0)
        key_a = rope(pair[:, 0:128], cosines, sines)
        key_b = rope(pair[:, 256:384], cosines, sines)
        value_a, value_b = pair[:, 128:256], pair[:, 256:384]
        low_keys = lower_lanes((512, LANES))
        turned = half_turn(key_a)
        keys[rows, 0:128] = jnp.where(low_keys, key_a, turned).astype(BF16)
        keys[rows, 128:256] = jnp.where(low_keys, turned, key_a).astype(BF16)
        keys[rows, 256:384] = jnp.where(low_keys, key_b, half_turn(key_b)).astype(BF16)
        turned = half_turn(value_a)
        values[rows, 0:128] = jnp.where(low_keys, value_a, turned).astype(BF16)
        values[rows, 128:256] = jnp.where(low_keys, turned, value_a).astype(BF16)
        values[rows, 256:384] = jnp.where(low_keys, half_turn(value_b), value_b).astype(BF16)

    def heads_of(ref, rows, group):
        stacked = []
        for k in range(3):
            number = 3 * group + k
            tile = ref[rows, LANES * (number // 2) : LANES * (number // 2) + LANES]
            keep = low_rows if number % 2 == 0 else jnp.logical_not(low_rows)
            stacked.append(jnp.where(keep, tile.astype(F32), 0.0).astype(BF16))
        return jnp.concatenate(stacked, axis=0)

    def tiles_of_heads(parts):
        found = [jnp.where(low_rows, parts[2 * k], parts[2 * k + 1]) for k in range(4)]
        return found + [jnp.where(low_rows, parts[8], 0.0)]

    for mb in range(0, 2):
        rows = pl.ds(mb * ROWS, ROWS)
        key_rows = pl.ds(mb * 512, 512)
        cosines, sines = cos_pair[0][0, mb], sin_pair[0][0, mb]
        made = product(hidden_all[pl.ds(mb * 512, ROWS), :], w_q[...]) + bias_q_ref[...]
        for k in range(5):
            turned = rope(made[:, LANES * k : LANES * k + LANES], cosines, sines)
            queries[rows, LANES * k : LANES * k + LANES] = (turned * HEAD_SIZE ** (-0.5)).astype(BF16)
        masked = jnp.where(place_q_ref[mb] >= place_k_ref[mb], 0.0, MASKED)
        masked = jnp.concatenate([masked] * 3, axis=0)
        parts = []
        for group in range(KEY_VALUE_HEADS):
            lanes = slice(LANES * group, LANES * group + LANES)
            scores = times_transposed(heads_of(queries, rows, group), keys[key_rows, lanes])
            scores = scores + masked
            top = jnp.max(scores, axis=-1, keepdims=True)
            powers = jnp.exp(scores - top)
            found = powers * (1.0 / jnp.sum(powers, axis=-1, keepdims=True))
            found = found.astype(BF16)
            probs[mb, group] = found
            out = product(found, values[key_rows, lanes])
            outs[mb, group] = out
            parts += [out[ROWS * k : ROWS * k + ROWS] for k in range(3)]
        for k, tile in enumerate(tiles_of_heads(parts)):
            attended[rows, LANES * k : LANES * k + LANES] = tile.astype(BF16)

    for copy in other_blocks:
        copy.wait()
    for k in range(8):
        place_rows(w_down, head_tile(24 + k), tail_tile(24 + k), 192 * k)
    for ref, base in ((w_gate, 8), (w_up, 16)):
        for k in range(4):
            for i in range(6):
                if i < 4:
                    even = head_tile(base + 2 * k)[144 * i : 144 * i + 144, :].astype(F32)
                    odd = head_tile(base + 2 * k + 1)[144 * i : 144 * i + 144, :].astype(F32)
                else:
                    even = tail_tile(base + 2 * k)[144 * (i - 4) : 144 * (i - 4) + 144, :].astype(F32)
                    odd = tail_tile(base + 2 * k + 1)[144 * (i - 4) : 144 * (i - 4) + 144, :].astype(F32)
                ref[144 * k : 144 * k + 144, 256 * i : 256 * i + 128] = jnp.concatenate(
                    [even[0:72], odd[0:72]], axis=0
                ).astype(BF16)
                ref[144 * k : 144 * k + 144, 256 * i + 128 : 256 * i + 256] = jnp.concatenate(
                    [even[72:144], odd[72:144]], axis=0
                ).astype(BF16)

    lane = lax.broadcasted_iota(jnp.int32, (2 * ROWS, WIDE), 1)
    x_own = tokens_pair[0][0].astype(F32).reshape(2 * ROWS, WIDE)
    x_own = jnp.where(lane < MODEL_WIDTH, x_own, 0.0)
    resid_mid = x_own + product(attended[...], w_out[...])
    normed_two, scale_two = normed_rows(resid_mid)
    hidden_two = (normed_two * gain_two).astype(BF16)
    hidden_turned = hidden_two.T
    grad_low = grad_ref[...]
    block_acc[...] = resid_mid
    d_hidden[...] = jnp.zeros_like(d_hidden)

    def store_pair(at, even, odd, table, first):
        rows = pl.ds(pl.multiple_of(slots[table + at] + first, 16), even.shape[0])
        both_all[1 - core, rows, :] = even.astype(BF16)
        both_all[core, rows, :] = odd.astype(BF16)

    def feed_forward(chunk, first, table):
        cols = slice(chunk * 512, chunk * 512 + 512)
        gate = product(hidden_two, w_gate[:, cols])
        up = product(hidden_two, w_up[:, cols])
        sigma = 1.0 / (1.0 + jnp.exp(-gate))
        act = (gate * sigma * up).astype(BF16)
        act_all[:, cols] = act
        down = w_down[cols, :]
        d_act = times_transposed(grad_low, down)
        block_acc[...] += product(act, down)
        d_up = (d_act * gate * sigma).astype(BF16)
        d_gate = (d_act * up * sigma * (1.0 + gate * (1.0 - sigma))).astype(BF16)
        d_hidden[...] += times_transposed(d_gate, w_gate[:, cols]) + times_transposed(d_up, w_up[:, cols])
        for base, cotangent in ((4, d_gate), (8, d_up)):
            made = product(hidden_turned, cotangent)
            for k in range(4):
                part = made[144 * k : 144 * k + 144, :]
                even = jnp.concatenate([part[0:72, LANES * j : LANES * j + LANES] for j in range(4)], axis=0)
                odd = jnp.concatenate([part[72:144, LANES * j : LANES * j + LANES] for j in range(4)], axis=0)
                store_pair(base + k, even, odd, table, (chunk - first) * 288)

    feed_forward(0, 0, TO_HEAD)
    feed_forward(1, 0, TO_HEAD)
    feed_forward(2, 2, TO_TAIL)

    def store_rows(at, even, odd):
        even_head, even_tail = even
        odd_head, odd_tail = odd
        store_pair(at, even_head, odd_head, TO_HEAD, 0)
        store_pair(at, even_tail, odd_tail, TO_TAIL, 0)

    for k in range(0, 4):
        made = rows_product(act_all[:, pl.ds(k * 384, 384)], grad_low)
        store_rows(12 + k, tiles_of_rows(made[0:192]), tiles_of_rows(made[192:384]))

    def deliveries(z, sem):
        copies = []
        inside = pl.multiple_of(HEAD_ROWS * lax.rem(z + 4 - place, 4), HEAD_ROWS)
        for base, outs_of in ((both_all.at[0], parts_out[0:4]), (both_all.at[1], parts_out[4:10])):
            rest = [(outs_of[2], PART * k) for k in range(3)] if len(outs_of) == 4 else [(out, 0) for out in outs_of[2:5]]
            targets = [(outs_of[0], 0, FIRST_AT), (outs_of[1], 0, TAIL_AT)]
            targets += [(out, into, PART * k) for k, (out, into) in enumerate(rest)]
            targets.append((outs_of[-1], 0, 3 * PART))
            for out, into, start in targets:
                copies.append(
                    pltpu.make_async_copy(
                        base.at[pl.ds(pl.multiple_of(start + inside, 16), HEAD_ROWS)],
                        out.at[pl.ds(pl.multiple_of(into + inside, 16), HEAD_ROWS)],
                        out_sems.at[sem + len(copies)],
                    )
                )
        return copies

    early = deliveries(1, 12) + deliveries(2, 24) + deliveries(3, 36)
    for copy in early:
        copy.start()

    for mb in range(2):
        block_out_ref[mb] = block_acc[ROWS * mb : ROWS * mb + ROWS, :].T[0:MODEL_WIDTH].astype(BF16)

    d_two = d_hidden[...]
    gain_two_sum = jnp.sum(d_two * normed_two, axis=0, keepdims=True)
    d_norm = d_two * gain_two
    d_mid = grad_low.astype(F32) + scale_two * (d_norm - normed_two * row_mean(d_norm * normed_two))
    d_branch = d_mid.astype(BF16)
    d_attended[...] = times_transposed(d_branch, w_out[...]).astype(BF16)
    grad_out = rows_product(attended[...], d_branch)

    for mb in range(0, 2):
        rows = pl.ds(mb * ROWS, ROWS)
        key_rows = pl.ds(mb * 512, 512)
        parts = []
        d_keys = []
        d_values = []
        for group in range(KEY_VALUE_HEADS):
            lanes = slice(LANES * group, LANES * group + LANES)
            query_rows = heads_of(queries, rows, group)
            cotangent = heads_of(d_attended, rows, group)
            found = probs[mb, group]
            d_probs = times_transposed(cotangent, values[key_rows, lanes])
            delta = jnp.sum(outs[mb, group] * cotangent.astype(F32), axis=-1, keepdims=True)
            d_scores = (found.astype(F32) * (d_probs - delta)).astype(BF16)
            out = product(d_scores, keys[key_rows, lanes]) * HEAD_SIZE ** (-0.5)
            parts += [out[ROWS * k : ROWS * k + ROWS] for k in range(3)]
            d_key = rows_product(d_scores, query_rows)
            d_value = rows_product(found, cotangent)
            d_keys.append(d_key + half_turn(d_key))
            d_values.append(d_value + half_turn(d_value))
        cosines, sines = cos_pair[0][0, mb], sin_pair[0][0, mb]
        for k, tile in enumerate(tiles_of_heads(parts)):
            d_query[rows, LANES * k : LANES * k + LANES] = rope_back(tile, cosines, sines).astype(BF16)
        low_keys = lower_lanes((512, LANES))
        cosines = jnp.concatenate([at_slot(cos_pair, slot)[mb] for slot in range(4)], axis=0)
        sines = jnp.concatenate([at_slot(sin_pair, slot)[mb] for slot in range(4)], axis=0)
        key_a = rope_back(jnp.where(low_keys, d_keys[0], d_keys[1]), cosines, sines)
        key_b = rope_back(d_keys[2], cosines, sines)
        dkv_all[key_rows, 0:128] = key_a.astype(BF16)
        dkv_all[key_rows, 128:256] = jnp.where(low_keys, d_values[0], d_values[1]).astype(BF16)
        dkv_all[key_rows, 256:384] = jnp.where(low_keys, key_b, d_values[2]).astype(BF16)
        for slot in range(4):
            target = dkv_send if slot % 2 else dkv_keep
            target[slot // 2, mb] = dkv_all[pl.ds(mb * 512 + slot * ROWS, ROWS), :]

    dkv = dkv_all[...]
    d_q = d_query[...]
    dq_wq = times_transposed(d_q, w_q[...])
    normed = jnp.concatenate([normed_all[512 * mb : 512 * mb + ROWS, :] for mb in range(2)], axis=0)
    scale = lax.rsqrt(row_mean(x_own * x_own) + EPS_NORM)
    d_norm = dq_wq * gain_one
    base_ref[...] = d_mid + scale * (d_norm - normed * row_mean(d_norm * normed))
    bias_q_sum = jnp.sum(d_q.astype(F32), axis=0, keepdims=True)
    bias_kv_sum = jnp.sum(dkv.astype(F32), axis=0, keepdims=True)
    gain_sum = jnp.zeros((1, WIDE), F32)
    for mb in range(2):
        gain_sum += jnp.sum(dq_wq[ROWS * mb : ROWS * mb + ROWS] * normed_all[512 * mb : 512 * mb + ROWS, :], axis=0, keepdims=True)
    for k in range(4):
        part = slice(256 * k, 256 * k + 256)
        gain_sum += jnp.sum(times_transposed(dkv_all[part, :], w_kv[...]) * normed_all[part, :], axis=0, keepdims=True)

    hidden_own = jnp.concatenate([hidden_all[0:ROWS, :], hidden_all[512 : 512 + ROWS, :]], axis=0)
    grad_q = rows_product(hidden_own, d_q)
    grad_kv = rows_product(hidden_all[...], dkv)
    rest = grad_kv[0:576, 256:384]
    low = lower_lanes((288, LANES))
    key_tiles = (grad_kv[0:576, 0:128], jnp.where(low, rest[0:288], half_turn(rest[288:576])))
    value_tiles = (grad_kv[0:576, 128:256], jnp.where(low, half_turn(rest[0:288]), rest[288:576]))
    query_tiles = [tiles_of_rows(grad_q[192 * k : 192 * k + 192]) for k in range(3)]
    out_tiles = [tiles_of_rows(grad_out[192 * k : 192 * k + 192]) for k in range(3)]
    store_rows(0, query_tiles[0], query_tiles[1])
    store_rows(1, query_tiles[2], key_tiles)
    store_rows(2, value_tiles, out_tiles[0])
    store_rows(3, out_tiles[1], out_tiles[2])
    def flat_rows(first, second, third, pair):
        tile = lambda row, k: row[:, LANES * k : LANES * k + LANES]
        low = lower_lanes((1, LANES))
        across_two = lambda one, two: jnp.where(low, half_turn(one), half_turn(two))
        lines = [tile(first, k) for k in range(4)]
        lines.append(side_by_side(tile(first, 4), tile(second, 0)))
        lines += [across_two(tile(second, k), tile(second, k + 1)) for k in range(4)]
        lines += [tile(third, k) for k in range(4)]
        lines.append(side_by_side(tile(third, 4), tile(pair, 0)))
        lines.append(across_two(tile(pair, 0), tile(pair, 2)))
        lines.append(tile(pair, 1))
        lines.append(jnp.where(low, half_turn(tile(pair, 2)), 0.0))
        return lines

    at = FIRST_AT + PART
    for row, line in enumerate(flat_rows(gain_sum, gain_two_sum, bias_q_sum, bias_kv_sum)):
        vector_ref[row : row + 1, :] = line
    vector_ref[17:24, :] = jnp.zeros((7, LANES), F32)
    vector = vector_ref[...]
    high = vector.astype(BF16).astype(F32)
    both = jnp.concatenate([high, vector - high], axis=0).astype(BF16)
    for k in range(2):
        both_all[k, at : at + 2 * VECTOR_ROWS, :] = both
    last = deliveries(0, 0)
    last.append(pltpu.make_async_copy(both_all.at[0, pl.ds(at, 2 * VECTOR_ROWS)], parts_out[0].at[pl.ds(PART, 2 * VECTOR_ROWS)], out_sems.at[48]))
    last.append(pltpu.make_async_copy(both_all.at[1, pl.ds(at, 2 * VECTOR_ROWS)], parts_out[4].at[pl.ds(PART, 2 * VECTOR_ROWS)], out_sems.at[49]))
    for copy in last:
        copy.start()
    for copy in early + last:
        copy.wait()


def run_layer(slots, heads, tails, *others):
    shape = jax.ShapeDtypeStruct
    vmem = pl.BlockSpec(memory_space=pltpu.VMEM)
    anywhere = pl.BlockSpec(memory_space=pl.ANY)
    scratch = [
        ((BLOCKS, HEAD_ROWS, LANES), BF16),
        ((BLOCKS, TAIL_ROWS, LANES), BF16),
        ((WIDE, WIDE), BF16),
        ((WIDE, WIDE), BF16),
        ((WIDE, FF), BF16),
        ((WIDE, FF), BF16),
        ((FF, WIDE), BF16),
        ((1024, WIDE), F32),
        ((1024, WIDE), BF16),
        ((1024, 384), BF16),
        ((1024, 384), BF16),
        ((256, WIDE), BF16),
        ((2, 3, 384, 512), BF16),
        ((256, WIDE), BF16),
        ((256, FF), BF16),
        ((256, WIDE), F32),
        ((256, WIDE), F32),
        ((256, WIDE), BF16),
        ((1024, 384), BF16),
        ((256, WIDE), BF16),
        ((2, ALL_ROWS, LANES), BF16),
        ((VECTOR_ROWS, LANES), F32),
        ((2, 3, 384, LANES), F32),
    ]
    return pl.pallas_call(
        layer_kernel,
        out_shape=(
            shape((2, MODEL_WIDTH, ROWS), BF16),
            *[shape((count, LANES), BF16) for _, count in SEND_PARTS + KEEP_PARTS],
            shape((2, 2, ROWS, 384), BF16),
            shape((2, 2, ROWS, 384), BF16),
            shape((256, WIDE), F32),
            shape((WIDE, 384), BF16),
        ),
        in_specs=[pl.BlockSpec(memory_space=pltpu.SMEM)] + [anywhere] * 12 + [vmem] * 12,
        out_specs=(vmem,) + (anywhere,) * 10 + (vmem,) * 4,
        scratch_shapes=[pltpu.VMEM(dims, kind) for dims, kind in scratch]
        + [pltpu.SemaphoreType.DMA((48,)), pltpu.SemaphoreType.DMA((50,))],
        compiler_params=pltpu.CompilerParams(vmem_limit_bytes=50 * 1024 * 1024),
        name="layer",
    )(slots, *heads, *tails, *others)


def adamw(param, grad, mom_one, mom_two, rate, decay):
    new_one = BETA_ONE * mom_one + (1.0 - BETA_ONE) * grad
    new_two = BETA_TWO * mom_two + (1.0 - BETA_TWO) * grad * grad
    fixed_one = new_one / (1.0 - BETA_ONE**STEP)
    fixed_two = new_two / (1.0 - BETA_TWO**STEP)
    new_param = param - rate * (fixed_one / (jnp.sqrt(fixed_two) + EPS_ADAM) + decay * param)
    return (new_param, new_one, new_two)


def inner_groups():
    inner = inner_count()
    data_inner = inner // lax.axis_size("ctx")
    data_count = lax.axis_size("dp")
    return [list(range(k, k + data_inner)) for k in range(0, data_count, data_inner)]


def whole_block(flat):
    if inner_count() == 1:
        return flat
    flat = lax.all_gather(flat, "ctx", axis=0, tiled=True)
    return lax.all_gather(flat, "dp", axis=0, tiled=True, axis_index_groups=inner_groups())


def own_slice(block):
    if inner_count() == 1:
        return block
    block = lax.psum_scatter(
        block, "dp", scatter_dimension=0, tiled=True, axis_index_groups=inner_groups()
    )
    return lax.psum_scatter(block, "ctx", scatter_dimension=0, tiled=True)


def bias_tiles(bias_key, bias_value):
    return jnp.concatenate([bias_key[:128], bias_value[:128], bias_key[128:], bias_value[128:]])


def local(tokens_in, places, out_grad, weights, first_moment, second_moment, vectors, vector_first, vector_second):
    kind = kind_of(device_number() // inner_count()).astype(jnp.int32).reshape(1)
    block = whole_block(weights).reshape(BLOCK_ROWS, LANES)
    head, tail = to_tiles(kind, block)

    head, tail, tokens_in, places = together(head, tail, tokens_in, places)
    own_tokens = tokens_in.reshape(2, ROWS, MODEL_WIDTH)
    own_places = places.reshape(2, ROWS)
    marks = jnp.stack([own_places // 16, own_places % 16], axis=-1).astype(BF16)
    packed = jnp.concatenate(
        [own_tokens, marks, jnp.zeros((2, ROWS, WIDE - MODEL_WIDTH - 2), BF16)], axis=-1
    )
    padding = ((0, 0), (0, WIDE - MODEL_WIDTH))
    gains = jnp.pad(vectors[: 2 * MODEL_WIDTH].reshape(2, MODEL_WIDTH), padding)
    bias_q = jnp.pad(vectors[2 * MODEL_WIDTH : 3 * MODEL_WIDTH].reshape(1, MODEL_WIDTH), padding)
    bias_kv = bias_tiles(vectors[1728:1920], vectors[1920:2112]).reshape(1, 384)
    grad = jnp.pad(out_grad.reshape(2 * ROWS, MODEL_WIDTH), padding)
    spare = VECTOR_ROWS * LANES - vectors.shape[0]
    vector_state = [
        jnp.pad(array, (0, spare), constant_values=1.0).reshape(VECTOR_ROWS, LANES)
        for array in (vectors, vector_first, vector_second)
    ]
    table = jnp.concatenate([kind, (coordinates(device_number() // inner_count())["z"]).astype(jnp.int32).reshape(1)])
    others = (slot_table(), gains, bias_q, bias_kv, grad, vector_state, table)
    heads, tails, (near, far), (cosines, sines), others = gather_all(head, tail, packed, others)
    slots, gains, bias_q, bias_kv, grad, vector_state, table = others
    cosines_far, sines_far = place_tables(far)
    place_all = jnp.stack([places_of(near), places_of(far)], axis=1)
    place_q = place_all[0, 0][..., None]
    place_k = jnp.transpose(place_all.reshape(4, 2, ROWS), (1, 0, 2)).reshape(2, 1, 4 * ROWS)

    block_out, *found = run_layer(
        slots, heads, tails, near, far, cosines, cosines_far, sines, sines_far, place_q, place_k, gains, bias_q, bias_kv, grad
    )
    sends, keeps = found[:4], found[4:10]
    dkv_send, dkv_keep, base, w_kv = found[10:]
    parts, pairs = scatter_blocks(sends, keeps, dkv_send, dkv_keep)
    inputs = (packed, gains, w_kv, base, *pairs)
    state = (weights, first_moment, second_moment)
    if inner_count() == 1:
        blocks = [array.reshape(BLOCK_ROWS, LANES) for array in state]
        *updated, input_grad = finish(table, parts, inputs, [*vector_state, *blocks])
        new_vector_state = [array.reshape(-1)[: vectors.shape[0]] for array in updated[:3]]
        new_state = [array.reshape(-1) for array in updated[3:]]
    else:
        block_grad, vector, input_grad = finish(table, parts, inputs, [])
        vector = lax.psum(vector, "ctx")
        vector = lax.psum(vector, "dp", axis_index_groups=inner_groups())
        grad_own = own_slice(block_grad.reshape(-1))
        vector_grad = vector.reshape(-1)[: vectors.shape[0]]
        new_state = adamw(weights, grad_own, first_moment, second_moment, RATE_MATRIX, DECAY)
        new_vector_state = adamw(vectors, vector_grad, vector_first, vector_second, RATE_VECTOR, 0.0)
    shape = tokens_in.shape
    return (
        jnp.transpose(block_out, (0, 2, 1)).reshape(shape),
        jnp.transpose(input_grad, (0, 2, 1)).reshape(shape),
        *new_state,
        *new_vector_state,
    )


def solution(mesh):
    in_specs = (
        P(None, "dp", "ctx", None),
        P(None, "dp", "ctx"),
        P(None, "dp", "ctx", None),
        P(("dp", "ctx")),
        P(("dp", "ctx")),
        P(("dp", "ctx")),
        P(),
        P(),
        P(),
    )
    out_specs = (
        P(None, "dp", "ctx", None),
        P(None, "dp", "ctx", None),
        P(("dp", "ctx")),
        P(("dp", "ctx")),
        P(("dp", "ctx")),
        P(),
        P(),
        P(),
    )
    return jax.shard_map(local, mesh=mesh, in_specs=in_specs, out_specs=out_specs, check_vma=False)
```
